32 devices in a mesh: tm: 16 (over z, x, core), grp: 2 (over y).
Axes of the slice: x: 2, y: 2, z: 4, core: 2. Of those that a mesh axis runs over, the one named last changes fastest.
Arguments:
- frames_in: bfloat16 [256, 32, 8, 256], P('tm', 'grp'), may hold values from -6 to 6
- span_frames: int32 [16], P('tm'), may hold values from 5 to 13, as said below
- w_spatial: bfloat16 [3, 3, 256, 256], replicated, may hold values from -0.125 to 0.125
- w_temporal: bfloat16 [3, 256, 256], replicated, may hold values from -0.21875 to 0.21875
- w_down: bfloat16 [2, 2, 256, 256], replicated, may hold values from -0.1875 to 0.1875
- cotangent: bfloat16 [256, 16, 4, 256], P('tm', 'grp'), may hold values from -6 to 6
Outputs:
- down_out: bfloat16 [256, 16, 4, 256], P('tm', 'grp')
- grad_x: bfloat16 [256, 32, 8, 256], P('tm', 'grp')
- grad_spatial: float32 [3, 3, 256, 256], replicated
- grad_temporal: float32 [3, 256, 256], replicated
- grad_down: float32 [2, 2, 256, 256], replicated
The draws below stay inside these ranges and needn't reach their ends.
Inputs may be any that keep to these rules, and one draw needn't show every extreme that they name: `span_frames`: each entry is 1 + 4k for a whole k >= 1; some time block uses the largest count 16 - 3.
All inputs are finite; a program needn't handle non-finite values.
Results may differ from the reference program's by a relative error of at most 0.01.
Values may be sent and summed in bfloat16 or wider, within the bound.
No kernel may reach another device: no remote copies, remote signals or barrier semaphores. Data moves between devices by JAX's collectives and lax.ppermute only.
A program may use at most 64 MiB of HBM per device.

```python
import jax
import jax.numpy as jnp
from jax import lax

CH = 256
F_CAP = 16
COLS = 8
FRAMES = 256
HEIGHT = 32
N_TM = 16


def draw_span_frames(key, part):
    key = jax.random.fold_in(key, 7)
    steps_key, chosen_key = jax.random.split(key)
    largest = (F_CAP - 4) // 4
    multiples = jax.random.randint(steps_key, (N_TM,), 1, largest + 1)
    chosen = jax.random.randint(chosen_key, (), 0, N_TM)
    multiples = jnp.where(jnp.arange(N_TM) == chosen, largest, multiples)
    return (1 + 4 * multiples).astype(jnp.int32)


def levels(stream_key, shape, cuts, low, high):
    factor_of = 1.0
    for position, shards_of in cuts:
        heights = jax.random.uniform(jax.random.fold_in(jax.random.fold_in(stream_key, 6), position), (shards_of,), jnp.float32, low / len(cuts), high / len(cuts))
        factor_of = factor_of * jnp.repeat(jnp.exp(heights), shape[position] // shards_of).reshape((-1,) + (1,) * (len(shape) - 1 - position))
    return factor_of


def centred(own_key, shape, deviation, limit, shards=(), kind=jnp.bfloat16):
    entries = deviation * jax.random.normal(own_key, shape, jnp.float32)
    if shards:
        entries = entries * levels(own_key, shape, shards, -0.22, 0.18)
    return jnp.clip(entries, -limit, limit).astype(kind)


def setup_inputs(seed: int = 0) -> dict:
    streams_of = jax.random.split(jax.random.key(seed), 7)
    return {
        "frames_in": centred(streams_of[0], (FRAMES, HEIGHT, COLS, CH), 1.0, 6.0, ((0, 16), (1, 2))),
        "span_frames": draw_span_frames(jax.random.fold_in(streams_of[6], 71), 0),
        "w_spatial": centred(streams_of[2], (3, 3, CH, CH), (9 * CH) ** -0.5, 0.125),
        "w_temporal": centred(streams_of[3], (3, CH, CH), (3 * CH) ** -0.5, 0.21875),
        "w_down": centred(streams_of[4], (2, 2, CH, CH), (4 * CH) ** -0.5, 0.1875),
        "cotangent": centred(streams_of[5], (FRAMES, HEIGHT // 2, COLS // 2, CH), 1.0, 6.0, ((0, 16), (1, 2))),
    }


def activate(values):
    scaled = values * lax.rsqrt(lax.optimization_barrier(jnp.mean(values * values, axis=-1, keepdims=True)) + 1e-06)
    return jax.nn.silu(scaled)

def conv_forward(padded, weights, height, width):
    total = None
    for row_off in range(3):
        for col_off in range(3):
            piece = padded[:, row_off:row_off + height, col_off:col_off + width].astype(jnp.float32)
            term = jnp.einsum('fhwc,cd->fhwd', piece, weights[row_off, col_off].astype(jnp.float32))
            total = term if total is None else total + term
    return total

def conv_backward(padded, weights, height, width):
    total = None
    for row_off in range(3):
        for col_off in range(3):
            piece = padded[:, 2 - row_off:2 - row_off + height, 2 - col_off:2 - col_off + width].astype(jnp.float32)
            term = jnp.einsum('fhwd,cd->fhwc', piece, weights[row_off, col_off].astype(jnp.float32))
            total = term if total is None else total + term
    return total

def spatial_grad(padded, grads, height, width):
    rows_out = []
    for row_off in range(3):
        cols_out = []
        for col_off in range(3):
            piece = padded[:, row_off:row_off + height, col_off:col_off + width].astype(jnp.float32)
            cols_out.append(jnp.einsum('fhwc,fhwd->cd', piece, grads.astype(jnp.float32)))
        rows_out.append(jnp.stack(cols_out))
    return jnp.stack(rows_out)

def place(grads, incoming, count):
    anchor = count * 0
    return lax.dynamic_update_slice(grads, incoming, (count, anchor, anchor, anchor))

def reference(frames_in, span_frames, w_spatial, w_temporal, w_down, cotangent):
    frame_ids = jnp.arange(FRAMES, dtype=jnp.int32)
    valid = (frame_ids % F_CAP < span_frames[frame_ids // F_CAP]).astype(jnp.float32)[:, None, None, None]
    x_float = frames_in.astype(jnp.float32)
    activated, pullback = jax.vjp(activate, x_float)
    acts = (activated * valid).astype(jnp.bfloat16)
    acts_pad = jnp.pad(acts, ((0, 0), (1, 1), (1, 1), (0, 0)))
    spatial = conv_forward(acts_pad, w_spatial, HEIGHT, COLS).astype(jnp.bfloat16)
    spat_spans = spatial.reshape(N_TM, F_CAP, HEIGHT, COLS, CH)
    picks = span_frames[:, None] - 2 + jnp.arange(2, dtype=jnp.int32)[None, :]
    edge_frames = jnp.take_along_axis(spat_spans, picks[:, :, None, None, None], axis=1)
    previous = jnp.concatenate([jnp.zeros((1, 2, HEIGHT, COLS, CH), jnp.bfloat16), edge_frames[:-1]], 0)
    extended = jnp.concatenate([previous, spat_spans], 1)
    temporal_sum = None
    for k in range(3):
        term = jnp.einsum('nfhwc,cd->nfhwd', extended[:, k:k + F_CAP].astype(jnp.float32), w_temporal[k].astype(jnp.float32))
        temporal_sum = term if temporal_sum is None else temporal_sum + term
    temporal_sum = temporal_sum.reshape(FRAMES, HEIGHT, COLS, CH)
    y_out = ((x_float + temporal_sum) * valid).astype(jnp.bfloat16)
    y_blocks = y_out.reshape(FRAMES, HEIGHT // 2, 2, COLS // 2, 2, CH).astype(jnp.float32)
    cot_float = cotangent.astype(jnp.float32)
    down_float = w_down.astype(jnp.float32)
    down_out = jnp.einsum('fiajbc,abcd->fijd', y_blocks, down_float).astype(jnp.bfloat16)
    grad_pre = jnp.einsum('fijd,abcd->fiajbc', cot_float, down_float).reshape(FRAMES, HEIGHT, COLS, CH)
    grad_y = (grad_pre * valid).astype(jnp.bfloat16)
    grad_down = jnp.einsum('fiajbc,fijd->abcd', y_blocks, cot_float)
    grad_spans = grad_y.reshape(N_TM, F_CAP, HEIGHT, COLS, CH)
    incoming = jnp.concatenate([grad_spans[1:, :2], jnp.zeros((1, 2, HEIGHT, COLS, CH), jnp.bfloat16)], 0)
    padded_grads = jnp.concatenate([grad_spans, jnp.zeros((N_TM, 2, HEIGHT, COLS, CH), jnp.bfloat16)], 1)
    placed = jax.vmap(place)(padded_grads, incoming, span_frames)
    grad_sum = None
    for k in range(3):
        term = jnp.einsum('nfhwd,cd->nfhwc', placed[:, 2 - k:2 - k + F_CAP].astype(jnp.float32), w_temporal[k].astype(jnp.float32))
        grad_sum = term if grad_sum is None else grad_sum + term
    grad_s = (grad_sum.reshape(FRAMES, HEIGHT, COLS, CH) * valid).astype(jnp.bfloat16)
    grad_temporal = jnp.stack([jnp.einsum('nfhwc,nfhwd->cd', extended[:, k:k + F_CAP].astype(jnp.float32), grad_spans.astype(jnp.float32)) for k in range(3)])
    grads_pad = jnp.pad(grad_s, ((0, 0), (1, 1), (1, 1), (0, 0)))
    grad_a = conv_backward(grads_pad, w_spatial, HEIGHT, COLS)
    grad_spatial = spatial_grad(acts_pad, grad_s, HEIGHT, COLS)
    grad_x = (grad_y.astype(jnp.float32) + valid * pullback(grad_a)[0]).astype(jnp.bfloat16)
    return (down_out, grad_x, grad_spatial, grad_temporal, grad_down)
```

```python
import functools

import jax
import jax.numpy as jnp
from jax import lax
from jax.experimental import pallas as pl
from jax.experimental.pallas import tpu as pltpu
from jax.sharding import PartitionSpec as P

SLOTS = 16
OWN = 14
CH = 256
BF = jnp.bfloat16
F32 = jnp.float32


def mm(a, b):
    return lax.dot_general(a, b, (((1,), (0,)), ((), ())), preferred_element_type=F32)


def mm_nt(a, b):
    return lax.dot_general(a, b, (((1,), (1,)), ((), ())), preferred_element_type=F32)


def iotas(rows, cols):
    return (
        lax.broadcasted_iota(jnp.int32, (rows, cols), 0),
        lax.broadcasted_iota(jnp.int32, (rows, cols), 1),
    )


def to_slots(rows, frames, keep):
    a, b = iotas(rows * SLOTS, frames * rows)
    hit = (a // SLOTS == b % rows) & keep(b // rows, a % SLOTS)
    return jnp.where(hit, 1.0, 0.0).astype(BF)


def to_frames(rows):
    a, b = iotas(SLOTS * rows, rows * SLOTS)
    hit = (a % rows == b // SLOTS) & (a // rows == b % SLOTS)
    return jnp.where(hit, 1.0, 0.0).astype(BF)


def own_frames(count):
    return lambda frame, slot: (frame == slot) & (slot < count)


def own_and_next(count):
    return lambda frame, slot: ((frame < OWN) & (frame == slot) & (slot < count)) | (
        (frame >= OWN) & (slot == count + frame - OWN)
    )


def silu_norm(v):
    scaled = v * lax.rsqrt(jnp.mean(v * v, axis=-1, keepdims=True) + 1e-06)
    return scaled / (1.0 + jnp.exp(-scaled))


def slot_mask(shape, count):
    return lax.broadcasted_iota(jnp.int32, shape, len(shape) - 2) < count


def grad_of_temporal(gy, wt_ref, count):
    n = gy.shape[0]
    flat = gy.reshape(n * SLOTS, CH)
    total = mm_nt(flat, wt_ref[2]).reshape(n, SLOTS, CH)
    for k in (1, 0):
        term = mm_nt(flat, wt_ref[k]).reshape(n, SLOTS, CH)
        total = total + pltpu.roll(term, SLOTS - (2 - k), 1)
    return jnp.where(slot_mask(total.shape, count), total, 0.0).astype(BF)


def first_kernel(
    scal, x_ref, top_ref, bot_ref, cot_ref, nxt_ref, wt_ref, wd_ref,
    xt_ref, acts_ref, cott_ref, gy_ref, gs_ref, gw_ref, at_ref,
):
    count, has_top, has_bot = scal[0], scal[1], scal[2]
    rows, cols = xt_ref.shape[0], xt_ref.shape[1]
    edge = jnp.zeros((rows + 2, SLOTS, CH), BF)
    acts_ref[:, 0] = edge
    acts_ref[:, cols + 1] = edge
    gs_ref[:, 0] = edge[:rows]
    gs_ref[:, cols + 1] = edge[:rows]

    place = to_slots(16, SLOTS, own_frames(count))

    def rows_of(q, _):
        at = pl.multiple_of(q * 16, 16)
        piece = x_ref[:, pl.ds(at, 16), :].reshape(SLOTS * 16, CH)
        v = mm(place, piece)
        xt_ref[pl.ds(2 * q, 2)] = v.astype(BF).reshape(2, cols, SLOTS, CH)
        a = silu_norm(v)
        acts_ref[pl.ds(2 * q + 1, 2), 1 : cols + 1] = a.astype(BF).reshape(2, cols, SLOTS, CH)
        at_ref[:, pl.ds(pl.multiple_of(q * 256 + 128, 128), 256)] = a.T.astype(BF)
        return 0

    lax.fori_loop(0, rows // 2, rows_of, 0)

    place_edge = to_slots(cols, OWN, own_frames(count))
    for ref, flag, row in ((top_ref, has_top, 0), (bot_ref, has_bot, rows + 1)):
        a = silu_norm(mm(place_edge, ref[...])) * flag.astype(F32)
        acts_ref[row, 1 : cols + 1] = a.astype(BF).reshape(cols, SLOTS, CH)
        at_ref[:, row * 128 : row * 128 + 128] = a.T.astype(BF)

    place_next = to_slots(16, SLOTS, own_and_next(count))
    for q in range(rows * cols // 64):
        piece = jnp.concatenate(
            [cot_ref[0:OWN, q * 16 : q * 16 + 16, :], nxt_ref[:, q * 16 : q * 16 + 16, :]], 0
        ).reshape(SLOTS * 16, CH)
        placed = mm(place_next, piece).astype(BF)
        cott_ref[q * 4 : q * 4 + 4] = placed.reshape(4, 4, SLOTS, CH)
        for i in range(2):
            for j in range(2):
                g = mm_nt(placed, wd_ref[i * 2 + j]).astype(BF).reshape(4, 4, SLOTS, CH)
                for r in range(4):
                    for c in range(4):
                        gy_ref[2 * (q * 4 + r) + i, 2 * c + j] = g[r, c]

    def grads_of(q, _):
        g = gy_ref[pl.ds(4 * q, 4)].reshape(4 * cols, SLOTS, CH)
        s = grad_of_temporal(g, wt_ref, count)
        gs_ref[pl.ds(4 * q, 4), 1 : cols + 1] = s.reshape(4, cols, SLOTS, CH)
        return 0

    lax.fori_loop(0, rows // 4, grads_of, 0)

    wide = rows * cols * SLOTS
    for i in range(3):
        for j in range(3):
            right = gs_ref[:, 2 - j : 2 - j + cols].reshape(wide, CH)
            gw_ref[i * 3 + j] = mm(at_ref[:, i * 128 : i * 128 + wide], right).astype(BF)


def spatial_kernel(scal, acts_ref, ws_ref, sp_ref, edge_ref):
    count = scal[0]
    rows, cols = sp_ref.shape[0], sp_ref.shape[1]
    a, b = iotas(32, 256)
    pick = (a // 2 == b // SLOTS) & (b % SLOTS == count - 2 + a % 2)
    pick = jnp.where(pick, 1.0, 0.0).astype(BF)

    def rows_of(q, _):
        total = None
        for i in range(3):
            for j in range(3):
                left = acts_ref[pl.ds(4 * q + i, 4), j : j + cols].reshape(4 * cols * SLOTS, CH)
                term = mm(left, ws_ref[i * 3 + j])
                total = term if total is None else total + term
        out = total.astype(BF)
        sp_ref[pl.ds(4 * q, 4)] = out.reshape(4, cols, SLOTS, CH)
        for half in range(2):
            edge_ref[2 * q + half] = mm(pick, out[half * 256 : half * 256 + 256]).astype(BF)
        return 0

    lax.fori_loop(0, rows // 4, rows_of, 0)


def backward_kernel(
    scal, xt_ref, gy_ref, gs_ref, top_ref, bot_ref, wt_ref, wd_ref, ws_ref, out_ref, pad_ref
):
    count, has_top, has_bot = scal[0], scal[1], scal[2]
    rows, cols = xt_ref.shape[0], xt_ref.shape[1]
    pad_ref[1 : rows + 1] = gs_ref[...]
    place_edge = to_slots(cols // 2, SLOTS, own_and_next(count))
    for ref, flag, i, row in ((top_ref, has_top, 1, 0), (bot_ref, has_bot, 0, rows + 1)):
        placed = mm(place_edge, ref[...]).astype(BF)
        pair = [
            mm_nt(placed, wd_ref[i * 2 + j]).astype(BF).reshape(cols // 2, SLOTS, CH) for j in range(2)
        ]
        g = jnp.stack(pair, axis=1).reshape(cols, SLOTS, CH)
        s = grad_of_temporal(g, wt_ref, count) * flag.astype(BF)
        pad_ref[row, 0] = jnp.zeros((SLOTS, CH), BF)
        pad_ref[row, 1 : cols + 1] = s
        pad_ref[row, cols + 1] = jnp.zeros((SLOTS, CH), BF)

    back = to_frames(16)

    def rows_of(q, _):
        total = None
        for i in range(3):
            for j in range(3):
                left = pad_ref[pl.ds(4 * q + 2 - i, 4), 2 - j : 2 - j + cols].reshape(
                    4 * cols * SLOTS, CH
                )
                term = mm_nt(left, ws_ref[i * 3 + j])
                total = term if total is None else total + term
        v = xt_ref[pl.ds(4 * q, 4)].reshape(4 * cols * SLOTS, CH).astype(F32)
        r = lax.rsqrt(jnp.mean(v * v, axis=-1, keepdims=True) + 1e-06)
        u = v * r
        s = 1.0 / (1.0 + jnp.exp(-u))
        gu = total * (s * (1.0 + u * (1.0 - s)))
        dot = jnp.mean(gu * u, axis=-1, keepdims=True)
        gv = r * (gu - u * dot)
        gx = gy_ref[pl.ds(4 * q, 4)].reshape(4 * cols * SLOTS, CH).astype(F32) + gv
        gx = gx.reshape(4 * cols, SLOTS, CH)
        gx = jnp.where(slot_mask(gx.shape, count), gx, 0.0).astype(BF).reshape(4 * cols * SLOTS, CH)
        for half in range(2):
            o = mm(back, gx[half * 256 : half * 256 + 256]).astype(BF)
            at = pl.multiple_of((2 * q + half) * 16, 16)
            out_ref[:, pl.ds(at, 16), :] = o.reshape(SLOTS, 16, CH)
        return 0

    lax.fori_loop(0, rows // 4, rows_of, 0)


def forward_kernel(
    scal, xt_ref, sp_ref, prev_ref, cott_ref, gy_ref, wt_ref, wd_ref,
    down_ref, gw_ref, y_ref, st_ref, g1_ref, g0_ref, g2_ref,
):
    count = scal[0]
    rows, cols = xt_ref.shape[0], xt_ref.shape[1]
    a, b = iotas(256, 32)
    place = (a // SLOTS == b // 2) & (a % SLOTS == OWN + b % 2)
    place = jnp.where(place, 1.0, 0.0).astype(BF)

    def rows_of(q, _):
        s = sp_ref[pl.ds(2 * q, 2)].reshape(256, CH)
        s = (s.astype(F32) + mm(place, prev_ref[q])).astype(BF)
        st_ref[:, pl.ds(pl.multiple_of(q * 256, 256), 256)] = s.T
        total = mm(s, wt_ref[2]).reshape(2 * cols, SLOTS, CH)
        for k in (1, 0):
            total = total + pltpu.roll(mm(s, wt_ref[k]).reshape(2 * cols, SLOTS, CH), 2 - k, 1)
        x = xt_ref[pl.ds(2 * q, 2)].reshape(2 * cols, SLOTS, CH).astype(F32)
        mask = slot_mask(x.shape, count)
        y = jnp.where(mask, x + total, 0.0).astype(BF)
        y_ref[pl.ds(2 * q, 2)] = y.reshape(2, cols, SLOTS, CH)
        g = gy_ref[pl.ds(2 * q, 2)].reshape(2 * cols, SLOTS, CH).astype(F32)
        g = jnp.where(mask, g, 0.0)
        for ref, k in ((g2_ref, 2), (g1_ref, 1), (g0_ref, 0)):
            shifted = g if k == 2 else pltpu.roll(g, SLOTS - (2 - k), 1)
            ref[pl.ds(2 * q, 2)] = shifted.astype(BF).reshape(2, cols, SLOTS, CH)
        return 0

    lax.fori_loop(0, rows // 2, rows_of, 0)

    wide = rows * cols * SLOTS
    for k, ref in ((0, g0_ref), (1, g1_ref), (2, g2_ref)):
        gw_ref[k] = mm(st_ref[...], ref[...].reshape(wide, CH)).astype(BF)

    small = wide // 4
    total = None
    cot = cott_ref[...].reshape(small, CH)
    for i in range(2):
        for j in range(2):
            tiles = [
                y_ref[2 * r + i, 2 * c + j] for r in range(rows // 2) for c in range(cols // 2)
            ]
            piece = jnp.concatenate(tiles, axis=0)
            term = mm(piece, wd_ref[i * 2 + j])
            total = term if total is None else total + term
            gw_ref[3 + i * 2 + j] = mm(piece.T, cot).astype(BF)
    down = total.astype(BF)
    back = to_frames(16)
    for q in range(small // 256):
        o = mm(back, down[q * 256 : q * 256 + 256]).astype(BF)
        down_ref[:, q * 16 : q * 16 + 16, :] = o.reshape(SLOTS, 16, CH)


def call(kernel, outs, scratch, name, flops, *args):
    specs = [pl.BlockSpec(memory_space=pltpu.SMEM)] + [
        pl.BlockSpec(memory_space=pltpu.VMEM) for _ in args[1:]
    ]
    shapes = [jax.ShapeDtypeStruct(s, BF) for s in outs]
    moved = sum(a.size * a.dtype.itemsize for a in args) + sum(s.size * 2 for s in shapes)
    return pl.pallas_call(
        kernel,
        out_shape=shapes,
        in_specs=specs,
        out_specs=[pl.BlockSpec(memory_space=pltpu.VMEM) for _ in outs],
        scratch_shapes=[pltpu.VMEM(s, BF) for s in scratch],
        compiler_params=pltpu.CompilerParams(vmem_limit_bytes=32 * 2**20),
        cost_estimate=pl.CostEstimate(flops=flops, bytes_accessed=moved, transcendentals=0),
        name=name,
    )(*args)


AXES = ("tm", "grp")


def exchange_plan(tm, grp):
    low = grp.bit_length() - 1
    high = tm.bit_length() - 1
    bits_g = list(range(low))
    bits_t = list(range(low, low + high))
    core, rest = bits_t[0], bits_t[1:]
    first = rest[:1] + bits_g + rest[1:]
    second = rest[1:2] + rest[:1] + bits_g + rest[2:]
    return core, [(core, core)] + list(zip(first, second))


def sum_over_devices(value, tm, grp):
    total = tm * grp
    core, stages = exchange_plan(tm, grp)
    me = lax.axis_index("tm") * grp + lax.axis_index("grp")
    odd = (me >> core) & 1

    def swap(v, stage):
        pairs = [(d, d ^ (1 << stage[(d >> core) & 1])) for d in range(total)]
        return lax.ppermute(v, AXES, pairs)

    def bit_of(stage):
        return jnp.where(odd == 0, (me >> stage[0]) & 1, (me >> stage[1]) & 1)

    halved = []
    for stage in stages:
        rows = value.shape[0]
        if rows % 16 == 0 and rows > 16:
            half = rows // 2
            bit = bit_of(stage)
            keep = lax.dynamic_slice_in_dim(value, bit * half, half, 0)
            send = lax.dynamic_slice_in_dim(value, (1 - bit) * half, half, 0)
            got = swap(send, stage)
            value = (keep.astype(F32) + got.astype(F32)).astype(BF)
            halved.append((stage, bit))
        else:
            value = (value.astype(F32) + swap(value, stage).astype(F32)).astype(BF)
    for stage, bit in reversed(halved):
        got = swap(value, stage)
        value = jnp.where(
            bit == 0, jnp.concatenate([value, got], 0), jnp.concatenate([got, value], 0)
        )
    return value


def along(value, axis, by):
    count = lax.axis_size(axis)
    pairs = [(i, i + by) for i in range(count) if 0 <= i + by < count]
    return lax.ppermute(value, axis, pairs)


def edge_rows(values, rows, members, band):
    frames, wide, _ = values.shape
    flat = (frames * rows, CH)
    if members == 2:
        at = jnp.where(band == 0, wide - rows, 0)
        sent = lax.dynamic_slice_in_dim(values, at, rows, 1).reshape(flat)
        got = lax.ppermute(sent, "grp", [(0, 1), (1, 0)])
        return got, got
    return (
        along(values[:, wide - rows :].reshape(flat), "grp", 1),
        along(values[:, :rows].reshape(flat), "grp", -1),
    )


def body(tm, grp, frames_in, span_frames, w_spatial, w_temporal, w_down, cotangent):
    slots, rows, cols, ch = frames_in.shape
    wide = rows * cols
    x = frames_in.reshape(slots, wide, ch)
    cot = cotangent.reshape(slots, wide // 4, ch)
    ws = w_spatial.reshape(9, ch, ch)
    wd = w_down.reshape(4, ch, ch)
    count = span_frames[0]
    band = lax.axis_index("grp")
    scal = jnp.stack(
        [count, (band > 0).astype(jnp.int32), (band < grp - 1).astype(jnp.int32)]
    )
    tap = 2 * slots * wide * ch * ch

    nxt = along(cot[:2], "tm", -1)
    top, bot = edge_rows(x[:OWN], cols, grp, band)
    cot_all = jnp.concatenate([cot[:OWN], nxt], 0)
    cot_top, cot_bot = edge_rows(cot_all, cols // 2, grp, band)

    tile = (rows, cols, slots, ch)
    xt, acts, cott, gy, gs, gw_s = call(
        first_kernel,
        [tile, (rows + 2, cols + 2, slots, ch), (rows // 2, cols // 2, slots, ch), tile,
         (rows, cols + 2, slots, ch), (9, ch, ch)],
        [(ch, (rows + 2) * 128)],
        "grad_spatial",
        14 * tap,
        scal, x, top, bot, cot, nxt, w_temporal, wd,
    )
    sum_s = sum_over_devices(gw_s.reshape(9 * ch, ch), tm, grp)
    sp, edge = call(
        spatial_kernel, [tile, (rows // 2, 32, ch)], [], "spatial", 9 * tap, scal, acts, ws
    )
    prev = along(edge, "tm", 1)
    (grad_x,) = call(
        backward_kernel,
        [(slots, wide, ch)],
        [(rows + 2, cols + 2, slots, ch)],
        "grad_x",
        10 * tap,
        scal, xt, gy, gs, cot_top, cot_bot, w_temporal, wd, ws,
    )
    down, gw_t = call(
        forward_kernel,
        [(slots, wide // 4, ch), (7, ch, ch)],
        [tile, (ch, slots * wide), tile, tile, tile],
        "forward",
        8 * tap,
        scal, xt, sp, prev, cott, gy, w_temporal, wd,
    )
    sum_t = sum_over_devices(gw_t.reshape(7 * ch, ch), tm, grp).astype(F32)
    return (
        down.reshape(cotangent.shape),
        grad_x.reshape(frames_in.shape),
        sum_s.astype(F32).reshape(w_spatial.shape),
        sum_t[: 3 * ch].reshape(w_temporal.shape),
        sum_t[3 * ch :].reshape(w_down.shape),
    )


def solution(mesh):
    return jax.shard_map(
        functools.partial(body, mesh.shape["tm"], mesh.shape["grp"]),
        mesh=mesh,
        in_specs=(P("tm", "grp", None, None), P("tm"), P(), P(), P(), P("tm", "grp", None, None)),
        out_specs=(P("tm", "grp", None, None), P("tm", "grp", None, None), P(), P(), P()),
        check_vma=False,
    )
```

```python
import functools

import jax
import jax.numpy as jnp
from jax import lax
from jax.experimental import pallas as pl
from jax.experimental.pallas import tpu as pltpu
from jax.sharding import PartitionSpec as P

SLOTS = 16
OWN = 14
CH = 256
BF = jnp.bfloat16
F32 = jnp.float32


def mm(a, b):
    return lax.dot_general(a, b, (((1,), (0,)), ((), ())), preferred_element_type=F32)


def mm_nt(a, b):
    return lax.dot_general(a, b, (((1,), (1,)), ((), ())), preferred_element_type=F32)


def iotas(rows, cols):
    return (
        lax.broadcasted_iota(jnp.int32, (rows, cols), 0),
        lax.broadcasted_iota(jnp.int32, (rows, cols), 1),
    )


def to_slots(rows, frames, keep):
    a, b = iotas(rows * SLOTS, frames * rows)
    hit = (a // SLOTS == b % rows) & keep(b // rows, a % SLOTS)
    return jnp.where(hit, 1.0, 0.0).astype(BF)


def to_frames(rows):
    a, b = iotas(SLOTS * rows, rows * SLOTS)
    hit = (a % rows == b // SLOTS) & (a // rows == b % SLOTS)
    return jnp.where(hit, 1.0, 0.0).astype(BF)


def own_frames(count):
    return lambda frame, slot: (frame == slot) & (slot < count)


def own_and_next(count):
    return lambda frame, slot: ((frame < OWN) & (frame == slot) & (slot < count)) | (
        (frame >= OWN) & (slot == count + frame - OWN)
    )


def silu_norm(v):
    scaled = v * lax.rsqrt(jnp.mean(v * v, axis=-1, keepdims=True) + 1e-06)
    return scaled / (1.0 + jnp.exp(-scaled))


def slot_mask(shape, count):
    return lax.broadcasted_iota(jnp.int32, shape, len(shape) - 2) < count


def grad_of_temporal(gy, wt_ref, count):
    n = gy.shape[0]
    flat = gy.reshape(n * SLOTS, CH)
    total = mm_nt(flat, wt_ref[2]).reshape(n, SLOTS, CH)
    for k in (1, 0):
        term = mm_nt(flat, wt_ref[k]).reshape(n, SLOTS, CH)
        total = total + pltpu.roll(term, SLOTS - (2 - k), 1)
    return jnp.where(slot_mask(total.shape, count), total, 0.0).astype(BF)


def first_kernel(
    scal, x_ref, top_ref, bot_ref, cot_ref, nxt_ref, wt_ref, wd_ref,
    xt_ref, acts_ref, cott_ref, gy_ref, gs_ref, gw_ref, at_ref,
):
    count, has_top, has_bot = scal[0], scal[1], scal[2]
    rows, cols = xt_ref.shape[0], xt_ref.shape[1]
    edge = jnp.zeros((rows + 2, SLOTS, CH), BF)
    acts_ref[:, 0] = edge
    acts_ref[:, cols + 1] = edge
    gs_ref[:, 0] = edge[:rows]
    gs_ref[:, cols + 1] = edge[:rows]

    place = to_slots(16, SLOTS, own_frames(count))

    def rows_of(q, _):
        at = pl.multiple_of(q * 16, 16)
        piece = x_ref[:, pl.ds(at, 16), :].reshape(SLOTS * 16, CH)
        v = mm(place, piece)
        xt_ref[pl.ds(2 * q, 2)] = v.astype(BF).reshape(2, cols, SLOTS, CH)
        a = silu_norm(v)
        acts_ref[pl.ds(2 * q + 1, 2), 1 : cols + 1] = a.astype(BF).reshape(2, cols, SLOTS, CH)
        at_ref[:, pl.ds(pl.multiple_of(q * 256 + 128, 128), 256)] = a.T.astype(BF)
        return 0

    lax.fori_loop(0, rows // 2, rows_of, 0)

    place_edge = to_slots(cols, OWN, own_frames(count))
    for ref, flag, row in ((top_ref, has_top, 0), (bot_ref, has_bot, rows + 1)):
        a = silu_norm(mm(place_edge, ref[...])) * flag.astype(F32)
        acts_ref[row, 1 : cols + 1] = a.astype(BF).reshape(cols, SLOTS, CH)
        at_ref[:, row * 128 : row * 128 + 128] = a.T.astype(BF)

    place_next = to_slots(16, SLOTS, own_and_next(count))
    for q in range(rows * cols // 64):
        piece = jnp.concatenate(
            [cot_ref[0:OWN, q * 16 : q * 16 + 16, :], nxt_ref[:, q * 16 : q * 16 + 16, :]], 0
        ).reshape(SLOTS * 16, CH)
        placed = mm(place_next, piece).astype(BF)
        cott_ref[q * 4 : q * 4 + 4] = placed.reshape(4, 4, SLOTS, CH)
        for i in range(2):
            for j in range(2):
                g = mm_nt(placed, wd_ref[i * 2 + j]).astype(BF).reshape(4, 4, SLOTS, CH)
                for r in range(4):
                    for c in range(4):
                        gy_ref[2 * (q * 4 + r) + i, 2 * c + j] = g[r, c]

    def grads_of(q, _):
        g = gy_ref[pl.ds(4 * q, 4)].reshape(4 * cols, SLOTS, CH)
        s = grad_of_temporal(g, wt_ref, count)
        gs_ref[pl.ds(4 * q, 4), 1 : cols + 1] = s.reshape(4, cols, SLOTS, CH)
        return 0

    lax.fori_loop(0, rows // 4, grads_of, 0)

    wide = rows * cols * SLOTS
    for i in range(3):
        for j in range(3):
            right = gs_ref[:, 2 - j : 2 - j + cols].reshape(wide, CH)
            gw_ref[i * 3 + j] = mm(at_ref[:, i * 128 : i * 128 + wide], right).astype(BF)


def spatial_kernel(scal, acts_ref, ws_ref, sp_ref, edge_ref):
    count = scal[0]
    rows, cols = sp_ref.shape[0], sp_ref.shape[1]
    a, b = iotas(32, 256)
    pick = (a // 2 == b // SLOTS) & (b % SLOTS == count - 2 + a % 2)
    pick = jnp.where(pick, 1.0, 0.0).astype(BF)

    def rows_of(q, _):
        total = None
        for i in range(3):
            for j in range(3):
                left = acts_ref[pl.ds(4 * q + i, 4), j : j + cols].reshape(4 * cols * SLOTS, CH)
                term = mm(left, ws_ref[i * 3 + j])
                total = term if total is None else total + term
        out = total.astype(BF)
        sp_ref[pl.ds(4 * q, 4)] = out.reshape(4, cols, SLOTS, CH)
        for half in range(2):
            edge_ref[2 * q + half] = mm(pick, out[half * 256 : half * 256 + 256]).astype(BF)
        return 0

    lax.fori_loop(0, rows // 4, rows_of, 0)


def backward_kernel(
    scal, xt_ref, gy_ref, gs_ref, top_ref, bot_ref, wt_ref, wd_ref, ws_ref, out_ref, pad_ref
):
    count, has_top, has_bot = scal[0], scal[1], scal[2]
    rows, cols = xt_ref.shape[0], xt_ref.shape[1]
    pad_ref[1 : rows + 1] = gs_ref[...]
    place_edge = to_slots(cols // 2, SLOTS, own_and_next(count))
    for ref, flag, i, row in ((top_ref, has_top, 1, 0), (bot_ref, has_bot, 0, rows + 1)):
        placed = mm(place_edge, ref[...]).astype(BF)
        pair = [
            mm_nt(placed, wd_ref[i * 2 + j]).astype(BF).reshape(cols // 2, SLOTS, CH) for j in range(2)
        ]
        g = jnp.stack(pair, axis=1).reshape(cols, SLOTS, CH)
        s = grad_of_temporal(g, wt_ref, count) * flag.astype(BF)
        pad_ref[row, 0] = jnp.zeros((SLOTS, CH), BF)
        pad_ref[row, 1 : cols + 1] = s
        pad_ref[row, cols + 1] = jnp.zeros((SLOTS, CH), BF)

    back = to_frames(16)

    def rows_of(q, _):
        total = None
        for i in range(3):
            for j in range(3):
                left = pad_ref[pl.ds(4 * q + 2 - i, 4), 2 - j : 2 - j + cols].reshape(
                    4 * cols * SLOTS, CH
                )
                term = mm_nt(left, ws_ref[i * 3 + j])
                total = term if total is None else total + term
        v = xt_ref[pl.ds(4 * q, 4)].reshape(4 * cols * SLOTS, CH).astype(F32)
        r = lax.rsqrt(jnp.mean(v * v, axis=-1, keepdims=True) + 1e-06)
        u = v * r
        s = 1.0 / (1.0 + jnp.exp(-u))
        gu = total * (s * (1.0 + u * (1.0 - s)))
        dot = jnp.mean(gu * u, axis=-1, keepdims=True)
        gv = r * (gu - u * dot)
        gx = gy_ref[pl.ds(4 * q, 4)].reshape(4 * cols * SLOTS, CH).astype(F32) + gv
        gx = gx.reshape(4 * cols, SLOTS, CH)
        gx = jnp.where(slot_mask(gx.shape, count), gx, 0.0).astype(BF).reshape(4 * cols * SLOTS, CH)
        for half in range(2):
            o = mm(back, gx[half * 256 : half * 256 + 256]).astype(BF)
            at = pl.multiple_of((2 * q + half) * 16, 16)
            out_ref[:, pl.ds(at, 16), :] = o.reshape(SLOTS, 16, CH)
        return 0

    lax.fori_loop(0, rows // 4, rows_of, 0)


def forward_kernel(
    scal, xt_ref, sp_ref, prev_ref, cott_ref, gy_ref, wt_ref, wd_ref,
    down_ref, gw_ref, y_ref, st_ref, g1_ref, g0_ref, g2_ref,
):
    count = scal[0]
    rows, cols = xt_ref.shape[0], xt_ref.shape[1]
    a, b = iotas(256, 32)
    place = (a // SLOTS == b // 2) & (a % SLOTS == OWN + b % 2)
    place = jnp.where(place, 1.0, 0.0).astype(BF)

    def rows_of(q, _):
        s = sp_ref[pl.ds(2 * q, 2)].reshape(256, CH)
        s = (s.astype(F32) + mm(place, prev_ref[q])).astype(BF)
        st_ref[:, pl.ds(pl.multiple_of(q * 256, 256), 256)] = s.T
        total = mm(s, wt_ref[2]).reshape(2 * cols, SLOTS, CH)
        for k in (1, 0):
            total = total + pltpu.roll(mm(s, wt_ref[k]).reshape(2 * cols, SLOTS, CH), 2 - k, 1)
        x = xt_ref[pl.ds(2 * q, 2)].reshape(2 * cols, SLOTS, CH).astype(F32)
        mask = slot_mask(x.shape, count)
        y = jnp.where(mask, x + total, 0.0).astype(BF)
        y_ref[pl.ds(2 * q, 2)] = y.reshape(2, cols, SLOTS, CH)
        g = gy_ref[pl.ds(2 * q, 2)].reshape(2 * cols, SLOTS, CH).astype(F32)
        g = jnp.where(mask, g, 0.0)
        for ref, k in ((g2_ref, 2), (g1_ref, 1), (g0_ref, 0)):
            shifted = g if k == 2 else pltpu.roll(g, SLOTS - (2 - k), 1)
            ref[pl.ds(2 * q, 2)] = shifted.astype(BF).reshape(2, cols, SLOTS, CH)
        return 0

    lax.fori_loop(0, rows // 2, rows_of, 0)

    wide = rows * cols * SLOTS
    for k, ref in ((0, g0_ref), (1, g1_ref), (2, g2_ref)):
        gw_ref[k] = mm(st_ref[...], ref[...].reshape(wide, CH)).astype(BF)

    small = wide // 4
    total = None
    cot = cott_ref[...].reshape(small, CH)
    for i in range(2):
        for j in range(2):
            tiles = [
                y_ref[2 * r + i, 2 * c + j] for r in range(rows // 2) for c in range(cols // 2)
            ]
            piece = jnp.concatenate(tiles, axis=0)
            term = mm(piece, wd_ref[i * 2 + j])
            total = term if total is None else total + term
            gw_ref[3 + i * 2 + j] = mm(piece.T, cot).astype(BF)
    down = total.astype(BF)
    back = to_frames(16)
    for q in range(small // 256):
        o = mm(back, down[q * 256 : q * 256 + 256]).astype(BF)
        down_ref[:, q * 16 : q * 16 + 16, :] = o.reshape(SLOTS, 16, CH)


def call(kernel, outs, scratch, name, flops, *args):
    specs = [pl.BlockSpec(memory_space=pltpu.SMEM)] + [
        pl.BlockSpec(memory_space=pltpu.VMEM) for _ in args[1:]
    ]
    shapes = [jax.ShapeDtypeStruct(s, BF) for s in outs]
    moved = sum(a.size * a.dtype.itemsize for a in args) + sum(s.size * 2 for s in shapes)
    return pl.pallas_call(
        kernel,
        out_shape=shapes,
        in_specs=specs,
        out_specs=[pl.BlockSpec(memory_space=pltpu.VMEM) for _ in outs],
        scratch_shapes=[pltpu.VMEM(s, BF) for s in scratch],
        compiler_params=pltpu.CompilerParams(vmem_limit_bytes=10 * 2**20),
        cost_estimate=pl.CostEstimate(flops=flops, bytes_accessed=moved, transcendentals=0),
        name=name,
    )(*args)


AXES = ("tm", "grp")


def exchange_plan(tm, grp):
    low = grp.bit_length() - 1
    high = tm.bit_length() - 1
    bits_g = list(range(low))
    bits_t = list(range(low, low + high))
    core, rest = bits_t[0], bits_t[1:]
    first = rest[:1] + bits_g + rest[1:]
    second = rest[1:2] + rest[:1] + bits_g + rest[2:]
    return core, [(core, core)] + list(zip(first, second))


def scatter_sum(value, tm, grp):
    total = tm * grp
    core, stages = exchange_plan(tm, grp)
    me = lax.axis_index("tm") * grp + lax.axis_index("grp")
    odd = (me >> core) & 1
    bits = len(stages)
    value = value.reshape((2,) * bits + (value.shape[0] // total, value.shape[1]))
    left = [list(reversed(range(bits)))] * 2

    for stage in stages:
        pairs = [(d, d ^ (1 << stage[(d >> core) & 1])) for d in range(total)]
        where = [left[c].index(stage[c]) for c in range(2)]

        def half(flip):
            parts = [
                lax.dynamic_index_in_dim(
                    value, ((me >> stage[c]) & 1) ^ flip, where[c], keepdims=False
                )
                for c in range(2)
            ]
            return parts[0] if stage[0] == stage[1] else jnp.where(odd == 0, parts[0], parts[1])

        got = lax.ppermute(half(1), AXES, pairs)
        value = (half(0).astype(F32) + got.astype(F32)).astype(BF)
        left = [[b for b in left[c] if b != stage[c]] for c in range(2)]
    return value


def along(value, axis, by):
    count = lax.axis_size(axis)
    pairs = [(i, i + by) for i in range(count) if 0 <= i + by < count]
    return lax.ppermute(value, axis, pairs)


def edge_rows(values, rows, members, band):
    frames, wide, _ = values.shape
    flat = (frames * rows, CH)
    if members == 2:
        at = jnp.where(band == 0, wide - rows, 0)
        sent = lax.dynamic_slice_in_dim(values, at, rows, 1).reshape(flat)
        got = lax.ppermute(sent, "grp", [(0, 1), (1, 0)])
        return got, got
    return (
        along(values[:, wide - rows :].reshape(flat), "grp", 1),
        along(values[:, :rows].reshape(flat), "grp", -1),
    )


def body(tm, grp, frames_in, span_frames, w_spatial, w_temporal, w_down, cotangent):
    slots, rows, cols, ch = frames_in.shape
    wide = rows * cols
    x = frames_in.reshape(slots, wide, ch)
    cot = cotangent.reshape(slots, wide // 4, ch)
    ws = w_spatial.reshape(9, ch, ch)
    wd = w_down.reshape(4, ch, ch)
    count = span_frames[0]
    band = lax.axis_index("grp")
    scal = jnp.stack(
        [count, (band > 0).astype(jnp.int32), (band < grp - 1).astype(jnp.int32)]
    )
    tap = 2 * slots * wide * ch * ch

    nxt = along(cot[:2], "tm", -1)
    top, bot = edge_rows(x[:OWN], cols, grp, band)
    cot_all = jnp.concatenate([cot[:OWN], nxt], 0)
    cot_top, cot_bot = edge_rows(cot_all, cols // 2, grp, band)

    tile = (rows, cols, slots, ch)
    xt, acts, cott, gy, gs, gw_s = call(
        first_kernel,
        [tile, (rows + 2, cols + 2, slots, ch), (rows // 2, cols // 2, slots, ch), tile,
         (rows, cols + 2, slots, ch), (9, ch, ch)],
        [(ch, (rows + 2) * 128)],
        "grad_spatial",
        14 * tap,
        scal, x, top, bot, cot, nxt, w_temporal, wd,
    )
    sum_s = lax.psum(gw_s.reshape(9 * ch, ch), AXES)
    sp, edge = call(
        spatial_kernel, [tile, (rows // 2, 32, ch)], [], "spatial", 9 * tap, scal, acts, ws
    )
    prev = along(edge, "tm", 1)
    (grad_x,) = call(
        backward_kernel,
        [(slots, wide, ch)],
        [(rows + 2, cols + 2, slots, ch)],
        "grad_x",
        10 * tap,
        scal, xt, gy, gs, cot_top, cot_bot, w_temporal, wd, ws,
    )
    down, gw_t = call(
        forward_kernel,
        [(slots, wide // 4, ch), (7, ch, ch)],
        [tile, (ch, slots * wide), tile, tile, tile],
        "forward",
        8 * tap,
        scal, xt, sp, prev, cott, gy, w_temporal, wd,
    )
    part = scatter_sum(gw_t.reshape(7 * ch, ch), tm, grp)
    sum_t = lax.all_gather(part, AXES, axis=0, tiled=True).astype(F32)
    return (
        down.reshape(cotangent.shape),
        grad_x.reshape(frames_in.shape),
        sum_s.astype(F32).reshape(w_spatial.shape),
        sum_t[: 3 * ch].reshape(w_temporal.shape),
        sum_t[3 * ch :].reshape(w_down.shape),
    )


def solution(mesh):
    return jax.shard_map(
        functools.partial(body, mesh.shape["tm"], mesh.shape["grp"]),
        mesh=mesh,
        in_specs=(P("tm", "grp", None, None), P("tm"), P(), P(), P(), P("tm", "grp", None, None)),
        out_specs=(P("tm", "grp", None, None), P("tm", "grp", None, None), P(), P(), P()),
        check_vma=False,
    )
```

```python
import functools

import jax
import jax.numpy as jnp
from jax import lax
from jax.experimental import pallas as pl
from jax.experimental.pallas import tpu as pltpu
from jax.sharding import PartitionSpec as P

SLOTS = 16
OWN = 14
CH = 256
BF = jnp.bfloat16
F32 = jnp.float32


def mm(a, b):
    return lax.dot_general(a, b, (((1,), (0,)), ((), ())), preferred_element_type=F32)


def mm_nt(a, b):
    return lax.dot_general(a, b, (((1,), (1,)), ((), ())), preferred_element_type=F32)


def iotas(rows, cols):
    return (
        lax.broadcasted_iota(jnp.int32, (rows, cols), 0),
        lax.broadcasted_iota(jnp.int32, (rows, cols), 1),
    )


def to_slots(rows, frames, keep):
    a, b = iotas(rows * SLOTS, frames * rows)
    hit = (a // SLOTS == b % rows) & keep(b // rows, a % SLOTS)
    return jnp.where(hit, 1.0, 0.0).astype(BF)


def to_frames(rows):
    a, b = iotas(SLOTS * rows, rows * SLOTS)
    hit = (a % rows == b // SLOTS) & (a // rows == b % SLOTS)
    return jnp.where(hit, 1.0, 0.0).astype(BF)


def own_frames(count):
    return lambda frame, slot: (frame == slot) & (slot < count)


def own_and_next(count):
    return lambda frame, slot: ((frame < OWN) & (frame == slot) & (slot < count)) | (
        (frame >= OWN) & (slot == count + frame - OWN)
    )


def silu_norm(v):
    scaled = v * lax.rsqrt(jnp.mean(v * v, axis=-1, keepdims=True) + 1e-06)
    return scaled / (1.0 + jnp.exp(-scaled))


def slot_mask(shape, count):
    return lax.broadcasted_iota(jnp.int32, shape, len(shape) - 2) < count


def grad_of_temporal(gy, wt_ref, count):
    n = gy.shape[0]
    flat = gy.reshape(n * SLOTS, CH)
    total = mm_nt(flat, wt_ref[2]).reshape(n, SLOTS, CH)
    for k in (1, 0):
        term = mm_nt(flat, wt_ref[k]).reshape(n, SLOTS, CH)
        total = total + pltpu.roll(term, SLOTS - (2 - k), 1)
    return jnp.where(slot_mask(total.shape, count), total, 0.0).astype(BF)


def place_bits():
    t, g = lax.axis_index("tm"), lax.axis_index("grp")
    return t & 1, ((t >> 1) & 1) + 2 * (g & 1), (t >> 2) & 3


def split_cores(value, keep_ref, send_ref, k):
    core, _, _ = place_bits()
    low, high = value[:, : CH // 2].astype(BF), value[:, CH // 2 :].astype(BF)
    keep_ref[:, k] = jnp.where(core == 0, low, high).reshape(16, 16, CH // 2)
    send_ref[:, k] = jnp.where(core == 0, high, low).reshape(16, 16, CH // 2)


def edges_kernel(bands, count_ref, x_ref, cot_ref, *rest):
    outs, nxt_ref, buf, sems = rest[: len(rest) - 3], rest[-3], rest[-2], rest[-1]
    count = count_ref[0]
    band = lax.axis_index("grp")
    wide = x_ref.shape[1]
    if bands == 2:
        starts = [jnp.where(band == 0, wide - 16, 0)]
        lower = [band == 0]
    else:
        starts, lower = [wide - 16, 0], [True, False]
    copies = [
        pltpu.make_async_copy(
            x_ref.at[:, pl.ds(pl.multiple_of(at, 16), 16), :], buf.at[k], sems.at[k]
        )
        for k, at in enumerate(starts)
    ]
    for copy in copies:
        copy.start()
    nxt_ref[...] = cot_ref[0:2]
    place = to_slots(16, SLOTS, own_frames(count))
    for k, copy in enumerate(copies):
        copy.wait()
        v = mm(place, buf[k].reshape(SLOTS * 16, CH))
        v = jnp.where(lower[k], v[128:], v[:128])
        outs[k][...] = silu_norm(v).astype(BF)


def acts_kernel(count_ref, x_ref, _, xt_ref, acts_ref, at_ref):
    count = count_ref[0]
    rows, cols = xt_ref.shape[0], xt_ref.shape[1]
    edge = jnp.zeros((rows + 2, SLOTS, CH), BF)
    acts_ref[:, 0] = edge
    acts_ref[:, cols + 1] = edge
    place = to_slots(16, SLOTS, own_frames(count))

    def rows_of(q, _):
        at = pl.multiple_of(q * 16, 16)
        piece = x_ref[:, pl.ds(at, 16), :].reshape(SLOTS * 16, CH)
        v = mm(place, piece)
        xt_ref[pl.ds(2 * q, 2)] = v.astype(BF).reshape(2, cols, SLOTS, CH)
        a = silu_norm(v)
        acts_ref[pl.ds(2 * q + 1, 2), 1 : cols + 1] = a.astype(BF).reshape(2, cols, SLOTS, CH)
        at_ref[:, pl.ds(pl.multiple_of(q * 256 + 128, 128), 256)] = a.T.astype(BF)
        return 0

    lax.fori_loop(0, rows // 2, rows_of, 0)


def spatial_kernel(
    bands, count_ref, top_ref, bot_ref, acts_in, at_in, ws_ref, acts_ref, at_ref, sp_ref, edge_ref
):
    count = count_ref[0]
    band = lax.axis_index("grp")
    rows, cols = sp_ref.shape[0], sp_ref.shape[1]
    for ref, flag, row in ((top_ref, band > 0, 0), (bot_ref, band < bands - 1, rows + 1)):
        a = jnp.where(flag, ref[...].astype(F32), 0.0)
        acts_ref[row, 1 : cols + 1] = a.astype(BF).reshape(cols, SLOTS, CH)
        at_ref[:, row * 128 : row * 128 + 128] = a.T.astype(BF)
    a, b = iotas(32, 256)
    pick = (a // 2 == b // SLOTS) & (b % SLOTS == count - 2 + a % 2)
    pick = jnp.where(pick, 1.0, 0.0).astype(BF)

    def rows_of(q, _):
        total = None
        for i in range(3):
            for j in range(3):
                left = acts_ref[pl.ds(4 * q + i, 4), j : j + cols].reshape(4 * cols * SLOTS, CH)
                term = mm(left, ws_ref[i * 3 + j])
                total = term if total is None else total + term
        out = total.astype(BF)
        sp_ref[pl.ds(4 * q, 4)] = out.reshape(4, cols, SLOTS, CH)
        for half in range(2):
            edge_ref[2 * q + half] = mm(pick, out[half * 256 : half * 256 + 256]).astype(BF)
        return 0

    lax.fori_loop(0, rows // 4, rows_of, 0)


def grad_spatial_kernel(
    count_ref, at_ref, cot_ref, nxt_ref, wt_ref, wd_ref,
    cott_ref, gy_ref, gs_ref, last_ref, first_ref, keep_ref, send_ref,
):
    count = count_ref[0]
    rows, cols = gy_ref.shape[0], gy_ref.shape[1]
    edge = jnp.zeros((rows, SLOTS, CH), BF)
    gs_ref[:, 0] = edge
    gs_ref[:, cols + 1] = edge

    place_next = to_slots(16, SLOTS, own_and_next(count))
    for q in range(rows * cols // 64):
        piece = jnp.concatenate(
            [cot_ref[0:OWN, q * 16 : q * 16 + 16, :], nxt_ref[:, q * 16 : q * 16 + 16, :]], 0
        ).reshape(SLOTS * 16, CH)
        placed = mm(place_next, piece).astype(BF)
        cott_ref[q * 4 : q * 4 + 4] = placed.reshape(4, 4, SLOTS, CH)
        for i in range(2):
            for j in range(2):
                g = mm_nt(placed, wd_ref[i * 2 + j]).astype(BF).reshape(4, 4, SLOTS, CH)
                for r in range(4):
                    for c in range(4):
                        gy_ref[2 * (q * 4 + r) + i, 2 * c + j] = g[r, c]
    last_ref[...] = cott_ref[rows // 2 - 1].reshape(cols // 2 * SLOTS, CH)
    first_ref[...] = cott_ref[0].reshape(cols // 2 * SLOTS, CH)

    def grads_of(q, _):
        g = gy_ref[pl.ds(4 * q, 4)].reshape(4 * cols, SLOTS, CH)
        s = grad_of_temporal(g, wt_ref, count)
        gs_ref[pl.ds(4 * q, 4), 1 : cols + 1] = s.reshape(4, cols, SLOTS, CH)
        return 0

    lax.fori_loop(0, rows // 4, grads_of, 0)

    wide = rows * cols * SLOTS
    for i in range(3):
        for j in range(3):
            right = gs_ref[:, 2 - j : 2 - j + cols].reshape(wide, CH)
            value = mm(at_ref[:, i * 128 : i * 128 + wide], right)
            split_cores(value, keep_ref, send_ref, i * 3 + j)


def forward_kernel(
    count_ref, xt_ref, sp_ref, prev_ref, cott_ref, gy_ref, wt_ref, wd_ref, _,
    down_ref, keep_ref, send_ref, y_ref, st_ref, g1_ref, g0_ref, g2_ref,
):
    count = count_ref[0]
    rows, cols = xt_ref.shape[0], xt_ref.shape[1]
    a, b = iotas(256, 32)
    place = (a // SLOTS == b // 2) & (a % SLOTS == OWN + b % 2)
    place = jnp.where(place, 1.0, 0.0).astype(BF)

    def rows_of(q, _):
        s = sp_ref[pl.ds(2 * q, 2)].reshape(256, CH)
        s = (s.astype(F32) + mm(place, prev_ref[q])).astype(BF)
        st_ref[:, pl.ds(pl.multiple_of(q * 256, 256), 256)] = s.T
        total = mm(s, wt_ref[2]).reshape(2 * cols, SLOTS, CH)
        for k in (1, 0):
            total = total + pltpu.roll(mm(s, wt_ref[k]).reshape(2 * cols, SLOTS, CH), 2 - k, 1)
        x = xt_ref[pl.ds(2 * q, 2)].reshape(2 * cols, SLOTS, CH).astype(F32)
        mask = slot_mask(x.shape, count)
        y = jnp.where(mask, x + total, 0.0).astype(BF)
        y_ref[pl.ds(2 * q, 2)] = y.reshape(2, cols, SLOTS, CH)
        g = gy_ref[pl.ds(2 * q, 2)].reshape(2 * cols, SLOTS, CH).astype(F32)
        g = jnp.where(mask, g, 0.0)
        for ref, k in ((g2_ref, 2), (g1_ref, 1), (g0_ref, 0)):
            shifted = g if k == 2 else pltpu.roll(g, SLOTS - (2 - k), 1)
            ref[pl.ds(2 * q, 2)] = shifted.astype(BF).reshape(2, cols, SLOTS, CH)
        return 0

    lax.fori_loop(0, rows // 2, rows_of, 0)

    wide = rows * cols * SLOTS
    for k, ref in ((0, g0_ref), (1, g1_ref), (2, g2_ref)):
        split_cores(mm(st_ref[...], ref[...].reshape(wide, CH)), keep_ref, send_ref, k)

    small = wide // 4
    total = None
    cot = cott_ref[...].reshape(small, CH)
    for i in range(2):
        for j in range(2):
            tiles = [
                y_ref[2 * r + i, 2 * c + j] for r in range(rows // 2) for c in range(cols // 2)
            ]
            piece = jnp.concatenate(tiles, axis=0)
            term = mm(piece, wd_ref[i * 2 + j])
            total = term if total is None else total + term
            split_cores(mm(piece.T, cot), keep_ref, send_ref, 3 + i * 2 + j)
    down = total.astype(BF)
    back = to_frames(16)
    for q in range(small // 256):
        o = mm(back, down[q * 256 : q * 256 + 256]).astype(BF)
        down_ref[:, q * 16 : q * 16 + 16, :] = o.reshape(SLOTS, 16, CH)


def grad_x_kernel(
    part, bands, count_ref, xt_ref, gy_ref, gs_ref, halo_ref, wt_ref, wd_ref, ws_ref, *rest
):
    out_ref, pad_ref, buf, sem = rest[-4:]
    count = count_ref[0]
    band = lax.axis_index("grp")
    rows, cols = xt_ref.shape[0], xt_ref.shape[1]
    half = rows // 2
    if part == 0:
        flag, i, row = band > 0, 1, 0
        pad_ref[1 : half + 2] = gs_ref[0 : half + 1]
    else:
        flag, i, row = band < bands - 1, 0, half + 1
        pad_ref[0 : half + 1] = gs_ref[half - 1 :]
    pair = [
        mm_nt(halo_ref[...], wd_ref[i * 2 + j]).astype(BF).reshape(cols // 2, SLOTS, CH)
        for j in range(2)
    ]
    g = jnp.stack(pair, axis=1).reshape(cols, SLOTS, CH)
    s = grad_of_temporal(g, wt_ref, jnp.where(flag, count, 0))
    pad_ref[row, 0] = jnp.zeros((SLOTS, CH), BF)
    pad_ref[row, 1 : cols + 1] = s
    pad_ref[row, cols + 1] = jnp.zeros((SLOTS, CH), BF)
    back = to_frames(16)

    def rows_of(q, _):
        total = None
        for i in range(3):
            for j in range(3):
                left = pad_ref[pl.ds(4 * q + 2 - i, 4), 2 - j : 2 - j + cols].reshape(
                    4 * cols * SLOTS, CH
                )
                term = mm_nt(left, ws_ref[i * 3 + j])
                total = term if total is None else total + term
        at = part * half + 4 * q
        v = xt_ref[pl.ds(at, 4)].reshape(4 * cols * SLOTS, CH).astype(F32)
        r = lax.rsqrt(jnp.mean(v * v, axis=-1, keepdims=True) + 1e-06)
        u = v * r
        s = 1.0 / (1.0 + jnp.exp(-u))
        gu = total * (s * (1.0 + u * (1.0 - s)))
        dot = jnp.mean(gu * u, axis=-1, keepdims=True)
        gv = r * (gu - u * dot)
        gx = gy_ref[pl.ds(at, 4)].reshape(4 * cols * SLOTS, CH).astype(F32) + gv
        gx = gx.reshape(4 * cols, SLOTS, CH)
        gx = jnp.where(slot_mask(gx.shape, count), gx, 0.0).astype(BF).reshape(4 * cols * SLOTS, CH)
        for k in range(2):
            o = mm(back, gx[k * 256 : k * 256 + 256]).astype(BF)
            buf[:, pl.ds(pl.multiple_of((2 * q + k) * 16, 16), 16), :] = o.reshape(SLOTS, 16, CH)
        return 0

    lax.fori_loop(0, half // 4, rows_of, 0)
    size = half * cols
    copy = pltpu.make_async_copy(buf, out_ref.at[:, part * size : part * size + size, :], sem)
    copy.start()
    copy.wait()


def plane_send_kernel(keep_ref, got_ref, *rest):
    outs = rest[-4:]
    _, p, _ = place_bits()
    for r in range(4):
        at = pl.ds((p ^ r) * 4, 4)
        outs[r][...] = (keep_ref[at].astype(F32) + got_ref[at].astype(F32)).astype(BF)


def total_at(refs, z):
    return functools.reduce(lambda a, b: a + b, [ref[z].astype(F32) for ref in refs]).astype(BF)


def line_send_kernel(*refs):
    ins, outs = refs[:4], refs[-4:]
    _, _, z = place_bits()
    for r in range(4):
        outs[r][...] = total_at(ins, z ^ r)


def line_sum_kernel(a_ref, b_ref, c_ref, d_ref, out_ref):
    parts = [ref[...].astype(F32) for ref in (a_ref, b_ref, c_ref, d_ref)]
    out_ref[...] = (parts[0] + parts[1] + parts[2] + parts[3]).astype(BF)


def line_gather_kernel(a_ref, b_ref, c_ref, d_ref, out_ref):
    _, _, z = place_bits()
    for r, ref in enumerate((a_ref, b_ref, c_ref, d_ref)):
        out_ref[z ^ r] = ref[...]


def plane_gather_kernel(a_ref, b_ref, c_ref, d_ref, out_ref):
    _, p, _ = place_bits()
    for r, ref in enumerate((a_ref, b_ref, c_ref, d_ref)):
        out_ref[pl.ds((p ^ r) * 4, 4)] = ref[...]


def finish_kernel(own_ref, got_ref, *rest):
    outs, buf, sems = rest[:-2], rest[-2], rest[-1]
    core, _, _ = place_bits()
    copies = []
    k = 0
    for out in outs:
        for m in range(out.shape[0]):
            own = own_ref[:, k].reshape(CH, CH // 2).astype(F32)
            got = got_ref[:, k].reshape(CH, CH // 2).astype(F32)
            buf[k, :, : CH // 2] = jnp.where(core == 0, own, got)
            buf[k, :, CH // 2 :] = jnp.where(core == 0, got, own)
            copies.append(pltpu.make_async_copy(buf.at[k], out.at[m], sems.at[k]))
            copies[-1].start()
            k += 1
    for copy in copies:
        copy.wait()


VMEM = pl.BlockSpec(memory_space=pltpu.VMEM)
SMEM = pl.BlockSpec(memory_space=pltpu.SMEM)
ANY = pl.BlockSpec(memory_space=pl.ANY)


def call(kernel, name, ins, outs, scratch=(), flops=0, alias=None):
    shapes = [jax.ShapeDtypeStruct(o[1], o[2] if len(o) > 2 else BF) for o in outs]
    moved = sum(a.size * a.dtype.itemsize for s, a in ins if s is not ANY)
    moved += sum(s.size * s.dtype.itemsize for s in shapes)
    return pl.pallas_call(
        kernel,
        out_shape=shapes,
        in_specs=[s for s, _ in ins],
        out_specs=[o[0] for o in outs],
        scratch_shapes=list(scratch),
        compiler_params=pltpu.CompilerParams(vmem_limit_bytes=10 * 2**20),
        cost_estimate=pl.CostEstimate(flops=flops, bytes_accessed=moved, transcendentals=0),
        input_output_aliases=alias or {},
        name=name,
    )(*[a for _, a in ins])


AXES = ("tm", "grp")


def plan(tm, grp):
    low, total = grp.bit_length() - 1, (tm * grp).bit_length() - 1
    used = [low, low + 1, 0, low + 2, low + 3]
    return used + [b for b in range(total) if b not in used]


def swap(value, tm, grp, *bits):
    flip = sum(1 << b for b in bits)
    return lax.ppermute(value, AXES, [(d, d ^ flip) for d in range(tm * grp)])


def core_round(send, tm, grp):
    return swap(send, tm, grp, plan(tm, grp)[0])


def plane_send(keep, got, after):
    n = keep.shape[1]
    ins = [(VMEM, keep), (VMEM, got)] + [(ANY, a) for a in after]
    return call(plane_send_kernel, "plane_send", ins, [(VMEM, (4, n, 16, CH // 2))] * 4)


def plane_round(parts, tm, grp):
    _, x, y = plan(tm, grp)[:3]
    return [parts[0], swap(parts[1], tm, grp, x), swap(parts[2], tm, grp, y), swap(parts[3], tm, grp, x, y)]


def line_send(parts, after):
    shape = parts[0].shape[1:]
    ins = [(VMEM, a) for a in parts] + [(ANY, a) for a in after]
    return call(line_send_kernel, "line_send", ins, [(VMEM, shape)] * 4)


def line_round(parts, tm, grp):
    _, _, _, a, b = plan(tm, grp)[:5]
    return [parts[0], swap(parts[1], tm, grp, a), swap(parts[2], tm, grp, b), swap(parts[3], tm, grp, a, b)]


def gather_back(parts, shapes, tm, grp):
    (mine,) = call(line_sum_kernel, "line_sum", [(VMEM, a) for a in parts], [(VMEM, parts[0].shape)])
    for bit in plan(tm, grp)[5:]:
        mine = (mine.astype(F32) + swap(mine, tm, grp, bit).astype(F32)).astype(BF)
    parts = line_round([mine] * 4, tm, grp)
    (mine,) = call(
        line_gather_kernel, "line_gather", [(VMEM, a) for a in parts], [(VMEM, (4,) + mine.shape)]
    )
    parts = plane_round([mine] * 4, tm, grp)
    (mine,) = call(
        plane_gather_kernel, "plane_gather", [(VMEM, a) for a in parts], [(VMEM, (16,) + mine.shape[1:])]
    )
    got = core_round(mine, tm, grp)
    n = mine.shape[1]
    return call(
        finish_kernel,
        "finish",
        [(VMEM, mine), (VMEM, got)],
        [(ANY, (m, CH, CH), F32) for m in shapes],
        [pltpu.VMEM((n, CH, CH), F32), pltpu.SemaphoreType.DMA((n,))],
    )


def along(value, axis, by):
    count = lax.axis_size(axis)
    pairs = [(i, i + by) for i in range(count) if 0 <= i + by < count]
    return lax.ppermute(value, axis, pairs)


def from_bands(parts):
    if len(parts) == 1:
        got = lax.ppermute(parts[0], "grp", [(0, 1), (1, 0)])
        return got, got
    return along(parts[0], "grp", 1), along(parts[1], "grp", -1)


def body(tm, grp, frames_in, span_frames, w_spatial, w_temporal, w_down, cotangent):
    slots, rows, cols, ch = frames_in.shape
    wide = rows * cols
    x = frames_in.reshape(slots, wide, ch)
    cot = cotangent.reshape(slots, wide // 4, ch)
    ws = w_spatial.reshape(9, ch, ch)
    wd = w_down.reshape(4, ch, ch)
    wt = w_temporal
    count = (SMEM, span_frames)
    tap = 2 * slots * wide * ch * ch
    tile = (rows, cols, slots, ch)
    padded = (rows + 2, cols + 2, slots, ch)
    dma = pltpu.SemaphoreType.DMA

    sides = 1 if grp == 2 else 2
    *edge, nxt = call(
        functools.partial(edges_kernel, grp),
        "edges",
        [count, (ANY, x), (VMEM, cot)],
        [(VMEM, (cols * slots, ch))] * sides + [(VMEM, (2, wide // 4, ch))],
        [pltpu.VMEM((sides, slots, 16, ch), BF), dma((sides,))],
        flops=tap // 8,
    )
    top, bot = from_bands(edge)
    nxt_got = along(nxt, "tm", -1)
    xt, acts, at = call(
        acts_kernel,
        "acts",
        [count, (VMEM, x), (ANY, nxt)],
        [(VMEM, tile), (VMEM, padded), (VMEM, (ch, (rows + 2) * 128))],
        flops=2 * tap,
    )
    acts, at, sp, last_two = call(
        functools.partial(spatial_kernel, grp),
        "spatial",
        [count, (VMEM, top), (VMEM, bot), (VMEM, acts), (VMEM, at), (VMEM, ws)],
        [(VMEM, padded), (VMEM, at.shape), (VMEM, tile), (VMEM, (rows // 2, 32, ch))],
        flops=9 * tap,
        alias={3: 0, 4: 1},
    )
    prev = along(last_two, "tm", 1)
    half = (16, 9, 16, ch // 2)
    cott, gy, gs, last, first, keep_a, send_a = call(
        grad_spatial_kernel,
        "grad_spatial",
        [count, (VMEM, at), (VMEM, cot), (VMEM, nxt_got), (VMEM, wt), (VMEM, wd)],
        [(VMEM, (rows // 2, cols // 2, slots, ch)), (VMEM, tile), (VMEM, (rows, cols + 2, slots, ch)),
         (VMEM, (cols // 2 * slots, ch)), (VMEM, (cols // 2 * slots, ch)), (VMEM, half), (VMEM, half)],
        flops=14 * tap,
    )
    got_a = core_round(send_a, tm, grp)
    cot_top, cot_bot = along(last, "grp", 1), along(first, "grp", -1)
    half = (16, 7, 16, ch // 2)
    down, keep_b, send_b = call(
        forward_kernel,
        "forward",
        [count, (VMEM, xt), (VMEM, sp), (VMEM, prev), (VMEM, cott), (VMEM, gy), (VMEM, wt), (VMEM, wd),
         (ANY, send_a)],
        [(VMEM, (slots, wide // 4, ch)), (VMEM, half), (VMEM, half)],
        [pltpu.VMEM(s, BF) for s in (tile, (ch, slots * wide), tile, tile, tile)],
        flops=10 * tap,
    )
    got_b = core_round(send_b, tm, grp)
    parts_a = plane_send(keep_a, got_a, [send_b])

    def grad_x_part(part, halo, after):
        return call(
            functools.partial(grad_x_kernel, part, grp),
            f"grad_x_{part}",
            [count, (VMEM, xt), (VMEM, gy), (VMEM, gs), (VMEM, halo), (VMEM, wt), (VMEM, wd), (VMEM, ws)]
            + [(ANY, a) for a in after],
            [(ANY, (slots, wide, ch))],
            [pltpu.VMEM((rows // 2 + 2, cols + 2, slots, ch), BF),
             pltpu.VMEM((slots, wide // 2, ch), BF), dma],
            flops=5 * tap,
            alias={8: 0} if part else None,
        )[0]

    grad_x = grad_x_part(0, cot_top, [parts_a[3], send_b])
    parts_a = plane_round(parts_a, tm, grp)
    parts_b = plane_send(keep_b, got_b, [grad_x])
    parts_a = line_send(parts_a, [parts_b[0]])
    grad_x = grad_x_part(1, cot_bot, [grad_x, parts_a[3], parts_b[3]])
    parts_b = plane_round(parts_b, tm, grp)
    parts_a = line_round(parts_a, tm, grp)
    parts_b = line_send(parts_b, [grad_x])
    parts_b = line_round(parts_b, tm, grp)
    (sum_s,) = gather_back(parts_a, [9], tm, grp)
    sum_t, sum_d = gather_back(parts_b, [3, 4], tm, grp)
    return (
        down.reshape(cotangent.shape),
        grad_x.reshape(frames_in.shape),
        sum_s.reshape(w_spatial.shape),
        sum_t,
        sum_d.reshape(w_down.shape),
    )


def solution(mesh):
    return jax.shard_map(
        functools.partial(body, mesh.shape["tm"], mesh.shape["grp"]),
        mesh=mesh,
        in_specs=(P("tm", "grp", None, None), P("tm"), P(), P(), P(), P("tm", "grp", None, None)),
        out_specs=(P("tm", "grp", None, None), P("tm", "grp", None, None), P(), P(), P()),
        check_vma=False,
    )
```

```python
import functools

import jax
import jax.numpy as jnp
from jax import lax
from jax.experimental import pallas as pl
from jax.experimental.pallas import tpu as pltpu
from jax.sharding import PartitionSpec as P

SLOTS = 16
OWN = 14
CH = 256
BF = jnp.bfloat16
F32 = jnp.float32


def mm(a, b):
    return lax.dot_general(a, b, (((1,), (0,)), ((), ())), preferred_element_type=F32)


def mm_nt(a, b):
    return lax.dot_general(a, b, (((1,), (1,)), ((), ())), preferred_element_type=F32)


def iotas(rows, cols):
    return (
        lax.broadcasted_iota(jnp.int32, (rows, cols), 0),
        lax.broadcasted_iota(jnp.int32, (rows, cols), 1),
    )


def to_slots(rows, frames, keep):
    a, b = iotas(rows * SLOTS, frames * rows)
    hit = (a // SLOTS == b % rows) & keep(b // rows, a % SLOTS)
    return jnp.where(hit, 1.0, 0.0).astype(BF)


def to_frames(rows):
    a, b = iotas(SLOTS * rows, rows * SLOTS)
    hit = (a % rows == b // SLOTS) & (a // rows == b % SLOTS)
    return jnp.where(hit, 1.0, 0.0).astype(BF)


def own_frames(count):
    return lambda frame, slot: (frame == slot) & (slot < count)


def own_and_next(count):
    return lambda frame, slot: ((frame < OWN) & (frame == slot) & (slot < count)) | (
        (frame >= OWN) & (slot == count + frame - OWN)
    )


def silu_norm(v):
    scaled = v * lax.rsqrt(jnp.mean(v * v, axis=-1, keepdims=True) + 1e-06)
    return scaled / (1.0 + jnp.exp(-scaled))


def slot_mask(shape, count):
    return lax.broadcasted_iota(jnp.int32, shape, len(shape) - 2) < count


def grad_of_temporal(gy, wt_ref, count):
    n = gy.shape[0]
    flat = gy.reshape(n * SLOTS, CH)
    total = mm_nt(flat, wt_ref[2]).reshape(n, SLOTS, CH)
    for k in (1, 0):
        term = mm_nt(flat, wt_ref[k]).reshape(n, SLOTS, CH)
        total = total + pltpu.roll(term, SLOTS - (2 - k), 1)
    return jnp.where(slot_mask(total.shape, count), total, 0.0).astype(BF)


def place_bits():
    t, g = lax.axis_index("tm"), lax.axis_index("grp")
    return t & 1, ((t >> 1) & 1) + 2 * (g & 1), (t >> 2) & 3


def split_cores(value, keep_ref, send_ref, k):
    core, _, _ = place_bits()
    low, high = value[:, : CH // 2].astype(BF), value[:, CH // 2 :].astype(BF)
    keep_ref[:, k] = jnp.where(core == 0, low, high).reshape(16, 16, CH // 2)
    send_ref[:, k] = jnp.where(core == 0, high, low).reshape(16, 16, CH // 2)


def edges_kernel(bands, count_ref, x_ref, cot_ref, *rest):
    outs, nxt_ref, buf, sems = rest[: len(rest) - 3], rest[-3], rest[-2], rest[-1]
    count = count_ref[0]
    band = lax.axis_index("grp")
    wide = x_ref.shape[1]
    if bands == 2:
        starts = [jnp.where(band == 0, wide - 16, 0)]
        lower = [band == 0]
    else:
        starts, lower = [wide - 16, 0], [True, False]
    copies = [
        pltpu.make_async_copy(
            x_ref.at[:, pl.ds(pl.multiple_of(at, 16), 16), :], buf.at[k], sems.at[k]
        )
        for k, at in enumerate(starts)
    ]
    for copy in copies:
        copy.start()
    nxt_ref[...] = cot_ref[0:2]
    place = to_slots(16, SLOTS, own_frames(count))
    for k, copy in enumerate(copies):
        copy.wait()
        v = mm(place, buf[k].reshape(SLOTS * 16, CH))
        v = jnp.where(lower[k], v[128:], v[:128])
        outs[k][...] = silu_norm(v).astype(BF)


def acts_kernel(count_ref, x_ref, _, xt_ref, acts_ref, at_ref):
    count = count_ref[0]
    rows, cols = xt_ref.shape[0], xt_ref.shape[1]
    edge = jnp.zeros((rows + 2, SLOTS, CH), BF)
    acts_ref[:, 0] = edge
    acts_ref[:, cols + 1] = edge
    place = to_slots(16, SLOTS, own_frames(count))

    def rows_of(q, _):
        at = pl.multiple_of(q * 16, 16)
        piece = x_ref[:, pl.ds(at, 16), :].reshape(SLOTS * 16, CH)
        v = mm(place, piece)
        xt_ref[pl.ds(2 * q, 2)] = v.astype(BF).reshape(2, cols, SLOTS, CH)
        a = silu_norm(v)
        acts_ref[pl.ds(2 * q + 1, 2), 1 : cols + 1] = a.astype(BF).reshape(2, cols, SLOTS, CH)
        at_ref[:, pl.ds(pl.multiple_of(q * 256 + 128, 128), 256)] = a.T.astype(BF)
        return 0

    lax.fori_loop(0, rows // 2, rows_of, 0)


def spatial_kernel(
    bands, count_ref, top_ref, bot_ref, acts_in, ws_ref, _, acts_ref, sp_ref, edge_ref
):
    count = count_ref[0]
    band = lax.axis_index("grp")
    rows, cols = sp_ref.shape[0], sp_ref.shape[1]
    for ref, flag, row in ((top_ref, band > 0, 0), (bot_ref, band < bands - 1, rows + 1)):
        a = jnp.where(flag, ref[...].astype(F32), 0.0)
        acts_ref[row, 1 : cols + 1] = a.astype(BF).reshape(cols, SLOTS, CH)
    a, b = iotas(32, 256)
    pick = (a // 2 == b // SLOTS) & (b % SLOTS == count - 2 + a % 2)
    pick = jnp.where(pick, 1.0, 0.0).astype(BF)

    def rows_of(q, _):
        total = None
        for i in range(3):
            for j in range(3):
                left = acts_ref[pl.ds(4 * q + i, 4), j : j + cols].reshape(4 * cols * SLOTS, CH)
                term = mm(left, ws_ref[i * 3 + j])
                total = term if total is None else total + term
        out = total.astype(BF)
        sp_ref[pl.ds(4 * q, 4)] = out.reshape(4, cols, SLOTS, CH)
        for half in range(2):
            edge_ref[2 * q + half] = mm(pick, out[half * 256 : half * 256 + 256]).astype(BF)
        return 0

    lax.fori_loop(0, rows // 4, rows_of, 0)


def grad_spatial_kernel(
    bands, count_ref, at_in, top_ref, bot_ref, cot_ref, nxt_ref, wt_ref, wd_ref,
    at_ref, cott_ref, gy_ref, gs_ref, keep_ref, send_ref, *edge_refs,
):
    count = count_ref[0]
    band = lax.axis_index("grp")
    rows, cols = gy_ref.shape[0], gy_ref.shape[1]
    for ref, flag, row in ((top_ref, band > 0, 0), (bot_ref, band < bands - 1, rows + 1)):
        a = jnp.where(flag, ref[...].astype(F32), 0.0)
        at_ref[:, row * 128 : row * 128 + 128] = a.T.astype(BF)
    edge = jnp.zeros((rows, SLOTS, CH), BF)
    gs_ref[:, 0] = edge
    gs_ref[:, cols + 1] = edge

    place_next = to_slots(16, SLOTS, own_and_next(count))
    for q in range(rows * cols // 64):
        piece = jnp.concatenate(
            [cot_ref[0:OWN, q * 16 : q * 16 + 16, :], nxt_ref[:, q * 16 : q * 16 + 16, :]], 0
        ).reshape(SLOTS * 16, CH)
        placed = mm(place_next, piece).astype(BF)
        cott_ref[q * 4 : q * 4 + 4] = placed.reshape(4, 4, SLOTS, CH)
        for i in range(2):
            for j in range(2):
                g = mm_nt(placed, wd_ref[i * 2 + j]).astype(BF).reshape(4, 4, SLOTS, CH)
                for r in range(4):
                    for c in range(4):
                        gy_ref[2 * (q * 4 + r) + i, 2 * c + j] = g[r, c]
    last = cott_ref[rows // 2 - 1].reshape(cols // 2 * SLOTS, CH)
    first = cott_ref[0].reshape(cols // 2 * SLOTS, CH)
    if bands == 2:
        edge_refs[0][...] = jnp.where(band == 0, last, first)
    else:
        edge_refs[0][...] = last
        edge_refs[1][...] = first

    def grads_of(q, _):
        g = gy_ref[pl.ds(4 * q, 4)].reshape(4 * cols, SLOTS, CH)
        s = grad_of_temporal(g, wt_ref, count)
        gs_ref[pl.ds(4 * q, 4), 1 : cols + 1] = s.reshape(4, cols, SLOTS, CH)
        return 0

    lax.fori_loop(0, rows // 4, grads_of, 0)

    wide = rows * cols * SLOTS
    for i in range(3):
        for j in range(3):
            right = gs_ref[:, 2 - j : 2 - j + cols].reshape(wide, CH)
            value = mm(at_ref[:, i * 128 : i * 128 + wide], right)
            split_cores(value, keep_ref, send_ref, i * 3 + j)


def forward_kernel(
    count_ref, xt_ref, sp_ref, prev_ref, cott_ref, gy_ref, wt_ref, wd_ref, *rest
):
    down_ref, keep_ref, send_ref, y_ref, st_ref, g1_ref, g0_ref, g2_ref = rest[-8:]
    count = count_ref[0]
    rows, cols = xt_ref.shape[0], xt_ref.shape[1]
    a, b = iotas(256, 32)
    place = (a // SLOTS == b // 2) & (a % SLOTS == OWN + b % 2)
    place = jnp.where(place, 1.0, 0.0).astype(BF)

    def rows_of(q, _):
        s = sp_ref[pl.ds(2 * q, 2)].reshape(256, CH)
        s = (s.astype(F32) + mm(place, prev_ref[q])).astype(BF)
        st_ref[:, pl.ds(pl.multiple_of(q * 256, 256), 256)] = s.T
        total = mm(s, wt_ref[2]).reshape(2 * cols, SLOTS, CH)
        for k in (1, 0):
            total = total + pltpu.roll(mm(s, wt_ref[k]).reshape(2 * cols, SLOTS, CH), 2 - k, 1)
        x = xt_ref[pl.ds(2 * q, 2)].reshape(2 * cols, SLOTS, CH).astype(F32)
        mask = slot_mask(x.shape, count)
        y = jnp.where(mask, x + total, 0.0).astype(BF)
        y_ref[pl.ds(2 * q, 2)] = y.reshape(2, cols, SLOTS, CH)
        g = gy_ref[pl.ds(2 * q, 2)].reshape(2 * cols, SLOTS, CH).astype(F32)
        g = jnp.where(mask, g, 0.0)
        for ref, k in ((g2_ref, 2), (g1_ref, 1), (g0_ref, 0)):
            shifted = g if k == 2 else pltpu.roll(g, SLOTS - (2 - k), 1)
            ref[pl.ds(2 * q, 2)] = shifted.astype(BF).reshape(2, cols, SLOTS, CH)
        return 0

    lax.fori_loop(0, rows // 2, rows_of, 0)

    wide = rows * cols * SLOTS
    for k, ref in ((0, g0_ref), (1, g1_ref), (2, g2_ref)):
        split_cores(mm(st_ref[...], ref[...].reshape(wide, CH)), keep_ref, send_ref, k)

    small = wide // 4
    total = None
    cot = cott_ref[...].reshape(small, CH)
    for i in range(2):
        for j in range(2):
            tiles = [
                y_ref[2 * r + i, 2 * c + j] for r in range(rows // 2) for c in range(cols // 2)
            ]
            piece = jnp.concatenate(tiles, axis=0)
            term = mm(piece, wd_ref[i * 2 + j])
            total = term if total is None else total + term
            split_cores(mm(piece.T, cot), keep_ref, send_ref, 3 + i * 2 + j)
    down = total.astype(BF)
    back = to_frames(16)
    for q in range(small // 256):
        o = mm(back, down[q * 256 : q * 256 + 256]).astype(BF)
        down_ref[:, q * 16 : q * 16 + 16, :] = o.reshape(SLOTS, 16, CH)


def grad_x_kernel(
    bands, count_ref, xt_ref, gy_ref, gs_ref, top_ref, bot_ref, wt_ref, wd_ref, ws_ref, *rest
):
    out_ref, pad_ref, buf, sems = rest[-4:]
    count = count_ref[0]
    band = lax.axis_index("grp")
    rows, cols = xt_ref.shape[0], xt_ref.shape[1]
    pad_ref[1 : rows + 1] = gs_ref[...]
    edge = jnp.zeros((SLOTS, CH), BF)
    for ref, flag, i, row in ((top_ref, band > 0, 1, 0), (bot_ref, band < bands - 1, 0, rows + 1)):
        pair = [
            mm_nt(ref[...], wd_ref[i * 2 + j]).astype(BF).reshape(cols // 2, SLOTS, CH)
            for j in range(2)
        ]
        g = jnp.stack(pair, axis=1).reshape(cols, SLOTS, CH)
        pad_ref[row, 0] = edge
        pad_ref[row, 1 : cols + 1] = grad_of_temporal(g, wt_ref, jnp.where(flag, count, 0))
        pad_ref[row, cols + 1] = edge
    back = to_frames(16)

    def rows_of(q, _):
        total = None
        for i in range(3):
            for j in range(3):
                left = pad_ref[pl.ds(4 * q + 2 - i, 4), 2 - j : 2 - j + cols].reshape(
                    4 * cols * SLOTS, CH
                )
                term = mm_nt(left, ws_ref[i * 3 + j])
                total = term if total is None else total + term
        at = 4 * q
        v = xt_ref[pl.ds(at, 4)].reshape(4 * cols * SLOTS, CH).astype(F32)
        r = lax.rsqrt(jnp.mean(v * v, axis=-1, keepdims=True) + 1e-06)
        u = v * r
        s = 1.0 / (1.0 + jnp.exp(-u))
        gu = total * (s * (1.0 + u * (1.0 - s)))
        dot = jnp.mean(gu * u, axis=-1, keepdims=True)
        gv = r * (gu - u * dot)
        gx = gy_ref[pl.ds(at, 4)].reshape(4 * cols * SLOTS, CH).astype(F32) + gv
        gx = gx.reshape(4 * cols, SLOTS, CH)
        gx = jnp.where(slot_mask(gx.shape, count), gx, 0.0).astype(BF).reshape(4 * cols * SLOTS, CH)
        for k in range(2):
            o = mm(back, gx[k * 256 : k * 256 + 256]).astype(BF)
            buf[:, pl.ds(pl.multiple_of((2 * q + k) * 16, 16), 16), :] = o.reshape(SLOTS, 16, CH)
        return 0

    lax.fori_loop(0, rows // 4, rows_of, 0)
    copy = pltpu.make_async_copy(buf, out_ref, sems.at[0])
    copy.start()
    copy.wait()


def plane_send_kernel(keep_ref, got_ref, *rest):
    outs = rest[-4:]
    _, p, _ = place_bits()
    for r in range(4):
        at = pl.ds((p ^ r) * 4, 4)
        outs[r][...] = (keep_ref[at].astype(F32) + got_ref[at].astype(F32)).astype(BF)


def total_at(refs, z):
    return functools.reduce(lambda a, b: a + b, [ref[z].astype(F32) for ref in refs]).astype(BF)


def line_send_kernel(chains, *refs):
    outs = refs[-4:]
    _, _, z = place_bits()
    for r in range(4):
        at = 0
        for c in range(chains):
            ins = refs[4 * c : 4 * c + 4]
            n = ins[0].shape[1]
            outs[r][at : at + n] = total_at(ins, z ^ r)
            at += n


def line_sum_kernel(a_ref, b_ref, c_ref, d_ref, out_ref):
    parts = [ref[...].astype(F32) for ref in (a_ref, b_ref, c_ref, d_ref)]
    out_ref[...] = (parts[0] + parts[1] + parts[2] + parts[3]).astype(BF)


def line_gather_kernel(a_ref, b_ref, c_ref, d_ref, out_ref):
    _, _, z = place_bits()
    for r, ref in enumerate((a_ref, b_ref, c_ref, d_ref)):
        out_ref[z ^ r] = ref[...]


def plane_gather_kernel(a_ref, b_ref, c_ref, d_ref, *rest):
    out_ref = rest[-1]
    _, p, _ = place_bits()
    for r, ref in enumerate((a_ref, b_ref, c_ref, d_ref)):
        out_ref[pl.ds((p ^ r) * 4, 4)] = ref[...]


def pass_kernel(*_):
    pass


def finish_kernel(own, half_ref, *rest):
    buf, sems = rest[-2:]
    outs = rest[-5:-2]
    core, _, _ = place_bits()
    at = pl.multiple_of((core if own else 1 - core) * (CH // 2), CH // 2)
    copies = []
    k = 0
    for out in outs:
        for m in range(out.shape[0]):
            buf[k] = half_ref[:, k].reshape(CH, CH // 2).astype(F32)
            copies.append(
                pltpu.make_async_copy(buf.at[k], out.at[m, :, pl.ds(at, CH // 2)], sems.at[k])
            )
            copies[-1].start()
            k += 1
    for copy in copies:
        copy.wait()


VMEM = pl.BlockSpec(memory_space=pltpu.VMEM)
SMEM = pl.BlockSpec(memory_space=pltpu.SMEM)
ANY = pl.BlockSpec(memory_space=pl.ANY)
HBM = pl.BlockSpec(memory_space=pltpu.HBM)


def call(kernel, name, ins, outs, scratch=(), flops=0, alias=None):
    shapes = [jax.ShapeDtypeStruct(o[1], o[2] if len(o) > 2 else BF) for o in outs]
    moved = sum(a.size * a.dtype.itemsize for s, a in ins if s is not ANY)
    moved += sum(s.size * s.dtype.itemsize for s in shapes)
    return pl.pallas_call(
        kernel,
        out_shape=shapes,
        in_specs=[s for s, _ in ins],
        out_specs=[o[0] for o in outs],
        scratch_shapes=list(scratch),
        compiler_params=pltpu.CompilerParams(vmem_limit_bytes=10 * 2**20),
        cost_estimate=pl.CostEstimate(flops=flops, bytes_accessed=moved, transcendentals=0),
        input_output_aliases=alias or {},
        name=name,
    )(*[a for _, a in ins])


AXES = ("tm", "grp")


def plan(tm, grp):
    low, total = grp.bit_length() - 1, (tm * grp).bit_length() - 1
    used = [low, low + 1, 0, low + 2, low + 3]
    return used + [b for b in range(total) if b not in used]


def swap(value, tm, grp, *bits):
    flip = sum(1 << b for b in bits)
    return lax.ppermute(value, AXES, [(d, d ^ flip) for d in range(tm * grp)])


def core_round(send, tm, grp):
    return swap(send, tm, grp, plan(tm, grp)[0])


def plane_send(keep, got, after):
    n = keep.shape[1]
    ins = [(VMEM, keep), (VMEM, got)] + [(ANY, a) for a in after]
    return call(plane_send_kernel, "plane_send", ins, [(VMEM, (4, n, 16, CH // 2))] * 4)


def plane_round(parts, tm, grp):
    _, x, y = plan(tm, grp)[:3]
    return [parts[0], swap(parts[1], tm, grp, x), swap(parts[2], tm, grp, y), swap(parts[3], tm, grp, x, y)]


def line_send(*chains):
    n = sum(parts[0].shape[1] for parts in chains)
    ins = [(VMEM, a) for parts in chains for a in parts]
    kernel = functools.partial(line_send_kernel, len(chains))
    return call(kernel, "line_send", ins, [(VMEM, (n, 16, CH // 2))] * 4)


def line_round(parts, tm, grp):
    _, _, _, a, b = plan(tm, grp)[:5]
    return [parts[0], swap(parts[1], tm, grp, a), swap(parts[2], tm, grp, b), swap(parts[3], tm, grp, a, b)]


def line_gather(parts, tm, grp):
    (mine,) = call(line_sum_kernel, "line_sum", [(VMEM, a) for a in parts], [(VMEM, parts[0].shape)])
    for bit in plan(tm, grp)[5:]:
        mine = (mine.astype(F32) + swap(mine, tm, grp, bit).astype(F32)).astype(BF)
    parts = line_round([mine] * 4, tm, grp)
    return call(
        line_gather_kernel, "line_gather", [(VMEM, a) for a in parts], [(VMEM, (4,) + mine.shape)]
    )[0]


def plane_gather(mine, parts, after):
    ins = [(VMEM, a) for a in parts] + [(ANY, a) for a in after]
    return call(plane_gather_kernel, "plane_gather", ins, [(VMEM, (16,) + mine.shape[1:])])[0]


def finish(own, half, before):
    n = half.shape[1]
    return call(
        functools.partial(finish_kernel, own),
        "finish",
        [(VMEM, half)] + [(HBM, a) for a in before],
        [(HBM, (m, CH, CH), F32) for m in (9, 3, 4)],
        [pltpu.VMEM((n, CH, CH // 2), F32), pltpu.SemaphoreType.DMA((n,))],
        alias={1 + i: i for i in range(len(before))},
    )


def along(value, axis, by):
    count = lax.axis_size(axis)
    pairs = [(i, i + by) for i in range(count) if 0 <= i + by < count]
    return lax.ppermute(value, axis, pairs)


def from_bands(parts):
    if len(parts) == 1:
        got = lax.ppermute(parts[0], "grp", [(0, 1), (1, 0)])
        return got, got
    return along(parts[0], "grp", 1), along(parts[1], "grp", -1)


def body(tm, grp, frames_in, span_frames, w_spatial, w_temporal, w_down, cotangent):
    slots, rows, cols, ch = frames_in.shape
    wide = rows * cols
    x = frames_in.reshape(slots, wide, ch)
    cot = cotangent.reshape(slots, wide // 4, ch)
    ws = w_spatial.reshape(9, ch, ch)
    wd = w_down.reshape(4, ch, ch)
    wt = w_temporal
    count = (SMEM, span_frames)
    tap = 2 * slots * wide * ch * ch
    tile = (rows, cols, slots, ch)
    padded = (rows + 2, cols + 2, slots, ch)
    dma = pltpu.SemaphoreType.DMA

    sides = 1 if grp == 2 else 2
    *edge, nxt = call(
        functools.partial(edges_kernel, grp),
        "edges",
        [count, (HBM, x), (VMEM, cot)],
        [(VMEM, (cols * slots, ch))] * sides + [(VMEM, (2, wide // 4, ch))],
        [pltpu.VMEM((sides, slots, 16, ch), BF), dma((sides,))],
        flops=tap // 8,
    )
    top, bot = from_bands(edge)
    nxt_got = along(nxt, "tm", -1)
    xt, acts, at = call(
        acts_kernel,
        "acts",
        [count, (VMEM, x), (ANY, nxt)],
        [(VMEM, tile), (VMEM, padded), (VMEM, (ch, (rows + 2) * 128))],
        flops=2 * tap,
    )
    half = (16, 9, 16, ch // 2)
    at, cott, gy, gs, keep_a, send_a, *edge = call(
        functools.partial(grad_spatial_kernel, grp),
        "grad_spatial",
        [count, (VMEM, at), (VMEM, top), (VMEM, bot), (VMEM, cot), (VMEM, nxt_got), (VMEM, wt), (VMEM, wd)],
        [(VMEM, at.shape), (VMEM, (rows // 2, cols // 2, slots, ch)), (VMEM, tile),
         (VMEM, (rows, cols + 2, slots, ch)), (VMEM, half), (VMEM, half)]
        + [(VMEM, (cols // 2 * slots, ch))] * sides,
        flops=14 * tap,
        alias={1: 0},
    )
    got_a = core_round(send_a, tm, grp)
    acts, sp, last_two = call(
        functools.partial(spatial_kernel, grp),
        "spatial",
        [count, (VMEM, top), (VMEM, bot), (VMEM, acts), (VMEM, ws), (ANY, send_a)],
        [(VMEM, padded), (VMEM, tile), (VMEM, (rows // 2, 32, ch))],
        flops=9 * tap,
        alias={3: 0},
    )
    prev = along(last_two, "tm", 1)
    parts_a = plane_send(keep_a, got_a, [last_two])
    cot_top, cot_bot = from_bands(edge)
    half = (16, 7, 16, ch // 2)
    down, keep_b, send_b = call(
        forward_kernel,
        "forward",
        [count, (VMEM, xt), (VMEM, sp), (VMEM, prev), (VMEM, cott), (VMEM, gy), (VMEM, wt), (VMEM, wd)]
        + [(ANY, a) for a in parts_a],
        [(VMEM, (slots, wide // 4, ch)), (VMEM, half), (VMEM, half)],
        [pltpu.VMEM(s, BF) for s in (tile, (ch, slots * wide), tile, tile, tile)],
        flops=10 * tap,
    )
    parts_a = plane_round(parts_a, tm, grp)
    (send_b,) = call(
        pass_kernel,
        "pass",
        [(ANY, send_b)] + [(ANY, a) for a in parts_a[1:]],
        [(ANY, send_b.shape)],
        alias={0: 0},
    )
    parts_b = plane_send(keep_b, core_round(send_b, tm, grp), [])
    parts_b = plane_round(parts_b, tm, grp)
    mine = line_gather(line_round(line_send(parts_a, parts_b), tm, grp), tm, grp)
    parts = plane_round([mine] * 4, tm, grp)
    (grad_x,) = call(
        functools.partial(grad_x_kernel, grp),
        "grad_x",
        [count, (VMEM, xt), (VMEM, gy), (VMEM, gs), (VMEM, cot_top), (VMEM, cot_bot), (VMEM, wt),
         (VMEM, wd), (VMEM, ws), (ANY, mine)],
        [(HBM, (slots, wide, ch))],
        [pltpu.VMEM(padded, BF), pltpu.VMEM((slots, wide, ch), BF), dma((1,))],
        flops=10 * tap,
    )
    mine = plane_gather(mine, parts, [grad_x])
    got = core_round(mine, tm, grp)
    outs = list(finish(True, mine, []))
    sum_s, sum_t, sum_d = finish(False, got, outs)
    return (
        down.reshape(cotangent.shape),
        grad_x.reshape(frames_in.shape),
        sum_s.reshape(w_spatial.shape),
        sum_t,
        sum_d.reshape(w_down.shape),
    )


def solution(mesh):
    return jax.shard_map(
        functools.partial(body, mesh.shape["tm"], mesh.shape["grp"]),
        mesh=mesh,
        in_specs=(P("tm", "grp", None, None), P("tm"), P(), P(), P(), P("tm", "grp", None, None)),
        out_specs=(P("tm", "grp", None, None), P("tm", "grp", None, None), P(), P(), P()),
        check_vma=False,
    )
```

```python
import functools

import jax
import jax.numpy as jnp
from jax import lax
from jax.experimental import pallas as pl
from jax.experimental.pallas import tpu as pltpu
from jax.sharding import PartitionSpec as P

SLOTS = 16
OWN = 14
CH = 256
BF = jnp.bfloat16
F32 = jnp.float32


def mm(a, b):
    return lax.dot_general(a, b, (((1,), (0,)), ((), ())), preferred_element_type=F32)


def mm_nt(a, b):
    return lax.dot_general(a, b, (((1,), (1,)), ((), ())), preferred_element_type=F32)


def iotas(rows, cols):
    return (
        lax.broadcasted_iota(jnp.int32, (rows, cols), 0),
        lax.broadcasted_iota(jnp.int32, (rows, cols), 1),
    )


def to_slots(rows, frames, keep):
    a, b = iotas(rows * SLOTS, frames * rows)
    hit = (a // SLOTS == b % rows) & keep(b // rows, a % SLOTS)
    return jnp.where(hit, 1.0, 0.0).astype(BF)


def to_frames(rows):
    a, b = iotas(SLOTS * rows, rows * SLOTS)
    hit = (a % rows == b // SLOTS) & (a // rows == b % SLOTS)
    return jnp.where(hit, 1.0, 0.0).astype(BF)


def own_frames(count):
    return lambda frame, slot: (frame == slot) & (slot < count)


def own_and_next(count):
    return lambda frame, slot: ((frame < OWN) & (frame == slot) & (slot < count)) | (
        (frame >= OWN) & (slot == count + frame - OWN)
    )


def silu_norm(v):
    scaled = v * lax.rsqrt(jnp.mean(v * v, axis=-1, keepdims=True) + 1e-06)
    return scaled / (1.0 + jnp.exp(-scaled))


def slot_mask(shape, count):
    return lax.broadcasted_iota(jnp.int32, shape, len(shape) - 2) < count


def grad_of_temporal(gy, wt_ref, count):
    n = gy.shape[0]
    flat = gy.reshape(n * SLOTS, CH)
    total = mm_nt(flat, wt_ref[2]).reshape(n, SLOTS, CH)
    for k in (1, 0):
        term = mm_nt(flat, wt_ref[k]).reshape(n, SLOTS, CH)
        total = total + pltpu.roll(term, SLOTS - (2 - k), 1)
    return jnp.where(slot_mask(total.shape, count), total, 0.0).astype(BF)


def halving_bits():
    t, g = lax.axis_index("tm"), lax.axis_index("grp")
    x, y, z0, z1 = (t >> 1) & 1, g & 1, (t >> 2) & 1, (t >> 3) & 1
    return t & 1, ((x, y, z0, z1), (z0, x, y, z1))


def round_bit(k):
    core, (first, second) = halving_bits()
    return jnp.where(core == 0, first[k], second[k])


def split_cores(value, keep_ref, send_ref, k):
    core, _ = halving_bits()
    low, high = value[:, : CH // 2].astype(BF), value[:, CH // 2 :].astype(BF)
    keep_ref[:, k] = jnp.where(core == 0, low, high).reshape(16, 16, CH // 2)
    send_ref[:, k] = jnp.where(core == 0, high, low).reshape(16, 16, CH // 2)


def edges_kernel(bands, count_ref, x_ref, cot_ref, *rest):
    outs, (nxt_ref, token_ref, buf, sems) = rest[:-4], rest[-4:]
    token_ref[...] = jnp.zeros_like(token_ref)
    count = count_ref[0]
    band = lax.axis_index("grp")
    wide = x_ref.shape[1]
    if bands == 2:
        starts = [jnp.where(band == 0, wide - 16, 0)]
        lower = [band == 0]
    else:
        starts, lower = [wide - 16, 0], [True, False]
    copies = [
        pltpu.make_async_copy(
            x_ref.at[:, pl.ds(pl.multiple_of(at, 16), 16), :], buf.at[k], sems.at[k]
        )
        for k, at in enumerate(starts)
    ]
    for copy in copies:
        copy.start()
    nxt_ref[...] = cot_ref[0:2]
    place = to_slots(16, SLOTS, own_frames(count))
    for k, copy in enumerate(copies):
        copy.wait()
        v = mm(place, buf[k].reshape(SLOTS * 16, CH))
        v = jnp.where(lower[k], v[128:], v[:128])
        outs[k][...] = silu_norm(v).astype(BF)


def acts_kernel(count_ref, x_hbm, _, xt_ref, acts_ref, at_ref, x_ref, sems):
    count = count_ref[0]
    pieces = sems.shape[0]
    size = x_hbm.shape[1] // pieces

    def copy_of(k):
        at = pl.ds(pl.multiple_of(k * size, size), size)
        return pltpu.make_async_copy(x_hbm.at[:, at, :], x_ref.at[:, at, :], sems.at[k])

    for k in range(pieces):
        copy_of(k).start()
    rows, cols = xt_ref.shape[0], xt_ref.shape[1]
    edge = jnp.zeros((rows + 2, SLOTS, CH), BF)
    acts_ref[:, 0] = edge
    acts_ref[:, cols + 1] = edge
    place = to_slots(16, SLOTS, own_frames(count))

    def rows_of(q, _):
        at = pl.multiple_of(q * 16, 16)

        @pl.when(q % 2 == 0)
        def _():
            copy_of(q // 2).wait()

        piece = x_ref[:, pl.ds(at, 16), :].reshape(SLOTS * 16, CH)
        v = mm(place, piece)
        xt_ref[pl.ds(2 * q, 2)] = v.astype(BF).reshape(2, cols, SLOTS, CH)
        a = silu_norm(v)
        acts_ref[pl.ds(2 * q + 1, 2), 1 : cols + 1] = a.astype(BF).reshape(2, cols, SLOTS, CH)
        at_ref[:, pl.ds(pl.multiple_of(q * 256 + 128, 128), 256)] = a.T.astype(BF)
        return 0

    lax.fori_loop(0, rows // 2, rows_of, 0)


def spatial_kernel(
    bands, count_ref, top_ref, bot_ref, acts_in, ws_ref, _, acts_ref, sp_ref, edge_ref
):
    count = count_ref[0]
    band = lax.axis_index("grp")
    rows, cols = sp_ref.shape[0], sp_ref.shape[1]
    for ref, flag, row in ((top_ref, band > 0, 0), (bot_ref, band < bands - 1, rows + 1)):
        a = jnp.where(flag, ref[...].astype(F32), 0.0)
        acts_ref[row, 1 : cols + 1] = a.astype(BF).reshape(cols, SLOTS, CH)
    a, b = iotas(32, 256)
    pick = (a // 2 == b // SLOTS) & (b % SLOTS == count - 2 + a % 2)
    pick = jnp.where(pick, 1.0, 0.0).astype(BF)

    def rows_of(q, _):
        total = None
        for i in range(3):
            for j in range(3):
                left = acts_ref[pl.ds(4 * q + i, 4), j : j + cols].reshape(4 * cols * SLOTS, CH)
                term = mm(left, ws_ref[i * 3 + j])
                total = term if total is None else total + term
        out = total.astype(BF)
        sp_ref[pl.ds(4 * q, 4)] = out.reshape(4, cols, SLOTS, CH)
        for half in range(2):
            edge_ref[2 * q + half] = mm(pick, out[half * 256 : half * 256 + 256]).astype(BF)
        return 0

    lax.fori_loop(0, rows // 4, rows_of, 0)


def grad_spatial_kernel(
    bands, count_ref, at_in, top_ref, bot_ref, cot_ref, nxt_ref, wt_ref, wd_ref,
    at_ref, cott_ref, gy_ref, gs_ref, keep_ref, send_ref, *edge_refs,
):
    count = count_ref[0]
    band = lax.axis_index("grp")
    rows, cols = gy_ref.shape[0], gy_ref.shape[1]
    for ref, flag, row in ((top_ref, band > 0, 0), (bot_ref, band < bands - 1, rows + 1)):
        a = jnp.where(flag, ref[...].astype(F32), 0.0)
        at_ref[:, row * 128 : row * 128 + 128] = a.T.astype(BF)
    edge = jnp.zeros((rows, SLOTS, CH), BF)
    gs_ref[:, 0] = edge
    gs_ref[:, cols + 1] = edge

    place_next = to_slots(16, SLOTS, own_and_next(count))
    for q in range(rows * cols // 64):
        piece = jnp.concatenate(
            [cot_ref[0:OWN, q * 16 : q * 16 + 16, :], nxt_ref[:, q * 16 : q * 16 + 16, :]], 0
        ).reshape(SLOTS * 16, CH)
        placed = mm(place_next, piece).astype(BF)
        cott_ref[q * 4 : q * 4 + 4] = placed.reshape(4, 4, SLOTS, CH)
        for i in range(2):
            for j in range(2):
                g = mm_nt(placed, wd_ref[i * 2 + j]).astype(BF).reshape(4, 4, SLOTS, CH)
                for r in range(4):
                    for c in range(4):
                        gy_ref[2 * (q * 4 + r) + i, 2 * c + j] = g[r, c]
    last = cott_ref[rows // 2 - 1].reshape(cols // 2 * SLOTS, CH)
    first = cott_ref[0].reshape(cols // 2 * SLOTS, CH)
    if bands == 2:
        edge_refs[0][...] = jnp.where(band == 0, last, first)
    else:
        edge_refs[0][...] = last
        edge_refs[1][...] = first

    def grads_of(q, _):
        g = gy_ref[pl.ds(4 * q, 4)].reshape(4 * cols, SLOTS, CH)
        s = grad_of_temporal(g, wt_ref, count)
        gs_ref[pl.ds(4 * q, 4), 1 : cols + 1] = s.reshape(4, cols, SLOTS, CH)
        return 0

    lax.fori_loop(0, rows // 4, grads_of, 0)

    wide = rows * cols * SLOTS
    for i in range(3):
        for j in range(3):
            right = gs_ref[:, 2 - j : 2 - j + cols].reshape(wide, CH)
            value = mm(at_ref[:, i * 128 : i * 128 + wide], right)
            split_cores(value, keep_ref, send_ref, i * 3 + j)


def forward_kernel(
    count_ref, xt_ref, sp_ref, prev_ref, cott_ref, gy_ref, wt_ref, wd_ref, *rest
):
    down_ref, keep_ref, send_ref, y_ref, st_ref, g1_ref, g0_ref, g2_ref = rest[-8:]
    count = count_ref[0]
    rows, cols = xt_ref.shape[0], xt_ref.shape[1]
    a, b = iotas(256, 32)
    place = (a // SLOTS == b // 2) & (a % SLOTS == OWN + b % 2)
    place = jnp.where(place, 1.0, 0.0).astype(BF)

    def rows_of(q, _):
        s = sp_ref[pl.ds(2 * q, 2)].reshape(256, CH)
        s = (s.astype(F32) + mm(place, prev_ref[q])).astype(BF)
        st_ref[:, pl.ds(pl.multiple_of(q * 256, 256), 256)] = s.T
        total = mm(s, wt_ref[2]).reshape(2 * cols, SLOTS, CH)
        for k in (1, 0):
            total = total + pltpu.roll(mm(s, wt_ref[k]).reshape(2 * cols, SLOTS, CH), 2 - k, 1)
        x = xt_ref[pl.ds(2 * q, 2)].reshape(2 * cols, SLOTS, CH).astype(F32)
        mask = slot_mask(x.shape, count)
        y = jnp.where(mask, x + total, 0.0).astype(BF)
        y_ref[pl.ds(2 * q, 2)] = y.reshape(2, cols, SLOTS, CH)
        g = gy_ref[pl.ds(2 * q, 2)].reshape(2 * cols, SLOTS, CH).astype(F32)
        g = jnp.where(mask, g, 0.0)
        for ref, k in ((g2_ref, 2), (g1_ref, 1), (g0_ref, 0)):
            shifted = g if k == 2 else pltpu.roll(g, SLOTS - (2 - k), 1)
            ref[pl.ds(2 * q, 2)] = shifted.astype(BF).reshape(2, cols, SLOTS, CH)
        return 0

    lax.fori_loop(0, rows // 2, rows_of, 0)

    wide = rows * cols * SLOTS
    for k, ref in ((0, g0_ref), (1, g1_ref), (2, g2_ref)):
        split_cores(mm(st_ref[...], ref[...].reshape(wide, CH)), keep_ref, send_ref, k)

    small = wide // 4
    total = None
    cot = cott_ref[...].reshape(small, CH)
    for i in range(2):
        for j in range(2):
            tiles = [
                y_ref[2 * r + i, 2 * c + j] for r in range(rows // 2) for c in range(cols // 2)
            ]
            piece = jnp.concatenate(tiles, axis=0)
            term = mm(piece, wd_ref[i * 2 + j])
            total = term if total is None else total + term
            split_cores(mm(piece.T, cot), keep_ref, send_ref, 3 + i * 2 + j)
    down = total.astype(BF)
    back = to_frames(16)
    for q in range(small // 256):
        o = mm(back, down[q * 256 : q * 256 + 256]).astype(BF)
        down_ref[:, q * 16 : q * 16 + 16, :] = o.reshape(SLOTS, 16, CH)


def grad_x_kernel(
    part, bands, count_ref, xt_ref, gy_ref, gs_ref, halo_ref, wt_ref, wd_ref, ws_ref, *rest
):
    out_ref, token_ref, pad_ref, buf, sems = rest[-5:]
    count = count_ref[0]
    band = lax.axis_index("grp")
    rows, cols = xt_ref.shape[0], xt_ref.shape[1]
    half = rows // 2
    if part == 0:
        flag, i, row = band > 0, 1, 0
        pad_ref[1 : half + 2] = gs_ref[0 : half + 1]
    else:
        flag, i, row = band < bands - 1, 0, half + 1
        pad_ref[0 : half + 1] = gs_ref[half - 1 :]
    edge = jnp.zeros((SLOTS, CH), BF)
    pair = [
        mm_nt(halo_ref[...], wd_ref[i * 2 + j]).astype(BF).reshape(cols // 2, SLOTS, CH)
        for j in range(2)
    ]
    g = jnp.stack(pair, axis=1).reshape(cols, SLOTS, CH)
    pad_ref[row, 0] = edge
    pad_ref[row, 1 : cols + 1] = grad_of_temporal(g, wt_ref, jnp.where(flag, count, 0))
    pad_ref[row, cols + 1] = edge
    back = to_frames(16)

    def rows_of(q, _):
        total = None
        for i in range(3):
            for j in range(3):
                left = pad_ref[pl.ds(4 * q + 2 - i, 4), 2 - j : 2 - j + cols].reshape(
                    4 * cols * SLOTS, CH
                )
                term = mm_nt(left, ws_ref[i * 3 + j])
                total = term if total is None else total + term
        at = part * half + 4 * q
        v = xt_ref[pl.ds(at, 4)].reshape(4 * cols * SLOTS, CH).astype(F32)
        r = lax.rsqrt(jnp.mean(v * v, axis=-1, keepdims=True) + 1e-06)
        u = v * r
        s = 1.0 / (1.0 + jnp.exp(-u))
        gu = total * (s * (1.0 + u * (1.0 - s)))
        dot = jnp.mean(gu * u, axis=-1, keepdims=True)
        gv = r * (gu - u * dot)
        gx = gy_ref[pl.ds(at, 4)].reshape(4 * cols * SLOTS, CH).astype(F32) + gv
        gx = gx.reshape(4 * cols, SLOTS, CH)
        gx = jnp.where(slot_mask(gx.shape, count), gx, 0.0).astype(BF).reshape(4 * cols * SLOTS, CH)
        for k in range(2):
            o = mm(back, gx[k * 256 : k * 256 + 256]).astype(BF)
            buf[:, pl.ds(pl.multiple_of((2 * q + k) * 16, 16), 16), :] = o.reshape(SLOTS, 16, CH)
        return 0

    lax.fori_loop(0, half // 4, rows_of, 0)
    size = half * cols
    copy = pltpu.make_async_copy(buf, out_ref.at[:, part * size : part * size + size, :], sems.at[0])
    token_ref[...] = jnp.zeros_like(token_ref)
    copy.start()
    copy.wait()


def halve_kernel(k, chains, *refs):
    send_ref, keep_ref = refs[-2:]
    bit = round_bit(k)
    m = send_ref.shape[0]
    at = 0
    for c in range(chains):
        a, b = refs[2 * c : 2 * c + 2]
        n = a.shape[1]
        for ref, side in ((send_ref, 1 - bit), (keep_ref, bit)):
            part = pl.ds(side * m, m)
            ref[:, at : at + n] = (a[part].astype(F32) + b[part].astype(F32)).astype(BF)
        at += n


def add_kernel(a_ref, b_ref, out_ref):
    out_ref[...] = (a_ref[...].astype(F32) + b_ref[...].astype(F32)).astype(BF)


def double_kernel(k, own_ref, got_ref, *rest):
    out_ref = rest[-1]
    bit = round_bit(k)
    m = own_ref.shape[0]
    out_ref[pl.ds(bit * m, m)] = own_ref[...]
    out_ref[pl.ds((1 - bit) * m, m)] = got_ref[...]


def pass_kernel(*_):
    pass


def finish_kernel(which, *refs):
    buf, sems = refs[-2:]
    outs, token_ref = refs[-6:-3], refs[-3]
    token_ref[...] = jnp.zeros_like(token_ref)
    core, (first, second) = halving_bits()
    mine = jnp.where(core == 0, first[0], second[0])
    other = jnp.where(core == 0, second[0], first[0])
    copies = []
    k = 0
    for ref, (sibling, far) in zip(refs, which):
        rows = other if sibling else mine
        rows = pl.ds(pl.multiple_of((1 - rows if far else rows) * (CH // 2), CH // 2), CH // 2)
        cols = pl.ds(pl.multiple_of((1 - core if sibling else core) * (CH // 2), CH // 2), CH // 2)
        m = 0
        for out in outs:
            for o in range(out.shape[0]):
                buf[k] = ref[:, m].reshape(CH // 2, CH // 2).astype(F32)
                copies.append(pltpu.make_async_copy(buf.at[k], out.at[o, rows, cols], sems.at[k]))
                copies[-1].start()
                k += 1
                m += 1
    for copy in copies:
        copy.wait()


VMEM = pl.BlockSpec(memory_space=pltpu.VMEM)
SMEM = pl.BlockSpec(memory_space=pltpu.SMEM)
ANY = pl.BlockSpec(memory_space=pl.ANY)
HBM = pl.BlockSpec(memory_space=pltpu.HBM)
TOKEN = (VMEM, (8, 128), F32)


def call(kernel, name, ins, outs, scratch=(), flops=0, alias=None, grant=10):
    shapes = [jax.ShapeDtypeStruct(o[1], o[2] if len(o) > 2 else BF) for o in outs]
    moved = sum(a.size * a.dtype.itemsize for s, a in ins if s is not ANY)
    moved += sum(s.size * s.dtype.itemsize for s in shapes)
    return pl.pallas_call(
        kernel,
        out_shape=shapes,
        in_specs=[s for s, _ in ins],
        out_specs=[o[0] for o in outs],
        scratch_shapes=list(scratch),
        compiler_params=pltpu.CompilerParams(vmem_limit_bytes=grant * 2**20),
        cost_estimate=pl.CostEstimate(flops=flops, bytes_accessed=moved, transcendentals=0),
        input_output_aliases=alias or {},
        name=name,
    )(*[a for _, a in ins])


AXES = ("tm", "grp")


def plan(tm, grp):
    low, total = grp.bit_length() - 1, (tm * grp).bit_length() - 1
    used = [low, low + 1, 0, low + 2, low + 3]
    return used, [b for b in range(total) if b not in used]


def swap(value, tm, grp, first, second):
    core = plan(tm, grp)[0][0]
    pairs = [(d, d ^ (1 << (second if (d >> core) & 1 else first))) for d in range(tm * grp)]
    return lax.ppermute(value, AXES, pairs)


def core_round(value, tm, grp):
    core = plan(tm, grp)[0][0]
    return swap(value, tm, grp, core, core)


def link_round(k, value, tm, grp):
    _, x, y, z0, z1 = plan(tm, grp)[0]
    return swap(value, tm, grp, (x, y, z0, z1)[k], (z0, x, y, z1)[k])


def halve(k, chains, after=()):
    n = sum(a.shape[1] for a, _ in chains)
    shape = (chains[0][0].shape[0] // 2, n, 16, CH // 2)
    ins = [(VMEM, a) for pair in chains for a in pair] + [(ANY, a) for a in after]
    kernel = functools.partial(halve_kernel, k, len(chains))
    return call(kernel, f"halve_{k}", ins, [(VMEM, shape)] * 2)


def double(k, own, got, after=()):
    shape = (own.shape[0] * 2,) + own.shape[1:]
    ins = [(VMEM, own), (VMEM, got)] + [(ANY, a) for a in after]
    return call(functools.partial(double_kernel, k), f"double_{k}", ins, [(VMEM, shape)])[0]


def passed(value, after):
    ins = [(ANY, value)] + [(ANY, a) for a in after]
    return call(pass_kernel, "pass", ins, [(ANY, value.shape)], alias={0: 0})[0]


def finish(quarters, before):
    n = quarters[0][0].shape[1] * len(quarters)
    *outs, token = (
        call(
            functools.partial(finish_kernel, [q[1:] for q in quarters]),
            "finish",
            [(VMEM, q[0]) for q in quarters] + [(HBM, a) for a in before],
            [(HBM, (m, CH, CH), F32) for m in (9, 3, 4)] + [TOKEN],
            [pltpu.VMEM((n, CH // 2, CH // 2), F32), pltpu.SemaphoreType.DMA((n,))],
            alias={len(quarters) + i: i for i in range(len(before))},
        )
    )
    return outs, token


def along(value, axis, by):
    count = lax.axis_size(axis)
    pairs = [(i, i + by) for i in range(count) if 0 <= i + by < count]
    return lax.ppermute(value, axis, pairs)


def from_bands(parts):
    if len(parts) == 1:
        got = lax.ppermute(parts[0], "grp", [(0, 1), (1, 0)])
        return got, got
    return along(parts[0], "grp", 1), along(parts[1], "grp", -1)


def body(tm, grp, frames_in, span_frames, w_spatial, w_temporal, w_down, cotangent):
    slots, rows, cols, ch = frames_in.shape
    wide = rows * cols
    x = frames_in.reshape(slots, wide, ch)
    cot = cotangent.reshape(slots, wide // 4, ch)
    ws = w_spatial.reshape(9, ch, ch)
    wd = w_down.reshape(4, ch, ch)
    wt = w_temporal
    count = (SMEM, span_frames)
    tap = 2 * slots * wide * ch * ch
    tile = (rows, cols, slots, ch)
    padded = (rows + 2, cols + 2, slots, ch)
    dma = pltpu.SemaphoreType.DMA

    sides = 1 if grp == 2 else 2
    *edge, nxt, token = call(
        functools.partial(edges_kernel, grp),
        "edges",
        [count, (HBM, x), (VMEM, cot)],
        [(VMEM, (cols * slots, ch))] * sides + [(VMEM, (2, wide // 4, ch)), TOKEN],
        [pltpu.VMEM((sides, slots, 16, ch), BF), dma((sides,))],
        flops=tap // 8,
        grant=56,
    )
    top, bot = from_bands(edge)
    nxt_got = along(nxt, "tm", -1)
    xt, acts, at = call(
        acts_kernel,
        "acts",
        [count, (HBM, x), (ANY, token)],
        [(VMEM, tile), (VMEM, padded), (VMEM, (ch, (rows + 2) * 128))],
        [pltpu.VMEM((slots, wide, ch), BF), dma((4,))],
        flops=2 * tap,
    )
    half = (16, 9, 16, ch // 2)
    at, cott, gy, gs, keep_a, send_a, *edge = call(
        functools.partial(grad_spatial_kernel, grp),
        "grad_spatial",
        [count, (VMEM, at), (VMEM, top), (VMEM, bot), (VMEM, cot), (VMEM, nxt_got), (VMEM, wt), (VMEM, wd)],
        [(VMEM, at.shape), (VMEM, (rows // 2, cols // 2, slots, ch)), (VMEM, tile),
         (VMEM, (rows, cols + 2, slots, ch)), (VMEM, half), (VMEM, half)]
        + [(VMEM, (cols // 2 * slots, ch))] * sides,
        flops=14 * tap,
        alias={1: 0},
    )
    got_a = core_round(send_a, tm, grp)
    acts, sp, last_two = call(
        functools.partial(spatial_kernel, grp),
        "spatial",
        [count, (VMEM, top), (VMEM, bot), (VMEM, acts), (VMEM, ws), (ANY, send_a)],
        [(VMEM, padded), (VMEM, tile), (VMEM, (rows // 2, 32, ch))],
        flops=9 * tap,
        alias={3: 0},
    )
    prev = along(last_two, "tm", 1)
    send_a, keep_a = halve(0, [(keep_a, got_a)], [last_two])
    cot_top, cot_bot = from_bands(edge)
    half = (16, 7, 16, ch // 2)
    down, keep_b, send_b = call(
        forward_kernel,
        "forward",
        [count, (VMEM, xt), (VMEM, sp), (VMEM, prev), (VMEM, cott), (VMEM, gy), (VMEM, wt), (VMEM, wd)]
        + [(ANY, send_a)],
        [(VMEM, (slots, wide // 4, ch)), (VMEM, half), (VMEM, half)],
        [pltpu.VMEM(s, BF) for s in (tile, (ch, slots * wide), tile, tile, tile)],
        flops=10 * tap,
    )
    got_a = link_round(0, send_a, tm, grp)
    send_b = passed(send_b, [got_a])
    send_b, keep_b = halve(0, [(keep_b, core_round(send_b, tm, grp))])
    got_b = link_round(0, send_b, tm, grp)
    send, keep = halve(1, [(keep_a, got_a), (keep_b, got_b)])
    for k in (2, 3):
        send, keep = halve(k, [(keep, link_round(k - 1, send, tm, grp))])
    got = link_round(3, send, tm, grp)
    (mine,) = call(add_kernel, "add", [(VMEM, keep), (VMEM, got)], [(VMEM, keep.shape)])
    for bit in plan(tm, grp)[1]:
        mine = (mine.astype(F32) + swap(mine, tm, grp, bit, bit).astype(F32)).astype(BF)
    for k in (3, 2):
        mine = double(k, mine, link_round(k, mine, tm, grp))

    def grad_x_part(part, halo, before, after):
        return call(
            functools.partial(grad_x_kernel, part, grp),
            "grad_x",
            [count, (VMEM, xt), (VMEM, gy), (VMEM, gs), (VMEM, halo), (VMEM, wt), (VMEM, wd), (VMEM, ws)]
            + [(HBM, a) for a in before] + [(ANY, a) for a in after],
            [(HBM, (slots, wide, ch)), TOKEN],
            [pltpu.VMEM((rows // 2 + 2, cols + 2, slots, ch), BF),
             pltpu.VMEM((slots, wide // 2, ch), BF), dma((1,))],
            flops=5 * tap,
            alias={8: 0} if before else None,
        )

    got = link_round(1, mine, tm, grp)
    grad_x, token = grad_x_part(0, cot_top, [], [mine])
    mine = double(1, mine, got, [token])
    far = link_round(0, mine, tm, grp)
    side = core_round(mine, tm, grp)
    grad_x, token = grad_x_part(1, cot_bot, [grad_x], [mine])
    outs, ended = finish([(mine, False, False), (side, True, False)], [])
    far = passed(far, [token, ended])
    side = core_round(far, tm, grp)
    outs, _ = finish([(far, False, True)], outs)
    outs, _ = finish([(side, True, True)], outs)
    sum_s, sum_t, sum_d = outs
    return (
        down.reshape(cotangent.shape),
        grad_x.reshape(frames_in.shape),
        sum_s.reshape(w_spatial.shape),
        sum_t,
        sum_d.reshape(w_down.shape),
    )


def solution(mesh):
    return jax.shard_map(
        functools.partial(body, mesh.shape["tm"], mesh.shape["grp"]),
        mesh=mesh,
        in_specs=(P("tm", "grp", None, None), P("tm"), P(), P(), P(), P("tm", "grp", None, None)),
        out_specs=(P("tm", "grp", None, None), P("tm", "grp", None, None), P(), P(), P()),
        check_vma=False,
    )
```

```python
import functools

import jax
import jax.numpy as jnp
from jax import lax
from jax.experimental import pallas as pl
from jax.experimental.pallas import tpu as pltpu
from jax.sharding import PartitionSpec as P

SLOTS = 16
OWN = 14
CH = 256
BF = jnp.bfloat16
F32 = jnp.float32


def mm(a, b):
    return lax.dot_general(a, b, (((1,), (0,)), ((), ())), preferred_element_type=F32)


def mm_nt(a, b):
    return lax.dot_general(a, b, (((1,), (1,)), ((), ())), preferred_element_type=F32)


def iotas(rows, cols):
    return (
        lax.broadcasted_iota(jnp.int32, (rows, cols), 0),
        lax.broadcasted_iota(jnp.int32, (rows, cols), 1),
    )


def to_slots(rows, frames, keep):
    a, b = iotas(rows * SLOTS, frames * rows)
    hit = (a // SLOTS == b % rows) & keep(b // rows, a % SLOTS)
    return jnp.where(hit, 1.0, 0.0).astype(BF)


def to_frames(rows):
    a, b = iotas(SLOTS * rows, rows * SLOTS)
    hit = (a % rows == b // SLOTS) & (a // rows == b % SLOTS)
    return jnp.where(hit, 1.0, 0.0).astype(BF)


def own_frames(count):
    return lambda frame, slot: (frame == slot) & (slot < count)


def own_and_next(count):
    return lambda frame, slot: ((frame < OWN) & (frame == slot) & (slot < count)) | (
        (frame >= OWN) & (slot == count + frame - OWN)
    )


def silu_norm(v):
    scaled = v * lax.rsqrt(jnp.mean(v * v, axis=-1, keepdims=True) + 1e-06)
    return scaled / (1.0 + jnp.exp(-scaled))


def slot_mask(shape, count):
    return lax.broadcasted_iota(jnp.int32, shape, len(shape) - 2) < count


def grad_of_temporal(gy, wt_ref, count):
    n = gy.shape[0]
    flat = gy.reshape(n * SLOTS, CH)
    total = mm_nt(flat, wt_ref[2]).reshape(n, SLOTS, CH)
    for k in (1, 0):
        term = mm_nt(flat, wt_ref[k]).reshape(n, SLOTS, CH)
        total = total + pltpu.roll(term, SLOTS - (2 - k), 1)
    return jnp.where(slot_mask(total.shape, count), total, 0.0).astype(BF)


def place_bits():
    t, g = lax.axis_index("tm"), lax.axis_index("grp")
    return t & 1, ((t >> 1) & 1) + 2 * (g & 1) + 4 * ((t >> 2) & 1)


def split_cores(value, keep_ref, send_ref, k):
    core, _ = place_bits()
    low, high = value[:, : CH // 2].astype(BF), value[:, CH // 2 :].astype(BF)
    keep_ref[:, k] = jnp.where(core == 0, low, high).reshape(8, 32, CH // 2)
    send_ref[:, k] = jnp.where(core == 0, high, low).reshape(8, 32, CH // 2)


def edges_kernel(bands, count_ref, x_ref, cot_ref, *rest):
    outs, (nxt_ref, token_ref) = rest[:-2], rest[-2:]
    token_ref[...] = jnp.zeros_like(token_ref)
    count = count_ref[0]
    band = lax.axis_index("grp")
    wide = x_ref.shape[1]
    if bands == 2:
        starts, lower = [jnp.where(band == 0, wide - 16, 0)], [band == 0]
    else:
        starts, lower = [wide - 16, 0], [True, False]
    nxt_ref[...] = cot_ref[0:2]
    place = to_slots(16, SLOTS, own_frames(count))
    for k, at in enumerate(starts):
        piece = x_ref[:, pl.ds(pl.multiple_of(at, 16), 16), :].reshape(SLOTS * 16, CH)
        v = mm(place, piece)
        v = jnp.where(lower[k], v[128:], v[:128])
        outs[k][...] = silu_norm(v).astype(BF)


def acts_kernel(count_ref, x_ref, _, xt_ref, acts_ref, at_ref):
    count = count_ref[0]
    rows, cols = xt_ref.shape[0], xt_ref.shape[1]
    edge = jnp.zeros((rows + 2, SLOTS, CH), BF)
    acts_ref[:, 0] = edge
    acts_ref[:, cols + 1] = edge
    place = to_slots(16, SLOTS, own_frames(count))

    def rows_of(q, _):
        at = pl.multiple_of(q * 16, 16)
        piece = x_ref[:, pl.ds(at, 16), :].reshape(SLOTS * 16, CH)
        v = mm(place, piece)
        xt_ref[pl.ds(2 * q, 2)] = v.astype(BF).reshape(2, cols, SLOTS, CH)
        a = silu_norm(v)
        acts_ref[pl.ds(2 * q + 1, 2), 1 : cols + 1] = a.astype(BF).reshape(2, cols, SLOTS, CH)
        at_ref[:, pl.ds(pl.multiple_of(q * 256 + 128, 128), 256)] = a.T.astype(BF)
        return 0

    lax.fori_loop(0, rows // 2, rows_of, 0)


def spatial_kernel(
    bands, count_ref, top_ref, bot_ref, acts_in, ws_ref, acts_ref, sp_ref, edge_ref
):
    count = count_ref[0]
    band = lax.axis_index("grp")
    rows, cols = sp_ref.shape[0], sp_ref.shape[1]
    for ref, flag, row in ((top_ref, band > 0, 0), (bot_ref, band < bands - 1, rows + 1)):
        a = jnp.where(flag, ref[...].astype(F32), 0.0)
        acts_ref[row, 1 : cols + 1] = a.astype(BF).reshape(cols, SLOTS, CH)
    a, b = iotas(32, 256)
    pick = (a // 2 == b // SLOTS) & (b % SLOTS == count - 2 + a % 2)
    pick = jnp.where(pick, 1.0, 0.0).astype(BF)

    def rows_of(q, _):
        total = None
        for i in range(3):
            for j in range(3):
                left = acts_ref[pl.ds(4 * q + i, 4), j : j + cols].reshape(4 * cols * SLOTS, CH)
                term = mm(left, ws_ref[i * 3 + j])
                total = term if total is None else total + term
        out = total.astype(BF)
        sp_ref[pl.ds(4 * q, 4)] = out.reshape(4, cols, SLOTS, CH)
        for half in range(2):
            edge_ref[2 * q + half] = mm(pick, out[half * 256 : half * 256 + 256]).astype(BF)
        return 0

    lax.fori_loop(0, rows // 4, rows_of, 0)


def grad_spatial_kernel(
    bands, count_ref, at_in, top_ref, bot_ref, cot_ref, nxt_ref, wt_ref, wd_ref, _,
    at_ref, cott_ref, gy_ref, gs_ref, keep_ref, send_ref, *edge_refs,
):
    count = count_ref[0]
    band = lax.axis_index("grp")
    rows, cols = gy_ref.shape[0], gy_ref.shape[1]
    for ref, flag, row in ((top_ref, band > 0, 0), (bot_ref, band < bands - 1, rows + 1)):
        a = jnp.where(flag, ref[...].astype(F32), 0.0)
        at_ref[:, row * 128 : row * 128 + 128] = a.T.astype(BF)
    edge = jnp.zeros((rows, SLOTS, CH), BF)
    gs_ref[:, 0] = edge
    gs_ref[:, cols + 1] = edge

    place_next = to_slots(16, SLOTS, own_and_next(count))
    for q in range(rows * cols // 64):
        four = slice(q * 4, q * 4 + 4)
        piece = jnp.concatenate(
            [cot_ref[0:OWN, four].reshape(OWN, 16, CH), nxt_ref[:, four].reshape(2, 16, CH)], 0
        ).reshape(SLOTS * 16, CH)
        placed = mm(place_next, piece).astype(BF)
        cott_ref[q * 4 : q * 4 + 4] = placed.reshape(4, 4, SLOTS, CH)
        for i in range(2):
            for j in range(2):
                g = mm_nt(placed, wd_ref[i * 2 + j]).astype(BF).reshape(4, 4, SLOTS, CH)
                for r in range(4):
                    for c in range(4):
                        gy_ref[2 * (q * 4 + r) + i, 2 * c + j] = g[r, c]
    last = cott_ref[rows // 2 - 1].reshape(cols // 2 * SLOTS, CH)
    first = cott_ref[0].reshape(cols // 2 * SLOTS, CH)
    if bands == 2:
        edge_refs[0][...] = jnp.where(band == 0, last, first)
    else:
        edge_refs[0][...] = last
        edge_refs[1][...] = first

    def grads_of(q, _):
        g = gy_ref[pl.ds(4 * q, 4)].reshape(4 * cols, SLOTS, CH)
        s = grad_of_temporal(g, wt_ref, count)
        gs_ref[pl.ds(4 * q, 4), 1 : cols + 1] = s.reshape(4, cols, SLOTS, CH)
        return 0

    lax.fori_loop(0, rows // 4, grads_of, 0)

    wide = rows * cols * SLOTS
    for i in range(3):
        for j in range(3):
            right = gs_ref[:, 2 - j : 2 - j + cols].reshape(wide, CH)
            value = mm(at_ref[:, i * 128 : i * 128 + wide], right)
            split_cores(value, keep_ref, send_ref, i * 3 + j)


def forward_kernel(
    count_ref, xt_ref, sp_ref, prev_ref, cott_ref, gy_ref, wt_ref, wd_ref, *rest
):
    down_ref, keep_ref, send_ref, y_ref, st_ref, g1_ref, g0_ref, g2_ref = rest[-8:]
    count = count_ref[0]
    rows, cols = xt_ref.shape[0], xt_ref.shape[1]
    a, b = iotas(256, 32)
    place = (a // SLOTS == b // 2) & (a % SLOTS == OWN + b % 2)
    place = jnp.where(place, 1.0, 0.0).astype(BF)

    def rows_of(q, _):
        s = sp_ref[pl.ds(2 * q, 2)].reshape(256, CH)
        s = (s.astype(F32) + mm(place, prev_ref[q])).astype(BF)
        st_ref[:, pl.ds(pl.multiple_of(q * 256, 256), 256)] = s.T
        total = mm(s, wt_ref[2]).reshape(2 * cols, SLOTS, CH)
        for k in (1, 0):
            total = total + pltpu.roll(mm(s, wt_ref[k]).reshape(2 * cols, SLOTS, CH), 2 - k, 1)
        x = xt_ref[pl.ds(2 * q, 2)].reshape(2 * cols, SLOTS, CH).astype(F32)
        mask = slot_mask(x.shape, count)
        y = jnp.where(mask, x + total, 0.0).astype(BF)
        y_ref[pl.ds(2 * q, 2)] = y.reshape(2, cols, SLOTS, CH)
        g = gy_ref[pl.ds(2 * q, 2)].reshape(2 * cols, SLOTS, CH).astype(F32)
        g = jnp.where(mask, g, 0.0)
        for ref, k in ((g2_ref, 2), (g1_ref, 1), (g0_ref, 0)):
            shifted = g if k == 2 else pltpu.roll(g, SLOTS - (2 - k), 1)
            ref[pl.ds(2 * q, 2)] = shifted.astype(BF).reshape(2, cols, SLOTS, CH)
        return 0

    lax.fori_loop(0, rows // 2, rows_of, 0)

    wide = rows * cols * SLOTS
    for k, ref in ((0, g0_ref), (1, g1_ref), (2, g2_ref)):
        split_cores(mm(st_ref[...], ref[...].reshape(wide, CH)), keep_ref, send_ref, k)

    small = wide // 4
    total = None
    cot = cott_ref[...].reshape(small, CH)
    for i in range(2):
        for j in range(2):
            tiles = [
                y_ref[2 * r + i, 2 * c + j] for r in range(rows // 2) for c in range(cols // 2)
            ]
            piece = jnp.concatenate(tiles, axis=0)
            term = mm(piece, wd_ref[i * 2 + j])
            total = term if total is None else total + term
            split_cores(mm(piece.T, cot), keep_ref, send_ref, 3 + i * 2 + j)
    down = total.astype(BF)
    back = to_frames(16)
    for q in range(small // 256):
        o = mm(back, down[q * 256 : q * 256 + 256]).astype(BF)
        down_ref[:, q * 4 : q * 4 + 4] = o.reshape(SLOTS, 4, cols // 2, CH)


def grad_x_kernel(
    part, bands, count_ref, xt_ref, gy_ref, gs_ref, halo_ref, wt_ref, wd_ref, ws_ref, *rest
):
    out_ref, token_ref, pad_ref, buf, sems = rest[-5:]
    count = count_ref[0]
    band = lax.axis_index("grp")
    rows, cols = xt_ref.shape[0], xt_ref.shape[1]
    half = rows // 2
    if part == 0:
        flag, i, row = band > 0, 1, 0
        pad_ref[1 : half + 2] = gs_ref[0 : half + 1]
    else:
        flag, i, row = band < bands - 1, 0, half + 1
        pad_ref[0 : half + 1] = gs_ref[half - 1 :]
    edge = jnp.zeros((SLOTS, CH), BF)
    pair = [
        mm_nt(halo_ref[...], wd_ref[i * 2 + j]).astype(BF).reshape(cols // 2, SLOTS, CH)
        for j in range(2)
    ]
    g = jnp.stack(pair, axis=1).reshape(cols, SLOTS, CH)
    pad_ref[row, 0] = edge
    pad_ref[row, 1 : cols + 1] = grad_of_temporal(g, wt_ref, jnp.where(flag, count, 0))
    pad_ref[row, cols + 1] = edge
    back = to_frames(16)

    def rows_of(q, _):
        total = None
        for i in range(3):
            for j in range(3):
                left = pad_ref[pl.ds(4 * q + 2 - i, 4), 2 - j : 2 - j + cols].reshape(
                    4 * cols * SLOTS, CH
                )
                term = mm_nt(left, ws_ref[i * 3 + j])
                total = term if total is None else total + term
        at = part * half + 4 * q
        v = xt_ref[pl.ds(at, 4)].reshape(4 * cols * SLOTS, CH).astype(F32)
        r = lax.rsqrt(jnp.mean(v * v, axis=-1, keepdims=True) + 1e-06)
        u = v * r
        s = 1.0 / (1.0 + jnp.exp(-u))
        gu = total * (s * (1.0 + u * (1.0 - s)))
        dot = jnp.mean(gu * u, axis=-1, keepdims=True)
        gv = r * (gu - u * dot)
        gx = gy_ref[pl.ds(at, 4)].reshape(4 * cols * SLOTS, CH).astype(F32) + gv
        gx = gx.reshape(4 * cols, SLOTS, CH)
        gx = jnp.where(slot_mask(gx.shape, count), gx, 0.0).astype(BF).reshape(4 * cols * SLOTS, CH)
        for k in range(2):
            o = mm(back, gx[k * 256 : k * 256 + 256]).astype(BF)
            buf[:, pl.ds(pl.multiple_of((2 * q + k) * 16, 16), 16), :] = o.reshape(SLOTS, 16, CH)
        return 0

    lax.fori_loop(0, half // 4, rows_of, 0)
    size = half * cols
    copy = pltpu.make_async_copy(buf, out_ref.at[:, part * size : part * size + size, :], sems.at[0])
    token_ref[...] = jnp.zeros_like(token_ref)
    copy.start()
    copy.wait()


def scatter_kernel(keep_a, got_a, keep_b, got_b, *outs):
    _, p = place_bits()
    n = keep_a.shape[1]
    for r, out in enumerate(outs):
        c = p ^ r
        out[:n] = (keep_a[c].astype(F32) + got_a[c].astype(F32)).astype(BF)
        out[n:] = (keep_b[c].astype(F32) + got_b[c].astype(F32)).astype(BF)


def sum_kernel(*refs):
    total = refs[0][...].astype(F32)
    for ref in refs[1:8]:
        total = total + ref[...].astype(F32)
    refs[-1][...] = total.astype(BF)


def gather_kernel(*refs):
    _, p = place_bits()
    for r in range(8):
        refs[-1][p ^ r] = refs[r][...]


def add_kernel(a_ref, b_ref, out_ref):
    out_ref[...] = (a_ref[...].astype(F32) + b_ref[...].astype(F32)).astype(BF)


def pass_kernel(*_):
    pass


def finish_kernel(own, half_ref, *rest):
    buf, sems = rest[-2:]
    outs = rest[-5:-2]
    core, _ = place_bits()
    at = pl.multiple_of((core if own else 1 - core) * (CH // 2), CH // 2)
    copies = []
    k = 0
    for out in outs:
        for m in range(out.shape[0]):
            buf[k] = half_ref[:, k].reshape(CH, CH // 2).astype(F32)
            copies.append(
                pltpu.make_async_copy(buf.at[k], out.at[m, :, pl.ds(at, CH // 2)], sems.at[k])
            )
            copies[-1].start()
            k += 1
    for copy in copies:
        copy.wait()


VMEM = pl.BlockSpec(memory_space=pltpu.VMEM)
SMEM = pl.BlockSpec(memory_space=pltpu.SMEM)
ANY = pl.BlockSpec(memory_space=pl.ANY)
HBM = pl.BlockSpec(memory_space=pltpu.HBM)
TOKEN = (VMEM, (8, 128), F32)


def call(kernel, name, ins, outs, scratch=(), flops=0, alias=None, grant=10):
    shapes = [jax.ShapeDtypeStruct(o[1], o[2] if len(o) > 2 else BF) for o in outs]
    moved = sum(a.size * a.dtype.itemsize for s, a in ins if s is not ANY)
    moved += sum(s.size * s.dtype.itemsize for s in shapes)
    return pl.pallas_call(
        kernel,
        out_shape=shapes,
        in_specs=[s for s, _ in ins],
        out_specs=[o[0] for o in outs],
        scratch_shapes=list(scratch),
        compiler_params=pltpu.CompilerParams(vmem_limit_bytes=grant * 2**20),
        cost_estimate=pl.CostEstimate(flops=flops, bytes_accessed=moved, transcendentals=0),
        input_output_aliases=alias or {},
        name=name,
    )(*[a for _, a in ins])


AXES = ("tm", "grp")


def plan(tm, grp):
    low, total = grp.bit_length() - 1, (tm * grp).bit_length() - 1
    eight = [low + 1, 0, low + 2]
    return low, eight, [b for b in range(total) if b != low and b not in eight]


def swap(value, tm, grp, *bits):
    flip = sum(1 << b for b in bits)
    return lax.ppermute(value, AXES, [(d, d ^ flip) for d in range(tm * grp)])


def core_round(value, tm, grp):
    return swap(value, tm, grp, plan(tm, grp)[0])


def eight_round(parts, tm, grp):
    bits = plan(tm, grp)[1]
    return parts[:1] + [
        swap(parts[r], tm, grp, *(b for i, b in enumerate(bits) if r >> i & 1)) for r in range(1, 8)
    ]


def passed(value, after):
    ins = [(ANY, value)] + [(ANY, a) for a in after]
    return call(pass_kernel, "pass", ins, [(ANY, value.shape)], alias={0: 0})[0]


def finish(own, half, before):
    n = half.shape[1]
    return list(
        call(
            functools.partial(finish_kernel, own),
            "finish",
            [(VMEM, half)] + [(HBM, a) for a in before],
            [(HBM, (m, CH, CH), F32) for m in (9, 3, 4)],
            [pltpu.VMEM((n, CH, CH // 2), F32), pltpu.SemaphoreType.DMA((n,))],
            alias={1 + i: i for i in range(len(before))},
        )
    )


def along(value, axis, by):
    count = lax.axis_size(axis)
    pairs = [(i, i + by) for i in range(count) if 0 <= i + by < count]
    return lax.ppermute(value, axis, pairs)


def from_bands(parts):
    if len(parts) == 1:
        got = lax.ppermute(parts[0], "grp", [(0, 1), (1, 0)])
        return got, got
    return along(parts[0], "grp", 1), along(parts[1], "grp", -1)


def body(tm, grp, frames_in, span_frames, w_spatial, w_temporal, w_down, cotangent):
    slots, rows, cols, ch = frames_in.shape
    wide = rows * cols
    x = frames_in.reshape(slots, wide, ch)
    ws = w_spatial.reshape(9, ch, ch)
    wd = w_down.reshape(4, ch, ch)
    wt = w_temporal
    count = (SMEM, span_frames)
    tap = 2 * slots * wide * ch * ch
    tile = (rows, cols, slots, ch)
    padded = (rows + 2, cols + 2, slots, ch)
    dma = pltpu.SemaphoreType.DMA

    sides = 1 if grp == 2 else 2
    *edge, nxt, token = call(
        functools.partial(edges_kernel, grp),
        "edges",
        [count, (VMEM, x), (VMEM, cotangent)],
        [(VMEM, (cols * slots, ch))] * sides + [(VMEM, (2,) + cotangent.shape[1:]), TOKEN],
        flops=tap // 8,
    )
    top, bot = from_bands(edge)
    nxt_got = along(nxt, "tm", -1)
    xt, acts, at = call(
        acts_kernel,
        "acts",
        [count, (VMEM, x), (ANY, token)],
        [(VMEM, tile), (VMEM, padded), (VMEM, (ch, (rows + 2) * 128))],
        flops=2 * tap,
    )
    acts, sp, last_two = call(
        functools.partial(spatial_kernel, grp),
        "spatial",
        [count, (VMEM, top), (VMEM, bot), (VMEM, acts), (VMEM, ws)],
        [(VMEM, padded), (VMEM, tile), (VMEM, (rows // 2, 32, ch))],
        flops=9 * tap,
        alias={3: 0},
    )
    prev = along(last_two, "tm", 1)
    half = (8, 9, 32, ch // 2)
    at, cott, gy, gs, keep_a, send_a, *edge = call(
        functools.partial(grad_spatial_kernel, grp),
        "grad_spatial",
        [count, (VMEM, at), (VMEM, top), (VMEM, bot), (VMEM, cotangent), (VMEM, nxt_got), (VMEM, wt), (VMEM, wd),
         (ANY, last_two)],
        [(VMEM, at.shape), (VMEM, (rows // 2, cols // 2, slots, ch)), (VMEM, tile),
         (VMEM, (rows, cols + 2, slots, ch)), (VMEM, half), (VMEM, half)]
        + [(VMEM, (cols // 2 * slots, ch))] * sides,
        flops=14 * tap,
        alias={1: 0},
    )
    got_a = core_round(passed(send_a, [prev]), tm, grp)
    cot_top, cot_bot = from_bands(edge)
    half = (8, 7, 32, ch // 2)
    down, keep_b, send_b = call(
        forward_kernel,
        "forward",
        [count, (VMEM, xt), (VMEM, sp), (VMEM, prev), (VMEM, cott), (VMEM, gy), (VMEM, wt), (VMEM, wd)]
        + [(ANY, send_a)],
        [(VMEM, cotangent.shape), (VMEM, half), (VMEM, half)],
        [pltpu.VMEM(s, BF) for s in (tile, (ch, slots * wide), tile, tile, tile)],
        flops=10 * tap,
    )
    def grad_x_part(part, halo, before, after):
        return call(
            functools.partial(grad_x_kernel, part, grp),
            "grad_x",
            [count, (VMEM, xt), (VMEM, gy), (VMEM, gs), (VMEM, halo), (VMEM, wt), (VMEM, wd), (VMEM, ws)]
            + [(HBM, a) for a in before] + [(ANY, a) for a in after],
            [(HBM, (slots, wide, ch)), TOKEN],
            [pltpu.VMEM((rows // 2 + 2, cols + 2, slots, ch), BF),
             pltpu.VMEM((slots, wide // 2, ch), BF), dma((1,))],
            flops=5 * tap,
            alias={8: 0} if before else None,
        )

    send_b = passed(send_b, [got_a])
    got_b = core_round(send_b, tm, grp)
    parts = call(
        scatter_kernel,
        "scatter",
        [(VMEM, a) for a in (keep_a, got_a, keep_b, got_b)],
        [(VMEM, (16, 32, ch // 2))] * 8,
    )
    grad_x, token = grad_x_part(0, cot_top, [], [parts[7]])
    parts = eight_round(list(parts), tm, grp)
    ins = [(VMEM, a) for a in parts] + [(ANY, token)]
    (mine,) = call(sum_kernel, "sum", ins, [(VMEM, parts[0].shape)])
    for bit in plan(tm, grp)[2]:
        got = swap(mine, tm, grp, bit)
        (mine,) = call(add_kernel, "add", [(VMEM, mine), (VMEM, got)], [(VMEM, mine.shape)])
    parts = eight_round([mine] * 8, tm, grp)
    grad_x, token = grad_x_part(1, cot_bot, [grad_x], [mine])
    ins = [(VMEM, a) for a in parts] + [(ANY, token)]
    (mine,) = call(gather_kernel, "gather", ins, [(VMEM, (8,) + mine.shape)])
    got = core_round(mine, tm, grp)
    outs = finish(True, mine, [])
    sum_s, sum_t, sum_d = finish(False, got, outs)
    return (
        down,
        grad_x.reshape(frames_in.shape),
        sum_s.reshape(w_spatial.shape),
        sum_t,
        sum_d.reshape(w_down.shape),
    )


def solution(mesh):
    return jax.shard_map(
        functools.partial(body, mesh.shape["tm"], mesh.shape["grp"]),
        mesh=mesh,
        in_specs=(P("tm", "grp", None, None), P("tm"), P(), P(), P(), P("tm", "grp", None, None)),
        out_specs=(P("tm", "grp", None, None), P("tm", "grp", None, None), P(), P(), P()),
        check_vma=False,
    )
```

```python
import functools

import jax
import jax.numpy as jnp
from jax import lax
from jax.experimental import pallas as pl
from jax.experimental.pallas import tpu as pltpu
from jax.sharding import PartitionSpec as P

SLOTS = 16
OWN = 14
CH = 256
BF = jnp.bfloat16
F32 = jnp.float32


def mm(a, b):
    return lax.dot_general(a, b, (((1,), (0,)), ((), ())), preferred_element_type=F32)


def mm_nt(a, b):
    return lax.dot_general(a, b, (((1,), (1,)), ((), ())), preferred_element_type=F32)


def iotas(rows, cols):
    return (
        lax.broadcasted_iota(jnp.int32, (rows, cols), 0),
        lax.broadcasted_iota(jnp.int32, (rows, cols), 1),
    )


def to_slots(rows, frames, keep):
    a, b = iotas(rows * SLOTS, frames * rows)
    hit = (a // SLOTS == b % rows) & keep(b // rows, a % SLOTS)
    return jnp.where(hit, 1.0, 0.0).astype(BF)


def to_frames(rows):
    a, b = iotas(SLOTS * rows, rows * SLOTS)
    hit = (a % rows == b // SLOTS) & (a // rows == b % SLOTS)
    return jnp.where(hit, 1.0, 0.0).astype(BF)


def own_frames(count):
    return lambda frame, slot: (frame == slot) & (slot < count)


def own_and_next(count):
    return lambda frame, slot: ((frame < OWN) & (frame == slot) & (slot < count)) | (
        (frame >= OWN) & (slot == count + frame - OWN)
    )


def silu_norm(v):
    scaled = v * lax.rsqrt(jnp.mean(v * v, axis=-1, keepdims=True) + 1e-06)
    return scaled * (0.5 + 0.5 * jnp.tanh(0.5 * scaled))


def slot_mask(shape, count):
    return lax.broadcasted_iota(jnp.int32, shape, len(shape) - 2) < count


def grad_of_temporal(gy, wt_ref, count):
    n = gy.shape[0]
    flat = gy.reshape(n * SLOTS, CH)
    total = mm_nt(flat, wt_ref[2]).reshape(n, SLOTS, CH)
    for k in (1, 0):
        term = mm_nt(flat, wt_ref[k]).reshape(n, SLOTS, CH)
        total = total + pltpu.roll(term, SLOTS - (2 - k), 1)
    return jnp.where(slot_mask(total.shape, count), total, 0.0).astype(BF)


def place_bits():
    t, g = lax.axis_index("tm"), lax.axis_index("grp")
    return t & 1, ((t >> 1) & 1) + 2 * (g & 1), (t >> 2) & 3


def split_cores(value, keep_ref, send_ref, k):
    core, _, _ = place_bits()
    low, high = value[:, : CH // 2].astype(BF), value[:, CH // 2 :].astype(BF)
    keep_ref[:, k] = jnp.where(core == 0, low, high).reshape(16, 16, CH // 2)
    send_ref[:, k] = jnp.where(core == 0, high, low).reshape(16, 16, CH // 2)


def edges_kernel(bands, count_ref, x_ref, cot_ref, *rest):
    outs, (nxt_ref, token_ref) = rest[:-2], rest[-2:]
    token_ref[...] = jnp.zeros_like(token_ref)
    count = count_ref[0]
    band = lax.axis_index("grp")
    wide = x_ref.shape[1]
    if bands == 2:
        starts, lower = [jnp.where(band == 0, wide - 16, 0)], [band == 0]
    else:
        starts, lower = [wide - 16, 0], [True, False]
    nxt_ref[...] = cot_ref[0:2]
    place = to_slots(16, SLOTS, own_frames(count))
    for k, at in enumerate(starts):
        piece = x_ref[:, pl.ds(pl.multiple_of(at, 16), 16), :].reshape(SLOTS * 16, CH)
        v = mm(place, piece)
        v = jnp.where(lower[k], v[128:], v[:128])
        outs[k][...] = silu_norm(v).astype(BF)


def acts_kernel(count_ref, x_ref, _, xt_ref, acts_ref, at_ref):
    count = count_ref[0]
    rows, cols = xt_ref.shape[0], xt_ref.shape[1]
    edge = jnp.zeros((rows + 2, SLOTS, CH), BF)
    acts_ref[:, 0] = edge
    acts_ref[:, cols + 1] = edge
    place = to_slots(16, SLOTS, own_frames(count))

    def rows_of(q, _):
        at = pl.multiple_of(q * 16, 16)
        piece = x_ref[:, pl.ds(at, 16), :].reshape(SLOTS * 16, CH)
        v = mm(place, piece)
        xt_ref[pl.ds(2 * q, 2)] = v.astype(BF).reshape(2, cols, SLOTS, CH)
        a = silu_norm(v).astype(BF)
        acts_ref[pl.ds(2 * q + 1, 2), 1 : cols + 1] = a.reshape(2, cols, SLOTS, CH)
        flipped = a.T
        for i in range(3):
            at = pl.multiple_of((2 * q + 3 - i) * 128, 128)
            at_ref[i * CH : i * CH + CH, pl.ds(at, 256)] = flipped
        return 0

    lax.fori_loop(0, rows // 2, rows_of, 0)


def spatial_kernel(
    bands, count_ref, top_ref, bot_ref, acts_in, ws_ref, acts_ref, sp_ref, edge_ref
):
    count = count_ref[0]
    band = lax.axis_index("grp")
    rows, cols = sp_ref.shape[0], sp_ref.shape[1]
    for ref, flag, row in ((top_ref, band > 0, 0), (bot_ref, band < bands - 1, rows + 1)):
        a = jnp.where(flag, ref[...].astype(F32), 0.0)
        acts_ref[row, 1 : cols + 1] = a.astype(BF).reshape(cols, SLOTS, CH)
    a, b = iotas(32, 256)
    pick = (a // 2 == b // SLOTS) & (b % SLOTS == count - 2 + a % 2)
    pick = jnp.where(pick, 1.0, 0.0).astype(BF)

    def rows_of(q, _):
        left = [
            acts_ref[pl.ds(4 * q + i, 4), j : j + cols].reshape(4 * cols * SLOTS, CH)
            for i in range(3)
            for j in range(3)
        ]
        out = mm(jnp.concatenate(left, axis=1), ws_ref[...].reshape(9 * CH, CH)).astype(BF)
        sp_ref[pl.ds(4 * q, 4)] = out.reshape(4, cols, SLOTS, CH)
        for half in range(2):
            edge_ref[2 * q + half] = mm(pick, out[half * 256 : half * 256 + 256]).astype(BF)
        return 0

    lax.fori_loop(0, rows // 4, rows_of, 0)


def grad_spatial_kernel(
    bands, count_ref, at_in, top_ref, bot_ref, cot_ref, nxt_ref, wt_ref, wd_ref, _,
    at_ref, cott_ref, gy_ref, gs_ref, keep_ref, send_ref, *edge_refs,
):
    count = count_ref[0]
    band = lax.axis_index("grp")
    rows, cols = gy_ref.shape[0], gy_ref.shape[1]
    for ref, flag, i, row in ((top_ref, band > 0, 0, 0), (bot_ref, band < bands - 1, 2, rows + 1)):
        a = jnp.where(flag, ref[...].astype(F32), 0.0)
        at = (row - i + 2) * 128
        at_ref[i * CH : i * CH + CH, at : at + 128] = a.T.astype(BF)
    edge = jnp.zeros((rows, SLOTS, CH), BF)
    gs_ref[:, 0] = edge
    gs_ref[:, cols + 1] = edge

    place_next = to_slots(16, SLOTS, own_and_next(count))
    for q in range(rows * cols // 64):
        four = slice(q * 4, q * 4 + 4)
        piece = jnp.concatenate(
            [cot_ref[0:OWN, four].reshape(OWN, 16, CH), nxt_ref[:, four].reshape(2, 16, CH)], 0
        ).reshape(SLOTS * 16, CH)
        placed = mm(place_next, piece).astype(BF)
        cott_ref[q * 4 : q * 4 + 4] = placed.reshape(4, 4, SLOTS, CH)
        for i in range(2):
            for j in range(2):
                g = mm_nt(placed, wd_ref[i * 2 + j]).astype(BF).reshape(4, 4, SLOTS, CH)
                for r in range(4):
                    for c in range(4):
                        gy_ref[2 * (q * 4 + r) + i, 2 * c + j] = g[r, c]
    last = cott_ref[rows // 2 - 1].reshape(cols // 2 * SLOTS, CH)
    first = cott_ref[0].reshape(cols // 2 * SLOTS, CH)
    if bands == 2:
        edge_refs[0][...] = jnp.where(band == 0, last, first)
    else:
        edge_refs[0][...] = last
        edge_refs[1][...] = first

    def grads_of(q, _):
        g = gy_ref[pl.ds(4 * q, 4)].reshape(4 * cols, SLOTS, CH)
        s = grad_of_temporal(g, wt_ref, count)
        gs_ref[pl.ds(4 * q, 4), 1 : cols + 1] = s.reshape(4, cols, SLOTS, CH)
        g = jnp.where(slot_mask(g.shape, count), g.astype(F32), 0.0)
        gy_ref[pl.ds(4 * q, 4)] = g.astype(BF).reshape(4, cols, SLOTS, CH)
        return 0

    lax.fori_loop(0, rows // 4, grads_of, 0)

    wide = rows * cols * SLOTS
    for j in range(3):
        right = gs_ref[:, 2 - j : 2 - j + cols].reshape(wide, CH)
        value = mm(at_ref[:, 256 : 256 + wide], right)
        for i in range(3):
            split_cores(value[i * CH : i * CH + CH], keep_ref, send_ref, i * 3 + j)


def forward_kernel(
    count_ref, xt_ref, sp_ref, prev_ref, cott_ref, gy_ref, wt_ref, wd_ref, *rest
):
    down_ref, keep_ref, send_ref, y_ref, st_ref, yt_ref = rest[-6:]
    count = count_ref[0]
    rows, cols = xt_ref.shape[0], xt_ref.shape[1]
    a, b = iotas(256, 32)
    place = (a // SLOTS == b // 2) & (a % SLOTS == OWN + b % 2)
    place = jnp.where(place, 1.0, 0.0).astype(BF)

    def rows_of(q, _):
        s = sp_ref[pl.ds(4 * q, 4)].reshape(4 * cols * SLOTS, CH).astype(F32)
        s = s + jnp.concatenate([mm(place, prev_ref[2 * q]), mm(place, prev_ref[2 * q + 1])], 0)
        s = s.reshape(4 * cols, SLOTS, CH)
        total = None
        for k in range(3):
            shifted = s if k == 2 else pltpu.roll(s, 2 - k, 1)
            shifted = shifted.astype(BF).reshape(4 * cols * SLOTS, CH)
            at = pl.ds(pl.multiple_of(q * 512, 512), 512)
            st_ref[k * CH : k * CH + CH, at] = shifted.T
            term = mm(shifted, wt_ref[k])
            total = term if total is None else total + term
        x = xt_ref[pl.ds(4 * q, 4)].reshape(4 * cols, SLOTS, CH).astype(F32)
        y = jnp.where(slot_mask(x.shape, count), x + total.reshape(x.shape), 0.0).astype(BF)
        y_ref[pl.ds(4 * q, 4)] = y.reshape(4, cols, SLOTS, CH)
        return 0

    lax.fori_loop(0, rows // 4, rows_of, 0)

    wide = rows * cols * SLOTS
    value = mm(st_ref[...], gy_ref[...].reshape(wide, CH))
    for k in range(3):
        split_cores(value[k * CH : k * CH + CH], keep_ref, send_ref, k)

    small = wide // 4
    total = None
    for i in range(2):
        for j in range(2):
            tiles = [
                y_ref[2 * r + i, 2 * c + j] for r in range(rows // 2) for c in range(cols // 2)
            ]
            piece = jnp.concatenate(tiles, axis=0)
            k = i * 2 + j
            yt_ref[k * CH : k * CH + CH] = piece.T
            term = mm(piece, wd_ref[k])
            total = term if total is None else total + term
    down_ref[...] = total.astype(BF)
    value = mm(yt_ref[...], cott_ref[...].reshape(small, CH))
    for k in range(4):
        split_cores(value[k * CH : k * CH + CH], keep_ref, send_ref, 3 + k)


def grad_x_kernel(
    bands, count_ref, xt_ref, gy_ref, gs_ref, top_ref, bot_ref, wt_ref, wd_ref, ws_ref, slot_ref, *rest
):
    out_ref, down_ref, token_ref, pad_ref, buf, sems = rest[-6:]
    token_ref[...] = jnp.zeros_like(token_ref)
    count = count_ref[0]
    band = lax.axis_index("grp")
    rows, cols = xt_ref.shape[0], xt_ref.shape[1]
    pad_ref[1 : rows + 1] = gs_ref[...]
    edge = jnp.zeros((SLOTS, CH), BF)
    for ref, flag, i, row in ((top_ref, band > 0, 1, 0), (bot_ref, band < bands - 1, 0, rows + 1)):
        pair = [
            mm_nt(ref[...], wd_ref[i * 2 + j]).astype(BF).reshape(cols // 2, SLOTS, CH)
            for j in range(2)
        ]
        g = jnp.stack(pair, axis=1).reshape(cols, SLOTS, CH)
        pad_ref[row, 0] = edge
        pad_ref[row, 1 : cols + 1] = grad_of_temporal(g, wt_ref, jnp.where(flag, count, 0))
        pad_ref[row, cols + 1] = edge
    back = to_frames(16)

    def rows_of(q, _):
        total = None
        for i in range(3):
            for j in range(3):
                left = pad_ref[pl.ds(4 * q + 2 - i, 4), 2 - j : 2 - j + cols].reshape(
                    4 * cols * SLOTS, CH
                )
                term = mm_nt(left, ws_ref[i * 3 + j])
                total = term if total is None else total + term
        at = 4 * q
        v = xt_ref[pl.ds(at, 4)].reshape(4 * cols * SLOTS, CH).astype(F32)
        r = lax.rsqrt(jnp.mean(v * v, axis=-1, keepdims=True) + 1e-06)
        u = v * r
        s = 0.5 + 0.5 * jnp.tanh(0.5 * u)
        gu = total * (s * (1.0 + u * (1.0 - s)))
        dot = jnp.mean(gu * u, axis=-1, keepdims=True)
        gv = r * (gu - u * dot)
        gx = gy_ref[pl.ds(at, 4)].reshape(4 * cols * SLOTS, CH).astype(F32) + gv
        gx = gx.reshape(4 * cols, SLOTS, CH)
        gx = jnp.where(slot_mask(gx.shape, count), gx, 0.0).astype(BF).reshape(4 * cols * SLOTS, CH)
        for k in range(2):
            o = mm(back, gx[k * 256 : k * 256 + 256]).astype(BF)
            buf[:, pl.ds(pl.multiple_of((2 * q + k) * 16, 16), 16), :] = o.reshape(SLOTS, 16, CH)
        return 0

    lax.fori_loop(0, rows // 4, rows_of, 0)
    copy = pltpu.make_async_copy(buf, out_ref, sems.at[0])
    copy.start()
    for q in range(down_ref.shape[1] // 4):
        o = mm(back, slot_ref[q * 256 : q * 256 + 256]).astype(BF)
        down_ref[:, q * 4 : q * 4 + 4] = o.reshape(SLOTS, 4, cols // 2, CH)
    copy.wait()


def plane_send_kernel(keep_a, got_a, keep_b, got_b, *outs):
    _, p, _ = place_bits()
    n = keep_a.shape[1]
    for r, out in enumerate(outs):
        at = pl.ds((p ^ r) * 4, 4)
        out[:, :n] = (keep_a[at].astype(F32) + got_a[at].astype(F32)).astype(BF)
        out[:, n:] = (keep_b[at].astype(F32) + got_b[at].astype(F32)).astype(BF)


def line_send_kernel(a_ref, b_ref, c_ref, d_ref, *rest):
    outs = rest[-4:]
    _, _, z = place_bits()
    for r in range(4):
        parts = [ref[z ^ r].astype(F32) for ref in (a_ref, b_ref, c_ref, d_ref)]
        outs[r][...] = (parts[0] + parts[1] + parts[2] + parts[3]).astype(BF)


def line_sum_kernel(a_ref, b_ref, c_ref, d_ref, out_ref):
    parts = [ref[...].astype(F32) for ref in (a_ref, b_ref, c_ref, d_ref)]
    out_ref[...] = (parts[0] + parts[1] + parts[2] + parts[3]).astype(BF)


def line_gather_kernel(a_ref, b_ref, c_ref, d_ref, out_ref):
    _, _, z = place_bits()
    for r, ref in enumerate((a_ref, b_ref, c_ref, d_ref)):
        out_ref[z ^ r] = ref[...]


def add_kernel(a_ref, b_ref, out_ref):
    out_ref[...] = (a_ref[...].astype(F32) + b_ref[...].astype(F32)).astype(BF)


def pass_kernel(*_):
    pass


def finish_kernel(which, *refs):
    buf, sems = refs[-2:]
    outs, token_ref = refs[-6:-3], refs[-3]
    token_ref[...] = jnp.zeros_like(token_ref)
    core, p, _ = place_bits()
    copies = []
    for f, (ref, (sibling, r)) in enumerate(zip(refs, which)):
        rows = pl.ds(pl.multiple_of((p ^ r) * 64, 64), 64)
        cols = (1 - core if sibling else core) * (CH // 2)
        cols = pl.ds(pl.multiple_of(cols, CH // 2), CH // 2)
        m = 0
        for o, out in enumerate(outs):
            n = out.shape[0]
            for k in range(n):
                buf[f, m + k] = ref[:, m + k].reshape(64, CH // 2).astype(F32)
            copy = pltpu.make_async_copy(
                buf.at[f, pl.ds(m, n)], out.at[:, rows, cols], sems.at[f, o]
            )
            copy.start()
            copies.append(copy)
            m += n
    for copy in copies:
        copy.wait()


VMEM = pl.BlockSpec(memory_space=pltpu.VMEM)
SMEM = pl.BlockSpec(memory_space=pltpu.SMEM)
ANY = pl.BlockSpec(memory_space=pl.ANY)
HBM = pl.BlockSpec(memory_space=pltpu.HBM)
TOKEN = (VMEM, (8, 128), F32)


def call(kernel, name, ins, outs, scratch=(), flops=0, alias=None, grant=10):
    shapes = [jax.ShapeDtypeStruct(o[1], o[2] if len(o) > 2 else BF) for o in outs]
    moved = sum(a.size * a.dtype.itemsize for s, a in ins if s is not ANY)
    moved += sum(s.size * s.dtype.itemsize for s in shapes)
    return pl.pallas_call(
        kernel,
        out_shape=shapes,
        in_specs=[s for s, _ in ins],
        out_specs=[o[0] for o in outs],
        scratch_shapes=list(scratch),
        compiler_params=pltpu.CompilerParams(vmem_limit_bytes=grant * 2**20),
        cost_estimate=pl.CostEstimate(flops=flops, bytes_accessed=moved, transcendentals=0),
        input_output_aliases=alias or {},
        name=name,
    )(*[a for _, a in ins])


AXES = ("tm", "grp")


def plan(tm, grp):
    low, total = grp.bit_length() - 1, (tm * grp).bit_length() - 1
    plane, line = [low + 1, 0], [low + 2, low + 3]
    return low, plane, line, [b for b in range(total) if b not in [low] + plane + line]


def swap(value, tm, grp, *bits):
    flip = sum(1 << b for b in bits)
    return lax.ppermute(value, AXES, [(d, d ^ flip) for d in range(tm * grp)])


def core_round(value, tm, grp):
    return swap(value, tm, grp, plan(tm, grp)[0])


def four_round(parts, bits, tm, grp):
    return [
        parts[0],
        swap(parts[1], tm, grp, bits[0]),
        swap(parts[2], tm, grp, bits[1]),
        swap(parts[3], tm, grp, *bits),
    ]


def passed(value, after):
    ins = [(ANY, value)] + [(ANY, a) for a in after]
    return call(pass_kernel, "pass", ins, [(ANY, value.shape)], alias={0: 0})[0]


def finish(blocks, before, after):
    n = blocks[0][0].shape[1]
    *outs, token = call(
        functools.partial(finish_kernel, [b[1:] for b in blocks]),
        "finish",
        [(VMEM, b[0]) for b in blocks] + [(HBM, a) for a in before] + [(ANY, a) for a in after],
        [(HBM, (m, CH, CH), F32) for m in (9, 3, 4)] + [TOKEN],
        [pltpu.VMEM((len(blocks), n, 64, CH // 2), F32), pltpu.SemaphoreType.DMA((len(blocks), 3))],
        alias={len(blocks) + i: i for i in range(len(before))},
    )
    return outs, token


def along(value, axis, by):
    count = lax.axis_size(axis)
    pairs = [(i, i + by) for i in range(count) if 0 <= i + by < count]
    return lax.ppermute(value, axis, pairs)


def from_bands(parts):
    if len(parts) == 1:
        got = lax.ppermute(parts[0], "grp", [(0, 1), (1, 0)])
        return got, got
    return along(parts[0], "grp", 1), along(parts[1], "grp", -1)


def body(tm, grp, frames_in, span_frames, w_spatial, w_temporal, w_down, cotangent):
    slots, rows, cols, ch = frames_in.shape
    wide = rows * cols
    x = frames_in.reshape(slots, wide, ch)
    ws = w_spatial.reshape(9, ch, ch)
    wd = w_down.reshape(4, ch, ch)
    wt = w_temporal
    count = (SMEM, span_frames)
    tap = 2 * slots * wide * ch * ch
    tile = (rows, cols, slots, ch)
    padded = (rows + 2, cols + 2, slots, ch)
    dma = pltpu.SemaphoreType.DMA

    sides = 1 if grp == 2 else 2
    *edge, nxt, token = call(
        functools.partial(edges_kernel, grp),
        "edges",
        [count, (VMEM, x), (VMEM, cotangent)],
        [(VMEM, (cols * slots, ch))] * sides + [(VMEM, (2,) + cotangent.shape[1:]), TOKEN],
        flops=tap // 8,
    )
    top, bot = from_bands(edge)
    nxt_got = along(nxt, "tm", -1)
    xt, acts, at = call(
        acts_kernel,
        "acts",
        [count, (VMEM, x), (ANY, token)],
        [(VMEM, tile), (VMEM, padded), (VMEM, (3 * ch, (rows + 4) * 128))],
        flops=2 * tap,
    )
    acts, sp, last_two = call(
        functools.partial(spatial_kernel, grp),
        "spatial",
        [count, (VMEM, top), (VMEM, bot), (VMEM, acts), (VMEM, ws)],
        [(VMEM, padded), (VMEM, tile), (VMEM, (rows // 2, 32, ch))],
        flops=9 * tap,
        alias={3: 0},
    )
    prev = along(last_two, "tm", 1)
    half = (16, 9, 16, ch // 2)
    at, cott, gy, gs, keep_a, send_a, *edge = call(
        functools.partial(grad_spatial_kernel, grp),
        "grad_spatial",
        [count, (VMEM, at), (VMEM, top), (VMEM, bot), (VMEM, cotangent), (VMEM, nxt_got), (VMEM, wt), (VMEM, wd),
         (ANY, last_two)],
        [(VMEM, at.shape), (VMEM, (rows // 2, cols // 2, slots, ch)), (VMEM, tile),
         (VMEM, (rows, cols + 2, slots, ch)), (VMEM, half), (VMEM, half)]
        + [(VMEM, (cols // 2 * slots, ch))] * sides,
        flops=14 * tap,
        alias={1: 0},
    )
    send_a = passed(send_a, [prev])
    got_a = core_round(send_a, tm, grp)
    cot_top, cot_bot = from_bands(edge)
    half = (16, 7, 16, ch // 2)
    down, keep_b, send_b = call(
        forward_kernel,
        "forward",
        [count, (VMEM, xt), (VMEM, sp), (VMEM, prev), (VMEM, cott), (VMEM, gy), (VMEM, wt), (VMEM, wd),
         (ANY, send_a)],
        [(VMEM, (slots * wide // 4, ch)), (VMEM, half), (VMEM, half)],
        [pltpu.VMEM(v, BF) for v in (tile, (3 * ch, slots * wide), (4 * ch, slots * wide // 4))],
        flops=10 * tap,
        grant=14,
    )
    send_b = passed(send_b, [got_a, cot_top, cot_bot][: 1 + sides])
    got_b = core_round(send_b, tm, grp)
    _, plane, line, others = plan(tm, grp)
    parts = call(
        plane_send_kernel,
        "plane_send",
        [(VMEM, a) for a in (keep_a, got_a, keep_b, got_b)],
        [(VMEM, (4, 16, 16, ch // 2))] * 4,
    )
    grad_x, down, token = call(
        functools.partial(grad_x_kernel, grp),
        "grad_x",
        [count, (VMEM, xt), (VMEM, gy), (VMEM, gs), (VMEM, cot_top), (VMEM, cot_bot), (VMEM, wt),
         (VMEM, wd), (VMEM, ws), (VMEM, down), (ANY, parts[3])],
        [(HBM, (slots, wide, ch)), (VMEM, cotangent.shape), TOKEN],
        [pltpu.VMEM(padded, BF), pltpu.VMEM((slots, wide, ch), BF), dma((1,))],
        flops=10 * tap,
    )
    parts = four_round(list(parts), plane, tm, grp)
    parts = call(
        line_send_kernel,
        "line_send",
        [(VMEM, a) for a in parts] + [(ANY, token)],
        [(VMEM, (16, 16, ch // 2))] * 4,
    )
    parts = four_round(list(parts), line, tm, grp)
    (mine,) = call(line_sum_kernel, "line_sum", [(VMEM, a) for a in parts], [(VMEM, parts[0].shape)])
    for bit in others:
        got = swap(mine, tm, grp, bit)
        (mine,) = call(add_kernel, "add", [(VMEM, mine), (VMEM, got)], [(VMEM, mine.shape)])
    parts = four_round([mine] * 4, line, tm, grp)
    (mine,) = call(
        line_gather_kernel, "line_gather", [(VMEM, a) for a in parts], [(VMEM, (4,) + mine.shape)]
    )
    parts = four_round([mine] * 4, plane, tm, grp)
    side = core_round(mine, tm, grp)
    outs, token = finish([(mine, False, 0), (side, True, 0)], [], [])
    parts[1] = passed(parts[1], [token])
    sides = [side] + [core_round(part, tm, grp) for part in parts[1:]]
    blocks = [(parts[r], False, r) for r in (1, 2, 3)] + [(sides[r], True, r) for r in (1, 2)]
    outs, _ = finish(blocks, outs, [])
    outs, _ = finish([(sides[3], True, 3)], outs, [])
    sum_s, sum_t, sum_d = outs
    return (
        down,
        grad_x.reshape(frames_in.shape),
        sum_s.reshape(w_spatial.shape),
        sum_t,
        sum_d.reshape(w_down.shape),
    )


def solution(mesh):
    return jax.shard_map(
        functools.partial(body, mesh.shape["tm"], mesh.shape["grp"]),
        mesh=mesh,
        in_specs=(P("tm", "grp", None, None), P("tm"), P(), P(), P(), P("tm", "grp", None, None)),
        out_specs=(P("tm", "grp", None, None), P("tm", "grp", None, None), P(), P(), P()),
        check_vma=False,
    )
```

```python
import functools

import jax
import jax.numpy as jnp
from jax import lax
from jax.experimental import pallas as pl
from jax.experimental.pallas import tpu as pltpu
from jax.sharding import PartitionSpec as P

SLOTS = 16
OWN = 14
CH = 256
BF = jnp.bfloat16
F32 = jnp.float32


def mm(a, b):
    return lax.dot_general(a, b, (((1,), (0,)), ((), ())), preferred_element_type=F32)


def mm_nt(a, b):
    return lax.dot_general(a, b, (((1,), (1,)), ((), ())), preferred_element_type=F32)


def iotas(rows, cols):
    return (
        lax.broadcasted_iota(jnp.int32, (rows, cols), 0),
        lax.broadcasted_iota(jnp.int32, (rows, cols), 1),
    )


def to_slots(rows, frames, keep):
    a, b = iotas(rows * SLOTS, frames * rows)
    bits = rows.bit_length() - 1
    hit = ((a >> 4) == (b & (rows - 1))) & keep(b >> bits, a & 15)
    return jnp.where(hit, 1.0, 0.0).astype(BF)


def to_frames(rows):
    a, b = iotas(SLOTS * rows, rows * SLOTS)
    bits = rows.bit_length() - 1
    hit = ((a & (rows - 1)) == (b >> 4)) & ((a >> bits) == (b & 15))
    return jnp.where(hit, 1.0, 0.0).astype(BF)


def own_frames(count):
    return lambda frame, slot: (frame == slot) & (slot < count)


def own_and_next(count):
    return lambda frame, slot: ((frame < OWN) & (frame == slot) & (slot < count)) | (
        (frame >= OWN) & (slot == count + frame - OWN)
    )


def silu_norm(v):
    scaled = v * lax.rsqrt(jnp.mean(v * v, axis=-1, keepdims=True) + 1e-06)
    return scaled * (0.5 + 0.5 * jnp.tanh(0.5 * scaled))


def slot_mask(shape, count):
    return lax.broadcasted_iota(jnp.int32, shape, len(shape) - 2) < count


def grad_of_temporal(gy, wt_ref, count):
    n = gy.shape[0]
    flat = gy.reshape(n * SLOTS, CH)
    total = mm_nt(flat, wt_ref[2]).reshape(n, SLOTS, CH)
    for k in (1, 0):
        term = mm_nt(flat, wt_ref[k]).reshape(n, SLOTS, CH)
        total = total + pltpu.roll(term, SLOTS - (2 - k), 1)
    return jnp.where(slot_mask(total.shape, count), total, 0.0).astype(BF)


def place_bits():
    t, g = lax.axis_index("tm"), lax.axis_index("grp")
    return t & 1, ((t >> 1) & 1) + 2 * (g & 1), (t >> 2) & 3


def split_cores(value, keep_ref, send_ref, k):
    core, _, _ = place_bits()
    low, high = value[:, : CH // 2].astype(BF), value[:, CH // 2 :].astype(BF)
    keep_ref[:, k] = jnp.where(core == 0, low, high).reshape(16, 16, CH // 2)
    send_ref[:, k] = jnp.where(core == 0, high, low).reshape(16, 16, CH // 2)


def edges_kernel(bands, count_ref, x_ref, *rest):
    outs, token_ref = rest[:-1], rest[-1]
    token_ref[...] = jnp.zeros_like(token_ref)
    count = count_ref[0]
    band = lax.axis_index("grp")
    wide = x_ref.shape[1]
    if bands == 2:
        starts, lower = [jnp.where(band == 0, wide - 16, 0)], [band == 0]
    else:
        starts, lower = [wide - 16, 0], [True, False]
    place = to_slots(16, SLOTS, own_frames(count))
    for k, at in enumerate(starts):
        piece = x_ref[:, pl.ds(pl.multiple_of(at, 16), 16), :].reshape(SLOTS * 16, CH)
        v = mm(place, piece)
        v = jnp.where(lower[k], v[128:], v[:128])
        outs[k][...] = silu_norm(v).astype(BF)


def acts_kernel(count_ref, x_ref, _, xt_ref, acts_ref, at_ref):
    count = count_ref[0]
    rows, cols = xt_ref.shape[0], xt_ref.shape[1]
    edge = jnp.zeros((rows + 2, SLOTS, CH), BF)
    acts_ref[:, 0] = edge
    acts_ref[:, cols + 1] = edge
    place = to_slots(16, SLOTS, own_frames(count))

    def rows_of(q, _):
        at = pl.multiple_of(q * 16, 16)
        piece = x_ref[:, pl.ds(at, 16), :].reshape(SLOTS * 16, CH)
        v = mm(place, piece)
        xt_ref[pl.ds(2 * q, 2)] = v.astype(BF).reshape(2, cols, SLOTS, CH)
        a = silu_norm(v).astype(BF)
        acts_ref[pl.ds(2 * q + 1, 2), 1 : cols + 1] = a.reshape(2, cols, SLOTS, CH)
        flipped = a.T
        for i in range(3):
            at = pl.multiple_of((2 * q + 3 - i) * 128, 128)
            at_ref[i * CH : i * CH + CH, pl.ds(at, 256)] = flipped
        return 0

    lax.fori_loop(0, rows // 2, rows_of, 0, unroll=4)


def spatial_kernel(
    bands, count_ref, top_ref, bot_ref, acts_in, ws_ref, acts_ref, sp_ref, edge_ref
):
    count = count_ref[0]
    band = lax.axis_index("grp")
    rows, cols = sp_ref.shape[0], sp_ref.shape[1]
    for ref, flag, row in ((top_ref, band > 0, 0), (bot_ref, band < bands - 1, rows + 1)):
        a = jnp.where(flag, ref[...].astype(F32), 0.0)
        acts_ref[row, 1 : cols + 1] = a.astype(BF).reshape(cols, SLOTS, CH)
    a, b = iotas(32, 256)
    pick = ((a >> 1) == (b >> 4)) & ((b & 15) == count - 2 + (a & 1))
    pick = jnp.where(pick, 1.0, 0.0).astype(BF)

    def rows_of(q, _):
        left = [
            acts_ref[pl.ds(4 * q + i, 4), j : j + cols].reshape(4 * cols * SLOTS, CH)
            for i in range(3)
            for j in range(3)
        ]
        out = mm(jnp.concatenate(left, axis=1), ws_ref[...].reshape(9 * CH, CH)).astype(BF)
        sp_ref[pl.ds(4 * q, 4)] = out.reshape(4, cols, SLOTS, CH)
        for half in range(2):
            edge_ref[2 * q + half] = mm(pick, out[half * 256 : half * 256 + 256]).astype(BF)
        return 0

    lax.fori_loop(0, rows // 4, rows_of, 0, unroll=2)


def grad_spatial_kernel(
    bands, count_ref, at_in, top_ref, bot_ref, cot_ref, nxt_ref, wt_ref, wd_ref, _,
    at_ref, cott_ref, gy_ref, gs_ref, keep_ref, send_ref, *edge_refs,
):
    count = count_ref[0]
    band = lax.axis_index("grp")
    rows, cols = gy_ref.shape[0], gy_ref.shape[1]
    for ref, flag, i, row in ((top_ref, band > 0, 0, 0), (bot_ref, band < bands - 1, 2, rows + 1)):
        a = jnp.where(flag, ref[...].astype(F32), 0.0)
        at = (row - i + 2) * 128
        at_ref[i * CH : i * CH + CH, at : at + 128] = a.T.astype(BF)
    edge = jnp.zeros((rows, SLOTS, CH), BF)
    gs_ref[:, 0] = edge
    gs_ref[:, cols + 1] = edge

    place_next = to_slots(16, SLOTS, own_and_next(count))
    for q in range(rows * cols // 64):
        four = slice(q * 4, q * 4 + 4)
        piece = jnp.concatenate(
            [cot_ref[0:OWN, four].reshape(OWN, 16, CH), nxt_ref[:, four].reshape(2, 16, CH)], 0
        ).reshape(SLOTS * 16, CH)
        placed = mm(place_next, piece).astype(BF)
        cott_ref[q * 4 : q * 4 + 4] = placed.reshape(4, 4, SLOTS, CH)
        for i in range(2):
            for j in range(2):
                g = mm_nt(placed, wd_ref[i * 2 + j]).astype(BF).reshape(4, 4, SLOTS, CH)
                for r in range(4):
                    for c in range(4):
                        gy_ref[2 * (q * 4 + r) + i, 2 * c + j] = g[r, c]
    last = cott_ref[rows // 2 - 1].reshape(cols // 2 * SLOTS, CH)
    first = cott_ref[0].reshape(cols // 2 * SLOTS, CH)
    if bands == 2:
        edge_refs[0][...] = jnp.where(band == 0, last, first)
    else:
        edge_refs[0][...] = last
        edge_refs[1][...] = first

    def grads_of(q, _):
        g = gy_ref[pl.ds(4 * q, 4)].reshape(4 * cols, SLOTS, CH)
        s = grad_of_temporal(g, wt_ref, count)
        gs_ref[pl.ds(4 * q, 4), 1 : cols + 1] = s.reshape(4, cols, SLOTS, CH)
        g = jnp.where(slot_mask(g.shape, count), g.astype(F32), 0.0)
        gy_ref[pl.ds(4 * q, 4)] = g.astype(BF).reshape(4, cols, SLOTS, CH)
        return 0

    lax.fori_loop(0, rows // 4, grads_of, 0, unroll=2)

    wide = rows * cols * SLOTS
    for j in range(3):
        right = gs_ref[:, 2 - j : 2 - j + cols].reshape(wide, CH)
        value = mm(at_ref[:, 256 : 256 + wide], right)
        for i in range(3):
            split_cores(value[i * CH : i * CH + CH], keep_ref, send_ref, i * 3 + j)


def forward_kernel(
    count_ref, xt_ref, sp_ref, prev_ref, cott_ref, gy_ref, wt_ref, wd_ref, *rest
):
    down_ref, keep_ref, send_ref, y_ref, st_ref, yt_ref = rest[-6:]
    count = count_ref[0]
    rows, cols = xt_ref.shape[0], xt_ref.shape[1]
    a, b = iotas(256, 32)
    place = ((a >> 4) == (b >> 1)) & ((a & 15) == OWN + (b & 1))
    place = jnp.where(place, 1.0, 0.0).astype(BF)

    def rows_of(q, _):
        s = sp_ref[pl.ds(4 * q, 4)].reshape(4 * cols * SLOTS, CH).astype(F32)
        s = s + jnp.concatenate([mm(place, prev_ref[2 * q]), mm(place, prev_ref[2 * q + 1])], 0)
        s = s.reshape(4 * cols, SLOTS, CH)
        total = None
        for k in range(3):
            shifted = s if k == 2 else pltpu.roll(s, 2 - k, 1)
            shifted = shifted.astype(BF).reshape(4 * cols * SLOTS, CH)
            at = pl.ds(pl.multiple_of(q * 512, 512), 512)
            st_ref[k * CH : k * CH + CH, at] = shifted.T
            term = mm(shifted, wt_ref[k])
            total = term if total is None else total + term
        x = xt_ref[pl.ds(4 * q, 4)].reshape(4 * cols, SLOTS, CH).astype(F32)
        y = jnp.where(slot_mask(x.shape, count), x + total.reshape(x.shape), 0.0).astype(BF)
        y_ref[pl.ds(4 * q, 4)] = y.reshape(4, cols, SLOTS, CH)
        return 0

    lax.fori_loop(0, rows // 4, rows_of, 0, unroll=2)

    wide = rows * cols * SLOTS
    value = mm(st_ref[...], gy_ref[...].reshape(wide, CH))
    for k in range(3):
        split_cores(value[k * CH : k * CH + CH], keep_ref, send_ref, k)

    small = wide // 4
    total = None
    for i in range(2):
        for j in range(2):
            tiles = [
                y_ref[2 * r + i, 2 * c + j] for r in range(rows // 2) for c in range(cols // 2)
            ]
            piece = jnp.concatenate(tiles, axis=0)
            k = i * 2 + j
            yt_ref[k * CH : k * CH + CH] = piece.T
            term = mm(piece, wd_ref[k])
            total = term if total is None else total + term
    down_ref[...] = total.astype(BF)
    value = mm(yt_ref[...], cott_ref[...].reshape(small, CH))
    for k in range(4):
        split_cores(value[k * CH : k * CH + CH], keep_ref, send_ref, 3 + k)


def grad_x_kernel(
    bands, count_ref, xt_ref, gy_ref, gs_ref, top_ref, bot_ref, wt_ref, wd_ref, ws_ref, slot_ref, *rest
):
    out_ref, down_ref, token_ref, pad_ref, buf, sems = rest[-6:]
    token_ref[...] = jnp.zeros_like(token_ref)
    count = count_ref[0]
    band = lax.axis_index("grp")
    rows, cols = xt_ref.shape[0], xt_ref.shape[1]
    pad_ref[1 : rows + 1] = gs_ref[...]
    edge = jnp.zeros((SLOTS, CH), BF)
    for ref, flag, i, row in ((top_ref, band > 0, 1, 0), (bot_ref, band < bands - 1, 0, rows + 1)):
        pair = [
            mm_nt(ref[...], wd_ref[i * 2 + j]).astype(BF).reshape(cols // 2, SLOTS, CH)
            for j in range(2)
        ]
        g = jnp.stack(pair, axis=1).reshape(cols, SLOTS, CH)
        pad_ref[row, 0] = edge
        pad_ref[row, 1 : cols + 1] = grad_of_temporal(g, wt_ref, jnp.where(flag, count, 0))
        pad_ref[row, cols + 1] = edge
    back = to_frames(16)

    def rows_of(q, _):
        total = None
        for i in range(3):
            for j in range(3):
                left = pad_ref[pl.ds(4 * q + 2 - i, 4), 2 - j : 2 - j + cols].reshape(
                    4 * cols * SLOTS, CH
                )
                term = mm_nt(left, ws_ref[i * 3 + j])
                total = term if total is None else total + term
        at = 4 * q
        v = xt_ref[pl.ds(at, 4)].reshape(4 * cols * SLOTS, CH).astype(F32)
        r = lax.rsqrt(jnp.mean(v * v, axis=-1, keepdims=True) + 1e-06)
        u = v * r
        s = 0.5 + 0.5 * jnp.tanh(0.5 * u)
        gu = total * (s * (1.0 + u * (1.0 - s)))
        dot = jnp.mean(gu * u, axis=-1, keepdims=True)
        gv = r * (gu - u * dot)
        gx = gy_ref[pl.ds(at, 4)].reshape(4 * cols * SLOTS, CH).astype(F32) + gv
        gx = gx.reshape(4 * cols, SLOTS, CH)
        gx = jnp.where(slot_mask(gx.shape, count), gx, 0.0).astype(BF).reshape(4 * cols * SLOTS, CH)
        for k in range(2):
            o = mm(back, gx[k * 256 : k * 256 + 256]).astype(BF)
            buf[:, pl.ds(pl.multiple_of((2 * q + k) * 16, 16), 16), :] = o.reshape(SLOTS, 16, CH)
        return 0

    lax.fori_loop(0, rows // 4, rows_of, 0, unroll=2)
    copy = pltpu.make_async_copy(buf, out_ref, sems.at[0])
    copy.start()
    for q in range(down_ref.shape[1] // 4):
        o = mm(back, slot_ref[q * 256 : q * 256 + 256]).astype(BF)
        down_ref[:, q * 4 : q * 4 + 4] = o.reshape(SLOTS, 4, cols // 2, CH)
    copy.wait()


ORDER = (0, 3, 2, 1)


def plane_send_kernel(keep_a, got_a, keep_b, got_b, *outs):
    _, p, _ = place_bits()
    n = keep_a.shape[1]
    for r, out in zip(ORDER, outs):
        at = pl.ds((p ^ r) * 4, 4)
        out[:, :n] = (keep_a[at].astype(F32) + got_a[at].astype(F32)).astype(BF)
        out[:, n:] = (keep_b[at].astype(F32) + got_b[at].astype(F32)).astype(BF)


def line_send_kernel(a_ref, b_ref, c_ref, d_ref, *rest):
    outs = rest[-4:]
    _, _, z = place_bits()
    for k, r in enumerate(ORDER):
        parts = [ref[z ^ r].astype(F32) for ref in (a_ref, b_ref, c_ref, d_ref)]
        outs[k][...] = (parts[0] + parts[1] + parts[2] + parts[3]).astype(BF)


def line_sum_kernel(a_ref, b_ref, c_ref, d_ref, out_ref):
    parts = [ref[...].astype(F32) for ref in (a_ref, b_ref, c_ref, d_ref)]
    out_ref[...] = (parts[0] + parts[1] + parts[2] + parts[3]).astype(BF)


def line_gather_kernel(a_ref, b_ref, c_ref, d_ref, out_ref):
    _, _, z = place_bits()
    for r, ref in zip(ORDER, (a_ref, b_ref, c_ref, d_ref)):
        out_ref[z ^ r] = ref[...]


def plane_gather_kernel(a_ref, b_ref, c_ref, d_ref, out_ref):
    _, p, _ = place_bits()
    for r, ref in zip(ORDER, (a_ref, b_ref, c_ref, d_ref)):
        out_ref[pl.ds((p ^ r) * 4, 4)] = ref[...]


def add_kernel(a_ref, b_ref, out_ref):
    out_ref[...] = (a_ref[...].astype(F32) + b_ref[...].astype(F32)).astype(BF)


def pass_kernel(*_):
    pass


def finish_kernel(own, half_ref, *rest):
    buf, sems = rest[-2:]
    outs = rest[-5:-2]
    core, _, _ = place_bits()
    at = pl.multiple_of((core if own else 1 - core) * (CH // 2), CH // 2)
    copies = []
    k = 0
    for out in outs:
        for m in range(out.shape[0]):
            buf[k] = half_ref[:, k].reshape(CH, CH // 2).astype(F32)
            copies.append(
                pltpu.make_async_copy(buf.at[k], out.at[m, :, pl.ds(at, CH // 2)], sems.at[k])
            )
            copies[-1].start()
            k += 1
    for copy in copies:
        copy.wait()


VMEM = pl.BlockSpec(memory_space=pltpu.VMEM)
SMEM = pl.BlockSpec(memory_space=pltpu.SMEM)
ANY = pl.BlockSpec(memory_space=pl.ANY)
HBM = pl.BlockSpec(memory_space=pltpu.HBM)
TOKEN = (VMEM, (8, 128), F32)


def call(kernel, name, ins, outs, scratch=(), flops=0, alias=None, grant=10):
    shapes = [jax.ShapeDtypeStruct(o[1], o[2] if len(o) > 2 else BF) for o in outs]
    moved = sum(a.size * a.dtype.itemsize for s, a in ins if s is not ANY)
    moved += sum(s.size * s.dtype.itemsize for s in shapes)
    return pl.pallas_call(
        kernel,
        out_shape=shapes,
        in_specs=[s for s, _ in ins],
        out_specs=[o[0] for o in outs],
        scratch_shapes=list(scratch),
        compiler_params=pltpu.CompilerParams(vmem_limit_bytes=grant * 2**20),
        cost_estimate=pl.CostEstimate(flops=flops, bytes_accessed=moved, transcendentals=0),
        input_output_aliases=alias or {},
        name=name,
    )(*[a for _, a in ins])


AXES = ("tm", "grp")


def plan(tm, grp):
    low, total = grp.bit_length() - 1, (tm * grp).bit_length() - 1
    plane, line = [low + 1, 0], [low + 2, low + 3]
    return low, plane, line, [b for b in range(total) if b not in [low] + plane + line]


def swap(value, tm, grp, *bits):
    flip = sum(1 << b for b in bits)
    return lax.ppermute(value, AXES, [(d, d ^ flip) for d in range(tm * grp)])


def core_round(value, tm, grp):
    return swap(value, tm, grp, plan(tm, grp)[0])


def four_round(parts, bits, tm, grp):
    return [
        parts[0],
        swap(parts[1], tm, grp, *bits),
        swap(parts[2], tm, grp, bits[1]),
        swap(parts[3], tm, grp, bits[0]),
    ]


def passed(value, after):
    ins = [(ANY, value)] + [(ANY, a) for a in after]
    return call(pass_kernel, "pass", ins, [(ANY, value.shape)], alias={0: 0})[0]


def finish(own, half, before):
    n = half.shape[1]
    return list(
        call(
            functools.partial(finish_kernel, own),
            "finish",
            [(VMEM, half)] + [(HBM, a) for a in before],
            [(HBM, (m, CH, CH), F32) for m in (9, 3, 4)],
            [pltpu.VMEM((n, CH, CH // 2), F32), pltpu.SemaphoreType.DMA((n,))],
            alias={1 + i: i for i in range(len(before))},
        )
    )


def along(value, axis, by):
    count = lax.axis_size(axis)
    pairs = [(i, i + by) for i in range(count) if 0 <= i + by < count]
    return lax.ppermute(value, axis, pairs)


def from_bands(parts):
    if len(parts) == 1:
        got = lax.ppermute(parts[0], "grp", [(0, 1), (1, 0)])
        return got, got
    return along(parts[0], "grp", 1), along(parts[1], "grp", -1)


def body(tm, grp, frames_in, span_frames, w_spatial, w_temporal, w_down, cotangent):
    slots, rows, cols, ch = frames_in.shape
    wide = rows * cols
    x = frames_in.reshape(slots, wide, ch)
    ws = w_spatial.reshape(9, ch, ch)
    wd = w_down.reshape(4, ch, ch)
    wt = w_temporal
    count = (SMEM, span_frames)
    tap = 2 * slots * wide * ch * ch
    tile = (rows, cols, slots, ch)
    padded = (rows + 2, cols + 2, slots, ch)
    dma = pltpu.SemaphoreType.DMA

    sides = 1 if grp == 2 else 2
    *edge, token = call(
        functools.partial(edges_kernel, grp),
        "edges",
        [count, (VMEM, x)],
        [(VMEM, (cols * slots, ch))] * sides + [TOKEN],
        flops=tap // 8,
    )
    top, bot = from_bands(edge)
    nxt_got = along(cotangent[:2], "tm", -1)
    xt, acts, at = call(
        acts_kernel,
        "acts",
        [count, (VMEM, x), (ANY, token)],
        [(VMEM, tile), (VMEM, padded), (VMEM, (3 * ch, (rows + 4) * 128))],
        flops=2 * tap,
    )
    acts, sp, last_two = call(
        functools.partial(spatial_kernel, grp),
        "spatial",
        [count, (VMEM, top), (VMEM, bot), (VMEM, acts), (VMEM, ws)],
        [(VMEM, padded), (VMEM, tile), (VMEM, (rows // 2, 32, ch))],
        flops=9 * tap,
        alias={3: 0},
    )
    prev = along(last_two, "tm", 1)
    half = (16, 9, 16, ch // 2)
    at, cott, gy, gs, keep_a, send_a, *edge = call(
        functools.partial(grad_spatial_kernel, grp),
        "grad_spatial",
        [count, (VMEM, at), (VMEM, top), (VMEM, bot), (VMEM, cotangent), (VMEM, nxt_got), (VMEM, wt), (VMEM, wd),
         (ANY, last_two)],
        [(VMEM, at.shape), (VMEM, (rows // 2, cols // 2, slots, ch)), (VMEM, tile),
         (VMEM, (rows, cols + 2, slots, ch)), (VMEM, half), (VMEM, half)]
        + [(VMEM, (cols // 2 * slots, ch))] * sides,
        flops=14 * tap,
        alias={1: 0},
    )
    send_a = passed(send_a, [prev])
    got_a = core_round(send_a, tm, grp)
    cot_top, cot_bot = from_bands(edge)
    half = (16, 7, 16, ch // 2)
    down, keep_b, send_b = call(
        forward_kernel,
        "forward",
        [count, (VMEM, xt), (VMEM, sp), (VMEM, prev), (VMEM, cott), (VMEM, gy), (VMEM, wt), (VMEM, wd),
         (ANY, send_a)],
        [(VMEM, (slots * wide // 4, ch)), (VMEM, half), (VMEM, half)],
        [pltpu.VMEM(v, BF) for v in (tile, (3 * ch, slots * wide), (4 * ch, slots * wide // 4))],
        flops=10 * tap,
        grant=14,
    )
    send_b = passed(send_b, [got_a, cot_top, cot_bot][: 1 + sides])
    got_b = core_round(send_b, tm, grp)
    _, plane, line, others = plan(tm, grp)
    parts = call(
        plane_send_kernel,
        "plane_send",
        [(VMEM, a) for a in (keep_a, got_a, keep_b, got_b)],
        [(VMEM, (4, 16, 16, ch // 2))] * 4,
    )
    grad_x, down, token = call(
        functools.partial(grad_x_kernel, grp),
        "grad_x",
        [count, (VMEM, xt), (VMEM, gy), (VMEM, gs), (VMEM, cot_top), (VMEM, cot_bot), (VMEM, wt),
         (VMEM, wd), (VMEM, ws), (VMEM, down), (ANY, parts[3])],
        [(HBM, (slots, wide, ch)), (VMEM, cotangent.shape), TOKEN],
        [pltpu.VMEM(padded, BF), pltpu.VMEM((slots, wide, ch), BF), dma((1,))],
        flops=10 * tap,
    )
    parts = four_round(list(parts), plane, tm, grp)
    parts = call(
        line_send_kernel,
        "line_send",
        [(VMEM, a) for a in parts] + [(ANY, token)],
        [(VMEM, (16, 16, ch // 2))] * 4,
    )
    parts = four_round(list(parts), line, tm, grp)
    (mine,) = call(line_sum_kernel, "line_sum", [(VMEM, a) for a in parts], [(VMEM, parts[0].shape)])
    for bit in others:
        got = swap(mine, tm, grp, bit)
        (mine,) = call(add_kernel, "add", [(VMEM, mine), (VMEM, got)], [(VMEM, mine.shape)])
    parts = four_round([mine] * 4, line, tm, grp)
    (mine,) = call(
        line_gather_kernel, "line_gather", [(VMEM, a) for a in parts], [(VMEM, (4,) + mine.shape)]
    )
    parts = four_round([mine] * 4, plane, tm, grp)
    ins = [(VMEM, a) for a in parts]
    (mine,) = call(plane_gather_kernel, "plane_gather", ins, [(VMEM, (16,) + mine.shape[1:])])
    got = core_round(mine, tm, grp)
    outs = finish(True, mine, [])
    sum_s, sum_t, sum_d = finish(False, got, outs)
    return (
        down,
        grad_x.reshape(frames_in.shape),
        sum_s.reshape(w_spatial.shape),
        sum_t,
        sum_d.reshape(w_down.shape),
    )


def solution(mesh):
    return jax.shard_map(
        functools.partial(body, mesh.shape["tm"], mesh.shape["grp"]),
        mesh=mesh,
        in_specs=(P("tm", "grp", None, None), P("tm"), P(), P(), P(), P("tm", "grp", None, None)),
        out_specs=(P("tm", "grp", None, None), P("tm", "grp", None, None), P(), P(), P()),
        check_vma=False,
    )
```

```python
import functools

import jax
import jax.numpy as jnp
from jax import lax
from jax.experimental import pallas as pl
from jax.experimental.pallas import tpu as pltpu
from jax.sharding import PartitionSpec as P

SLOTS = 16
OWN = 14
CH = 256
BF = jnp.bfloat16
F32 = jnp.float32


def mm(a, b):
    return lax.dot_general(a, b, (((1,), (0,)), ((), ())), preferred_element_type=F32)


def mm_nt(a, b):
    return lax.dot_general(a, b, (((1,), (1,)), ((), ())), preferred_element_type=F32)


def iotas(rows, cols):
    return (
        lax.broadcasted_iota(jnp.int32, (rows, cols), 0),
        lax.broadcasted_iota(jnp.int32, (rows, cols), 1),
    )


def to_slots(rows, frames, keep):
    a, b = iotas(rows * SLOTS, frames * rows)
    bits = rows.bit_length() - 1
    hit = ((a >> 4) == (b & (rows - 1))) & keep(b >> bits, a & 15)
    return jnp.where(hit, 1.0, 0.0).astype(BF)


def to_frames(rows):
    a, b = iotas(SLOTS * rows, rows * SLOTS)
    bits = rows.bit_length() - 1
    hit = ((a & (rows - 1)) == (b >> 4)) & ((a >> bits) == (b & 15))
    return jnp.where(hit, 1.0, 0.0).astype(BF)


def own_frames(count):
    return lambda frame, slot: (frame == slot) & (slot < count)


def own_and_next(count):
    return lambda frame, slot: ((frame < OWN) & (frame == slot) & (slot < count)) | (
        (frame >= OWN) & (slot == count + frame - OWN)
    )


def silu_norm(v):
    scaled = v * lax.rsqrt(jnp.mean(v * v, axis=-1, keepdims=True) + 1e-06)
    return scaled * (0.5 + 0.5 * jnp.tanh(0.5 * scaled))


def slot_mask(shape, count):
    return lax.broadcasted_iota(jnp.int32, shape, len(shape) - 2) < count


def grad_of_temporal(gy, wt_ref, count):
    n = gy.shape[0]
    flat = gy.reshape(n * SLOTS, CH)
    total = mm_nt(flat, wt_ref[2]).reshape(n, SLOTS, CH)
    for k in (1, 0):
        term = mm_nt(flat, wt_ref[k]).reshape(n, SLOTS, CH)
        total = total + pltpu.roll(term, SLOTS - (2 - k), 1)
    return jnp.where(slot_mask(total.shape, count), total, 0.0).astype(BF)


def place_bits():
    t, g = lax.axis_index("tm"), lax.axis_index("grp")
    return t & 1, ((t >> 1) & 1) + 2 * (g & 1), (t >> 2) & 3


def split_cores(value, keep_ref, send_ref, k):
    core, _, _ = place_bits()
    low, high = value[:, : CH // 2].astype(BF), value[:, CH // 2 :].astype(BF)
    keep_ref[:, k] = jnp.where(core == 0, low, high).reshape(16, 16, CH // 2)
    send_ref[:, k] = jnp.where(core == 0, high, low).reshape(16, 16, CH // 2)


def edges_kernel(bands, count_ref, x_ref, cot_ref, *rest):
    outs, (nxt_ref, token_ref) = rest[:-2], rest[-2:]
    nxt_ref[...] = cot_ref[0:2]
    token_ref[...] = jnp.zeros_like(token_ref)
    count = count_ref[0]
    band = lax.axis_index("grp")
    wide = x_ref.shape[1]
    if bands == 2:
        starts, lower = [jnp.where(band == 0, wide - 16, 0)], [band == 0]
    else:
        starts, lower = [wide - 16, 0], [True, False]
    place = to_slots(16, SLOTS, own_frames(count))
    for k, at in enumerate(starts):
        piece = x_ref[:, pl.ds(pl.multiple_of(at, 16), 16), :].reshape(SLOTS * 16, CH)
        v = mm(place, piece)
        v = jnp.where(lower[k], v[128:], v[:128])
        outs[k][...] = silu_norm(v).astype(BF)


def acts_kernel(count_ref, x_ref, _, xt_ref, acts_ref, at_ref):
    count = count_ref[0]
    rows, cols = xt_ref.shape[0], xt_ref.shape[1]
    edge = jnp.zeros((rows + 2, SLOTS, CH), BF)
    acts_ref[:, 0] = edge
    acts_ref[:, cols + 1] = edge
    place = to_slots(16, SLOTS, own_frames(count))

    def rows_of(q, _):
        at = pl.multiple_of(q * 16, 16)
        piece = x_ref[:, pl.ds(at, 16), :].reshape(SLOTS * 16, CH)
        v = mm(place, piece)
        xt_ref[pl.ds(2 * q, 2)] = v.astype(BF).reshape(2, cols, SLOTS, CH)
        a = silu_norm(v).astype(BF)
        acts_ref[pl.ds(2 * q + 1, 2), 1 : cols + 1] = a.reshape(2, cols, SLOTS, CH)
        flipped = a.T
        for i in range(3):
            at = pl.multiple_of((2 * q + 3 - i) * 128, 128)
            at_ref[i * CH : i * CH + CH, pl.ds(at, 256)] = flipped
        return 0

    lax.fori_loop(0, rows // 2, rows_of, 0, unroll=4)


def spatial_kernel(
    bands, count_ref, top_ref, bot_ref, acts_in, ws_ref, _, acts_ref, sp_ref, edge_ref, sum_ref
):
    count = count_ref[0]
    band = lax.axis_index("grp")
    rows, cols = sp_ref.shape[0], sp_ref.shape[1]
    for ref, flag, row in ((top_ref, band > 0, 0), (bot_ref, band < bands - 1, rows + 1)):
        a = jnp.where(flag, ref[...].astype(F32), 0.0)
        acts_ref[row, 1 : cols + 1] = a.astype(BF).reshape(cols, SLOTS, CH)
    a, b = iotas(32, 256)
    pick = ((a >> 1) == (b >> 4)) & ((b & 15) == count - 2 + (a & 1))
    pick = jnp.where(pick, 1.0, 0.0).astype(BF)

    high = rows // 2
    for q in range(2):
        for i in range(3):
            for j in range(3):
                left = acts_ref[high * q + i : high * q + i + high, j : j + cols]
                term = mm(left.reshape(high * cols * SLOTS, CH), ws_ref[i * 3 + j])
                if i + j == 0:
                    sum_ref[...] = term
                elif i + j < 4:
                    sum_ref[...] += term
                else:
                    out = (sum_ref[...] + term).astype(BF)
        sp_ref[high * q : high * q + high] = out.reshape(high, cols, SLOTS, CH)
        for k in range(high // 2):
            edge_ref[high // 2 * q + k] = mm(pick, out[k * 256 : k * 256 + 256]).astype(BF)


def grad_spatial_kernel(
    bands, count_ref, at_in, top_ref, bot_ref, cot_ref, nxt_ref, wt_ref, wd_ref,
    at_ref, cott_ref, gy_ref, gs_ref, keep_ref, send_ref, *edge_refs,
):
    count = count_ref[0]
    band = lax.axis_index("grp")
    rows, cols = gy_ref.shape[0], gy_ref.shape[1]
    for ref, flag, i, row in ((top_ref, band > 0, 0, 0), (bot_ref, band < bands - 1, 2, rows + 1)):
        a = jnp.where(flag, ref[...].astype(F32), 0.0)
        at = (row - i + 2) * 128
        at_ref[i * CH : i * CH + CH, at : at + 128] = a.T.astype(BF)
    edge = jnp.zeros((rows, SLOTS, CH), BF)
    gs_ref[:, 0] = edge
    gs_ref[:, cols + 1] = edge

    place_next = to_slots(16, SLOTS, own_and_next(count))
    halves = []
    for q in range(rows * cols // 64):
        four = slice(q * 4, q * 4 + 4)
        piece = jnp.concatenate(
            [cot_ref[0:OWN, four].reshape(OWN, 16, CH), nxt_ref[:, four].reshape(2, 16, CH)], 0
        ).reshape(SLOTS * 16, CH)
        halves.append(mm(place_next, piece).astype(BF))
    placed = jnp.concatenate(halves, 0)
    cott_ref[...] = placed.reshape(rows // 2, cols // 2, SLOTS, CH)
    for i in range(2):
        for j in range(2):
            g = mm_nt(placed, wd_ref[i * 2 + j]).astype(BF).reshape(rows // 2, cols // 2, SLOTS, CH)
            for r in range(rows // 2):
                for c in range(cols // 2):
                    gy_ref[2 * r + i, 2 * c + j] = g[r, c]
    last = cott_ref[rows // 2 - 1].reshape(cols // 2 * SLOTS, CH)
    first = cott_ref[0].reshape(cols // 2 * SLOTS, CH)
    if bands == 2:
        edge_refs[0][...] = jnp.where(band == 0, last, first)
    else:
        edge_refs[0][...] = last
        edge_refs[1][...] = first

    def grads_of(q, _):
        g = gy_ref[pl.ds(8 * q, 8)].reshape(8 * cols, SLOTS, CH)
        s = grad_of_temporal(g, wt_ref, count)
        gs_ref[pl.ds(8 * q, 8), 1 : cols + 1] = s.reshape(8, cols, SLOTS, CH)
        g = jnp.where(slot_mask(g.shape, count), g.astype(F32), 0.0)
        gy_ref[pl.ds(8 * q, 8)] = g.astype(BF).reshape(8, cols, SLOTS, CH)
        return 0

    lax.fori_loop(0, rows // 8, grads_of, 0)

    wide = rows * cols * SLOTS
    for j in range(3):
        right = gs_ref[:, 2 - j : 2 - j + cols].reshape(wide, CH)
        value = mm(at_ref[:, 256 : 256 + wide], right)
        for i in range(3):
            split_cores(value[i * CH : i * CH + CH], keep_ref, send_ref, i * 3 + j)


def forward_kernel(
    count_ref, xt_ref, sp_ref, prev_ref, cott_ref, gy_ref, wt_ref, wd_ref, *rest
):
    down_ref, keep_ref, send_ref, y_ref, st_ref, yt_ref = rest[-6:]
    count = count_ref[0]
    rows, cols = xt_ref.shape[0], xt_ref.shape[1]
    a, b = iotas(256, 32)
    place = ((a >> 4) == (b >> 1)) & ((a & 15) == OWN + (b & 1))
    place = jnp.where(place, 1.0, 0.0).astype(BF)

    def rows_of(q, _):
        s = sp_ref[pl.ds(8 * q, 8)].reshape(8 * cols * SLOTS, CH).astype(F32)
        s = s + jnp.concatenate([mm(place, prev_ref[4 * q + k]) for k in range(4)], 0)
        s = s.reshape(8 * cols, SLOTS, CH)
        total = None
        for k in range(3):
            shifted = s if k == 2 else pltpu.roll(s, 2 - k, 1)
            shifted = shifted.astype(BF).reshape(8 * cols * SLOTS, CH)
            at = pl.ds(pl.multiple_of(q * 1024, 1024), 1024)
            st_ref[k * CH : k * CH + CH, at] = shifted.T
            term = mm(shifted, wt_ref[k])
            total = term if total is None else total + term
        x = xt_ref[pl.ds(8 * q, 8)].reshape(8 * cols, SLOTS, CH).astype(F32)
        y = jnp.where(slot_mask(x.shape, count), x + total.reshape(x.shape), 0.0).astype(BF)
        y_ref[pl.ds(8 * q, 8)] = y.reshape(8, cols, SLOTS, CH)
        return 0

    lax.fori_loop(0, rows // 8, rows_of, 0)

    wide = rows * cols * SLOTS
    value = mm(st_ref[...], gy_ref[...].reshape(wide, CH))
    for k in range(3):
        split_cores(value[k * CH : k * CH + CH], keep_ref, send_ref, k)

    small = wide // 4
    total = None
    for i in range(2):
        for j in range(2):
            tiles = [
                y_ref[2 * r + i, 2 * c + j] for r in range(rows // 2) for c in range(cols // 2)
            ]
            piece = jnp.concatenate(tiles, axis=0)
            k = i * 2 + j
            yt_ref[k * CH : k * CH + CH] = piece.T
            term = mm(piece, wd_ref[k])
            total = term if total is None else total + term
    down_ref[...] = total.astype(BF)
    value = mm(yt_ref[...], cott_ref[...].reshape(small, CH))
    for k in range(4):
        split_cores(value[k * CH : k * CH + CH], keep_ref, send_ref, 3 + k)


def grad_x_kernel(
    bands, count_ref, xt_ref, gy_ref, gs_ref, top_ref, bot_ref, wt_ref, wd_ref, ws_ref, slot_ref, *rest
):
    out_ref, down_ref, token_ref, pad_ref, buf, sems = rest[-6:]
    token_ref[...] = jnp.zeros_like(token_ref)
    count = count_ref[0]
    band = lax.axis_index("grp")
    rows, cols = xt_ref.shape[0], xt_ref.shape[1]
    pad_ref[1 : rows + 1] = gs_ref[...]
    edge = jnp.zeros((SLOTS, CH), BF)
    for ref, flag, i, row in ((top_ref, band > 0, 1, 0), (bot_ref, band < bands - 1, 0, rows + 1)):
        pair = [
            mm_nt(ref[...], wd_ref[i * 2 + j]).astype(BF).reshape(cols // 2, SLOTS, CH)
            for j in range(2)
        ]
        g = jnp.stack(pair, axis=1).reshape(cols, SLOTS, CH)
        pad_ref[row, 0] = edge
        pad_ref[row, 1 : cols + 1] = grad_of_temporal(g, wt_ref, jnp.where(flag, count, 0))
        pad_ref[row, cols + 1] = edge
    back = to_frames(16)

    def rows_of(q, _):
        total = None
        for i in range(3):
            for j in range(3):
                left = pad_ref[pl.ds(4 * q + 2 - i, 4), 2 - j : 2 - j + cols].reshape(
                    4 * cols * SLOTS, CH
                )
                term = mm_nt(left, ws_ref[i * 3 + j])
                total = term if total is None else total + term
        at = 4 * q
        v = xt_ref[pl.ds(at, 4)].reshape(4 * cols * SLOTS, CH).astype(F32)
        r = lax.rsqrt(jnp.mean(v * v, axis=-1, keepdims=True) + 1e-06)
        u = v * r
        s = 0.5 + 0.5 * jnp.tanh(0.5 * u)
        gu = total * (s * (1.0 + u * (1.0 - s)))
        dot = jnp.mean(gu * u, axis=-1, keepdims=True)
        gv = r * (gu - u * dot)
        gx = gy_ref[pl.ds(at, 4)].reshape(4 * cols * SLOTS, CH).astype(F32) + gv
        gx = gx.reshape(4 * cols, SLOTS, CH)
        gx = jnp.where(slot_mask(gx.shape, count), gx, 0.0).astype(BF).reshape(4 * cols * SLOTS, CH)
        for k in range(2):
            o = mm(back, gx[k * 256 : k * 256 + 256]).astype(BF)
            buf[:, pl.ds(pl.multiple_of((2 * q + k) * 16, 16), 16), :] = o.reshape(SLOTS, 16, CH)
        return 0

    lax.fori_loop(0, rows // 4, rows_of, 0)
    copy = pltpu.make_async_copy(buf, out_ref, sems.at[0])
    copy.start()
    for q in range(down_ref.shape[1] // 4):
        o = mm(back, slot_ref[q * 256 : q * 256 + 256]).astype(BF)
        down_ref[:, q * 4 : q * 4 + 4] = o.reshape(SLOTS, 4, cols // 2, CH)
    copy.wait()


ORDER = (0, 3, 2, 1)


def plane_send_kernel(keep_ref, got_ref, *rest):
    _, p, _ = place_bits()
    for r, out in zip(ORDER, rest[-4:]):
        at = pl.ds((p ^ r) * 4, 4)
        out[...] = (keep_ref[at].astype(F32) + got_ref[at].astype(F32)).astype(BF)


def line_send_kernel(*refs):
    outs = refs[8:]
    _, _, z = place_bits()
    for out, r in zip(outs, ORDER):
        at = 0
        for chain in (refs[:4], refs[4:8]):
            parts = [ref[z ^ r].astype(F32) for ref in chain]
            n = parts[0].shape[0]
            out[at : at + n] = (parts[0] + parts[1] + parts[2] + parts[3]).astype(BF)
            at += n


def line_sum_kernel(a_ref, b_ref, c_ref, d_ref, out_ref):
    parts = [ref[...].astype(F32) for ref in (a_ref, b_ref, c_ref, d_ref)]
    out_ref[...] = (parts[0] + parts[1] + parts[2] + parts[3]).astype(BF)


def line_gather_kernel(a_ref, b_ref, c_ref, d_ref, out_ref):
    _, _, z = place_bits()
    for r, ref in zip(ORDER, (a_ref, b_ref, c_ref, d_ref)):
        out_ref[z ^ r] = ref[...]


def plane_gather_kernel(a_ref, b_ref, c_ref, d_ref, _, out_ref):
    _, p, _ = place_bits()
    for r, ref in zip(ORDER, (a_ref, b_ref, c_ref, d_ref)):
        out_ref[pl.ds((p ^ r) * 4, 4)] = ref[...]


def add_kernel(a_ref, b_ref, out_ref):
    out_ref[...] = (a_ref[...].astype(F32) + b_ref[...].astype(F32)).astype(BF)


def pass_kernel(*_):
    pass


def finish_kernel(own, half_ref, *rest):
    buf, sems = rest[-2:]
    outs = rest[-5:-2]
    core, _, _ = place_bits()
    at = pl.multiple_of((core if own else 1 - core) * (CH // 2), CH // 2)
    copies = []
    k = 0
    for out in outs:
        for m in range(out.shape[0]):
            buf[k] = half_ref[:, k].reshape(CH, CH // 2).astype(F32)
            copies.append(
                pltpu.make_async_copy(buf.at[k], out.at[m, :, pl.ds(at, CH // 2)], sems.at[k])
            )
            copies[-1].start()
            k += 1
    for copy in copies:
        copy.wait()


VMEM = pl.BlockSpec(memory_space=pltpu.VMEM)
SMEM = pl.BlockSpec(memory_space=pltpu.SMEM)
ANY = pl.BlockSpec(memory_space=pl.ANY)
HBM = pl.BlockSpec(memory_space=pltpu.HBM)
TOKEN = (VMEM, (8, 128), F32)


def call(kernel, name, ins, outs, scratch=(), flops=0, alias=None, grant=10):
    shapes = [jax.ShapeDtypeStruct(o[1], o[2] if len(o) > 2 else BF) for o in outs]
    moved = sum(a.size * a.dtype.itemsize for s, a in ins if s is not ANY)
    moved += sum(s.size * s.dtype.itemsize for s in shapes)
    return pl.pallas_call(
        kernel,
        out_shape=shapes,
        in_specs=[s for s, _ in ins],
        out_specs=[o[0] for o in outs],
        scratch_shapes=list(scratch),
        compiler_params=pltpu.CompilerParams(vmem_limit_bytes=grant * 2**20),
        cost_estimate=pl.CostEstimate(flops=flops, bytes_accessed=moved, transcendentals=0),
        input_output_aliases=alias or {},
        name=name,
    )(*[a for _, a in ins])


AXES = ("tm", "grp")


def plan(tm, grp):
    low, total = grp.bit_length() - 1, (tm * grp).bit_length() - 1
    plane, line = [low + 1, 0], [low + 2, low + 3]
    return low, plane, line, [b for b in range(total) if b not in [low] + plane + line]


def swap(value, tm, grp, *bits):
    flip = sum(1 << b for b in bits)
    return lax.ppermute(value, AXES, [(d, d ^ flip) for d in range(tm * grp)])


def core_round(value, tm, grp):
    return swap(value, tm, grp, plan(tm, grp)[0])


def four_round(parts, bits, tm, grp):
    return [
        parts[0],
        swap(parts[1], tm, grp, *bits),
        swap(parts[2], tm, grp, bits[1]),
        swap(parts[3], tm, grp, bits[0]),
    ]


def plane_send(keep, got, after):
    ins = [(VMEM, keep), (VMEM, got)] + [(ANY, a) for a in after]
    shape = (4, keep.shape[1], 16, CH // 2)
    return list(call(plane_send_kernel, "plane_send", ins, [(VMEM, shape)] * 4))


def passed(value, after):
    ins = [(ANY, value)] + [(ANY, a) for a in after]
    return call(pass_kernel, "pass", ins, [(ANY, value.shape)], alias={0: 0})[0]


def finish(own, half, before):
    n = half.shape[1]
    return list(
        call(
            functools.partial(finish_kernel, own),
            "finish",
            [(VMEM, half)] + [(HBM, a) for a in before],
            [(HBM, (m, CH, CH), F32) for m in (9, 3, 4)],
            [pltpu.VMEM((n, CH, CH // 2), F32), pltpu.SemaphoreType.DMA((n,))],
            alias={1 + i: i for i in range(len(before))},
        )
    )


def along(value, axis, by):
    count = lax.axis_size(axis)
    pairs = [(i, i + by) for i in range(count) if 0 <= i + by < count]
    return lax.ppermute(value, axis, pairs)


def from_bands(parts):
    if len(parts) == 1:
        got = lax.ppermute(parts[0], "grp", [(0, 1), (1, 0)])
        return got, got
    return along(parts[0], "grp", 1), along(parts[1], "grp", -1)


def body(tm, grp, frames_in, span_frames, w_spatial, w_temporal, w_down, cotangent):
    slots, rows, cols, ch = frames_in.shape
    wide = rows * cols
    x = frames_in.reshape(slots, wide, ch)
    ws = w_spatial.reshape(9, ch, ch)
    wd = w_down.reshape(4, ch, ch)
    wt = w_temporal
    count = (SMEM, span_frames)
    tap = 2 * slots * wide * ch * ch
    tile = (rows, cols, slots, ch)
    padded = (rows + 2, cols + 2, slots, ch)
    dma = pltpu.SemaphoreType.DMA

    sides = 1 if grp == 2 else 2
    *edge, nxt, token = call(
        functools.partial(edges_kernel, grp),
        "edges",
        [count, (VMEM, x), (VMEM, cotangent)],
        [(VMEM, (cols * slots, ch))] * sides + [(VMEM, (2,) + cotangent.shape[1:]), TOKEN],
        flops=tap // 8,
    )
    top, bot = from_bands(edge)
    nxt_got = along(nxt, "tm", -1)
    xt, acts, at = call(
        acts_kernel,
        "acts",
        [count, (VMEM, x), (ANY, token)],
        [(VMEM, tile), (VMEM, padded), (VMEM, (3 * ch, (rows + 4) * 128))],
        flops=2 * tap,
    )
    half = (16, 9, 16, ch // 2)
    at, cott, gy, gs, keep_a, send_a, *edge = call(
        functools.partial(grad_spatial_kernel, grp),
        "grad_spatial",
        [count, (VMEM, at), (VMEM, top), (VMEM, bot), (VMEM, cotangent), (VMEM, nxt_got), (VMEM, wt), (VMEM, wd)],
        [(VMEM, at.shape), (VMEM, (rows // 2, cols // 2, slots, ch)), (VMEM, tile),
         (VMEM, (rows, cols + 2, slots, ch)), (VMEM, half), (VMEM, half)]
        + [(VMEM, (cols // 2 * slots, ch))] * sides,
        flops=14 * tap,
        alias={1: 0},
    )
    got_a = core_round(send_a, tm, grp)
    cot_top, cot_bot = from_bands(edge)
    acts, sp, last_two = call(
        functools.partial(spatial_kernel, grp),
        "spatial",
        [count, (VMEM, top), (VMEM, bot), (VMEM, acts), (VMEM, ws), (ANY, send_a)],
        [(VMEM, padded), (VMEM, tile), (VMEM, (rows // 2, 32, ch))],
        [pltpu.VMEM((slots * wide // 2, ch), F32)],
        flops=9 * tap,
        alias={3: 0},
    )
    prev = along(last_two, "tm", 1)
    _, plane, line, others = plan(tm, grp)
    parts_a = plane_send(keep_a, got_a, [last_two])
    half = (16, 7, 16, ch // 2)
    down, keep_b, send_b = call(
        forward_kernel,
        "forward",
        [count, (VMEM, xt), (VMEM, sp), (VMEM, prev), (VMEM, cott), (VMEM, gy), (VMEM, wt), (VMEM, wd),
         *((ANY, a) for a in parts_a)],
        [(VMEM, (slots * wide // 4, ch)), (VMEM, half), (VMEM, half)],
        [pltpu.VMEM(v, BF) for v in (tile, (3 * ch, slots * wide), (4 * ch, slots * wide // 4))],
        flops=10 * tap,
        grant=14,
    )
    parts_a = four_round(parts_a, plane, tm, grp)
    send_b = passed(send_b, parts_a[1:] + [cot_top, cot_bot][:sides])
    parts_b = plane_send(keep_b, core_round(send_b, tm, grp), [])
    parts_b = four_round(parts_b, plane, tm, grp)
    parts = call(
        line_send_kernel,
        "line_send",
        [(VMEM, a) for a in parts_a + parts_b],
        [(VMEM, (16, 16, ch // 2))] * 4,
    )
    parts = four_round(list(parts), line, tm, grp)
    (mine,) = call(line_sum_kernel, "line_sum", [(VMEM, a) for a in parts], [(VMEM, parts[0].shape)])
    for bit in others:
        got = swap(mine, tm, grp, bit)
        (mine,) = call(add_kernel, "add", [(VMEM, mine), (VMEM, got)], [(VMEM, mine.shape)])
    parts = four_round([mine] * 4, line, tm, grp)
    (mine,) = call(
        line_gather_kernel, "line_gather", [(VMEM, a) for a in parts], [(VMEM, (4,) + mine.shape)]
    )
    parts = four_round([mine] * 4, plane, tm, grp)
    grad_x, down, token = call(
        functools.partial(grad_x_kernel, grp),
        "grad_x",
        [count, (VMEM, xt), (VMEM, gy), (VMEM, gs), (VMEM, cot_top), (VMEM, cot_bot), (VMEM, wt),
         (VMEM, wd), (VMEM, ws), (VMEM, down), (ANY, mine)],
        [(HBM, (slots, wide, ch)), (VMEM, cotangent.shape), TOKEN],
        [pltpu.VMEM(padded, BF), pltpu.VMEM((slots, wide, ch), BF), dma((1,))],
        flops=10 * tap,
    )
    ins = [(VMEM, a) for a in parts] + [(ANY, token)]
    (mine,) = call(plane_gather_kernel, "plane_gather", ins, [(VMEM, (16,) + mine.shape[1:])])
    got = core_round(mine, tm, grp)
    outs = finish(True, mine, [])
    sum_s, sum_t, sum_d = finish(False, got, outs)
    return (
        down,
        grad_x.reshape(frames_in.shape),
        sum_s.reshape(w_spatial.shape),
        sum_t,
        sum_d.reshape(w_down.shape),
    )


def solution(mesh):
    return jax.shard_map(
        functools.partial(body, mesh.shape["tm"], mesh.shape["grp"]),
        mesh=mesh,
        in_specs=(P("tm", "grp", None, None), P("tm"), P(), P(), P(), P("tm", "grp", None, None)),
        out_specs=(P("tm", "grp", None, None), P("tm", "grp", None, None), P(), P(), P()),
        check_vma=False,
    )
```

```python
import functools

import jax
import jax.numpy as jnp
from jax import lax
from jax.experimental import pallas as pl
from jax.experimental.pallas import tpu as pltpu
from jax.sharding import PartitionSpec as P

SLOTS = 16
OWN = 14
CH = 256
BF = jnp.bfloat16
F32 = jnp.float32


def mm(a, b):
    return lax.dot_general(a, b, (((1,), (0,)), ((), ())), preferred_element_type=F32)


def mm_nt(a, b):
    return lax.dot_general(a, b, (((1,), (1,)), ((), ())), preferred_element_type=F32)


def iotas(rows, cols):
    return (
        lax.broadcasted_iota(jnp.int32, (rows, cols), 0),
        lax.broadcasted_iota(jnp.int32, (rows, cols), 1),
    )


def to_slots(rows, frames, keep):
    a, b = iotas(rows * SLOTS, frames * rows)
    bits = rows.bit_length() - 1
    hit = ((a >> 4) == (b & (rows - 1))) & keep(b >> bits, a & 15)
    return jnp.where(hit, 1.0, 0.0).astype(BF)


def to_frames(rows):
    a, b = iotas(SLOTS * rows, rows * SLOTS)
    bits = rows.bit_length() - 1
    hit = ((a & (rows - 1)) == (b >> 4)) & ((a >> bits) == (b & 15))
    return jnp.where(hit, 1.0, 0.0).astype(BF)


def own_frames(count):
    return lambda frame, slot: (frame == slot) & (slot < count)


def own_and_next(count):
    return lambda frame, slot: ((frame < OWN) & (frame == slot) & (slot < count)) | (
        (frame >= OWN) & (slot == count + frame - OWN)
    )


def silu_norm(v):
    scaled = v * lax.rsqrt(jnp.mean(v * v, axis=-1, keepdims=True) + 1e-06)
    return scaled * (0.5 + 0.5 * jnp.tanh(0.5 * scaled))


def slot_mask(shape, count):
    return lax.broadcasted_iota(jnp.int32, shape, len(shape) - 2) < count


def grad_of_temporal(gy, wt_ref, count):
    n = gy.shape[0]
    flat = gy.reshape(n * SLOTS, CH)
    total = mm_nt(flat, wt_ref[2]).reshape(n, SLOTS, CH)
    for k in (1, 0):
        term = mm_nt(flat, wt_ref[k]).reshape(n, SLOTS, CH)
        total = total + pltpu.roll(term, SLOTS - (2 - k), 1)
    return jnp.where(slot_mask(total.shape, count), total, 0.0).astype(BF)


def place_bits():
    t, g = lax.axis_index("tm"), lax.axis_index("grp")
    return t & 1, ((t >> 1) & 1) + 2 * (g & 1), (t >> 2) & 3


def split_cores(value, keep_ref, send_ref, k):
    core, _, _ = place_bits()
    low, high = value[:, : CH // 2].astype(BF), value[:, CH // 2 :].astype(BF)
    keep_ref[:, k] = jnp.where(core == 0, low, high).reshape(16, 16, CH // 2)
    send_ref[:, k] = jnp.where(core == 0, high, low).reshape(16, 16, CH // 2)


def edges_kernel(bands, count_ref, x_ref, cot_ref, *rest):
    outs, (nxt_ref, token_ref) = rest[:-2], rest[-2:]
    nxt_ref[...] = cot_ref[0:2]
    token_ref[...] = jnp.zeros_like(token_ref)
    count = count_ref[0]
    band = lax.axis_index("grp")
    wide = x_ref.shape[1]
    if bands == 2:
        starts, lower = [jnp.where(band == 0, wide - 16, 0)], [band == 0]
    else:
        starts, lower = [wide - 16, 0], [True, False]
    place = to_slots(16, SLOTS, own_frames(count))
    for k, at in enumerate(starts):
        piece = x_ref[:, pl.ds(pl.multiple_of(at, 16), 16), :].reshape(SLOTS * 16, CH)
        v = mm(place, piece)
        v = jnp.where(lower[k], v[128:], v[:128])
        outs[k][...] = silu_norm(v).astype(BF)


def acts_kernel(count_ref, x_ref, _, xt_ref, acts_ref, at_ref):
    count = count_ref[0]
    rows, cols = xt_ref.shape[0], xt_ref.shape[1]
    edge = jnp.zeros((rows + 2, SLOTS, CH), BF)
    acts_ref[:, 0] = edge
    acts_ref[:, cols + 1] = edge
    place = to_slots(16, SLOTS, own_frames(count))

    def rows_of(q, _):
        at = pl.multiple_of(q * 16, 16)
        piece = x_ref[:, pl.ds(at, 16), :].reshape(SLOTS * 16, CH)
        v = mm(place, piece)
        xt_ref[pl.ds(2 * q, 2)] = v.astype(BF).reshape(2, cols, SLOTS, CH)
        a = silu_norm(v).astype(BF)
        acts_ref[pl.ds(2 * q + 1, 2), 1 : cols + 1] = a.reshape(2, cols, SLOTS, CH)
        flipped = a.T
        for i in range(3):
            at = pl.multiple_of((2 * q + 3 - i) * 128, 128)
            at_ref[i * CH : i * CH + CH, pl.ds(at, 256)] = flipped
        return 0

    lax.fori_loop(0, rows // 2, rows_of, 0, unroll=4)


def spatial_kernel(
    bands, count_ref, top_ref, bot_ref, acts_in, ws_ref, _, acts_ref, sp_ref, edge_ref
):
    count = count_ref[0]
    band = lax.axis_index("grp")
    rows, cols = sp_ref.shape[0], sp_ref.shape[1]
    for ref, flag, row in ((top_ref, band > 0, 0), (bot_ref, band < bands - 1, rows + 1)):
        a = jnp.where(flag, ref[...].astype(F32), 0.0)
        acts_ref[row, 1 : cols + 1] = a.astype(BF).reshape(cols, SLOTS, CH)
    a, b = iotas(32, 256)
    pick = ((a >> 1) == (b >> 4)) & ((b & 15) == count - 2 + (a & 1))
    pick = jnp.where(pick, 1.0, 0.0).astype(BF)

    def rows_of(q, _):
        left = [
            acts_ref[pl.ds(2 * q + i, 2), j : j + cols].reshape(256, CH)
            for i in range(3)
            for j in range(3)
        ]
        out = mm(jnp.concatenate(left, axis=1), ws_ref[...].reshape(9 * CH, CH)).astype(BF)
        sp_ref[pl.ds(2 * q, 2)] = out.reshape(2, cols, SLOTS, CH)
        edge_ref[q] = mm(pick, out).astype(BF)
        return 0

    lax.fori_loop(0, rows // 2, rows_of, 0)


def grad_spatial_kernel(
    bands, count_ref, at_in, top_ref, bot_ref, cot_ref, nxt_ref, wt_ref, wd_ref,
    at_ref, cott_ref, gy_ref, gs_ref, keep_ref, send_ref, *edge_refs,
):
    count = count_ref[0]
    band = lax.axis_index("grp")
    rows, cols = gy_ref.shape[0], gy_ref.shape[1]
    for ref, flag, i, row in ((top_ref, band > 0, 0, 0), (bot_ref, band < bands - 1, 2, rows + 1)):
        a = jnp.where(flag, ref[...].astype(F32), 0.0)
        at = (row - i + 2) * 128
        at_ref[i * CH : i * CH + CH, at : at + 128] = a.T.astype(BF)
    edge = jnp.zeros((rows, SLOTS, CH), BF)
    gs_ref[:, 0] = edge
    gs_ref[:, cols + 1] = edge

    place_next = to_slots(16, SLOTS, own_and_next(count))
    halves = []
    for q in range(rows * cols // 64):
        four = slice(q * 4, q * 4 + 4)
        piece = jnp.concatenate(
            [cot_ref[0:OWN, four].reshape(OWN, 16, CH), nxt_ref[:, four].reshape(2, 16, CH)], 0
        ).reshape(SLOTS * 16, CH)
        halves.append(mm(place_next, piece).astype(BF))
    placed = jnp.concatenate(halves, 0)
    cott_ref[...] = placed.reshape(rows // 2, cols // 2, SLOTS, CH)
    for i in range(2):
        for j in range(2):
            g = mm_nt(placed, wd_ref[i * 2 + j]).astype(BF).reshape(rows // 2, cols // 2, SLOTS, CH)
            for r in range(rows // 2):
                for c in range(cols // 2):
                    gy_ref[2 * r + i, 2 * c + j] = g[r, c]
    last = cott_ref[rows // 2 - 1].reshape(cols // 2 * SLOTS, CH)
    first = cott_ref[0].reshape(cols // 2 * SLOTS, CH)
    if bands == 2:
        edge_refs[0][...] = jnp.where(band == 0, last, first)
    else:
        edge_refs[0][...] = last
        edge_refs[1][...] = first

    def grads_of(q, _):
        g = gy_ref[pl.ds(8 * q, 8)].reshape(8 * cols, SLOTS, CH)
        s = grad_of_temporal(g, wt_ref, count)
        gs_ref[pl.ds(8 * q, 8), 1 : cols + 1] = s.reshape(8, cols, SLOTS, CH)
        g = jnp.where(slot_mask(g.shape, count), g.astype(F32), 0.0)
        gy_ref[pl.ds(8 * q, 8)] = g.astype(BF).reshape(8, cols, SLOTS, CH)
        return 0

    lax.fori_loop(0, rows // 8, grads_of, 0)

    wide = rows * cols * SLOTS
    for j in range(3):
        right = gs_ref[:, 2 - j : 2 - j + cols].reshape(wide, CH)
        value = mm(at_ref[:, 256 : 256 + wide], right)
        for i in range(3):
            split_cores(value[i * CH : i * CH + CH], keep_ref, send_ref, i * 3 + j)


def forward_kernel(
    count_ref, xt_ref, sp_ref, prev_ref, cott_ref, gy_ref, wt_ref, wd_ref, *rest
):
    down_ref, keep_ref, send_ref, y_ref, st_ref, yt_ref = rest[-6:]
    count = count_ref[0]
    rows, cols = xt_ref.shape[0], xt_ref.shape[1]
    a, b = iotas(256, 32)
    place = ((a >> 4) == (b >> 1)) & ((a & 15) == OWN + (b & 1))
    place = jnp.where(place, 1.0, 0.0).astype(BF)

    def rows_of(q, _):
        s = sp_ref[pl.ds(8 * q, 8)].reshape(8 * cols * SLOTS, CH).astype(F32)
        s = s + jnp.concatenate([mm(place, prev_ref[4 * q + k]) for k in range(4)], 0)
        s = s.reshape(8 * cols, SLOTS, CH)
        total = None
        for k in range(3):
            shifted = s if k == 2 else pltpu.roll(s, 2 - k, 1)
            shifted = shifted.astype(BF).reshape(8 * cols * SLOTS, CH)
            at = pl.ds(pl.multiple_of(q * 1024, 1024), 1024)
            st_ref[k * CH : k * CH + CH, at] = shifted.T
            term = mm(shifted, wt_ref[k])
            total = term if total is None else total + term
        x = xt_ref[pl.ds(8 * q, 8)].reshape(8 * cols, SLOTS, CH).astype(F32)
        y = jnp.where(slot_mask(x.shape, count), x + total.reshape(x.shape), 0.0).astype(BF)
        y_ref[pl.ds(8 * q, 8)] = y.reshape(8, cols, SLOTS, CH)
        return 0

    lax.fori_loop(0, rows // 8, rows_of, 0)

    wide = rows * cols * SLOTS
    value = mm(st_ref[...], gy_ref[...].reshape(wide, CH))
    for k in range(3):
        split_cores(value[k * CH : k * CH + CH], keep_ref, send_ref, k)

    small = wide // 4
    total = None
    for i in range(2):
        for j in range(2):
            tiles = [
                y_ref[2 * r + i, 2 * c + j] for r in range(rows // 2) for c in range(cols // 2)
            ]
            piece = jnp.concatenate(tiles, axis=0)
            k = i * 2 + j
            yt_ref[k * CH : k * CH + CH] = piece.T
            term = mm(piece, wd_ref[k])
            total = term if total is None else total + term
    down_ref[...] = total.astype(BF)
    value = mm(yt_ref[...], cott_ref[...].reshape(small, CH))
    for k in range(4):
        split_cores(value[k * CH : k * CH + CH], keep_ref, send_ref, 3 + k)


def grad_x_kernel(
    bands, count_ref, xt_ref, gy_ref, gs_ref, top_ref, bot_ref, wt_ref, wd_ref, ws_ref, slot_ref, *rest
):
    out_ref, down_ref, token_ref, pad_ref, buf, sems = rest[-6:]
    token_ref[...] = jnp.zeros_like(token_ref)
    count = count_ref[0]
    band = lax.axis_index("grp")
    rows, cols = xt_ref.shape[0], xt_ref.shape[1]
    pad_ref[1 : rows + 1] = gs_ref[...]
    edge = jnp.zeros((SLOTS, CH), BF)
    for ref, flag, i, row in ((top_ref, band > 0, 1, 0), (bot_ref, band < bands - 1, 0, rows + 1)):
        pair = [
            mm_nt(ref[...], wd_ref[i * 2 + j]).astype(BF).reshape(cols // 2, SLOTS, CH)
            for j in range(2)
        ]
        g = jnp.stack(pair, axis=1).reshape(cols, SLOTS, CH)
        pad_ref[row, 0] = edge
        pad_ref[row, 1 : cols + 1] = grad_of_temporal(g, wt_ref, jnp.where(flag, count, 0))
        pad_ref[row, cols + 1] = edge
    back = to_frames(16)

    def rows_of(q, _):
        total = None
        for i in range(3):
            for j in range(3):
                left = pad_ref[pl.ds(4 * q + 2 - i, 4), 2 - j : 2 - j + cols].reshape(
                    4 * cols * SLOTS, CH
                )
                term = mm_nt(left, ws_ref[i * 3 + j])
                total = term if total is None else total + term
        at = 4 * q
        v = xt_ref[pl.ds(at, 4)].reshape(4 * cols * SLOTS, CH).astype(F32)
        r = lax.rsqrt(jnp.mean(v * v, axis=-1, keepdims=True) + 1e-06)
        u = v * r
        s = 0.5 + 0.5 * jnp.tanh(0.5 * u)
        gu = total * (s * (1.0 + u * (1.0 - s)))
        dot = jnp.mean(gu * u, axis=-1, keepdims=True)
        gv = r * (gu - u * dot)
        gx = gy_ref[pl.ds(at, 4)].reshape(4 * cols * SLOTS, CH).astype(F32) + gv
        gx = gx.reshape(4 * cols, SLOTS, CH)
        gx = jnp.where(slot_mask(gx.shape, count), gx, 0.0).astype(BF).reshape(4 * cols * SLOTS, CH)
        for k in range(2):
            o = mm(back, gx[k * 256 : k * 256 + 256]).astype(BF)
            buf[:, pl.ds(pl.multiple_of((2 * q + k) * 16, 16), 16), :] = o.reshape(SLOTS, 16, CH)
        return 0

    lax.fori_loop(0, rows // 4, rows_of, 0)
    copy = pltpu.make_async_copy(buf, out_ref, sems.at[0])
    copy.start()
    for q in range(down_ref.shape[1] // 4):
        o = mm(back, slot_ref[q * 256 : q * 256 + 256]).astype(BF)
        down_ref[:, q * 4 : q * 4 + 4] = o.reshape(SLOTS, 4, cols // 2, CH)
    copy.wait()


ORDER = (0, 3, 2, 1)


def plane_send_kernel(keep_ref, got_ref, *rest):
    _, p, _ = place_bits()
    for r, out in zip(ORDER, rest[-4:]):
        at = pl.ds((p ^ r) * 4, 4)
        out[...] = (keep_ref[at].astype(F32) + got_ref[at].astype(F32)).astype(BF)


def line_send_kernel(*refs):
    outs = refs[8:]
    _, _, z = place_bits()
    for out, r in zip(outs, ORDER):
        at = 0
        for chain in (refs[:4], refs[4:8]):
            parts = [ref[z ^ r].astype(F32) for ref in chain]
            n = parts[0].shape[0]
            out[at : at + n] = (parts[0] + parts[1] + parts[2] + parts[3]).astype(BF)
            at += n


def line_sum_kernel(a_ref, b_ref, c_ref, d_ref, *rest):
    out_ref = rest[-1]
    parts = [ref[...].astype(F32) for ref in (a_ref, b_ref, c_ref, d_ref)]
    out_ref[...] = (parts[0] + parts[1] + parts[2] + parts[3]).astype(BF)


def line_gather_kernel(a_ref, b_ref, c_ref, d_ref, out_ref):
    _, _, z = place_bits()
    for r, ref in zip(ORDER, (a_ref, b_ref, c_ref, d_ref)):
        out_ref[z ^ r] = ref[...]


def plane_gather_kernel(a_ref, b_ref, c_ref, d_ref, _, out_ref):
    _, p, _ = place_bits()
    for r, ref in zip(ORDER, (a_ref, b_ref, c_ref, d_ref)):
        out_ref[pl.ds((p ^ r) * 4, 4)] = ref[...]


def add_kernel(a_ref, b_ref, out_ref):
    out_ref[...] = (a_ref[...].astype(F32) + b_ref[...].astype(F32)).astype(BF)


def pass_kernel(*_):
    pass


def finish_kernel(own, half_ref, *rest):
    buf, sems = rest[-2:]
    outs = rest[-5:-2]
    core, _, _ = place_bits()
    at = pl.multiple_of((core if own else 1 - core) * (CH // 2), CH // 2)
    copies = []
    k = 0
    for out in outs:
        for m in range(out.shape[0]):
            buf[k] = half_ref[:, k].reshape(CH, CH // 2).astype(F32)
            copies.append(
                pltpu.make_async_copy(buf.at[k], out.at[m, :, pl.ds(at, CH // 2)], sems.at[k])
            )
            copies[-1].start()
            k += 1
    for copy in copies:
        copy.wait()


VMEM = pl.BlockSpec(memory_space=pltpu.VMEM)
SMEM = pl.BlockSpec(memory_space=pltpu.SMEM)
ANY = pl.BlockSpec(memory_space=pl.ANY)
HBM = pl.BlockSpec(memory_space=pltpu.HBM)
TOKEN = (VMEM, (8, 128), F32)


def call(kernel, name, ins, outs, scratch=(), flops=0, alias=None, grant=10):
    shapes = [jax.ShapeDtypeStruct(o[1], o[2] if len(o) > 2 else BF) for o in outs]
    moved = sum(a.size * a.dtype.itemsize for s, a in ins if s is not ANY)
    moved += sum(s.size * s.dtype.itemsize for s in shapes)
    return pl.pallas_call(
        kernel,
        out_shape=shapes,
        in_specs=[s for s, _ in ins],
        out_specs=[o[0] for o in outs],
        scratch_shapes=list(scratch),
        compiler_params=pltpu.CompilerParams(vmem_limit_bytes=grant * 2**20),
        cost_estimate=pl.CostEstimate(flops=flops, bytes_accessed=moved, transcendentals=0),
        input_output_aliases=alias or {},
        name=name,
    )(*[a for _, a in ins])


AXES = ("tm", "grp")


def plan(tm, grp):
    low, total = grp.bit_length() - 1, (tm * grp).bit_length() - 1
    plane, line = [low + 1, 0], [low + 2, low + 3]
    return low, plane, line, [b for b in range(total) if b not in [low] + plane + line]


def swap(value, tm, grp, *bits):
    flip = sum(1 << b for b in bits)
    return lax.ppermute(value, AXES, [(d, d ^ flip) for d in range(tm * grp)])


def core_round(value, tm, grp):
    return swap(value, tm, grp, plan(tm, grp)[0])


def four_round(parts, bits, tm, grp):
    return [
        parts[0],
        swap(parts[1], tm, grp, *bits),
        swap(parts[2], tm, grp, bits[1]),
        swap(parts[3], tm, grp, bits[0]),
    ]


def plane_send(keep, got, after):
    ins = [(VMEM, keep), (VMEM, got)] + [(ANY, a) for a in after]
    shape = (4, keep.shape[1], 16, CH // 2)
    return list(call(plane_send_kernel, "plane_send", ins, [(VMEM, shape)] * 4))


def passed(value, after):
    ins = [(ANY, value)] + [(ANY, a) for a in after]
    return call(pass_kernel, "pass", ins, [(ANY, value.shape)], alias={0: 0})[0]


def finish(own, half, before):
    n = half.shape[1]
    return list(
        call(
            functools.partial(finish_kernel, own),
            "finish",
            [(VMEM, half)] + [(HBM, a) for a in before],
            [(HBM, (m, CH, CH), F32) for m in (9, 3, 4)],
            [pltpu.VMEM((n, CH, CH // 2), F32), pltpu.SemaphoreType.DMA((n,))],
            alias={1 + i: i for i in range(len(before))},
        )
    )


def along(value, axis, by):
    count = lax.axis_size(axis)
    pairs = [(i, i + by) for i in range(count) if 0 <= i + by < count]
    return lax.ppermute(value, axis, pairs)


def from_bands(parts):
    if len(parts) == 1:
        got = lax.ppermute(parts[0], "grp", [(0, 1), (1, 0)])
        return got, got
    return along(parts[0], "grp", 1), along(parts[1], "grp", -1)


def body(tm, grp, frames_in, span_frames, w_spatial, w_temporal, w_down, cotangent):
    slots, rows, cols, ch = frames_in.shape
    wide = rows * cols
    x = frames_in.reshape(slots, wide, ch)
    ws = w_spatial.reshape(9, ch, ch)
    wd = w_down.reshape(4, ch, ch)
    wt = w_temporal
    count = (SMEM, span_frames)
    tap = 2 * slots * wide * ch * ch
    tile = (rows, cols, slots, ch)
    padded = (rows + 2, cols + 2, slots, ch)
    dma = pltpu.SemaphoreType.DMA

    sides = 1 if grp == 2 else 2
    *edge, nxt, token = call(
        functools.partial(edges_kernel, grp),
        "edges",
        [count, (VMEM, x), (VMEM, cotangent)],
        [(VMEM, (cols * slots, ch))] * sides + [(VMEM, (2,) + cotangent.shape[1:]), TOKEN],
        flops=tap // 8,
    )
    top, bot = from_bands(edge)
    nxt_got = along(nxt, "tm", -1)
    xt, acts, at = call(
        acts_kernel,
        "acts",
        [count, (VMEM, x), (ANY, token)],
        [(VMEM, tile), (VMEM, padded), (VMEM, (3 * ch, (rows + 4) * 128))],
        flops=2 * tap,
    )
    half = (16, 9, 16, ch // 2)
    at, cott, gy, gs, keep_a, send_a, *edge = call(
        functools.partial(grad_spatial_kernel, grp),
        "grad_spatial",
        [count, (VMEM, at), (VMEM, top), (VMEM, bot), (VMEM, cotangent), (VMEM, nxt_got), (VMEM, wt), (VMEM, wd)],
        [(VMEM, at.shape), (VMEM, (rows // 2, cols // 2, slots, ch)), (VMEM, tile),
         (VMEM, (rows, cols + 2, slots, ch)), (VMEM, half), (VMEM, half)]
        + [(VMEM, (cols // 2 * slots, ch))] * sides,
        flops=14 * tap,
        alias={1: 0},
    )
    got_a = core_round(send_a, tm, grp)
    cot_top, cot_bot = from_bands(edge)
    acts, sp, last_two = call(
        functools.partial(spatial_kernel, grp),
        "spatial",
        [count, (VMEM, top), (VMEM, bot), (VMEM, acts), (VMEM, ws), (ANY, send_a)],
        [(VMEM, padded), (VMEM, tile), (VMEM, (rows // 2, 32, ch))],
        flops=9 * tap,
        alias={3: 0},
    )
    prev = along(last_two, "tm", 1)
    _, plane, line, others = plan(tm, grp)
    parts_a = plane_send(keep_a, got_a, [last_two])
    half = (16, 7, 16, ch // 2)
    down, keep_b, send_b = call(
        forward_kernel,
        "forward",
        [count, (VMEM, xt), (VMEM, sp), (VMEM, prev), (VMEM, cott), (VMEM, gy), (VMEM, wt), (VMEM, wd),
         *((ANY, a) for a in parts_a)],
        [(VMEM, (slots * wide // 4, ch)), (VMEM, half), (VMEM, half)],
        [pltpu.VMEM(v, BF) for v in (tile, (3 * ch, slots * wide), (4 * ch, slots * wide // 4))],
        flops=10 * tap,
        grant=14,
    )
    parts_a = four_round(parts_a, plane, tm, grp)
    send_b = passed(send_b, parts_a[1:2])
    parts_b = plane_send(keep_b, core_round(send_b, tm, grp), [])
    parts_b = four_round(parts_b, plane, tm, grp)
    parts = call(
        line_send_kernel,
        "line_send",
        [(VMEM, a) for a in parts_a + parts_b],
        [(VMEM, (16, 16, ch // 2))] * 4,
    )
    parts = four_round(list(parts), line, tm, grp)
    ins = [(VMEM, a) for a in parts] + [(ANY, a) for a in [cot_top, cot_bot][:sides]]
    (mine,) = call(line_sum_kernel, "line_sum", ins, [(VMEM, parts[0].shape)])
    for bit in others:
        got = swap(mine, tm, grp, bit)
        (mine,) = call(add_kernel, "add", [(VMEM, mine), (VMEM, got)], [(VMEM, mine.shape)])
    parts = four_round([mine] * 4, line, tm, grp)
    (mine,) = call(
        line_gather_kernel, "line_gather", [(VMEM, a) for a in parts], [(VMEM, (4,) + mine.shape)]
    )
    parts = four_round([mine] * 4, plane, tm, grp)
    grad_x, down, token = call(
        functools.partial(grad_x_kernel, grp),
        "grad_x",
        [count, (VMEM, xt), (VMEM, gy), (VMEM, gs), (VMEM, cot_top), (VMEM, cot_bot), (VMEM, wt),
         (VMEM, wd), (VMEM, ws), (VMEM, down), (ANY, mine)],
        [(HBM, (slots, wide, ch)), (VMEM, cotangent.shape), TOKEN],
        [pltpu.VMEM(padded, BF), pltpu.VMEM((slots, wide, ch), BF), dma((1,))],
        flops=10 * tap,
    )
    ins = [(VMEM, a) for a in parts] + [(ANY, token)]
    (mine,) = call(plane_gather_kernel, "plane_gather", ins, [(VMEM, (16,) + mine.shape[1:])])
    got = core_round(mine, tm, grp)
    outs = finish(True, mine, [])
    sum_s, sum_t, sum_d = finish(False, got, outs)
    return (
        down,
        grad_x.reshape(frames_in.shape),
        sum_s.reshape(w_spatial.shape),
        sum_t,
        sum_d.reshape(w_down.shape),
    )


def solution(mesh):
    return jax.shard_map(
        functools.partial(body, mesh.shape["tm"], mesh.shape["grp"]),
        mesh=mesh,
        in_specs=(P("tm", "grp", None, None), P("tm"), P(), P(), P(), P("tm", "grp", None, None)),
        out_specs=(P("tm", "grp", None, None), P("tm", "grp", None, None), P(), P(), P()),
        check_vma=False,
    )
```

```python
import functools

import jax
import jax.numpy as jnp
from jax import lax
from jax.experimental import pallas as pl
from jax.experimental.pallas import tpu as pltpu
from jax.sharding import PartitionSpec as P

SLOTS = 16
OWN = 14
CH = 256
BF = jnp.bfloat16
F32 = jnp.float32


def mm(a, b):
    return lax.dot_general(a, b, (((1,), (0,)), ((), ())), preferred_element_type=F32)


def mm_nt(a, b):
    return lax.dot_general(a, b, (((1,), (1,)), ((), ())), preferred_element_type=F32)


def iotas(rows, cols):
    return (
        lax.broadcasted_iota(jnp.int32, (rows, cols), 0),
        lax.broadcasted_iota(jnp.int32, (rows, cols), 1),
    )


def to_slots(rows, frames, keep):
    a, b = iotas(rows * SLOTS, frames * rows)
    bits = rows.bit_length() - 1
    hit = ((a >> 4) == (b & (rows - 1))) & keep(b >> bits, a & 15)
    return jnp.where(hit, 1.0, 0.0).astype(BF)


def to_frames(rows):
    a, b = iotas(SLOTS * rows, rows * SLOTS)
    bits = rows.bit_length() - 1
    hit = ((a & (rows - 1)) == (b >> 4)) & ((a >> bits) == (b & 15))
    return jnp.where(hit, 1.0, 0.0).astype(BF)


def own_frames(count):
    return lambda frame, slot: (frame == slot) & (slot < count)


def own_and_next(count):
    return lambda frame, slot: ((frame < OWN) & (frame == slot) & (slot < count)) | (
        (frame >= OWN) & (slot == count + frame - OWN)
    )


def silu_norm(v):
    scaled = v * lax.rsqrt(jnp.mean(v * v, axis=-1, keepdims=True) + 1e-06)
    return scaled * (0.5 + 0.5 * jnp.tanh(0.5 * scaled))


def slot_mask(shape, count):
    return lax.broadcasted_iota(jnp.int32, shape, len(shape) - 2) < count


def grad_of_temporal(gy, wt_ref, count):
    n = gy.shape[0]
    flat = gy.reshape(n * SLOTS, CH)
    total = mm_nt(flat, wt_ref[2]).reshape(n, SLOTS, CH)
    for k in (1, 0):
        term = mm_nt(flat, wt_ref[k]).reshape(n, SLOTS, CH)
        total = total + pltpu.roll(term, SLOTS - (2 - k), 1)
    return jnp.where(slot_mask(total.shape, count), total, 0.0).astype(BF)


def place_bits():
    t, g = lax.axis_index("tm"), lax.axis_index("grp")
    return t & 1, ((t >> 1) & 1) + 2 * (g & 1), (t >> 2) & 3


def split_cores(value, keep_ref, send_ref, k):
    core, _, _ = place_bits()
    low, high = value[:, : CH // 2].astype(BF), value[:, CH // 2 :].astype(BF)
    keep_ref[:, k] = jnp.where(core == 0, low, high).reshape(16, 16, CH // 2)
    send_ref[:, k] = jnp.where(core == 0, high, low).reshape(16, 16, CH // 2)


def edges_kernel(bands, count_ref, x_ref, cot_ref, *rest):
    outs, nxt_ref = rest[:-1], rest[-1]
    nxt_ref[...] = cot_ref[0:2]
    count = count_ref[0]
    band = lax.axis_index("grp")
    wide = x_ref.shape[1]
    if bands == 2:
        starts, lower = [jnp.where(band == 0, wide - 16, 0)], [band == 0]
    else:
        starts, lower = [wide - 16, 0], [True, False]
    place = to_slots(16, SLOTS, own_frames(count))
    for k, at in enumerate(starts):
        piece = x_ref[:, pl.ds(pl.multiple_of(at, 16), 16), :].reshape(SLOTS * 16, CH)
        v = mm(place, piece)
        v = jnp.where(lower[k], v[128:], v[:128])
        outs[k][...] = silu_norm(v).astype(BF)


def acts_kernel(bands, count_ref, x_ref, top_ref, bot_ref, xt_ref, acts_ref, at_ref, last_ref):
    count = count_ref[0]
    band = lax.axis_index("grp")
    rows, cols = xt_ref.shape[0], xt_ref.shape[1]
    edge = jnp.zeros((rows + 2, SLOTS, CH), BF)
    acts_ref[:, 0] = edge
    acts_ref[:, cols + 1] = edge
    place = to_slots(16, SLOTS, own_frames(count))
    a, b = iotas(32, 256)
    pick = ((a >> 1) == (b >> 4)) & ((b & 15) == count - 2 + (a & 1))
    pick = jnp.where(pick, 1.0, 0.0).astype(BF)

    def rows_of(q, _):
        at = pl.multiple_of(q * 16, 16)
        piece = x_ref[:, pl.ds(at, 16), :].reshape(SLOTS * 16, CH)
        v = mm(place, piece)
        xt_ref[pl.ds(2 * q, 2)] = v.astype(BF).reshape(2, cols, SLOTS, CH)
        a = silu_norm(v).astype(BF)
        last_ref[q] = mm(pick, a).astype(BF)
        acts_ref[pl.ds(2 * q + 1, 2), 1 : cols + 1] = a.reshape(2, cols, SLOTS, CH)
        flipped = a.T
        for i in range(3):
            at = pl.multiple_of((2 * q + 3 - i) * 128, 128)
            at_ref[i * CH : i * CH + CH, pl.ds(at, 256)] = flipped
        return 0

    lax.fori_loop(0, rows // 2, rows_of, 0, unroll=4)
    halo = []
    for ref, flag, i, row in ((top_ref, band > 0, 0, 0), (bot_ref, band < bands - 1, 2, rows + 1)):
        a = jnp.where(flag, ref[...].astype(F32), 0.0).astype(BF)
        acts_ref[row, 1 : cols + 1] = a.reshape(cols, SLOTS, CH)
        at = (row - i + 2) * 128
        at_ref[i * CH : i * CH + CH, at : at + 128] = a.T
        halo.append(a)
    last_ref[rows // 2] = mm(pick, jnp.concatenate(halo, 0)).astype(BF)


def spatial_kernel(count_ref, acts_in, prev_ref, ws_ref, _, acts_ref, sp_ref):
    rows, cols = sp_ref.shape[0], sp_ref.shape[1]
    a, b = iotas(256, 32)
    place = ((a >> 4) == (b >> 1)) & ((a & 15) == OWN + (b & 1))
    place = jnp.where(place, 1.0, 0.0).astype(BF)
    for q in range(rows // 2 + 1):
        both = slice(0, rows + 2, rows + 1) if q == rows // 2 else slice(2 * q + 1, 2 * q + 3)
        prev = mm(place, prev_ref[q]).astype(BF).reshape(2, cols, SLOTS, CH)
        for k, row in enumerate(range(rows + 2)[both]):
            acts_ref[row, 1 : cols + 1] = acts_ref[row, 1 : cols + 1] + prev[k]

    def rows_of(q, _):
        total = None
        for i in range(3):
            for j in range(3):
                left = acts_ref[pl.ds(4 * q + i, 4), j : j + cols].reshape(4 * cols * SLOTS, CH)
                term = mm(left, ws_ref[i * 3 + j])
                total = term if total is None else total + term
        sp_ref[pl.ds(4 * q, 4)] = total.astype(BF).reshape(4, cols, SLOTS, CH)
        return 0

    lax.fori_loop(0, rows // 4, rows_of, 0)


def grad_spatial_kernel(
    bands, count_ref, at_ref, cot_ref, nxt_ref, wt_ref, wd_ref,
    cott_ref, gy_ref, gs_ref, keep_ref, send_ref, *edge_refs,
):
    count = count_ref[0]
    band = lax.axis_index("grp")
    rows, cols = gy_ref.shape[0], gy_ref.shape[1]
    edge = jnp.zeros((rows, SLOTS, CH), BF)
    gs_ref[:, 0] = edge
    gs_ref[:, cols + 1] = edge

    place_next = to_slots(16, SLOTS, own_and_next(count))
    halves = []
    for q in range(rows * cols // 64):
        four = slice(q * 4, q * 4 + 4)
        piece = jnp.concatenate(
            [cot_ref[0:OWN, four].reshape(OWN, 16, CH), nxt_ref[:, four].reshape(2, 16, CH)], 0
        ).reshape(SLOTS * 16, CH)
        halves.append(mm(place_next, piece).astype(BF))
    placed = jnp.concatenate(halves, 0)
    cott_ref[...] = placed.reshape(rows // 2, cols // 2, SLOTS, CH)
    for i in range(2):
        for j in range(2):
            g = mm_nt(placed, wd_ref[i * 2 + j]).astype(BF).reshape(rows // 2, cols // 2, SLOTS, CH)
            for r in range(rows // 2):
                for c in range(cols // 2):
                    gy_ref[2 * r + i, 2 * c + j] = g[r, c]
    last = cott_ref[rows // 2 - 1].reshape(cols // 2 * SLOTS, CH)
    first = cott_ref[0].reshape(cols // 2 * SLOTS, CH)
    if bands == 2:
        edge_refs[0][...] = jnp.where(band == 0, last, first)
    else:
        edge_refs[0][...] = last
        edge_refs[1][...] = first

    def grads_of(q, _):
        g = gy_ref[pl.ds(8 * q, 8)].reshape(8 * cols, SLOTS, CH)
        s = grad_of_temporal(g, wt_ref, count)
        gs_ref[pl.ds(8 * q, 8), 1 : cols + 1] = s.reshape(8, cols, SLOTS, CH)
        g = jnp.where(slot_mask(g.shape, count), g.astype(F32), 0.0)
        gy_ref[pl.ds(8 * q, 8)] = g.astype(BF).reshape(8, cols, SLOTS, CH)
        return 0

    lax.fori_loop(0, rows // 8, grads_of, 0)

    wide = rows * cols * SLOTS
    for j in range(3):
        right = gs_ref[:, 2 - j : 2 - j + cols].reshape(wide, CH)
        value = mm(at_ref[:, 256 : 256 + wide], right)
        for i in range(3):
            split_cores(value[i * CH : i * CH + CH], keep_ref, send_ref, i * 3 + j)


def forward_kernel(
    count_ref, xt_ref, sp_ref, cott_ref, gy_ref, wt_ref, wd_ref, *rest
):
    down_ref, keep_ref, send_ref, y_ref, st_ref, yt_ref = rest[-6:]
    count = count_ref[0]
    rows, cols = xt_ref.shape[0], xt_ref.shape[1]
    def rows_of(q, _):
        s = sp_ref[pl.ds(8 * q, 8)].reshape(8 * cols * SLOTS, CH).astype(F32)
        s = s.reshape(8 * cols, SLOTS, CH)
        total = None
        for k in range(3):
            shifted = s if k == 2 else pltpu.roll(s, 2 - k, 1)
            shifted = shifted.astype(BF).reshape(8 * cols * SLOTS, CH)
            at = pl.ds(pl.multiple_of(q * 1024, 1024), 1024)
            st_ref[k * CH : k * CH + CH, at] = shifted.T
            term = mm(shifted, wt_ref[k])
            total = term if total is None else total + term
        x = xt_ref[pl.ds(8 * q, 8)].reshape(8 * cols, SLOTS, CH).astype(F32)
        y = jnp.where(slot_mask(x.shape, count), x + total.reshape(x.shape), 0.0).astype(BF)
        y_ref[pl.ds(8 * q, 8)] = y.reshape(8, cols, SLOTS, CH)
        return 0

    lax.fori_loop(0, rows // 8, rows_of, 0)

    wide = rows * cols * SLOTS
    value = mm(st_ref[...], gy_ref[...].reshape(wide, CH))
    for k in range(3):
        split_cores(value[k * CH : k * CH + CH], keep_ref, send_ref, k)

    small = wide // 4
    total = None
    for i in range(2):
        for j in range(2):
            tiles = [
                y_ref[2 * r + i, 2 * c + j] for r in range(rows // 2) for c in range(cols // 2)
            ]
            piece = jnp.concatenate(tiles, axis=0)
            k = i * 2 + j
            yt_ref[k * CH : k * CH + CH] = piece.T
            term = mm(piece, wd_ref[k])
            total = term if total is None else total + term
    down_ref[...] = total.astype(BF)
    value = mm(yt_ref[...], cott_ref[...].reshape(small, CH))
    for k in range(4):
        split_cores(value[k * CH : k * CH + CH], keep_ref, send_ref, 3 + k)


def grad_x_kernel(
    bands, count_ref, xt_ref, gy_ref, gs_ref, top_ref, bot_ref, wt_ref, wd_ref, ws_ref, slot_ref, *rest
):
    out_ref, down_ref, token_ref, pad_ref, buf, sems = rest[-6:]
    token_ref[...] = jnp.zeros_like(token_ref)
    count = count_ref[0]
    band = lax.axis_index("grp")
    rows, cols = xt_ref.shape[0], xt_ref.shape[1]
    pad_ref[1 : rows + 1] = gs_ref[...]
    edge = jnp.zeros((SLOTS, CH), BF)
    for ref, flag, i, row in ((top_ref, band > 0, 1, 0), (bot_ref, band < bands - 1, 0, rows + 1)):
        pair = [
            mm_nt(ref[...], wd_ref[i * 2 + j]).astype(BF).reshape(cols // 2, SLOTS, CH)
            for j in range(2)
        ]
        g = jnp.stack(pair, axis=1).reshape(cols, SLOTS, CH)
        pad_ref[row, 0] = edge
        pad_ref[row, 1 : cols + 1] = grad_of_temporal(g, wt_ref, jnp.where(flag, count, 0))
        pad_ref[row, cols + 1] = edge
    back = to_frames(16)

    def rows_of(q, _):
        total = None
        for i in range(3):
            for j in range(3):
                left = pad_ref[pl.ds(4 * q + 2 - i, 4), 2 - j : 2 - j + cols].reshape(
                    4 * cols * SLOTS, CH
                )
                term = mm_nt(left, ws_ref[i * 3 + j])
                total = term if total is None else total + term
        at = 4 * q
        v = xt_ref[pl.ds(at, 4)].reshape(4 * cols * SLOTS, CH).astype(F32)
        r = lax.rsqrt(jnp.mean(v * v, axis=-1, keepdims=True) + 1e-06)
        u = v * r
        s = 0.5 + 0.5 * jnp.tanh(0.5 * u)
        gu = total * (s * (1.0 + u * (1.0 - s)))
        dot = jnp.mean(gu * u, axis=-1, keepdims=True)
        gv = r * (gu - u * dot)
        gx = gy_ref[pl.ds(at, 4)].reshape(4 * cols * SLOTS, CH).astype(F32) + gv
        gx = gx.reshape(4 * cols, SLOTS, CH)
        gx = jnp.where(slot_mask(gx.shape, count), gx, 0.0).astype(BF).reshape(4 * cols * SLOTS, CH)
        for k in range(2):
            o = mm(back, gx[k * 256 : k * 256 + 256]).astype(BF)
            buf[:, pl.ds(pl.multiple_of((2 * q + k) * 16, 16), 16), :] = o.reshape(SLOTS, 16, CH)
        return 0

    lax.fori_loop(0, rows // 4, rows_of, 0)
    copy = pltpu.make_async_copy(buf, out_ref, sems.at[0])
    copy.start()
    for q in range(down_ref.shape[1] // 4):
        o = mm(back, slot_ref[q * 256 : q * 256 + 256]).astype(BF)
        down_ref[:, q * 4 : q * 4 + 4] = o.reshape(SLOTS, 4, cols // 2, CH)
    copy.wait()


ORDER = (0, 3, 2, 1)


def plane_send_kernel(keep_ref, got_ref, *rest):
    _, p, _ = place_bits()
    for r, out in zip(ORDER, rest[-4:]):
        at = pl.ds((p ^ r) * 4, 4)
        out[...] = (keep_ref[at].astype(F32) + got_ref[at].astype(F32)).astype(BF)


def line_send_kernel(*refs):
    outs = refs[8:]
    _, _, z = place_bits()
    for out, r in zip(outs, ORDER):
        at = 0
        for chain in (refs[:4], refs[4:8]):
            parts = [ref[z ^ r].astype(F32) for ref in chain]
            n = parts[0].shape[0]
            out[at : at + n] = (parts[0] + parts[1] + parts[2] + parts[3]).astype(BF)
            at += n


def line_sum_kernel(a_ref, b_ref, c_ref, d_ref, *rest):
    out_ref = rest[-1]
    parts = [ref[...].astype(F32) for ref in (a_ref, b_ref, c_ref, d_ref)]
    out_ref[...] = (parts[0] + parts[1] + parts[2] + parts[3]).astype(BF)


def line_gather_kernel(a_ref, b_ref, c_ref, d_ref, out_ref):
    _, _, z = place_bits()
    for r, ref in zip(ORDER, (a_ref, b_ref, c_ref, d_ref)):
        out_ref[z ^ r] = ref[...]


def plane_gather_kernel(a_ref, b_ref, c_ref, d_ref, _, out_ref):
    _, p, _ = place_bits()
    for r, ref in zip(ORDER, (a_ref, b_ref, c_ref, d_ref)):
        out_ref[pl.ds((p ^ r) * 4, 4)] = ref[...]


def add_kernel(a_ref, b_ref, out_ref):
    out_ref[...] = (a_ref[...].astype(F32) + b_ref[...].astype(F32)).astype(BF)


def pass_kernel(*_):
    pass


def finish_kernel(own, half_ref, *rest):
    buf, sems = rest[-2:]
    outs = rest[-5:-2]
    core, _, _ = place_bits()
    at = pl.multiple_of((core if own else 1 - core) * (CH // 2), CH // 2)
    copies = []
    k = 0
    for out in outs:
        for m in range(out.shape[0]):
            buf[k] = half_ref[:, k].reshape(CH, CH // 2).astype(F32)
            copies.append(
                pltpu.make_async_copy(buf.at[k], out.at[m, :, pl.ds(at, CH // 2)], sems.at[k])
            )
            copies[-1].start()
            k += 1
    for copy in copies:
        copy.wait()


VMEM = pl.BlockSpec(memory_space=pltpu.VMEM)
SMEM = pl.BlockSpec(memory_space=pltpu.SMEM)
ANY = pl.BlockSpec(memory_space=pl.ANY)
HBM = pl.BlockSpec(memory_space=pltpu.HBM)
TOKEN = (VMEM, (8, 128), F32)


def call(kernel, name, ins, outs, scratch=(), flops=0, alias=None, grant=10):
    shapes = [jax.ShapeDtypeStruct(o[1], o[2] if len(o) > 2 else BF) for o in outs]
    moved = sum(a.size * a.dtype.itemsize for s, a in ins if s is not ANY)
    moved += sum(s.size * s.dtype.itemsize for s in shapes)
    return pl.pallas_call(
        kernel,
        out_shape=shapes,
        in_specs=[s for s, _ in ins],
        out_specs=[o[0] for o in outs],
        scratch_shapes=list(scratch),
        compiler_params=pltpu.CompilerParams(vmem_limit_bytes=grant * 2**20),
        cost_estimate=pl.CostEstimate(flops=flops, bytes_accessed=moved, transcendentals=0),
        input_output_aliases=alias or {},
        name=name,
    )(*[a for _, a in ins])


AXES = ("tm", "grp")


def plan(tm, grp):
    low, total = grp.bit_length() - 1, (tm * grp).bit_length() - 1
    plane, line = [low + 1, 0], [low + 2, low + 3]
    return low, plane, line, [b for b in range(total) if b not in [low] + plane + line]


def swap(value, tm, grp, *bits):
    flip = sum(1 << b for b in bits)
    return lax.ppermute(value, AXES, [(d, d ^ flip) for d in range(tm * grp)])


def core_round(value, tm, grp):
    return swap(value, tm, grp, plan(tm, grp)[0])


def four_round(parts, bits, tm, grp):
    return [
        parts[0],
        swap(parts[1], tm, grp, *bits),
        swap(parts[2], tm, grp, bits[1]),
        swap(parts[3], tm, grp, bits[0]),
    ]


def plane_send(keep, got, after):
    ins = [(VMEM, keep), (VMEM, got)] + [(ANY, a) for a in after]
    shape = (4, keep.shape[1], 16, CH // 2)
    return list(call(plane_send_kernel, "plane_send", ins, [(VMEM, shape)] * 4))


def passed(value, after):
    ins = [(ANY, value)] + [(ANY, a) for a in after]
    return call(pass_kernel, "pass", ins, [(ANY, value.shape)], alias={0: 0})[0]


def finish(own, half, before):
    n = half.shape[1]
    return list(
        call(
            functools.partial(finish_kernel, own),
            "finish",
            [(VMEM, half)] + [(HBM, a) for a in before],
            [(HBM, (m, CH, CH), F32) for m in (9, 3, 4)],
            [pltpu.VMEM((n, CH, CH // 2), F32), pltpu.SemaphoreType.DMA((n,))],
            alias={1 + i: i for i in range(len(before))},
        )
    )


def along(value, axis, by):
    count = lax.axis_size(axis)
    pairs = [(i, i + by) for i in range(count) if 0 <= i + by < count]
    return lax.ppermute(value, axis, pairs)


def from_bands(parts):
    if len(parts) == 1:
        got = lax.ppermute(parts[0], "grp", [(0, 1), (1, 0)])
        return got, got
    return along(parts[0], "grp", 1), along(parts[1], "grp", -1)


def body(tm, grp, frames_in, span_frames, w_spatial, w_temporal, w_down, cotangent):
    slots, rows, cols, ch = frames_in.shape
    wide = rows * cols
    x = frames_in.reshape(slots, wide, ch)
    ws = w_spatial.reshape(9, ch, ch)
    wd = w_down.reshape(4, ch, ch)
    wt = w_temporal
    count = (SMEM, span_frames)
    tap = 2 * slots * wide * ch * ch
    tile = (rows, cols, slots, ch)
    padded = (rows + 2, cols + 2, slots, ch)
    dma = pltpu.SemaphoreType.DMA

    sides = 1 if grp == 2 else 2
    *edge, nxt = call(
        functools.partial(edges_kernel, grp),
        "edges",
        [count, (VMEM, x), (VMEM, cotangent)],
        [(VMEM, (cols * slots, ch))] * sides + [(VMEM, (2,) + cotangent.shape[1:])],
        flops=tap // 8,
    )
    top, bot = from_bands(edge)
    nxt_got = along(nxt, "tm", -1)
    xt, acts, at, last_two = call(
        functools.partial(acts_kernel, grp),
        "acts",
        [count, (VMEM, x), (VMEM, top), (VMEM, bot)],
        [(VMEM, tile), (VMEM, padded), (VMEM, (3 * ch, (rows + 4) * 128)), (VMEM, (rows // 2 + 1, 32, ch))],
        flops=2 * tap,
    )
    prev = along(last_two, "tm", 1)
    half = (16, 9, 16, ch // 2)
    cott, gy, gs, keep_a, send_a, *edge = call(
        functools.partial(grad_spatial_kernel, grp),
        "grad_spatial",
        [count, (VMEM, at), (VMEM, cotangent), (VMEM, nxt_got), (VMEM, wt), (VMEM, wd)],
        [(VMEM, (rows // 2, cols // 2, slots, ch)), (VMEM, tile),
         (VMEM, (rows, cols + 2, slots, ch)), (VMEM, half), (VMEM, half)]
        + [(VMEM, (cols // 2 * slots, ch))] * sides,
        flops=14 * tap,
    )
    send_a = passed(send_a, [prev])
    got_a = core_round(send_a, tm, grp)
    cot_top, cot_bot = from_bands(edge)
    acts, sp = call(
        spatial_kernel,
        "spatial",
        [count, (VMEM, acts), (VMEM, prev), (VMEM, ws), (ANY, send_a)],
        [(VMEM, padded), (VMEM, tile)],
        flops=9 * tap,
        alias={1: 0},
    )
    _, plane, line, others = plan(tm, grp)
    parts_a = plane_send(keep_a, got_a, [sp])
    half = (16, 7, 16, ch // 2)
    down, keep_b, send_b = call(
        forward_kernel,
        "forward",
        [count, (VMEM, xt), (VMEM, sp), (VMEM, cott), (VMEM, gy), (VMEM, wt), (VMEM, wd),
         *((ANY, a) for a in parts_a)],
        [(VMEM, (slots * wide // 4, ch)), (VMEM, half), (VMEM, half)],
        [pltpu.VMEM(v, BF) for v in (tile, (3 * ch, slots * wide), (4 * ch, slots * wide // 4))],
        flops=10 * tap,
        grant=14,
    )
    parts_a = four_round(parts_a, plane, tm, grp)
    send_b = passed(send_b, parts_a[1:2])
    parts_b = plane_send(keep_b, core_round(send_b, tm, grp), [])
    parts_b = four_round(parts_b, plane, tm, grp)
    parts = call(
        line_send_kernel,
        "line_send",
        [(VMEM, a) for a in parts_a + parts_b],
        [(VMEM, (16, 16, ch // 2))] * 4,
    )
    parts = four_round(list(parts), line, tm, grp)
    ins = [(VMEM, a) for a in parts] + [(ANY, a) for a in [cot_top, cot_bot][:sides]]
    (mine,) = call(line_sum_kernel, "line_sum", ins, [(VMEM, parts[0].shape)])
    for bit in others:
        got = swap(mine, tm, grp, bit)
        (mine,) = call(add_kernel, "add", [(VMEM, mine), (VMEM, got)], [(VMEM, mine.shape)])
    parts = four_round([mine] * 4, line, tm, grp)
    (mine,) = call(
        line_gather_kernel, "line_gather", [(VMEM, a) for a in parts], [(VMEM, (4,) + mine.shape)]
    )
    parts = four_round([mine] * 4, plane, tm, grp)
    grad_x, down, token = call(
        functools.partial(grad_x_kernel, grp),
        "grad_x",
        [count, (VMEM, xt), (VMEM, gy), (VMEM, gs), (VMEM, cot_top), (VMEM, cot_bot), (VMEM, wt),
         (VMEM, wd), (VMEM, ws), (VMEM, down), (ANY, mine)],
        [(HBM, (slots, wide, ch)), (VMEM, cotangent.shape), TOKEN],
        [pltpu.VMEM(padded, BF), pltpu.VMEM((slots, wide, ch), BF), dma((1,))],
        flops=10 * tap,
    )
    ins = [(VMEM, a) for a in parts] + [(ANY, token)]
    (mine,) = call(plane_gather_kernel, "plane_gather", ins, [(VMEM, (16,) + mine.shape[1:])])
    got = core_round(mine, tm, grp)
    outs = finish(True, mine, [])
    sum_s, sum_t, sum_d = finish(False, got, outs)
    return (
        down,
        grad_x.reshape(frames_in.shape),
        sum_s.reshape(w_spatial.shape),
        sum_t,
        sum_d.reshape(w_down.shape),
    )


def solution(mesh):
    return jax.shard_map(
        functools.partial(body, mesh.shape["tm"], mesh.shape["grp"]),
        mesh=mesh,
        in_specs=(P("tm", "grp", None, None), P("tm"), P(), P(), P(), P("tm", "grp", None, None)),
        out_specs=(P("tm", "grp", None, None), P("tm", "grp", None, None), P(), P(), P()),
        check_vma=False,
    )
```

```python
import functools

import jax
import jax.numpy as jnp
from jax import lax
from jax.experimental import pallas as pl
from jax.experimental.pallas import tpu as pltpu
from jax.sharding import PartitionSpec as P

SLOTS = 16
OWN = 14
CH = 256
BF = jnp.bfloat16
F32 = jnp.float32


def mm(a, b):
    return lax.dot_general(a, b, (((1,), (0,)), ((), ())), preferred_element_type=F32)


def mm_nt(a, b):
    return lax.dot_general(a, b, (((1,), (1,)), ((), ())), preferred_element_type=F32)


def iotas(rows, cols):
    return (
        lax.broadcasted_iota(jnp.int32, (rows, cols), 0),
        lax.broadcasted_iota(jnp.int32, (rows, cols), 1),
    )


def to_slots(rows, frames, keep):
    a, b = iotas(rows * SLOTS, frames * rows)
    bits = rows.bit_length() - 1
    hit = ((a >> 4) == (b & (rows - 1))) & keep(b >> bits, a & 15)
    return jnp.where(hit, 1.0, 0.0).astype(BF)


def to_frames(rows):
    a, b = iotas(SLOTS * rows, rows * SLOTS)
    bits = rows.bit_length() - 1
    hit = ((a & (rows - 1)) == (b >> 4)) & ((a >> bits) == (b & 15))
    return jnp.where(hit, 1.0, 0.0).astype(BF)


def own_frames(count):
    return lambda frame, slot: (frame == slot) & (slot < count)


def own_and_next(count, blocks):
    after = jnp.where(lax.axis_index("tm") < blocks - 1, count, 64)
    return lambda frame, slot: ((frame < OWN) & (frame == slot) & (slot < count)) | (
        (frame >= OWN) & (slot == after + frame - OWN)
    )


def silu_norm(v):
    scaled = v * lax.rsqrt(jnp.mean(v * v, axis=-1, keepdims=True) + 1e-06)
    return scaled * (0.5 + 0.5 * jnp.tanh(0.5 * scaled))


def slot_mask(shape, count):
    return lax.broadcasted_iota(jnp.int32, shape, len(shape) - 2) < count


def grad_of_temporal(gy, wt_ref, count):
    n = gy.shape[0]
    flat = gy.reshape(n * SLOTS, CH)
    total = mm_nt(flat, wt_ref[2]).reshape(n, SLOTS, CH)
    for k in (1, 0):
        term = mm_nt(flat, wt_ref[k]).reshape(n, SLOTS, CH)
        total = total + pltpu.roll(term, SLOTS - (2 - k), 1)
    return jnp.where(slot_mask(total.shape, count), total, 0.0).astype(BF)


def place_bits():
    t, g = lax.axis_index("tm"), lax.axis_index("grp")
    return t & 1, ((t >> 1) & 1) + 2 * (g & 1), (t >> 2) & 3


def split_cores(value, keep_ref, send_ref, k):
    core, _, _ = place_bits()
    low, high = value[:, : CH // 2].astype(BF), value[:, CH // 2 :].astype(BF)
    keep_ref[:, k] = jnp.where(core == 0, low, high).reshape(16, 16, CH // 2)
    send_ref[:, k] = jnp.where(core == 0, high, low).reshape(16, 16, CH // 2)


def edges_kernel(bands, count_ref, x_ref, cot_ref, *rest):
    outs, nxt_ref = rest[:-1], rest[-1]
    nxt_ref[...] = cot_ref[0:2]
    count = count_ref[0]
    band = lax.axis_index("grp")
    wide = x_ref.shape[1]
    if bands == 2:
        starts, lower = [jnp.where(band == 0, wide - 16, 0)], [band == 0]
    else:
        starts, lower = [wide - 16, 0], [True, False]
    place = to_slots(16, SLOTS, own_frames(count))
    for k, at in enumerate(starts):
        piece = x_ref[:, pl.ds(pl.multiple_of(at, 16), 16), :].reshape(SLOTS * 16, CH)
        v = mm(place, piece)
        v = jnp.where(lower[k], v[128:], v[:128])
        outs[k][...] = silu_norm(v).astype(BF)


def acts_kernel(bands, count_ref, x_ref, top_ref, bot_ref, xt_ref, acts_ref, at_ref, last_ref):
    count = count_ref[0]
    band = lax.axis_index("grp")
    rows, cols = xt_ref.shape[0], xt_ref.shape[1]
    edge = jnp.zeros((rows + 2, SLOTS, CH), BF)
    acts_ref[:, 0] = edge
    acts_ref[:, cols + 1] = edge
    place = to_slots(16, SLOTS, own_frames(count))
    last = silu_norm(x_ref[pl.ds(count - 2, 2)].reshape(2 * rows * cols, CH).astype(F32))
    last_ref[0 : 2 * rows * cols] = last.astype(BF)

    def rows_of(q, _):
        at = pl.multiple_of(q * 16, 16)
        piece = x_ref[:, pl.ds(at, 16), :].reshape(SLOTS * 16, CH)
        v = mm(place, piece)
        xt_ref[pl.ds(2 * q, 2)] = v.astype(BF).reshape(2, cols, SLOTS, CH)
        a = silu_norm(v).astype(BF)
        acts_ref[pl.ds(2 * q + 1, 2), 1 : cols + 1] = a.reshape(2, cols, SLOTS, CH)
        flipped = a.T
        for i in range(3):
            at = pl.multiple_of((2 * q + 3 - i) * 128, 128)
            at_ref[i * CH : i * CH + CH, pl.ds(at, 256)] = flipped
        return 0

    lax.fori_loop(0, rows // 2, rows_of, 0, unroll=4)
    halo = []
    for ref, flag, i, row in ((top_ref, band > 0, 0, 0), (bot_ref, band < bands - 1, 2, rows + 1)):
        a = jnp.where(flag, ref[...].astype(F32), 0.0).astype(BF)
        acts_ref[row, 1 : cols + 1] = a.reshape(cols, SLOTS, CH)
        at = (row - i + 2) * 128
        at_ref[i * CH : i * CH + CH, at : at + 128] = a.T
        halo.append(a)
    a, b = iotas(32, 256)
    pick = ((a & 15) == (b >> 4)) & ((b & 15) == count - 2 + (a >> 4))
    pick = jnp.where(pick, 1.0, 0.0).astype(BF)
    last_ref[2 * rows * cols :] = mm(pick, jnp.concatenate(halo, 0)).astype(BF)


def spatial_kernel(count_ref, acts_in, prev_ref, ws_ref, _, acts_ref, sp_ref):
    rows, cols = sp_ref.shape[0], sp_ref.shape[1]
    a, b = iotas(256, 32)
    place = ((a >> 4) == (b & 15)) & ((a & 15) == OWN + (b >> 4)) & (lax.axis_index("tm") > 0)
    place = jnp.where(place, 1.0, 0.0).astype(BF)
    size = rows * cols
    for q in range(rows // 2 + 1):
        if q == rows // 2:
            both, prev = slice(0, rows + 2, rows + 1), prev_ref[2 * size :]
        else:
            both = slice(2 * q + 1, 2 * q + 3)
            parts = [prev_ref[f * size + q * 16 : f * size + q * 16 + 16] for f in range(2)]
            prev = jnp.concatenate(parts, 0)
        prev = mm(place, prev).astype(BF).reshape(2, cols, SLOTS, CH)
        for k, row in enumerate(range(rows + 2)[both]):
            acts_ref[row, 1 : cols + 1] = acts_ref[row, 1 : cols + 1] + prev[k]

    def rows_of(q, _):
        total = None
        for i in range(3):
            for j in range(3):
                left = acts_ref[pl.ds(4 * q + i, 4), j : j + cols].reshape(4 * cols * SLOTS, CH)
                term = mm(left, ws_ref[i * 3 + j])
                total = term if total is None else total + term
        sp_ref[pl.ds(4 * q, 4)] = total.astype(BF).reshape(4, cols, SLOTS, CH)
        return 0

    lax.fori_loop(0, rows // 4, rows_of, 0)


def grad_spatial_kernel(
    blocks, bands, count_ref, at_ref, cot_ref, nxt_ref, wt_ref, wd_ref,
    cott_ref, gy_ref, gs_ref, keep_ref, send_ref, *edge_refs,
):
    count = count_ref[0]
    band = lax.axis_index("grp")
    rows, cols = gy_ref.shape[0], gy_ref.shape[1]
    edge = jnp.zeros((rows, SLOTS, CH), BF)
    gs_ref[:, 0] = edge
    gs_ref[:, cols + 1] = edge

    place_next = to_slots(16, SLOTS, own_and_next(count, blocks))
    halves = []
    for q in range(rows * cols // 64):
        four = slice(q * 4, q * 4 + 4)
        piece = jnp.concatenate(
            [cot_ref[0:OWN, four].reshape(OWN, 16, CH), nxt_ref[:, four].reshape(2, 16, CH)], 0
        ).reshape(SLOTS * 16, CH)
        halves.append(mm(place_next, piece).astype(BF))
    placed = jnp.concatenate(halves, 0)
    cott_ref[...] = placed.reshape(rows // 2, cols // 2, SLOTS, CH)
    for i in range(2):
        for j in range(2):
            g = mm_nt(placed, wd_ref[i * 2 + j]).astype(BF).reshape(rows // 2, cols // 2, SLOTS, CH)
            for r in range(rows // 2):
                for c in range(cols // 2):
                    gy_ref[2 * r + i, 2 * c + j] = g[r, c]
    last = cott_ref[rows // 2 - 1].reshape(cols // 2 * SLOTS, CH)
    first = cott_ref[0].reshape(cols // 2 * SLOTS, CH)
    if bands == 2:
        edge_refs[0][...] = jnp.where(band == 0, last, first)
    else:
        edge_refs[0][...] = last
        edge_refs[1][...] = first

    def grads_of(q, _):
        g = gy_ref[pl.ds(8 * q, 8)].reshape(8 * cols, SLOTS, CH)
        s = grad_of_temporal(g, wt_ref, count)
        gs_ref[pl.ds(8 * q, 8), 1 : cols + 1] = s.reshape(8, cols, SLOTS, CH)
        g = jnp.where(slot_mask(g.shape, count), g.astype(F32), 0.0)
        gy_ref[pl.ds(8 * q, 8)] = g.astype(BF).reshape(8, cols, SLOTS, CH)
        return 0

    lax.fori_loop(0, rows // 8, grads_of, 0)

    wide = rows * cols * SLOTS
    for j in range(3):
        right = gs_ref[:, 2 - j : 2 - j + cols].reshape(wide, CH)
        value = mm(at_ref[:, 256 : 256 + wide], right)
        for i in range(3):
            split_cores(value[i * CH : i * CH + CH], keep_ref, send_ref, i * 3 + j)


def forward_kernel(
    count_ref, xt_ref, sp_ref, cott_ref, gy_ref, wt_ref, wd_ref, *rest
):
    down_ref, keep_ref, send_ref, y_ref, st_ref, yt_ref = rest[-6:]
    count = count_ref[0]
    rows, cols = xt_ref.shape[0], xt_ref.shape[1]
    def rows_of(q, _):
        s = sp_ref[pl.ds(8 * q, 8)].reshape(8 * cols * SLOTS, CH).astype(F32)
        s = s.reshape(8 * cols, SLOTS, CH)
        total = None
        for k in range(3):
            shifted = s if k == 2 else pltpu.roll(s, 2 - k, 1)
            shifted = shifted.astype(BF).reshape(8 * cols * SLOTS, CH)
            at = pl.ds(pl.multiple_of(q * 1024, 1024), 1024)
            st_ref[k * CH : k * CH + CH, at] = shifted.T
            term = mm(shifted, wt_ref[k])
            total = term if total is None else total + term
        x = xt_ref[pl.ds(8 * q, 8)].reshape(8 * cols, SLOTS, CH).astype(F32)
        y = jnp.where(slot_mask(x.shape, count), x + total.reshape(x.shape), 0.0).astype(BF)
        y_ref[pl.ds(8 * q, 8)] = y.reshape(8, cols, SLOTS, CH)
        return 0

    lax.fori_loop(0, rows // 8, rows_of, 0)

    wide = rows * cols * SLOTS
    value = mm(st_ref[...], gy_ref[...].reshape(wide, CH))
    for k in range(3):
        split_cores(value[k * CH : k * CH + CH], keep_ref, send_ref, k)

    small = wide // 4
    total = None
    for i in range(2):
        for j in range(2):
            tiles = [
                y_ref[2 * r + i, 2 * c + j] for r in range(rows // 2) for c in range(cols // 2)
            ]
            piece = jnp.concatenate(tiles, axis=0)
            k = i * 2 + j
            yt_ref[k * CH : k * CH + CH] = piece.T
            term = mm(piece, wd_ref[k])
            total = term if total is None else total + term
    down_ref[...] = total.astype(BF)
    value = mm(yt_ref[...], cott_ref[...].reshape(small, CH))
    for k in range(4):
        split_cores(value[k * CH : k * CH + CH], keep_ref, send_ref, 3 + k)


def grad_x_kernel(
    bands, count_ref, xt_ref, gy_ref, gs_ref, top_ref, bot_ref, wt_ref, wd_ref, ws_ref, slot_ref, *rest
):
    out_ref, down_ref, token_ref, pad_ref, buf, sems = rest[-6:]
    token_ref[...] = jnp.zeros_like(token_ref)
    count = count_ref[0]
    band = lax.axis_index("grp")
    rows, cols = xt_ref.shape[0], xt_ref.shape[1]
    pad_ref[1 : rows + 1] = gs_ref[...]
    edge = jnp.zeros((SLOTS, CH), BF)
    for ref, flag, i, row in ((top_ref, band > 0, 1, 0), (bot_ref, band < bands - 1, 0, rows + 1)):
        pair = [
            mm_nt(ref[...], wd_ref[i * 2 + j]).astype(BF).reshape(cols // 2, SLOTS, CH)
            for j in range(2)
        ]
        g = jnp.stack(pair, axis=1).reshape(cols, SLOTS, CH)
        pad_ref[row, 0] = edge
        pad_ref[row, 1 : cols + 1] = grad_of_temporal(g, wt_ref, jnp.where(flag, count, 0))
        pad_ref[row, cols + 1] = edge
    back = to_frames(16)

    def rows_of(q, _):
        total = None
        for i in range(3):
            for j in range(3):
                left = pad_ref[pl.ds(4 * q + 2 - i, 4), 2 - j : 2 - j + cols].reshape(
                    4 * cols * SLOTS, CH
                )
                term = mm_nt(left, ws_ref[i * 3 + j])
                total = term if total is None else total + term
        at = 4 * q
        v = xt_ref[pl.ds(at, 4)].reshape(4 * cols * SLOTS, CH).astype(F32)
        r = lax.rsqrt(jnp.mean(v * v, axis=-1, keepdims=True) + 1e-06)
        u = v * r
        s = 0.5 + 0.5 * jnp.tanh(0.5 * u)
        gu = total * (s * (1.0 + u * (1.0 - s)))
        dot = jnp.mean(gu * u, axis=-1, keepdims=True)
        gv = r * (gu - u * dot)
        gx = gy_ref[pl.ds(at, 4)].reshape(4 * cols * SLOTS, CH).astype(F32) + gv
        gx = gx.reshape(4 * cols, SLOTS, CH)
        gx = jnp.where(slot_mask(gx.shape, count), gx, 0.0).astype(BF).reshape(4 * cols * SLOTS, CH)
        for k in range(2):
            o = mm(back, gx[k * 256 : k * 256 + 256]).astype(BF)
            buf[:, pl.ds(pl.multiple_of((2 * q + k) * 16, 16), 16), :] = o.reshape(SLOTS, 16, CH)
        return 0

    lax.fori_loop(0, rows // 4, rows_of, 0)
    copy = pltpu.make_async_copy(buf, out_ref, sems.at[0])
    copy.start()
    for q in range(down_ref.shape[1] // 4):
        o = mm(back, slot_ref[q * 256 : q * 256 + 256]).astype(BF)
        down_ref[:, q * 4 : q * 4 + 4] = o.reshape(SLOTS, 4, cols // 2, CH)
    copy.wait()


ORDER = (0, 3, 2, 1)


def plane_send_kernel(keep_ref, got_ref, *rest):
    _, p, _ = place_bits()
    for r, out in zip(ORDER, rest[-4:]):
        at = pl.ds((p ^ r) * 4, 4)
        out[...] = (keep_ref[at].astype(F32) + got_ref[at].astype(F32)).astype(BF)


def line_send_kernel(*refs):
    outs = refs[8:]
    _, _, z = place_bits()
    for out, r in zip(outs, ORDER):
        at = 0
        for chain in (refs[:4], refs[4:8]):
            parts = [ref[z ^ r].astype(F32) for ref in chain]
            n = parts[0].shape[0]
            out[at : at + n] = (parts[0] + parts[1] + parts[2] + parts[3]).astype(BF)
            at += n


def line_sum_kernel(a_ref, b_ref, c_ref, d_ref, *rest):
    out_ref = rest[-1]
    parts = [ref[...].astype(F32) for ref in (a_ref, b_ref, c_ref, d_ref)]
    out_ref[...] = (parts[0] + parts[1] + parts[2] + parts[3]).astype(BF)


def line_gather_kernel(a_ref, b_ref, c_ref, d_ref, out_ref):
    _, _, z = place_bits()
    for r, ref in zip(ORDER, (a_ref, b_ref, c_ref, d_ref)):
        out_ref[z ^ r] = ref[...]


def plane_gather_kernel(a_ref, b_ref, c_ref, d_ref, _, out_ref):
    _, p, _ = place_bits()
    for r, ref in zip(ORDER, (a_ref, b_ref, c_ref, d_ref)):
        out_ref[pl.ds((p ^ r) * 4, 4)] = ref[...]


def add_kernel(a_ref, b_ref, out_ref):
    out_ref[...] = (a_ref[...].astype(F32) + b_ref[...].astype(F32)).astype(BF)


def pass_kernel(*_):
    pass


def finish_kernel(own, half_ref, *rest):
    buf, sems = rest[-2:]
    outs = rest[-5:-2]
    core, _, _ = place_bits()
    at = pl.multiple_of((core if own else 1 - core) * (CH // 2), CH // 2)
    copies = []
    k = 0
    for out in outs:
        for m in range(out.shape[0]):
            buf[k] = half_ref[:, k].reshape(CH, CH // 2).astype(F32)
            copies.append(
                pltpu.make_async_copy(buf.at[k], out.at[m, :, pl.ds(at, CH // 2)], sems.at[k])
            )
            copies[-1].start()
            k += 1
    for copy in copies:
        copy.wait()


VMEM = pl.BlockSpec(memory_space=pltpu.VMEM)
SMEM = pl.BlockSpec(memory_space=pltpu.SMEM)
ANY = pl.BlockSpec(memory_space=pl.ANY)
HBM = pl.BlockSpec(memory_space=pltpu.HBM)
TOKEN = (VMEM, (8, 128), F32)


def call(kernel, name, ins, outs, scratch=(), flops=0, alias=None, grant=10):
    shapes = [jax.ShapeDtypeStruct(o[1], o[2] if len(o) > 2 else BF) for o in outs]
    moved = sum(a.size * a.dtype.itemsize for s, a in ins if s is not ANY)
    moved += sum(s.size * s.dtype.itemsize for s in shapes)
    return pl.pallas_call(
        kernel,
        out_shape=shapes,
        in_specs=[s for s, _ in ins],
        out_specs=[o[0] for o in outs],
        scratch_shapes=list(scratch),
        compiler_params=pltpu.CompilerParams(vmem_limit_bytes=grant * 2**20),
        cost_estimate=pl.CostEstimate(flops=flops, bytes_accessed=moved, transcendentals=0),
        input_output_aliases=alias or {},
        name=name,
    )(*[a for _, a in ins])


AXES = ("tm", "grp")


def plan(tm, grp):
    low, total = grp.bit_length() - 1, (tm * grp).bit_length() - 1
    plane, line = [low + 1, 0], [low + 2, low + 3]
    return low, plane, line, [b for b in range(total) if b not in [low] + plane + line]


def swap(value, tm, grp, *bits):
    flip = sum(1 << b for b in bits)
    return lax.ppermute(value, AXES, [(d, d ^ flip) for d in range(tm * grp)])


def core_round(value, tm, grp):
    return swap(value, tm, grp, plan(tm, grp)[0])


def four_round(parts, bits, tm, grp):
    return [
        parts[0],
        swap(parts[1], tm, grp, *bits),
        swap(parts[2], tm, grp, bits[1]),
        swap(parts[3], tm, grp, bits[0]),
    ]


def plane_send(keep, got, after):
    ins = [(VMEM, keep), (VMEM, got)] + [(ANY, a) for a in after]
    shape = (4, keep.shape[1], 16, CH // 2)
    return list(call(plane_send_kernel, "plane_send", ins, [(VMEM, shape)] * 4))


def passed(value, after):
    ins = [(ANY, value)] + [(ANY, a) for a in after]
    return call(pass_kernel, "pass", ins, [(ANY, value.shape)], alias={0: 0})[0]


def finish(own, half, before):
    n = half.shape[1]
    return list(
        call(
            functools.partial(finish_kernel, own),
            "finish",
            [(VMEM, half)] + [(HBM, a) for a in before],
            [(HBM, (m, CH, CH), F32) for m in (9, 3, 4)],
            [pltpu.VMEM((n, CH, CH // 2), F32), pltpu.SemaphoreType.DMA((n,))],
            alias={1 + i: i for i in range(len(before))},
        )
    )


def along(value, axis, by):
    count = lax.axis_size(axis)
    pairs = [(i, i + by) for i in range(count) if 0 <= i + by < count]
    return lax.ppermute(value, axis, pairs)


def around(value, axis, by):
    count = lax.axis_size(axis)
    return lax.ppermute(value, axis, [(i, (i + by) % count) for i in range(count)])


def from_bands(parts):
    if len(parts) == 1:
        got = lax.ppermute(parts[0], "grp", [(0, 1), (1, 0)])
        return got, got
    return along(parts[0], "grp", 1), along(parts[1], "grp", -1)


def body(tm, grp, frames_in, span_frames, w_spatial, w_temporal, w_down, cotangent):
    slots, rows, cols, ch = frames_in.shape
    wide = rows * cols
    x = frames_in.reshape(slots, wide, ch)
    ws = w_spatial.reshape(9, ch, ch)
    wd = w_down.reshape(4, ch, ch)
    wt = w_temporal
    count = (SMEM, span_frames)
    tap = 2 * slots * wide * ch * ch
    tile = (rows, cols, slots, ch)
    padded = (rows + 2, cols + 2, slots, ch)
    dma = pltpu.SemaphoreType.DMA

    sides = 1 if grp == 2 else 2
    *edge, nxt = call(
        functools.partial(edges_kernel, grp),
        "edges",
        [count, (VMEM, x), (VMEM, cotangent)],
        [(VMEM, (cols * slots, ch))] * sides + [(VMEM, (2,) + cotangent.shape[1:])],
        flops=tap // 8,
    )
    top, bot = from_bands(edge)
    nxt_got = around(nxt, "tm", -1)
    xt, acts, at, last_two = call(
        functools.partial(acts_kernel, grp),
        "acts",
        [count, (VMEM, x), (VMEM, top), (VMEM, bot)],
        [(VMEM, tile), (VMEM, padded), (VMEM, (3 * ch, (rows + 4) * 128)), (VMEM, (2 * wide + 32, ch))],
        flops=2 * tap,
    )
    prev = around(last_two, "tm", 1)
    half = (16, 9, 16, ch // 2)
    cott, gy, gs, keep_a, send_a, *edge = call(
        functools.partial(grad_spatial_kernel, tm, grp),
        "grad_spatial",
        [count, (VMEM, at), (VMEM, cotangent), (VMEM, nxt_got), (VMEM, wt), (VMEM, wd)],
        [(VMEM, (rows // 2, cols // 2, slots, ch)), (VMEM, tile),
         (VMEM, (rows, cols + 2, slots, ch)), (VMEM, half), (VMEM, half)]
        + [(VMEM, (cols // 2 * slots, ch))] * sides,
        flops=14 * tap,
    )
    send_a = passed(send_a, [prev])
    got_a = core_round(send_a, tm, grp)
    cot_top, cot_bot = from_bands(edge)
    acts, sp = call(
        spatial_kernel,
        "spatial",
        [count, (VMEM, acts), (VMEM, prev), (VMEM, ws), (ANY, send_a)],
        [(VMEM, padded), (VMEM, tile)],
        flops=9 * tap,
        alias={1: 0},
    )
    _, plane, line, others = plan(tm, grp)
    parts_a = plane_send(keep_a, got_a, [sp])
    half = (16, 7, 16, ch // 2)
    down, keep_b, send_b = call(
        forward_kernel,
        "forward",
        [count, (VMEM, xt), (VMEM, sp), (VMEM, cott), (VMEM, gy), (VMEM, wt), (VMEM, wd),
         *((ANY, a) for a in parts_a)],
        [(VMEM, (slots * wide // 4, ch)), (VMEM, half), (VMEM, half)],
        [pltpu.VMEM(v, BF) for v in (tile, (3 * ch, slots * wide), (4 * ch, slots * wide // 4))],
        flops=10 * tap,
        grant=14,
    )
    parts_a = four_round(parts_a, plane, tm, grp)
    send_b = passed(send_b, parts_a[1:2])
    parts_b = plane_send(keep_b, core_round(send_b, tm, grp), [])
    parts_b = four_round(parts_b, plane, tm, grp)
    parts = call(
        line_send_kernel,
        "line_send",
        [(VMEM, a) for a in parts_a + parts_b],
        [(VMEM, (16, 16, ch // 2))] * 4,
    )
    parts = four_round(list(parts), line, tm, grp)
    ins = [(VMEM, a) for a in parts] + [(ANY, a) for a in [cot_top, cot_bot][:sides]]
    (mine,) = call(line_sum_kernel, "line_sum", ins, [(VMEM, parts[0].shape)])
    for bit in others:
        got = swap(mine, tm, grp, bit)
        (mine,) = call(add_kernel, "add", [(VMEM, mine), (VMEM, got)], [(VMEM, mine.shape)])
    parts = four_round([mine] * 4, line, tm, grp)
    (mine,) = call(
        line_gather_kernel, "line_gather", [(VMEM, a) for a in parts], [(VMEM, (4,) + mine.shape)]
    )
    parts = four_round([mine] * 4, plane, tm, grp)
    grad_x, down, token = call(
        functools.partial(grad_x_kernel, grp),
        "grad_x",
        [count, (VMEM, xt), (VMEM, gy), (VMEM, gs), (VMEM, cot_top), (VMEM, cot_bot), (VMEM, wt),
         (VMEM, wd), (VMEM, ws), (VMEM, down), (ANY, mine)],
        [(HBM, (slots, wide, ch)), (VMEM, cotangent.shape), TOKEN],
        [pltpu.VMEM(padded, BF), pltpu.VMEM((slots, wide, ch), BF), dma((1,))],
        flops=10 * tap,
    )
    ins = [(VMEM, a) for a in parts] + [(ANY, token)]
    (mine,) = call(plane_gather_kernel, "plane_gather", ins, [(VMEM, (16,) + mine.shape[1:])])
    got = core_round(mine, tm, grp)
    outs = finish(True, mine, [])
    sum_s, sum_t, sum_d = finish(False, got, outs)
    return (
        down,
        grad_x.reshape(frames_in.shape),
        sum_s.reshape(w_spatial.shape),
        sum_t,
        sum_d.reshape(w_down.shape),
    )


def solution(mesh):
    return jax.shard_map(
        functools.partial(body, mesh.shape["tm"], mesh.shape["grp"]),
        mesh=mesh,
        in_specs=(P("tm", "grp", None, None), P("tm"), P(), P(), P(), P("tm", "grp", None, None)),
        out_specs=(P("tm", "grp", None, None), P("tm", "grp", None, None), P(), P(), P()),
        check_vma=False,
    )
```

```python
import functools

import jax
import jax.numpy as jnp
from jax import lax
from jax.experimental import pallas as pl
from jax.experimental.pallas import tpu as pltpu
from jax.sharding import PartitionSpec as P

SLOTS = 16
OWN = 14
CH = 256
BF = jnp.bfloat16
F32 = jnp.float32


def mm(a, b):
    return lax.dot_general(a, b, (((1,), (0,)), ((), ())), preferred_element_type=F32)


def mm_nt(a, b):
    return lax.dot_general(a, b, (((1,), (1,)), ((), ())), preferred_element_type=F32)


def iotas(rows, cols):
    return (
        lax.broadcasted_iota(jnp.int32, (rows, cols), 0),
        lax.broadcasted_iota(jnp.int32, (rows, cols), 1),
    )


def to_slots(rows, frames, keep):
    a, b = iotas(rows * SLOTS, frames * rows)
    bits = rows.bit_length() - 1
    hit = ((a >> 4) == (b & (rows - 1))) & keep(b >> bits, a & 15)
    return jnp.where(hit, 1.0, 0.0).astype(BF)


def to_frames(rows):
    a, b = iotas(SLOTS * rows, rows * SLOTS)
    bits = rows.bit_length() - 1
    hit = ((a & (rows - 1)) == (b >> 4)) & ((a >> bits) == (b & 15))
    return jnp.where(hit, 1.0, 0.0).astype(BF)


def own_frames(count):
    return lambda frame, slot: (frame == slot) & (slot < count)


def own_and_next(count, blocks):
    after = jnp.where(lax.axis_index("tm") < blocks - 1, count, 64)
    return lambda frame, slot: ((frame < OWN) & (frame == slot) & (slot < count)) | (
        (frame >= OWN) & (slot == after + frame - OWN)
    )


def silu_norm(v):
    scaled = v * lax.rsqrt(jnp.mean(v * v, axis=-1, keepdims=True) + 1e-06)
    return scaled * (0.5 + 0.5 * jnp.tanh(0.5 * scaled))


def slot_mask(shape, count):
    return lax.broadcasted_iota(jnp.int32, shape, len(shape) - 2) < count


def grad_of_temporal(gy, wt_ref, count):
    n = gy.shape[0]
    flat = gy.reshape(n * SLOTS, CH)
    total = mm_nt(flat, wt_ref[2]).reshape(n, SLOTS, CH)
    for k in (1, 0):
        term = mm_nt(flat, wt_ref[k]).reshape(n, SLOTS, CH)
        total = total + pltpu.roll(term, SLOTS - (2 - k), 1)
    return jnp.where(slot_mask(total.shape, count), total, 0.0).astype(BF)


def place_bits():
    t, g = lax.axis_index("tm"), lax.axis_index("grp")
    return t & 1, ((t >> 1) & 1) + 2 * (g & 1), (t >> 2) & 3


def split_cores(value, keep_ref, send_ref, k):
    core, _, _ = place_bits()
    low, high = value[:, : CH // 2].astype(BF), value[:, CH // 2 :].astype(BF)
    keep_ref[:, k] = jnp.where(core == 0, low, high).reshape(16, 16, CH // 2)
    send_ref[:, k] = jnp.where(core == 0, high, low).reshape(16, 16, CH // 2)


def edges_kernel(bands, count_ref, x_ref, cot_ref, *rest):
    outs, nxt_ref = rest[:-1], rest[-1]
    nxt_ref[...] = cot_ref[0:2]
    count = count_ref[0]
    band = lax.axis_index("grp")
    wide = x_ref.shape[1]
    if bands == 2:
        starts, lower = [jnp.where(band == 0, wide - 16, 0)], [band == 0]
    else:
        starts, lower = [wide - 16, 0], [True, False]
    place = to_slots(16, SLOTS, own_frames(count))
    for k, at in enumerate(starts):
        piece = x_ref[:, pl.ds(pl.multiple_of(at, 16), 16), :].reshape(SLOTS * 16, CH)
        v = mm(place, piece)
        v = jnp.where(lower[k], v[128:], v[:128])
        outs[k][...] = silu_norm(v).astype(BF)


def acts_kernel(bands, count_ref, x_ref, top_ref, bot_ref, xt_ref, acts_ref, at_ref, last_ref):
    count = count_ref[0]
    band = lax.axis_index("grp")
    rows, cols = xt_ref.shape[0], xt_ref.shape[1]
    edge = jnp.zeros((rows + 2, SLOTS, CH), BF)
    acts_ref[:, 0] = edge
    acts_ref[:, cols + 1] = edge
    place = to_slots(16, SLOTS, own_frames(count))
    last = silu_norm(x_ref[pl.ds(count - 2, 2)].reshape(2 * rows * cols, CH).astype(F32))
    last_ref[0 : 2 * rows * cols] = last.astype(BF)

    def rows_of(q, _):
        at = pl.multiple_of(q * 16, 16)
        piece = x_ref[:, pl.ds(at, 16), :].reshape(SLOTS * 16, CH)
        v = mm(place, piece)
        xt_ref[pl.ds(2 * q, 2)] = v.astype(BF).reshape(2, cols, SLOTS, CH)
        a = silu_norm(v).astype(BF)
        acts_ref[pl.ds(2 * q + 1, 2), 1 : cols + 1] = a.reshape(2, cols, SLOTS, CH)
        flipped = a.T
        for i in range(3):
            at = pl.multiple_of((2 * q + 3 - i) * 128, 128)
            at_ref[i * CH : i * CH + CH, pl.ds(at, 256)] = flipped
        return 0

    lax.fori_loop(0, rows // 2, rows_of, 0, unroll=4)
    halo = []
    for ref, flag, i, row in ((top_ref, band > 0, 0, 0), (bot_ref, band < bands - 1, 2, rows + 1)):
        a = jnp.where(flag, ref[...].astype(F32), 0.0).astype(BF)
        acts_ref[row, 1 : cols + 1] = a.reshape(cols, SLOTS, CH)
        at = (row - i + 2) * 128
        at_ref[i * CH : i * CH + CH, at : at + 128] = a.T
        halo.append(a)
    a, b = iotas(32, 256)
    pick = ((a & 15) == (b >> 4)) & ((b & 15) == count - 2 + (a >> 4))
    pick = jnp.where(pick, 1.0, 0.0).astype(BF)
    last_ref[2 * rows * cols :] = mm(pick, jnp.concatenate(halo, 0)).astype(BF)


def spatial_kernel(count_ref, acts_in, prev_ref, ws_ref, *rest):
    acts_ref, sp_ref = rest[-2:]
    rows, cols = sp_ref.shape[0], sp_ref.shape[1]
    a, b = iotas(256, 32)
    place = ((a >> 4) == (b & 15)) & ((a & 15) == OWN + (b >> 4)) & (lax.axis_index("tm") > 0)
    place = jnp.where(place, 1.0, 0.0).astype(BF)
    size = rows * cols
    for q in range(rows // 2 + 1):
        if q == rows // 2:
            both, prev = slice(0, rows + 2, rows + 1), prev_ref[2 * size :]
        else:
            both = slice(2 * q + 1, 2 * q + 3)
            parts = [prev_ref[f * size + q * 16 : f * size + q * 16 + 16] for f in range(2)]
            prev = jnp.concatenate(parts, 0)
        prev = mm(place, prev).astype(BF).reshape(2, cols, SLOTS, CH)
        for k, row in enumerate(range(rows + 2)[both]):
            acts_ref[row, 1 : cols + 1] = acts_ref[row, 1 : cols + 1] + prev[k]

    def rows_of(q, _):
        total = None
        for i in range(3):
            for j in range(3):
                left = acts_ref[pl.ds(4 * q + i, 4), j : j + cols].reshape(4 * cols * SLOTS, CH)
                term = mm(left, ws_ref[i * 3 + j])
                total = term if total is None else total + term
        sp_ref[pl.ds(4 * q, 4)] = total.astype(BF).reshape(4, cols, SLOTS, CH)
        return 0

    lax.fori_loop(0, rows // 4, rows_of, 0)


def grad_spatial_kernel(
    blocks, bands, count_ref, at_ref, cot_ref, nxt_ref, wt_ref, wd_ref,
    cott_ref, gy_ref, gs_ref, keep_ref, send_ref, *edge_refs,
):
    count = count_ref[0]
    band = lax.axis_index("grp")
    rows, cols = gy_ref.shape[0], gy_ref.shape[1]
    edge = jnp.zeros((rows, SLOTS, CH), BF)
    gs_ref[:, 0] = edge
    gs_ref[:, cols + 1] = edge

    place_next = to_slots(16, SLOTS, own_and_next(count, blocks))
    halves = []
    for q in range(rows * cols // 64):
        four = slice(q * 4, q * 4 + 4)
        piece = jnp.concatenate(
            [cot_ref[0:OWN, four].reshape(OWN, 16, CH), nxt_ref[:, four].reshape(2, 16, CH)], 0
        ).reshape(SLOTS * 16, CH)
        halves.append(mm(place_next, piece).astype(BF))
    placed = jnp.concatenate(halves, 0)
    cott_ref[...] = placed.reshape(rows // 2, cols // 2, SLOTS, CH)
    for i in range(2):
        for j in range(2):
            g = mm_nt(placed, wd_ref[i * 2 + j]).astype(BF).reshape(rows // 2, cols // 2, SLOTS, CH)
            for r in range(rows // 2):
                for c in range(cols // 2):
                    gy_ref[2 * r + i, 2 * c + j] = g[r, c]
    last = cott_ref[rows // 2 - 1].reshape(cols // 2 * SLOTS, CH)
    first = cott_ref[0].reshape(cols // 2 * SLOTS, CH)
    if bands == 2:
        edge_refs[0][...] = jnp.where(band == 0, last, first)
    else:
        edge_refs[0][...] = last
        edge_refs[1][...] = first

    def grads_of(q, _):
        g = gy_ref[pl.ds(8 * q, 8)].reshape(8 * cols, SLOTS, CH)
        s = grad_of_temporal(g, wt_ref, count)
        gs_ref[pl.ds(8 * q, 8), 1 : cols + 1] = s.reshape(8, cols, SLOTS, CH)
        g = jnp.where(slot_mask(g.shape, count), g.astype(F32), 0.0)
        gy_ref[pl.ds(8 * q, 8)] = g.astype(BF).reshape(8, cols, SLOTS, CH)
        return 0

    lax.fori_loop(0, rows // 8, grads_of, 0)

    wide = rows * cols * SLOTS
    for j in range(3):
        right = gs_ref[:, 2 - j : 2 - j + cols].reshape(wide, CH)
        value = mm(at_ref[:, 256 : 256 + wide], right)
        for i in range(3):
            split_cores(value[i * CH : i * CH + CH], keep_ref, send_ref, i * 3 + j)


def forward_kernel(
    count_ref, xt_ref, sp_ref, cott_ref, gy_ref, wt_ref, wd_ref, *rest
):
    down_ref, keep_ref, send_ref, y_ref, st_ref, yt_ref = rest[-6:]
    count = count_ref[0]
    rows, cols = xt_ref.shape[0], xt_ref.shape[1]
    def rows_of(q, _):
        s = sp_ref[pl.ds(8 * q, 8)].reshape(8 * cols * SLOTS, CH).astype(F32)
        s = s.reshape(8 * cols, SLOTS, CH)
        total = None
        for k in range(3):
            shifted = s if k == 2 else pltpu.roll(s, 2 - k, 1)
            shifted = shifted.astype(BF).reshape(8 * cols * SLOTS, CH)
            at = pl.ds(pl.multiple_of(q * 1024, 1024), 1024)
            st_ref[k * CH : k * CH + CH, at] = shifted.T
            term = mm(shifted, wt_ref[k])
            total = term if total is None else total + term
        x = xt_ref[pl.ds(8 * q, 8)].reshape(8 * cols, SLOTS, CH).astype(F32)
        y = jnp.where(slot_mask(x.shape, count), x + total.reshape(x.shape), 0.0).astype(BF)
        y_ref[pl.ds(8 * q, 8)] = y.reshape(8, cols, SLOTS, CH)
        return 0

    lax.fori_loop(0, rows // 8, rows_of, 0)

    wide = rows * cols * SLOTS
    value = mm(st_ref[...], gy_ref[...].reshape(wide, CH))
    for k in range(3):
        split_cores(value[k * CH : k * CH + CH], keep_ref, send_ref, k)

    small = wide // 4
    total = None
    for i in range(2):
        for j in range(2):
            tiles = [
                y_ref[2 * r + i, 2 * c + j] for r in range(rows // 2) for c in range(cols // 2)
            ]
            piece = jnp.concatenate(tiles, axis=0)
            k = i * 2 + j
            yt_ref[k * CH : k * CH + CH] = piece.T
            term = mm(piece, wd_ref[k])
            total = term if total is None else total + term
    down_ref[...] = total.astype(BF)
    value = mm(yt_ref[...], cott_ref[...].reshape(small, CH))
    for k in range(4):
        split_cores(value[k * CH : k * CH + CH], keep_ref, send_ref, 3 + k)


def grad_x_kernel(
    bands, count_ref, xt_ref, gy_ref, gs_ref, top_ref, bot_ref, wt_ref, wd_ref, ws_ref, slot_ref, *rest
):
    out_ref, down_ref, token_ref, pad_ref, buf, sems = rest[-6:]
    token_ref[...] = jnp.zeros_like(token_ref)
    count = count_ref[0]
    band = lax.axis_index("grp")
    rows, cols = xt_ref.shape[0], xt_ref.shape[1]
    pad_ref[1 : rows + 1] = gs_ref[...]
    edge = jnp.zeros((SLOTS, CH), BF)
    for ref, flag, i, row in ((top_ref, band > 0, 1, 0), (bot_ref, band < bands - 1, 0, rows + 1)):
        pair = [
            mm_nt(ref[...], wd_ref[i * 2 + j]).astype(BF).reshape(cols // 2, SLOTS, CH)
            for j in range(2)
        ]
        g = jnp.stack(pair, axis=1).reshape(cols, SLOTS, CH)
        pad_ref[row, 0] = edge
        pad_ref[row, 1 : cols + 1] = grad_of_temporal(g, wt_ref, jnp.where(flag, count, 0))
        pad_ref[row, cols + 1] = edge
    back = to_frames(16)

    def rows_of(q, _):
        total = None
        for i in range(3):
            for j in range(3):
                left = pad_ref[pl.ds(4 * q + 2 - i, 4), 2 - j : 2 - j + cols].reshape(
                    4 * cols * SLOTS, CH
                )
                term = mm_nt(left, ws_ref[i * 3 + j])
                total = term if total is None else total + term
        at = 4 * q
        v = xt_ref[pl.ds(at, 4)].reshape(4 * cols * SLOTS, CH).astype(F32)
        r = lax.rsqrt(jnp.mean(v * v, axis=-1, keepdims=True) + 1e-06)
        u = v * r
        s = 0.5 + 0.5 * jnp.tanh(0.5 * u)
        gu = total * (s * (1.0 + u * (1.0 - s)))
        dot = jnp.mean(gu * u, axis=-1, keepdims=True)
        gv = r * (gu - u * dot)
        gx = gy_ref[pl.ds(at, 4)].reshape(4 * cols * SLOTS, CH).astype(F32) + gv
        gx = gx.reshape(4 * cols, SLOTS, CH)
        gx = jnp.where(slot_mask(gx.shape, count), gx, 0.0).astype(BF).reshape(4 * cols * SLOTS, CH)
        for k in range(2):
            o = mm(back, gx[k * 256 : k * 256 + 256]).astype(BF)
            buf[:, pl.ds(pl.multiple_of((2 * q + k) * 16, 16), 16), :] = o.reshape(SLOTS, 16, CH)
        return 0

    lax.fori_loop(0, rows // 4, rows_of, 0)
    copy = pltpu.make_async_copy(buf, out_ref, sems.at[0])
    copy.start()
    for q in range(down_ref.shape[1] // 4):
        o = mm(back, slot_ref[q * 256 : q * 256 + 256]).astype(BF)
        down_ref[:, q * 4 : q * 4 + 4] = o.reshape(SLOTS, 4, cols // 2, CH)
    copy.wait()


ORDER = (0, 3, 2, 1)


def plane_send_kernel(keep_ref, got_ref, *rest):
    _, p, _ = place_bits()
    for r, out in zip(ORDER, rest[-4:]):
        at = pl.ds((p ^ r) * 4, 4)
        out[...] = (keep_ref[at].astype(F32) + got_ref[at].astype(F32)).astype(BF)


def line_send_kernel(*refs):
    outs = refs[8:]
    _, _, z = place_bits()
    for out, r in zip(outs, ORDER):
        at = 0
        for chain in (refs[:4], refs[4:8]):
            parts = [ref[z ^ r].astype(F32) for ref in chain]
            n = parts[0].shape[0]
            out[at : at + n] = (parts[0] + parts[1] + parts[2] + parts[3]).astype(BF)
            at += n


def line_sum_kernel(a_ref, b_ref, c_ref, d_ref, *rest):
    out_ref = rest[-1]
    parts = [ref[...].astype(F32) for ref in (a_ref, b_ref, c_ref, d_ref)]
    out_ref[...] = (parts[0] + parts[1] + parts[2] + parts[3]).astype(BF)


def line_gather_kernel(a_ref, b_ref, c_ref, d_ref, out_ref):
    _, _, z = place_bits()
    for r, ref in zip(ORDER, (a_ref, b_ref, c_ref, d_ref)):
        out_ref[z ^ r] = ref[...]


def plane_gather_kernel(a_ref, b_ref, c_ref, d_ref, _, out_ref):
    _, p, _ = place_bits()
    for r, ref in zip(ORDER, (a_ref, b_ref, c_ref, d_ref)):
        out_ref[pl.ds((p ^ r) * 4, 4)] = ref[...]


def add_kernel(a_ref, b_ref, out_ref):
    out_ref[...] = (a_ref[...].astype(F32) + b_ref[...].astype(F32)).astype(BF)


def pass_kernel(*_):
    pass


def finish_kernel(own, half_ref, *rest):
    buf, sems = rest[-2:]
    outs = rest[-5:-2]
    core, _, _ = place_bits()
    at = pl.multiple_of((core if own else 1 - core) * (CH // 2), CH // 2)
    copies = []
    k = 0
    for out in outs:
        for m in range(out.shape[0]):
            buf[k] = half_ref[:, k].reshape(CH, CH // 2).astype(F32)
            copies.append(
                pltpu.make_async_copy(buf.at[k], out.at[m, :, pl.ds(at, CH // 2)], sems.at[k])
            )
            copies[-1].start()
            k += 1
    for copy in copies:
        copy.wait()


VMEM = pl.BlockSpec(memory_space=pltpu.VMEM)
SMEM = pl.BlockSpec(memory_space=pltpu.SMEM)
ANY = pl.BlockSpec(memory_space=pl.ANY)
HBM = pl.BlockSpec(memory_space=pltpu.HBM)
TOKEN = (VMEM, (8, 128), F32)


def call(kernel, name, ins, outs, scratch=(), flops=0, alias=None, grant=10):
    shapes = [jax.ShapeDtypeStruct(o[1], o[2] if len(o) > 2 else BF) for o in outs]
    moved = sum(a.size * a.dtype.itemsize for s, a in ins if s is not ANY)
    moved += sum(s.size * s.dtype.itemsize for s in shapes)
    return pl.pallas_call(
        kernel,
        out_shape=shapes,
        in_specs=[s for s, _ in ins],
        out_specs=[o[0] for o in outs],
        scratch_shapes=list(scratch),
        compiler_params=pltpu.CompilerParams(vmem_limit_bytes=grant * 2**20),
        cost_estimate=pl.CostEstimate(flops=flops, bytes_accessed=moved, transcendentals=0),
        input_output_aliases=alias or {},
        name=name,
    )(*[a for _, a in ins])


AXES = ("tm", "grp")


def plan(tm, grp):
    low, total = grp.bit_length() - 1, (tm * grp).bit_length() - 1
    plane, line = [low + 1, 0], [low + 2, low + 3]
    return low, plane, line, [b for b in range(total) if b not in [low] + plane + line]


def swap(value, tm, grp, *bits):
    flip = sum(1 << b for b in bits)
    return lax.ppermute(value, AXES, [(d, d ^ flip) for d in range(tm * grp)])


def core_round(value, tm, grp):
    return swap(value, tm, grp, plan(tm, grp)[0])


def four_round(parts, bits, tm, grp):
    return [
        parts[0],
        swap(parts[1], tm, grp, *bits),
        swap(parts[2], tm, grp, bits[1]),
        swap(parts[3], tm, grp, bits[0]),
    ]


def plane_send(keep, got, after):
    ins = [(VMEM, keep), (VMEM, got)] + [(ANY, a) for a in after]
    shape = (4, keep.shape[1], 16, CH // 2)
    return list(call(plane_send_kernel, "plane_send", ins, [(VMEM, shape)] * 4))


def passed(value, after):
    ins = [(ANY, value)] + [(ANY, a) for a in after]
    return call(pass_kernel, "pass", ins, [(ANY, value.shape)], alias={0: 0})[0]


def finish(own, half, before):
    n = half.shape[1]
    return list(
        call(
            functools.partial(finish_kernel, own),
            "finish",
            [(VMEM, half)] + [(HBM, a) for a in before],
            [(HBM, (m, CH, CH), F32) for m in (9, 3, 4)],
            [pltpu.VMEM((n, CH, CH // 2), F32), pltpu.SemaphoreType.DMA((n,))],
            alias={1 + i: i for i in range(len(before))},
        )
    )


def along(value, axis, by):
    count = lax.axis_size(axis)
    pairs = [(i, i + by) for i in range(count) if 0 <= i + by < count]
    return lax.ppermute(value, axis, pairs)


def around(value, axis, by):
    count = lax.axis_size(axis)
    return lax.ppermute(value, axis, [(i, (i + by) % count) for i in range(count)])


def from_bands(parts):
    if len(parts) == 1:
        got = lax.ppermute(parts[0], "grp", [(0, 1), (1, 0)])
        return got, got
    return along(parts[0], "grp", 1), along(parts[1], "grp", -1)


def body(tm, grp, frames_in, span_frames, w_spatial, w_temporal, w_down, cotangent):
    slots, rows, cols, ch = frames_in.shape
    wide = rows * cols
    x = frames_in.reshape(slots, wide, ch)
    ws = w_spatial.reshape(9, ch, ch)
    wd = w_down.reshape(4, ch, ch)
    wt = w_temporal
    count = (SMEM, span_frames)
    tap = 2 * slots * wide * ch * ch
    tile = (rows, cols, slots, ch)
    padded = (rows + 2, cols + 2, slots, ch)
    dma = pltpu.SemaphoreType.DMA

    sides = 1 if grp == 2 else 2
    *edge, nxt = call(
        functools.partial(edges_kernel, grp),
        "edges",
        [count, (VMEM, x), (VMEM, cotangent)],
        [(VMEM, (cols * slots, ch))] * sides + [(VMEM, (2,) + cotangent.shape[1:])],
        flops=tap // 8,
    )
    top, bot = from_bands(edge)
    nxt_got = around(nxt, "tm", -1)
    xt, acts, at, last_two = call(
        functools.partial(acts_kernel, grp),
        "acts",
        [count, (VMEM, x), (VMEM, top), (VMEM, bot)],
        [(VMEM, tile), (VMEM, padded), (VMEM, (3 * ch, (rows + 4) * 128)), (VMEM, (2 * wide + 32, ch))],
        flops=2 * tap,
    )
    prev = around(last_two, "tm", 1)
    half = (16, 9, 16, ch // 2)
    cott, gy, gs, keep_a, send_a, *edge = call(
        functools.partial(grad_spatial_kernel, tm, grp),
        "grad_spatial",
        [count, (VMEM, at), (VMEM, cotangent), (VMEM, nxt_got), (VMEM, wt), (VMEM, wd)],
        [(VMEM, (rows // 2, cols // 2, slots, ch)), (VMEM, tile),
         (VMEM, (rows, cols + 2, slots, ch)), (VMEM, half), (VMEM, half)]
        + [(VMEM, (cols // 2 * slots, ch))] * sides,
        flops=14 * tap,
    )
    send_a = passed(send_a, [prev])
    got_a = core_round(send_a, tm, grp)
    cot_top, cot_bot = from_bands(edge)
    _, plane, line, others = plan(tm, grp)
    parts_a = plane_send(keep_a, got_a, [])
    acts, sp = call(
        spatial_kernel,
        "spatial",
        [count, (VMEM, acts), (VMEM, prev), (VMEM, ws)] + [(ANY, a) for a in parts_a[1:]],
        [(VMEM, padded), (VMEM, tile)],
        flops=9 * tap,
        alias={1: 0},
    )
    parts_a = four_round(parts_a, plane, tm, grp)
    half = (16, 7, 16, ch // 2)
    down, keep_b, send_b = call(
        forward_kernel,
        "forward",
        [count, (VMEM, xt), (VMEM, sp), (VMEM, cott), (VMEM, gy), (VMEM, wt), (VMEM, wd),
         *((ANY, a) for a in parts_a[1:])],
        [(VMEM, (slots * wide // 4, ch)), (VMEM, half), (VMEM, half)],
        [pltpu.VMEM(v, BF) for v in (tile, (3 * ch, slots * wide), (4 * ch, slots * wide // 4))],
        flops=10 * tap,
        grant=14,
    )
    parts_b = plane_send(keep_b, core_round(send_b, tm, grp), [])
    parts_b = four_round(parts_b, plane, tm, grp)
    parts = call(
        line_send_kernel,
        "line_send",
        [(VMEM, a) for a in parts_a + parts_b],
        [(VMEM, (16, 16, ch // 2))] * 4,
    )
    parts = four_round(list(parts), line, tm, grp)
    ins = [(VMEM, a) for a in parts] + [(ANY, a) for a in [cot_top, cot_bot][:sides]]
    (mine,) = call(line_sum_kernel, "line_sum", ins, [(VMEM, parts[0].shape)])
    for bit in others:
        got = swap(mine, tm, grp, bit)
        (mine,) = call(add_kernel, "add", [(VMEM, mine), (VMEM, got)], [(VMEM, mine.shape)])
    parts = four_round([mine] * 4, line, tm, grp)
    (mine,) = call(
        line_gather_kernel, "line_gather", [(VMEM, a) for a in parts], [(VMEM, (4,) + mine.shape)]
    )
    parts = four_round([mine] * 4, plane, tm, grp)
    grad_x, down, token = call(
        functools.partial(grad_x_kernel, grp),
        "grad_x",
        [count, (VMEM, xt), (VMEM, gy), (VMEM, gs), (VMEM, cot_top), (VMEM, cot_bot), (VMEM, wt),
         (VMEM, wd), (VMEM, ws), (VMEM, down), (ANY, mine)],
        [(HBM, (slots, wide, ch)), (VMEM, cotangent.shape), TOKEN],
        [pltpu.VMEM(padded, BF), pltpu.VMEM((slots, wide, ch), BF), dma((1,))],
        flops=10 * tap,
    )
    ins = [(VMEM, a) for a in parts] + [(ANY, token)]
    (mine,) = call(plane_gather_kernel, "plane_gather", ins, [(VMEM, (16,) + mine.shape[1:])])
    got = core_round(mine, tm, grp)
    outs = finish(True, mine, [])
    sum_s, sum_t, sum_d = finish(False, got, outs)
    return (
        down,
        grad_x.reshape(frames_in.shape),
        sum_s.reshape(w_spatial.shape),
        sum_t,
        sum_d.reshape(w_down.shape),
    )


def solution(mesh):
    return jax.shard_map(
        functools.partial(body, mesh.shape["tm"], mesh.shape["grp"]),
        mesh=mesh,
        in_specs=(P("tm", "grp", None, None), P("tm"), P(), P(), P(), P("tm", "grp", None, None)),
        out_specs=(P("tm", "grp", None, None), P("tm", "grp", None, None), P(), P(), P()),
        check_vma=False,
    )
```

```python
import functools

import jax
import jax.numpy as jnp
from jax import lax
from jax.experimental import pallas as pl
from jax.experimental.pallas import tpu as pltpu
from jax.sharding import PartitionSpec as P

SLOTS = 16
OWN = 14
CH = 256
BF = jnp.bfloat16
F32 = jnp.float32


def mm(a, b):
    return lax.dot_general(a, b, (((1,), (0,)), ((), ())), preferred_element_type=F32)


def mm_nt(a, b):
    return lax.dot_general(a, b, (((1,), (1,)), ((), ())), preferred_element_type=F32)


def iotas(rows, cols):
    return (
        lax.broadcasted_iota(jnp.int32, (rows, cols), 0),
        lax.broadcasted_iota(jnp.int32, (rows, cols), 1),
    )


def to_slots(rows, frames, keep):
    a, b = iotas(rows * SLOTS, frames * rows)
    bits = rows.bit_length() - 1
    hit = ((a >> 4) == (b & (rows - 1))) & keep(b >> bits, a & 15)
    return jnp.where(hit, 1.0, 0.0).astype(BF)


def to_frames(rows):
    a, b = iotas(SLOTS * rows, rows * SLOTS)
    bits = rows.bit_length() - 1
    hit = ((a & (rows - 1)) == (b >> 4)) & ((a >> bits) == (b & 15))
    return jnp.where(hit, 1.0, 0.0).astype(BF)


def own_frames(count):
    return lambda frame, slot: (frame == slot) & (slot < count)


def own_and_next(count, blocks):
    after = jnp.where(lax.axis_index("tm") < blocks - 1, count, 64)
    return lambda frame, slot: ((frame < OWN) & (frame == slot) & (slot < count)) | (
        (frame >= OWN) & (slot == after + frame - OWN)
    )


def silu_norm(v):
    scaled = v * lax.rsqrt(jnp.mean(v * v, axis=-1, keepdims=True) + 1e-06)
    return scaled * (0.5 + 0.5 * jnp.tanh(0.5 * scaled))


def slot_mask(shape, count):
    return lax.broadcasted_iota(jnp.int32, shape, len(shape) - 2) < count


def grad_of_temporal(gy, wt_ref, count):
    n = gy.shape[0]
    flat = gy.reshape(n * SLOTS, CH)
    total = mm_nt(flat, wt_ref[2]).reshape(n, SLOTS, CH)
    for k in (1, 0):
        term = mm_nt(flat, wt_ref[k]).reshape(n, SLOTS, CH)
        total = total + pltpu.roll(term, SLOTS - (2 - k), 1)
    return jnp.where(slot_mask(total.shape, count), total, 0.0).astype(BF)


def place_bits():
    t, g = lax.axis_index("tm"), lax.axis_index("grp")
    return t & 1, ((t >> 1) & 1) + 2 * (g & 1), (t >> 2) & 3


def split_cores(value, keep_ref, send_ref, k):
    core, _, _ = place_bits()
    low, high = value[:, : CH // 2].astype(BF), value[:, CH // 2 :].astype(BF)
    keep_ref[:, k] = jnp.where(core == 0, low, high).reshape(16, 16, CH // 2)
    send_ref[:, k] = jnp.where(core == 0, high, low).reshape(16, 16, CH // 2)


def edges_kernel(bands, count_ref, x_ref, cot_ref, *rest):
    outs, nxt_ref = rest[:-1], rest[-1]
    nxt_ref[...] = cot_ref[0:2]
    count = count_ref[0]
    band = lax.axis_index("grp")
    wide = x_ref.shape[1]
    if bands == 2:
        starts, lower = [jnp.where(band == 0, wide - 16, 0)], [band == 0]
    else:
        starts, lower = [wide - 16, 0], [True, False]
    place = to_slots(16, SLOTS, own_frames(count))
    for k, at in enumerate(starts):
        piece = x_ref[:, pl.ds(pl.multiple_of(at, 16), 16), :].reshape(SLOTS * 16, CH)
        v = mm(place, piece)
        v = jnp.where(lower[k], v[128:], v[:128])
        outs[k][...] = silu_norm(v).astype(BF)


def acts_kernel(count_ref, x_ref, _, xt_ref, acts_ref, at_ref, last_ref):
    count = count_ref[0]
    rows, cols = xt_ref.shape[0], xt_ref.shape[1]
    edge = jnp.zeros((rows + 2, SLOTS, CH), BF)
    acts_ref[:, 0] = edge
    acts_ref[:, cols + 1] = edge
    place = to_slots(16, SLOTS, own_frames(count))
    last = silu_norm(x_ref[pl.ds(count - 2, 2)].reshape(2 * rows * cols, CH).astype(F32))
    last_ref[0 : 2 * rows * cols] = last.astype(BF)

    def rows_of(q, _):
        at = pl.multiple_of(q * 16, 16)
        piece = x_ref[:, pl.ds(at, 16), :].reshape(SLOTS * 16, CH)
        v = mm(place, piece)
        xt_ref[pl.ds(2 * q, 2)] = v.astype(BF).reshape(2, cols, SLOTS, CH)
        a = silu_norm(v).astype(BF)
        acts_ref[pl.ds(2 * q + 1, 2), 1 : cols + 1] = a.reshape(2, cols, SLOTS, CH)
        flipped = a.T
        for i in range(3):
            at = pl.multiple_of((2 * q + 3 - i) * 128, 128)
            at_ref[i * CH : i * CH + CH, pl.ds(at, 256)] = flipped
        return 0

    lax.fori_loop(0, rows // 2, rows_of, 0, unroll=4)


def halo_kernel(bands, count_ref, top_ref, bot_ref, *rest):
    acts_ref, at_ref, last_ref = rest[-3:]
    count = count_ref[0]
    band = lax.axis_index("grp")
    rows, cols = acts_ref.shape[0] - 2, acts_ref.shape[1] - 2
    halo = []
    for ref, flag, i, row in ((top_ref, band > 0, 0, 0), (bot_ref, band < bands - 1, 2, rows + 1)):
        a = jnp.where(flag, ref[...].astype(F32), 0.0).astype(BF)
        acts_ref[row, 1 : cols + 1] = a.reshape(cols, SLOTS, CH)
        at = (row - i + 2) * 128
        at_ref[i * CH : i * CH + CH, at : at + 128] = a.T
        halo.append(a)
    a, b = iotas(32, 256)
    pick = ((a & 15) == (b >> 4)) & ((b & 15) == count - 2 + (a >> 4))
    pick = jnp.where(pick, 1.0, 0.0).astype(BF)
    last_ref[2 * rows * cols :] = mm(pick, jnp.concatenate(halo, 0)).astype(BF)


def spatial_kernel(count_ref, acts_in, prev_ref, ws_ref, _, acts_ref, sp_ref):
    rows, cols = sp_ref.shape[0], sp_ref.shape[1]
    a, b = iotas(256, 32)
    place = ((a >> 4) == (b & 15)) & ((a & 15) == OWN + (b >> 4)) & (lax.axis_index("tm") > 0)
    place = jnp.where(place, 1.0, 0.0).astype(BF)
    size = rows * cols
    for q in range(rows // 2 + 1):
        if q == rows // 2:
            both, prev = slice(0, rows + 2, rows + 1), prev_ref[2 * size :]
        else:
            both = slice(2 * q + 1, 2 * q + 3)
            parts = [prev_ref[f * size + q * 16 : f * size + q * 16 + 16] for f in range(2)]
            prev = jnp.concatenate(parts, 0)
        prev = mm(place, prev).astype(BF).reshape(2, cols, SLOTS, CH)
        for k, row in enumerate(range(rows + 2)[both]):
            acts_ref[row, 1 : cols + 1] = acts_ref[row, 1 : cols + 1] + prev[k]

    def rows_of(q, _):
        total = None
        for i in range(3):
            for j in range(3):
                left = acts_ref[pl.ds(4 * q + i, 4), j : j + cols].reshape(4 * cols * SLOTS, CH)
                term = mm(left, ws_ref[i * 3 + j])
                total = term if total is None else total + term
        sp_ref[pl.ds(4 * q, 4)] = total.astype(BF).reshape(4, cols, SLOTS, CH)
        return 0

    lax.fori_loop(0, rows // 4, rows_of, 0)


def grad_spatial_kernel(
    blocks, bands, count_ref, at_ref, cot_ref, nxt_ref, wt_ref, wd_ref,
    cott_ref, gy_ref, gs_ref, keep_ref, send_ref, *edge_refs,
):
    count = count_ref[0]
    band = lax.axis_index("grp")
    rows, cols = gy_ref.shape[0], gy_ref.shape[1]
    edge = jnp.zeros((rows, SLOTS, CH), BF)
    gs_ref[:, 0] = edge
    gs_ref[:, cols + 1] = edge

    place_next = to_slots(16, SLOTS, own_and_next(count, blocks))
    halves = []
    for q in range(rows * cols // 64):
        four = slice(q * 4, q * 4 + 4)
        piece = jnp.concatenate(
            [cot_ref[0:OWN, four].reshape(OWN, 16, CH), nxt_ref[:, four].reshape(2, 16, CH)], 0
        ).reshape(SLOTS * 16, CH)
        halves.append(mm(place_next, piece).astype(BF))
    placed = jnp.concatenate(halves, 0)
    cott_ref[...] = placed.reshape(rows // 2, cols // 2, SLOTS, CH)
    for i in range(2):
        for j in range(2):
            g = mm_nt(placed, wd_ref[i * 2 + j]).astype(BF).reshape(rows // 2, cols // 2, SLOTS, CH)
            for r in range(rows // 2):
                for c in range(cols // 2):
                    gy_ref[2 * r + i, 2 * c + j] = g[r, c]
    last = cott_ref[rows // 2 - 1].reshape(cols // 2 * SLOTS, CH)
    first = cott_ref[0].reshape(cols // 2 * SLOTS, CH)
    if bands == 2:
        edge_refs[0][...] = jnp.where(band == 0, last, first)
    else:
        edge_refs[0][...] = last
        edge_refs[1][...] = first

    def grads_of(q, _):
        g = gy_ref[pl.ds(8 * q, 8)].reshape(8 * cols, SLOTS, CH)
        s = grad_of_temporal(g, wt_ref, count)
        gs_ref[pl.ds(8 * q, 8), 1 : cols + 1] = s.reshape(8, cols, SLOTS, CH)
        g = jnp.where(slot_mask(g.shape, count), g.astype(F32), 0.0)
        gy_ref[pl.ds(8 * q, 8)] = g.astype(BF).reshape(8, cols, SLOTS, CH)
        return 0

    lax.fori_loop(0, rows // 8, grads_of, 0)

    wide = rows * cols * SLOTS
    for j in range(3):
        right = gs_ref[:, 2 - j : 2 - j + cols].reshape(wide, CH)
        value = mm(at_ref[:, 256 : 256 + wide], right)
        for i in range(3):
            split_cores(value[i * CH : i * CH + CH], keep_ref, send_ref, i * 3 + j)


def forward_kernel(
    count_ref, xt_ref, sp_ref, cott_ref, gy_ref, wt_ref, wd_ref, *rest
):
    down_ref, keep_ref, send_ref, y_ref, st_ref, yt_ref = rest[-6:]
    count = count_ref[0]
    rows, cols = xt_ref.shape[0], xt_ref.shape[1]
    def rows_of(q, _):
        s = sp_ref[pl.ds(8 * q, 8)].reshape(8 * cols * SLOTS, CH).astype(F32)
        s = s.reshape(8 * cols, SLOTS, CH)
        total = None
        for k in range(3):
            shifted = s if k == 2 else pltpu.roll(s, 2 - k, 1)
            shifted = shifted.astype(BF).reshape(8 * cols * SLOTS, CH)
            at = pl.ds(pl.multiple_of(q * 1024, 1024), 1024)
            st_ref[k * CH : k * CH + CH, at] = shifted.T
            term = mm(shifted, wt_ref[k])
            total = term if total is None else total + term
        x = xt_ref[pl.ds(8 * q, 8)].reshape(8 * cols, SLOTS, CH).astype(F32)
        y = jnp.where(slot_mask(x.shape, count), x + total.reshape(x.shape), 0.0).astype(BF)
        y_ref[pl.ds(8 * q, 8)] = y.reshape(8, cols, SLOTS, CH)
        return 0

    lax.fori_loop(0, rows // 8, rows_of, 0)

    wide = rows * cols * SLOTS
    value = mm(st_ref[...], gy_ref[...].reshape(wide, CH))
    for k in range(3):
        split_cores(value[k * CH : k * CH + CH], keep_ref, send_ref, k)

    small = wide // 4
    total = None
    for i in range(2):
        for j in range(2):
            tiles = [
                y_ref[2 * r + i, 2 * c + j] for r in range(rows // 2) for c in range(cols // 2)
            ]
            piece = jnp.concatenate(tiles, axis=0)
            k = i * 2 + j
            yt_ref[k * CH : k * CH + CH] = piece.T
            term = mm(piece, wd_ref[k])
            total = term if total is None else total + term
    down_ref[...] = total.astype(BF)
    value = mm(yt_ref[...], cott_ref[...].reshape(small, CH))
    for k in range(4):
        split_cores(value[k * CH : k * CH + CH], keep_ref, send_ref, 3 + k)


def grad_x_kernel(
    bands, count_ref, xt_ref, gy_ref, gs_ref, top_ref, bot_ref, wt_ref, wd_ref, ws_ref, slot_ref, *rest
):
    out_ref, down_ref, token_ref, pad_ref, buf, sems = rest[-6:]
    token_ref[...] = jnp.zeros_like(token_ref)
    count = count_ref[0]
    band = lax.axis_index("grp")
    rows, cols = xt_ref.shape[0], xt_ref.shape[1]
    pad_ref[1 : rows + 1] = gs_ref[...]
    edge = jnp.zeros((SLOTS, CH), BF)
    for ref, flag, i, row in ((top_ref, band > 0, 1, 0), (bot_ref, band < bands - 1, 0, rows + 1)):
        pair = [
            mm_nt(ref[...], wd_ref[i * 2 + j]).astype(BF).reshape(cols // 2, SLOTS, CH)
            for j in range(2)
        ]
        g = jnp.stack(pair, axis=1).reshape(cols, SLOTS, CH)
        pad_ref[row, 0] = edge
        pad_ref[row, 1 : cols + 1] = grad_of_temporal(g, wt_ref, jnp.where(flag, count, 0))
        pad_ref[row, cols + 1] = edge
    back = to_frames(16)

    def rows_of(q, _):
        total = None
        for i in range(3):
            for j in range(3):
                left = pad_ref[pl.ds(4 * q + 2 - i, 4), 2 - j : 2 - j + cols].reshape(
                    4 * cols * SLOTS, CH
                )
                term = mm_nt(left, ws_ref[i * 3 + j])
                total = term if total is None else total + term
        at = 4 * q
        v = xt_ref[pl.ds(at, 4)].reshape(4 * cols * SLOTS, CH).astype(F32)
        r = lax.rsqrt(jnp.mean(v * v, axis=-1, keepdims=True) + 1e-06)
        u = v * r
        s = 0.5 + 0.5 * jnp.tanh(0.5 * u)
        gu = total * (s * (1.0 + u * (1.0 - s)))
        dot = jnp.mean(gu * u, axis=-1, keepdims=True)
        gv = r * (gu - u * dot)
        gx = gy_ref[pl.ds(at, 4)].reshape(4 * cols * SLOTS, CH).astype(F32) + gv
        gx = gx.reshape(4 * cols, SLOTS, CH)
        gx = jnp.where(slot_mask(gx.shape, count), gx, 0.0).astype(BF).reshape(4 * cols * SLOTS, CH)
        for k in range(2):
            o = mm(back, gx[k * 256 : k * 256 + 256]).astype(BF)
            buf[:, pl.ds(pl.multiple_of((2 * q + k) * 16, 16), 16), :] = o.reshape(SLOTS, 16, CH)
        return 0

    lax.fori_loop(0, rows // 4, rows_of, 0)
    copy = pltpu.make_async_copy(buf, out_ref, sems.at[0])
    copy.start()
    for q in range(down_ref.shape[1] // 4):
        o = mm(back, slot_ref[q * 256 : q * 256 + 256]).astype(BF)
        down_ref[:, q * 4 : q * 4 + 4] = o.reshape(SLOTS, 4, cols // 2, CH)
    copy.wait()


ORDER = (0, 3, 2, 1)


def plane_send_kernel(keep_ref, got_ref, *rest):
    _, p, _ = place_bits()
    for r, out in zip(ORDER, rest[-4:]):
        at = pl.ds((p ^ r) * 4, 4)
        out[...] = (keep_ref[at].astype(F32) + got_ref[at].astype(F32)).astype(BF)


def line_send_kernel(*refs):
    outs = refs[8:]
    _, _, z = place_bits()
    for out, r in zip(outs, ORDER):
        at = 0
        for chain in (refs[:4], refs[4:8]):
            parts = [ref[z ^ r].astype(F32) for ref in chain]
            n = parts[0].shape[0]
            out[at : at + n] = (parts[0] + parts[1] + parts[2] + parts[3]).astype(BF)
            at += n


def line_sum_kernel(a_ref, b_ref, c_ref, d_ref, *rest):
    out_ref = rest[-1]
    parts = [ref[...].astype(F32) for ref in (a_ref, b_ref, c_ref, d_ref)]
    out_ref[...] = (parts[0] + parts[1] + parts[2] + parts[3]).astype(BF)


def line_gather_kernel(a_ref, b_ref, c_ref, d_ref, out_ref):
    _, _, z = place_bits()
    for r, ref in zip(ORDER, (a_ref, b_ref, c_ref, d_ref)):
        out_ref[z ^ r] = ref[...]


def plane_gather_kernel(a_ref, b_ref, c_ref, d_ref, _, out_ref):
    _, p, _ = place_bits()
    for r, ref in zip(ORDER, (a_ref, b_ref, c_ref, d_ref)):
        out_ref[pl.ds((p ^ r) * 4, 4)] = ref[...]


def add_kernel(a_ref, b_ref, out_ref):
    out_ref[...] = (a_ref[...].astype(F32) + b_ref[...].astype(F32)).astype(BF)


def pass_kernel(*_):
    pass


def finish_kernel(own, half_ref, *rest):
    buf, sems = rest[-2:]
    outs = rest[-5:-2]
    core, _, _ = place_bits()
    at = pl.multiple_of((core if own else 1 - core) * (CH // 2), CH // 2)
    copies = []
    k = 0
    for out in outs:
        for m in range(out.shape[0]):
            buf[k] = half_ref[:, k].reshape(CH, CH // 2).astype(F32)
            copies.append(
                pltpu.make_async_copy(buf.at[k], out.at[m, :, pl.ds(at, CH // 2)], sems.at[k])
            )
            copies[-1].start()
            k += 1
    for copy in copies:
        copy.wait()


VMEM = pl.BlockSpec(memory_space=pltpu.VMEM)
SMEM = pl.BlockSpec(memory_space=pltpu.SMEM)
ANY = pl.BlockSpec(memory_space=pl.ANY)
HBM = pl.BlockSpec(memory_space=pltpu.HBM)
TOKEN = (VMEM, (8, 128), F32)


def call(kernel, name, ins, outs, scratch=(), flops=0, alias=None, grant=10):
    shapes = [jax.ShapeDtypeStruct(o[1], o[2] if len(o) > 2 else BF) for o in outs]
    moved = sum(a.size * a.dtype.itemsize for s, a in ins if s is not ANY)
    moved += sum(s.size * s.dtype.itemsize for s in shapes)
    return pl.pallas_call(
        kernel,
        out_shape=shapes,
        in_specs=[s for s, _ in ins],
        out_specs=[o[0] for o in outs],
        scratch_shapes=list(scratch),
        compiler_params=pltpu.CompilerParams(vmem_limit_bytes=grant * 2**20),
        cost_estimate=pl.CostEstimate(flops=flops, bytes_accessed=moved, transcendentals=0),
        input_output_aliases=alias or {},
        name=name,
    )(*[a for _, a in ins])


AXES = ("tm", "grp")


def plan(tm, grp):
    low, total = grp.bit_length() - 1, (tm * grp).bit_length() - 1
    plane, line = [low + 1, 0], [low + 2, low + 3]
    return low, plane, line, [b for b in range(total) if b not in [low] + plane + line]


def swap(value, tm, grp, *bits):
    flip = sum(1 << b for b in bits)
    return lax.ppermute(value, AXES, [(d, d ^ flip) for d in range(tm * grp)])


def core_round(value, tm, grp):
    return swap(value, tm, grp, plan(tm, grp)[0])


def four_round(parts, bits, tm, grp):
    return [
        parts[0],
        swap(parts[1], tm, grp, *bits),
        swap(parts[2], tm, grp, bits[1]),
        swap(parts[3], tm, grp, bits[0]),
    ]


def plane_send(keep, got, after):
    ins = [(VMEM, keep), (VMEM, got)] + [(ANY, a) for a in after]
    shape = (4, keep.shape[1], 16, CH // 2)
    return list(call(plane_send_kernel, "plane_send", ins, [(VMEM, shape)] * 4))


def passed(value, after):
    ins = [(ANY, value)] + [(ANY, a) for a in after]
    return call(pass_kernel, "pass", ins, [(ANY, value.shape)], alias={0: 0})[0]


def finish(own, half, before):
    n = half.shape[1]
    return list(
        call(
            functools.partial(finish_kernel, own),
            "finish",
            [(VMEM, half)] + [(HBM, a) for a in before],
            [(HBM, (m, CH, CH), F32) for m in (9, 3, 4)],
            [pltpu.VMEM((n, CH, CH // 2), F32), pltpu.SemaphoreType.DMA((n,))],
            alias={1 + i: i for i in range(len(before))},
        )
    )


def along(value, axis, by):
    count = lax.axis_size(axis)
    pairs = [(i, i + by) for i in range(count) if 0 <= i + by < count]
    return lax.ppermute(value, axis, pairs)


def around(value, axis, by):
    count = lax.axis_size(axis)
    return lax.ppermute(value, axis, [(i, (i + by) % count) for i in range(count)])


def from_bands(parts):
    if len(parts) == 1:
        got = lax.ppermute(parts[0], "grp", [(0, 1), (1, 0)])
        return got, got
    return along(parts[0], "grp", 1), along(parts[1], "grp", -1)


def body(tm, grp, frames_in, span_frames, w_spatial, w_temporal, w_down, cotangent):
    slots, rows, cols, ch = frames_in.shape
    wide = rows * cols
    x = frames_in.reshape(slots, wide, ch)
    ws = w_spatial.reshape(9, ch, ch)
    wd = w_down.reshape(4, ch, ch)
    wt = w_temporal
    count = (SMEM, span_frames)
    tap = 2 * slots * wide * ch * ch
    tile = (rows, cols, slots, ch)
    padded = (rows + 2, cols + 2, slots, ch)
    dma = pltpu.SemaphoreType.DMA

    sides = 1 if grp == 2 else 2
    *edge, nxt = call(
        functools.partial(edges_kernel, grp),
        "edges",
        [count, (VMEM, x), (VMEM, cotangent)],
        [(VMEM, (cols * slots, ch))] * sides + [(VMEM, (2,) + cotangent.shape[1:])],
        flops=tap // 8,
    )
    top, bot = from_bands(edge)
    nxt_got = around(nxt, "tm", -1)
    last_shape = (2 * wide + 32, ch)
    at_shape = (3 * ch, (rows + 4) * 128)
    xt, acts, at, last_two = call(
        acts_kernel,
        "acts",
        [count, (VMEM, x), (ANY, edge[0])],
        [(VMEM, tile), (VMEM, padded), (VMEM, at_shape), (VMEM, last_shape)],
        flops=2 * tap,
    )
    acts, at, last_two = call(
        functools.partial(halo_kernel, grp),
        "halo",
        [count, (VMEM, top), (VMEM, bot), (VMEM, acts), (VMEM, at), (VMEM, last_two)],
        [(VMEM, padded), (VMEM, at_shape), (VMEM, last_shape)],
        flops=tap // 8,
        alias={3: 0, 4: 1, 5: 2},
    )
    prev = around(last_two, "tm", 1)
    half = (16, 9, 16, ch // 2)
    cott, gy, gs, keep_a, send_a, *edge = call(
        functools.partial(grad_spatial_kernel, tm, grp),
        "grad_spatial",
        [count, (VMEM, at), (VMEM, cotangent), (VMEM, nxt_got), (VMEM, wt), (VMEM, wd)],
        [(VMEM, (rows // 2, cols // 2, slots, ch)), (VMEM, tile),
         (VMEM, (rows, cols + 2, slots, ch)), (VMEM, half), (VMEM, half)]
        + [(VMEM, (cols // 2 * slots, ch))] * sides,
        flops=14 * tap,
    )
    send_a = passed(send_a, [prev])
    got_a = core_round(send_a, tm, grp)
    cot_top, cot_bot = from_bands(edge)
    acts, sp = call(
        spatial_kernel,
        "spatial",
        [count, (VMEM, acts), (VMEM, prev), (VMEM, ws), (ANY, send_a)],
        [(VMEM, padded), (VMEM, tile)],
        flops=9 * tap,
        alias={1: 0},
    )
    _, plane, line, others = plan(tm, grp)
    parts_a = plane_send(keep_a, got_a, [sp])
    half = (16, 7, 16, ch // 2)
    down, keep_b, send_b = call(
        forward_kernel,
        "forward",
        [count, (VMEM, xt), (VMEM, sp), (VMEM, cott), (VMEM, gy), (VMEM, wt), (VMEM, wd),
         *((ANY, a) for a in parts_a)],
        [(VMEM, (slots * wide // 4, ch)), (VMEM, half), (VMEM, half)],
        [pltpu.VMEM(v, BF) for v in (tile, (3 * ch, slots * wide), (4 * ch, slots * wide // 4))],
        flops=10 * tap,
        grant=14,
    )
    parts_a = four_round(parts_a, plane, tm, grp)
    send_b = passed(send_b, parts_a[3:4])
    parts_b = plane_send(keep_b, core_round(send_b, tm, grp), [])
    parts_b = four_round(parts_b, plane, tm, grp)
    parts = call(
        line_send_kernel,
        "line_send",
        [(VMEM, a) for a in parts_a + parts_b],
        [(VMEM, (16, 16, ch // 2))] * 4,
    )
    parts = four_round(list(parts), line, tm, grp)
    ins = [(VMEM, a) for a in parts] + [(ANY, a) for a in [cot_top, cot_bot][:sides]]
    (mine,) = call(line_sum_kernel, "line_sum", ins, [(VMEM, parts[0].shape)])
    for bit in others:
        got = swap(mine, tm, grp, bit)
        (mine,) = call(add_kernel, "add", [(VMEM, mine), (VMEM, got)], [(VMEM, mine.shape)])
    parts = four_round([mine] * 4, line, tm, grp)
    (mine,) = call(
        line_gather_kernel, "line_gather", [(VMEM, a) for a in parts], [(VMEM, (4,) + mine.shape)]
    )
    parts = four_round([mine] * 4, plane, tm, grp)
    grad_x, down, token = call(
        functools.partial(grad_x_kernel, grp),
        "grad_x",
        [count, (VMEM, xt), (VMEM, gy), (VMEM, gs), (VMEM, cot_top), (VMEM, cot_bot), (VMEM, wt),
         (VMEM, wd), (VMEM, ws), (VMEM, down), (ANY, mine)],
        [(HBM, (slots, wide, ch)), (VMEM, cotangent.shape), TOKEN],
        [pltpu.VMEM(padded, BF), pltpu.VMEM((slots, wide, ch), BF), dma((1,))],
        flops=10 * tap,
    )
    ins = [(VMEM, a) for a in parts] + [(ANY, token)]
    (mine,) = call(plane_gather_kernel, "plane_gather", ins, [(VMEM, (16,) + mine.shape[1:])])
    got = core_round(mine, tm, grp)
    outs = finish(True, mine, [])
    sum_s, sum_t, sum_d = finish(False, got, outs)
    return (
        down,
        grad_x.reshape(frames_in.shape),
        sum_s.reshape(w_spatial.shape),
        sum_t,
        sum_d.reshape(w_down.shape),
    )


def solution(mesh):
    return jax.shard_map(
        functools.partial(body, mesh.shape["tm"], mesh.shape["grp"]),
        mesh=mesh,
        in_specs=(P("tm", "grp", None, None), P("tm"), P(), P(), P(), P("tm", "grp", None, None)),
        out_specs=(P("tm", "grp", None, None), P("tm", "grp", None, None), P(), P(), P()),
        check_vma=False,
    )
```

```python
import functools

import jax
import jax.numpy as jnp
from jax import lax
from jax.experimental import pallas as pl
from jax.experimental.pallas import tpu as pltpu
from jax.sharding import PartitionSpec as P

SLOTS = 16
OWN = 14
CH = 256
BF = jnp.bfloat16
F32 = jnp.float32


def mm(a, b):
    return lax.dot_general(a, b, (((1,), (0,)), ((), ())), preferred_element_type=F32)


def mm_nt(a, b):
    return lax.dot_general(a, b, (((1,), (1,)), ((), ())), preferred_element_type=F32)


def iotas(rows, cols):
    return (
        lax.broadcasted_iota(jnp.int32, (rows, cols), 0),
        lax.broadcasted_iota(jnp.int32, (rows, cols), 1),
    )


def to_slots(rows, frames, keep):
    a, b = iotas(rows * SLOTS, frames * rows)
    bits = rows.bit_length() - 1
    hit = ((a >> 4) == (b & (rows - 1))) & keep(b >> bits, a & 15)
    return jnp.where(hit, 1.0, 0.0).astype(BF)


def to_frames(rows):
    a, b = iotas(SLOTS * rows, rows * SLOTS)
    bits = rows.bit_length() - 1
    hit = ((a & (rows - 1)) == (b >> 4)) & ((a >> bits) == (b & 15))
    return jnp.where(hit, 1.0, 0.0).astype(BF)


def own_frames(count):
    return lambda frame, slot: (frame == slot) & (slot < count)


def own_and_next(count, blocks):
    after = jnp.where(lax.axis_index("tm") < blocks - 1, count, 64)
    return lambda frame, slot: ((frame < OWN) & (frame == slot) & (slot < count)) | (
        (frame >= OWN) & (slot == after + frame - OWN)
    )


def silu_norm(v):
    scaled = v * lax.rsqrt(jnp.mean(v * v, axis=-1, keepdims=True) + 1e-06)
    return scaled * (0.5 + 0.5 * jnp.tanh(0.5 * scaled))


def slot_mask(shape, count):
    return lax.broadcasted_iota(jnp.int32, shape, len(shape) - 2) < count


def grad_of_temporal(gy, wt_ref, count):
    n = gy.shape[0]
    flat = gy.reshape(n * SLOTS, CH)
    total = mm_nt(flat, wt_ref[2]).reshape(n, SLOTS, CH)
    for k in (1, 0):
        term = mm_nt(flat, wt_ref[k]).reshape(n, SLOTS, CH)
        total = total + pltpu.roll(term, SLOTS - (2 - k), 1)
    return jnp.where(slot_mask(total.shape, count), total, 0.0).astype(BF)


def place_bits():
    t, g = lax.axis_index("tm"), lax.axis_index("grp")
    return t & 1, ((t >> 1) & 1) + 2 * (g & 1), (t >> 2) & 3


def split_cores(value, keep_ref, send_ref, k):
    core, _, _ = place_bits()
    low, high = value[:, : CH // 2].astype(BF), value[:, CH // 2 :].astype(BF)
    keep_ref[:, k] = jnp.where(core == 0, low, high).reshape(16, 16, CH // 2)
    send_ref[:, k] = jnp.where(core == 0, high, low).reshape(16, 16, CH // 2)


def edges_kernel(bands, count_ref, x_ref, cot_ref, *rest):
    outs, nxt_ref = rest[:-1], rest[-1]
    nxt_ref[...] = cot_ref[0:2]
    count = count_ref[0]
    band = lax.axis_index("grp")
    wide = x_ref.shape[1]
    if bands == 2:
        starts, lower = [jnp.where(band == 0, wide - 16, 0)], [band == 0]
    else:
        starts, lower = [wide - 16, 0], [True, False]
    place = to_slots(16, SLOTS, own_frames(count))
    for k, at in enumerate(starts):
        piece = x_ref[:, pl.ds(pl.multiple_of(at, 16), 16), :].reshape(SLOTS * 16, CH)
        v = mm(place, piece)
        v = jnp.where(lower[k], v[128:], v[:128])
        outs[k][...] = silu_norm(v).astype(BF)


def acts_kernel(count_ref, x_ref, _, xt_ref, acts_ref, at_ref, last_ref):
    count = count_ref[0]
    rows, cols = xt_ref.shape[0], xt_ref.shape[1]
    edge = jnp.zeros((rows + 2, SLOTS, CH), BF)
    acts_ref[:, 0] = edge
    acts_ref[:, cols + 1] = edge
    place = to_slots(16, SLOTS, own_frames(count))
    last = silu_norm(x_ref[pl.ds(count - 2, 2)].reshape(2 * rows * cols, CH).astype(F32))
    last_ref[0 : 2 * rows * cols] = last.astype(BF)

    def rows_of(q, _):
        at = pl.multiple_of(q * 16, 16)
        piece = x_ref[:, pl.ds(at, 16), :].reshape(SLOTS * 16, CH)
        v = mm(place, piece)
        xt_ref[pl.ds(2 * q, 2)] = v.astype(BF).reshape(2, cols, SLOTS, CH)
        a = silu_norm(v).astype(BF)
        acts_ref[pl.ds(2 * q + 1, 2), 1 : cols + 1] = a.reshape(2, cols, SLOTS, CH)
        flipped = a.T
        for i in range(3):
            at = pl.multiple_of((2 * q + 3 - i) * 128, 128)
            at_ref[i * CH : i * CH + CH, pl.ds(at, 256)] = flipped
        return 0

    lax.fori_loop(0, rows // 2, rows_of, 0, unroll=4)


def halo_kernel(bands, count_ref, top_ref, bot_ref, *rest):
    acts_ref, at_ref, last_ref = rest[-3:]
    count = count_ref[0]
    band = lax.axis_index("grp")
    rows, cols = acts_ref.shape[0] - 2, acts_ref.shape[1] - 2
    halo = []
    for ref, flag, i, row in ((top_ref, band > 0, 0, 0), (bot_ref, band < bands - 1, 2, rows + 1)):
        a = jnp.where(flag, ref[...].astype(F32), 0.0).astype(BF)
        acts_ref[row, 1 : cols + 1] = a.reshape(cols, SLOTS, CH)
        at = (row - i + 2) * 128
        at_ref[i * CH : i * CH + CH, at : at + 128] = a.T
        halo.append(a)
    a, b = iotas(32, 256)
    pick = ((a & 15) == (b >> 4)) & ((b & 15) == count - 2 + (a >> 4))
    pick = jnp.where(pick, 1.0, 0.0).astype(BF)
    last_ref[2 * rows * cols :] = mm(pick, jnp.concatenate(halo, 0)).astype(BF)


def spatial_kernel(count_ref, acts_in, prev_ref, ws_ref, _, acts_ref, sp_ref):
    rows, cols = sp_ref.shape[0], sp_ref.shape[1]
    a, b = iotas(256, 32)
    place = ((a >> 4) == (b & 15)) & ((a & 15) == OWN + (b >> 4)) & (lax.axis_index("tm") > 0)
    place = jnp.where(place, 1.0, 0.0).astype(BF)
    size = rows * cols
    for q in range(rows // 2 + 1):
        if q == rows // 2:
            both, prev = slice(0, rows + 2, rows + 1), prev_ref[2 * size :]
        else:
            both = slice(2 * q + 1, 2 * q + 3)
            parts = [prev_ref[f * size + q * 16 : f * size + q * 16 + 16] for f in range(2)]
            prev = jnp.concatenate(parts, 0)
        prev = mm(place, prev).astype(BF).reshape(2, cols, SLOTS, CH)
        for k, row in enumerate(range(rows + 2)[both]):
            acts_ref[row, 1 : cols + 1] = acts_ref[row, 1 : cols + 1] + prev[k]

    def rows_of(q, _):
        total = None
        for i in range(3):
            for j in range(3):
                left = acts_ref[pl.ds(4 * q + i, 4), j : j + cols].reshape(4 * cols * SLOTS, CH)
                term = mm(left, ws_ref[i * 3 + j])
                total = term if total is None else total + term
        sp_ref[pl.ds(4 * q, 4)] = total.astype(BF).reshape(4, cols, SLOTS, CH)
        return 0

    lax.fori_loop(0, rows // 4, rows_of, 0)


def grad_spatial_kernel(
    blocks, bands, count_ref, at_ref, cot_ref, nxt_ref, wt_ref, wd_ref,
    cott_ref, gy_ref, gs_ref, keep_ref, send_ref, *edge_refs,
):
    count = count_ref[0]
    band = lax.axis_index("grp")
    rows, cols = gy_ref.shape[0], gy_ref.shape[1]
    edge = jnp.zeros((rows, SLOTS, CH), BF)
    gs_ref[:, 0] = edge
    gs_ref[:, cols + 1] = edge

    place_next = to_slots(16, SLOTS, own_and_next(count, blocks))
    halves = []
    for q in range(rows * cols // 64):
        four = slice(q * 4, q * 4 + 4)
        piece = jnp.concatenate(
            [cot_ref[0:OWN, four].reshape(OWN, 16, CH), nxt_ref[:, four].reshape(2, 16, CH)], 0
        ).reshape(SLOTS * 16, CH)
        halves.append(mm(place_next, piece).astype(BF))
    placed = jnp.concatenate(halves, 0)
    cott_ref[...] = placed.reshape(rows // 2, cols // 2, SLOTS, CH)
    for i in range(2):
        for j in range(2):
            g = mm_nt(placed, wd_ref[i * 2 + j]).astype(BF).reshape(rows // 2, cols // 2, SLOTS, CH)
            for r in range(rows // 2):
                for c in range(cols // 2):
                    gy_ref[2 * r + i, 2 * c + j] = g[r, c]
    last = cott_ref[rows // 2 - 1].reshape(cols // 2 * SLOTS, CH)
    first = cott_ref[0].reshape(cols // 2 * SLOTS, CH)
    if bands == 2:
        edge_refs[0][...] = jnp.where(band == 0, last, first)
    else:
        edge_refs[0][...] = last
        edge_refs[1][...] = first

    def grads_of(q, _):
        g = gy_ref[pl.ds(8 * q, 8)].reshape(8 * cols, SLOTS, CH)
        s = grad_of_temporal(g, wt_ref, count)
        gs_ref[pl.ds(8 * q, 8), 1 : cols + 1] = s.reshape(8, cols, SLOTS, CH)
        g = jnp.where(slot_mask(g.shape, count), g.astype(F32), 0.0)
        gy_ref[pl.ds(8 * q, 8)] = g.astype(BF).reshape(8, cols, SLOTS, CH)
        return 0

    lax.fori_loop(0, rows // 8, grads_of, 0)

    wide = rows * cols * SLOTS
    for j in range(3):
        right = gs_ref[:, 2 - j : 2 - j + cols].reshape(wide, CH)
        value = mm(at_ref[:, 256 : 256 + wide], right)
        for i in range(3):
            split_cores(value[i * CH : i * CH + CH], keep_ref, send_ref, i * 3 + j)


def forward_kernel(
    count_ref, xt_ref, sp_ref, cott_ref, gy_ref, wt_ref, wd_ref, *rest
):
    down_ref, keep_ref, send_ref, y_ref, st_ref, yt_ref = rest[-6:]
    count = count_ref[0]
    rows, cols = xt_ref.shape[0], xt_ref.shape[1]
    def rows_of(q, _):
        s = sp_ref[pl.ds(8 * q, 8)].reshape(8 * cols * SLOTS, CH).astype(F32)
        s = s.reshape(8 * cols, SLOTS, CH)
        total = None
        for k in range(3):
            shifted = s if k == 2 else pltpu.roll(s, 2 - k, 1)
            shifted = shifted.astype(BF).reshape(8 * cols * SLOTS, CH)
            at = pl.ds(pl.multiple_of(q * 1024, 1024), 1024)
            st_ref[k * CH : k * CH + CH, at] = shifted.T
            term = mm(shifted, wt_ref[k])
            total = term if total is None else total + term
        x = xt_ref[pl.ds(8 * q, 8)].reshape(8 * cols, SLOTS, CH).astype(F32)
        y = jnp.where(slot_mask(x.shape, count), x + total.reshape(x.shape), 0.0).astype(BF)
        y_ref[pl.ds(8 * q, 8)] = y.reshape(8, cols, SLOTS, CH)
        return 0

    lax.fori_loop(0, rows // 8, rows_of, 0)

    wide = rows * cols * SLOTS
    value = mm(st_ref[...], gy_ref[...].reshape(wide, CH))
    for k in range(3):
        split_cores(value[k * CH : k * CH + CH], keep_ref, send_ref, k)

    small = wide // 4
    total = None
    for i in range(2):
        for j in range(2):
            tiles = [
                y_ref[2 * r + i, 2 * c + j] for r in range(rows // 2) for c in range(cols // 2)
            ]
            piece = jnp.concatenate(tiles, axis=0)
            k = i * 2 + j
            yt_ref[k * CH : k * CH + CH] = piece.T
            term = mm(piece, wd_ref[k])
            total = term if total is None else total + term
    down_ref[...] = total.astype(BF)
    value = mm(yt_ref[...], cott_ref[...].reshape(small, CH))
    for k in range(4):
        split_cores(value[k * CH : k * CH + CH], keep_ref, send_ref, 3 + k)


def grad_x_kernel(
    bands, count_ref, xt_ref, gy_ref, gs_ref, top_ref, bot_ref, wt_ref, wd_ref, ws_ref, slot_ref, *rest
):
    out_ref, down_ref, token_ref, pad_ref, buf, sems = rest[-6:]
    token_ref[...] = jnp.zeros_like(token_ref)
    count = count_ref[0]
    band = lax.axis_index("grp")
    rows, cols = xt_ref.shape[0], xt_ref.shape[1]
    pad_ref[1 : rows + 1] = gs_ref[...]
    edge = jnp.zeros((SLOTS, CH), BF)
    for ref, flag, i, row in ((top_ref, band > 0, 1, 0), (bot_ref, band < bands - 1, 0, rows + 1)):
        pair = [
            mm_nt(ref[...], wd_ref[i * 2 + j]).astype(BF).reshape(cols // 2, SLOTS, CH)
            for j in range(2)
        ]
        g = jnp.stack(pair, axis=1).reshape(cols, SLOTS, CH)
        pad_ref[row, 0] = edge
        pad_ref[row, 1 : cols + 1] = grad_of_temporal(g, wt_ref, jnp.where(flag, count, 0))
        pad_ref[row, cols + 1] = edge
    back = to_frames(16)

    def rows_of(q, _):
        total = None
        for i in range(3):
            for j in range(3):
                left = pad_ref[pl.ds(4 * q + 2 - i, 4), 2 - j : 2 - j + cols].reshape(
                    4 * cols * SLOTS, CH
                )
                term = mm_nt(left, ws_ref[i * 3 + j])
                total = term if total is None else total + term
        at = 4 * q
        v = xt_ref[pl.ds(at, 4)].reshape(4 * cols * SLOTS, CH).astype(F32)
        r = lax.rsqrt(jnp.mean(v * v, axis=-1, keepdims=True) + 1e-06)
        u = v * r
        s = 0.5 + 0.5 * jnp.tanh(0.5 * u)
        gu = total * (s * (1.0 + u * (1.0 - s)))
        dot = jnp.mean(gu * u, axis=-1, keepdims=True)
        gv = r * (gu - u * dot)
        gx = gy_ref[pl.ds(at, 4)].reshape(4 * cols * SLOTS, CH).astype(F32) + gv
        gx = gx.reshape(4 * cols, SLOTS, CH)
        gx = jnp.where(slot_mask(gx.shape, count), gx, 0.0).astype(BF).reshape(4 * cols * SLOTS, CH)
        for k in range(2):
            o = mm(back, gx[k * 256 : k * 256 + 256]).astype(BF)
            buf[:, pl.ds(pl.multiple_of((2 * q + k) * 16, 16), 16), :] = o.reshape(SLOTS, 16, CH)
        return 0

    lax.fori_loop(0, rows // 4, rows_of, 0)
    copy = pltpu.make_async_copy(buf, out_ref, sems.at[0])
    copy.start()
    for q in range(down_ref.shape[1] // 4):
        o = mm(back, slot_ref[q * 256 : q * 256 + 256]).astype(BF)
        down_ref[:, q * 4 : q * 4 + 4] = o.reshape(SLOTS, 4, cols // 2, CH)
    copy.wait()


ORDER = (0, 3, 2, 1)


def plane_send_kernel(keep_ref, got_ref, *rest):
    _, p, _ = place_bits()
    for r, out in zip(ORDER, rest[-4:]):
        at = pl.ds((p ^ r) * 4, 4)
        out[...] = (keep_ref[at].astype(F32) + got_ref[at].astype(F32)).astype(BF)


def line_send_kernel(*refs):
    outs = refs[8:]
    _, _, z = place_bits()
    for out, r in zip(outs, ORDER):
        at = 0
        for chain in (refs[:4], refs[4:8]):
            parts = [ref[z ^ r].astype(F32) for ref in chain]
            n = parts[0].shape[0]
            out[at : at + n] = (parts[0] + parts[1] + parts[2] + parts[3]).astype(BF)
            at += n


def line_sum_kernel(a_ref, b_ref, c_ref, d_ref, *rest):
    out_ref = rest[-1]
    parts = [ref[...].astype(F32) for ref in (a_ref, b_ref, c_ref, d_ref)]
    out_ref[...] = (parts[0] + parts[1] + parts[2] + parts[3]).astype(BF)


def line_gather_kernel(a_ref, b_ref, c_ref, d_ref, out_ref):
    _, _, z = place_bits()
    for r, ref in zip(ORDER, (a_ref, b_ref, c_ref, d_ref)):
        out_ref[z ^ r] = ref[...]


def plane_gather_kernel(a_ref, b_ref, c_ref, d_ref, _, out_ref):
    _, p, _ = place_bits()
    for r, ref in zip(ORDER, (a_ref, b_ref, c_ref, d_ref)):
        out_ref[pl.ds((p ^ r) * 4, 4)] = ref[...]


def add_kernel(a_ref, b_ref, out_ref):
    out_ref[...] = (a_ref[...].astype(F32) + b_ref[...].astype(F32)).astype(BF)


def pass_kernel(*_):
    pass


def finish_kernel(own, half_ref, *rest):
    buf, sems = rest[-2:]
    outs = rest[-5:-2]
    core, _, _ = place_bits()
    at = pl.multiple_of((core if own else 1 - core) * (CH // 2), CH // 2)
    copies = []
    k = 0
    for out in outs:
        for m in range(out.shape[0]):
            buf[k] = half_ref[:, k].reshape(CH, CH // 2).astype(F32)
            copies.append(
                pltpu.make_async_copy(buf.at[k], out.at[m, :, pl.ds(at, CH // 2)], sems.at[k])
            )
            copies[-1].start()
            k += 1
    for copy in copies:
        copy.wait()


VMEM = pl.BlockSpec(memory_space=pltpu.VMEM)
SMEM = pl.BlockSpec(memory_space=pltpu.SMEM)
ANY = pl.BlockSpec(memory_space=pl.ANY)
HBM = pl.BlockSpec(memory_space=pltpu.HBM)
TOKEN = (VMEM, (8, 128), F32)


def call(kernel, name, ins, outs, scratch=(), flops=0, alias=None, grant=10, moved=None):
    shapes = [jax.ShapeDtypeStruct(o[1], o[2] if len(o) > 2 else BF) for o in outs]
    if moved is None:
        moved = sum(a.size * a.dtype.itemsize for s, a in ins if s is not ANY)
        moved += sum(s.size * s.dtype.itemsize for s in shapes)
    return pl.pallas_call(
        kernel,
        out_shape=shapes,
        in_specs=[s for s, _ in ins],
        out_specs=[o[0] for o in outs],
        scratch_shapes=list(scratch),
        compiler_params=pltpu.CompilerParams(vmem_limit_bytes=grant * 2**20),
        cost_estimate=pl.CostEstimate(flops=flops, bytes_accessed=moved, transcendentals=0),
        input_output_aliases=alias or {},
        name=name,
    )(*[a for _, a in ins])


AXES = ("tm", "grp")


def plan(tm, grp):
    low, total = grp.bit_length() - 1, (tm * grp).bit_length() - 1
    plane, line = [low + 1, 0], [low + 2, low + 3]
    return low, plane, line, [b for b in range(total) if b not in [low] + plane + line]


def swap(value, tm, grp, *bits):
    flip = sum(1 << b for b in bits)
    return lax.ppermute(value, AXES, [(d, d ^ flip) for d in range(tm * grp)])


def core_round(value, tm, grp):
    return swap(value, tm, grp, plan(tm, grp)[0])


def four_round(parts, bits, tm, grp):
    return [
        parts[0],
        swap(parts[1], tm, grp, *bits),
        swap(parts[2], tm, grp, bits[1]),
        swap(parts[3], tm, grp, bits[0]),
    ]


def plane_send(keep, got, after):
    ins = [(VMEM, keep), (VMEM, got)] + [(ANY, a) for a in after]
    shape = (4, keep.shape[1], 16, CH // 2)
    return list(call(plane_send_kernel, "plane_send", ins, [(VMEM, shape)] * 4))


def passed(value, after):
    ins = [(ANY, value)] + [(ANY, a) for a in after]
    return call(pass_kernel, "pass", ins, [(ANY, value.shape)], alias={0: 0})[0]


def finish(own, half, before):
    n = half.shape[1]
    return list(
        call(
            functools.partial(finish_kernel, own),
            "finish",
            [(VMEM, half)] + [(HBM, a) for a in before],
            [(HBM, (m, CH, CH), F32) for m in (9, 3, 4)],
            [pltpu.VMEM((n, CH, CH // 2), F32), pltpu.SemaphoreType.DMA((n,))],
            alias={1 + i: i for i in range(len(before))},
        )
    )


def along(value, axis, by):
    count = lax.axis_size(axis)
    pairs = [(i, i + by) for i in range(count) if 0 <= i + by < count]
    return lax.ppermute(value, axis, pairs)


def around(value, axis, by):
    count = lax.axis_size(axis)
    return lax.ppermute(value, axis, [(i, (i + by) % count) for i in range(count)])


def from_bands(parts):
    if len(parts) == 1:
        got = lax.ppermute(parts[0], "grp", [(0, 1), (1, 0)])
        return got, got
    return along(parts[0], "grp", 1), along(parts[1], "grp", -1)


def body(tm, grp, frames_in, span_frames, w_spatial, w_temporal, w_down, cotangent):
    slots, rows, cols, ch = frames_in.shape
    wide = rows * cols
    x = frames_in.reshape(slots, wide, ch)
    ws = w_spatial.reshape(9, ch, ch)
    wd = w_down.reshape(4, ch, ch)
    wt = w_temporal
    count = (SMEM, span_frames)
    tap = 2 * slots * wide * ch * ch
    tile = (rows, cols, slots, ch)
    padded = (rows + 2, cols + 2, slots, ch)
    dma = pltpu.SemaphoreType.DMA

    sides = 1 if grp == 2 else 2
    *edge, nxt = call(
        functools.partial(edges_kernel, grp),
        "edges",
        [count, (VMEM, x), (VMEM, cotangent)],
        [(VMEM, (cols * slots, ch))] * sides + [(VMEM, (2,) + cotangent.shape[1:])],
        flops=tap // 8,
    )
    top, bot = from_bands(edge)
    nxt_got = around(nxt, "tm", -1)
    last_shape = (2 * wide + 32, ch)
    at_shape = (3 * ch, (rows + 4) * 128)
    xt, acts, at, last_two = call(
        acts_kernel,
        "acts",
        [count, (VMEM, x), (ANY, edge[0])],
        [(VMEM, tile), (VMEM, padded), (VMEM, at_shape), (VMEM, last_shape)],
        flops=2 * tap,
    )
    acts, at, last_two = call(
        functools.partial(halo_kernel, grp),
        "halo",
        [count, (VMEM, top), (VMEM, bot), (VMEM, acts), (VMEM, at), (VMEM, last_two),
         (VMEM, cotangent), (VMEM, wt), (VMEM, wd)],
        [(VMEM, padded), (VMEM, at_shape), (VMEM, last_shape)],
        alias={3: 0, 4: 1, 5: 2},
        moved=1024,
    )
    prev = around(last_two, "tm", 1)
    half = (16, 9, 16, ch // 2)
    cott, gy, gs, keep_a, send_a, *edge = call(
        functools.partial(grad_spatial_kernel, tm, grp),
        "grad_spatial",
        [count, (VMEM, at), (VMEM, cotangent), (VMEM, nxt_got), (VMEM, wt), (VMEM, wd)],
        [(VMEM, (rows // 2, cols // 2, slots, ch)), (VMEM, tile),
         (VMEM, (rows, cols + 2, slots, ch)), (VMEM, half), (VMEM, half)]
        + [(VMEM, (cols // 2 * slots, ch))] * sides,
        flops=14 * tap,
    )
    send_a = passed(send_a, [prev])
    got_a = core_round(send_a, tm, grp)
    cot_top, cot_bot = from_bands(edge)
    acts, sp = call(
        spatial_kernel,
        "spatial",
        [count, (VMEM, acts), (VMEM, prev), (VMEM, ws), (ANY, send_a)],
        [(VMEM, padded), (VMEM, tile)],
        flops=9 * tap,
        alias={1: 0},
    )
    _, plane, line, others = plan(tm, grp)
    parts_a = plane_send(keep_a, got_a, [sp])
    half = (16, 7, 16, ch // 2)
    down, keep_b, send_b = call(
        forward_kernel,
        "forward",
        [count, (VMEM, xt), (VMEM, sp), (VMEM, cott), (VMEM, gy), (VMEM, wt), (VMEM, wd),
         *((ANY, a) for a in parts_a)],
        [(VMEM, (slots * wide // 4, ch)), (VMEM, half), (VMEM, half)],
        [pltpu.VMEM(v, BF) for v in (tile, (3 * ch, slots * wide), (4 * ch, slots * wide // 4))],
        flops=10 * tap,
        grant=14,
    )
    parts_a = four_round(parts_a, plane, tm, grp)
    send_b = passed(send_b, parts_a[1:2])
    parts_b = plane_send(keep_b, core_round(send_b, tm, grp), [])
    parts_b = four_round(parts_b, plane, tm, grp)
    parts = call(
        line_send_kernel,
        "line_send",
        [(VMEM, a) for a in parts_a + parts_b],
        [(VMEM, (16, 16, ch // 2))] * 4,
    )
    parts = four_round(list(parts), line, tm, grp)
    ins = [(VMEM, a) for a in parts]
    (mine,) = call(line_sum_kernel, "line_sum", ins, [(VMEM, parts[0].shape)])
    for bit in others:
        got = swap(mine, tm, grp, bit)
        (mine,) = call(add_kernel, "add", [(VMEM, mine), (VMEM, got)], [(VMEM, mine.shape)])
    parts = four_round([mine] * 4, line, tm, grp)
    (mine,) = call(
        line_gather_kernel, "line_gather", [(VMEM, a) for a in parts], [(VMEM, (4,) + mine.shape)]
    )
    parts = four_round([mine] * 4, plane, tm, grp)
    grad_x, down, token = call(
        functools.partial(grad_x_kernel, grp),
        "grad_x",
        [count, (VMEM, xt), (VMEM, gy), (VMEM, gs), (VMEM, cot_top), (VMEM, cot_bot), (VMEM, wt),
         (VMEM, wd), (VMEM, ws), (VMEM, down), (ANY, mine)],
        [(HBM, (slots, wide, ch)), (VMEM, cotangent.shape), TOKEN],
        [pltpu.VMEM(padded, BF), pltpu.VMEM((slots, wide, ch), BF), dma((1,))],
        flops=10 * tap,
    )
    ins = [(VMEM, a) for a in parts] + [(ANY, token)]
    (mine,) = call(plane_gather_kernel, "plane_gather", ins, [(VMEM, (16,) + mine.shape[1:])])
    got = core_round(mine, tm, grp)
    outs = finish(True, mine, [])
    sum_s, sum_t, sum_d = finish(False, got, outs)
    return (
        down,
        grad_x.reshape(frames_in.shape),
        sum_s.reshape(w_spatial.shape),
        sum_t,
        sum_d.reshape(w_down.shape),
    )


def solution(mesh):
    return jax.shard_map(
        functools.partial(body, mesh.shape["tm"], mesh.shape["grp"]),
        mesh=mesh,
        in_specs=(P("tm", "grp", None, None), P("tm"), P(), P(), P(), P("tm", "grp", None, None)),
        out_specs=(P("tm", "grp", None, None), P("tm", "grp", None, None), P(), P(), P()),
        check_vma=False,
    )
```

```python
import functools

import jax
import jax.numpy as jnp
from jax import lax
from jax.experimental import pallas as pl
from jax.experimental.pallas import tpu as pltpu
from jax.sharding import PartitionSpec as P

SLOTS = 16
OWN = 14
CH = 256
BF = jnp.bfloat16
F32 = jnp.float32


def mm(a, b):
    return lax.dot_general(a, b, (((1,), (0,)), ((), ())), preferred_element_type=F32)


def mm_nt(a, b):
    return lax.dot_general(a, b, (((1,), (1,)), ((), ())), preferred_element_type=F32)


def iotas(rows, cols):
    return (
        lax.broadcasted_iota(jnp.int32, (rows, cols), 0),
        lax.broadcasted_iota(jnp.int32, (rows, cols), 1),
    )


def to_slots(rows, frames, keep):
    a, b = iotas(rows * SLOTS, frames * rows)
    bits = rows.bit_length() - 1
    hit = ((a >> 4) == (b & (rows - 1))) & keep(b >> bits, a & 15)
    return jnp.where(hit, 1.0, 0.0).astype(BF)


def to_frames(rows):
    a, b = iotas(SLOTS * rows, rows * SLOTS)
    bits = rows.bit_length() - 1
    hit = ((a & (rows - 1)) == (b >> 4)) & ((a >> bits) == (b & 15))
    return jnp.where(hit, 1.0, 0.0).astype(BF)


def own_frames(count):
    return lambda frame, slot: (frame == slot) & (slot < count)


def own_and_next(count, blocks):
    after = jnp.where(lax.axis_index("tm") < blocks - 1, count, 64)
    return lambda frame, slot: ((frame < OWN) & (frame == slot) & (slot < count)) | (
        (frame >= OWN) & (slot == after + frame - OWN)
    )


def silu_norm(v):
    scaled = v * lax.rsqrt(jnp.mean(v * v, axis=-1, keepdims=True) + 1e-06)
    return scaled * (0.5 + 0.5 * jnp.tanh(0.5 * scaled))


def slot_mask(shape, count):
    return lax.broadcasted_iota(jnp.int32, shape, len(shape) - 2) < count


def grad_of_temporal(gy, wt_ref, count):
    n = gy.shape[0]
    flat = gy.reshape(n * SLOTS, CH)
    total = mm_nt(flat, wt_ref[2]).reshape(n, SLOTS, CH)
    for k in (1, 0):
        term = mm_nt(flat, wt_ref[k]).reshape(n, SLOTS, CH)
        total = total + pltpu.roll(term, SLOTS - (2 - k), 1)
    return jnp.where(slot_mask(total.shape, count), total, 0.0).astype(BF)


def place_bits():
    t, g = lax.axis_index("tm"), lax.axis_index("grp")
    return t & 1, ((t >> 1) & 1) + 2 * (g & 1), (t >> 2) & 3


def split_cores(value, keep_ref, send_ref, k):
    core, _, _ = place_bits()
    low, high = value[:, : CH // 2].astype(BF), value[:, CH // 2 :].astype(BF)
    keep_ref[:, k] = jnp.where(core == 0, low, high).reshape(16, 16, CH // 2)
    send_ref[:, k] = jnp.where(core == 0, high, low).reshape(16, 16, CH // 2)


def edges_kernel(bands, count_ref, x_ref, *outs):
    count = count_ref[0]
    band = lax.axis_index("grp")
    wide = x_ref.shape[1]
    if bands == 2:
        starts, lower = [jnp.where(band == 0, wide - 16, 0)], [band == 0]
    else:
        starts, lower = [wide - 16, 0], [True, False]
    place = to_slots(16, SLOTS, own_frames(count))
    for k, at in enumerate(starts):
        piece = x_ref[:, pl.ds(pl.multiple_of(at, 16), 16), :].reshape(SLOTS * 16, CH)
        v = mm(place, piece)
        v = jnp.where(lower[k], v[128:], v[:128])
        outs[k][...] = silu_norm(v).astype(BF)


def acts_kernel(count_ref, x_ref, _, xt_ref, acts_ref, at_ref, last_ref):
    count = count_ref[0]
    rows, cols = xt_ref.shape[0], xt_ref.shape[1]
    edge = jnp.zeros((rows + 2, SLOTS, CH), BF)
    acts_ref[:, 0] = edge
    acts_ref[:, cols + 1] = edge
    place = to_slots(16, SLOTS, own_frames(count))
    last = silu_norm(x_ref[pl.ds(count - 2, 2)].reshape(2 * rows * cols, CH).astype(F32))
    last_ref[0 : 2 * rows * cols] = last.astype(BF)

    def rows_of(q, _):
        at = pl.multiple_of(q * 16, 16)
        piece = x_ref[:, pl.ds(at, 16), :].reshape(SLOTS * 16, CH)
        v = mm(place, piece)
        xt_ref[pl.ds(2 * q, 2)] = v.astype(BF).reshape(2, cols, SLOTS, CH)
        a = silu_norm(v).astype(BF)
        acts_ref[pl.ds(2 * q + 1, 2), 1 : cols + 1] = a.reshape(2, cols, SLOTS, CH)
        flipped = a.T
        for i in range(3):
            at = pl.multiple_of((2 * q + 3 - i) * 128, 128)
            at_ref[i * CH : i * CH + CH, pl.ds(at, 256)] = flipped
        return 0

    lax.fori_loop(0, rows // 2, rows_of, 0, unroll=4)


def next_kernel(cot_ref, _, nxt_ref):
    nxt_ref[...] = cot_ref[0:2]


def halo_kernel(bands, count_ref, top_ref, bot_ref, *rest):
    acts_ref, at_ref, last_ref = rest[-3:]
    count = count_ref[0]
    band = lax.axis_index("grp")
    rows, cols = acts_ref.shape[0] - 2, acts_ref.shape[1] - 2
    halo = []
    for ref, flag, i, row in ((top_ref, band > 0, 0, 0), (bot_ref, band < bands - 1, 2, rows + 1)):
        a = jnp.where(flag, ref[...].astype(F32), 0.0).astype(BF)
        acts_ref[row, 1 : cols + 1] = a.reshape(cols, SLOTS, CH)
        at = (row - i + 2) * 128
        at_ref[i * CH : i * CH + CH, at : at + 128] = a.T
        halo.append(a)
    a, b = iotas(32, 256)
    pick = ((a & 15) == (b >> 4)) & ((b & 15) == count - 2 + (a >> 4))
    pick = jnp.where(pick, 1.0, 0.0).astype(BF)
    last_ref[2 * rows * cols :] = mm(pick, jnp.concatenate(halo, 0)).astype(BF)


def spatial_kernel(count_ref, acts_in, prev_ref, ws_ref, _, acts_ref, sp_ref):
    rows, cols = sp_ref.shape[0], sp_ref.shape[1]
    a, b = iotas(256, 32)
    place = ((a >> 4) == (b & 15)) & ((a & 15) == OWN + (b >> 4)) & (lax.axis_index("tm") > 0)
    place = jnp.where(place, 1.0, 0.0).astype(BF)
    size = rows * cols
    for q in range(rows // 2 + 1):
        if q == rows // 2:
            both, prev = slice(0, rows + 2, rows + 1), prev_ref[2 * size :]
        else:
            both = slice(2 * q + 1, 2 * q + 3)
            parts = [prev_ref[f * size + q * 16 : f * size + q * 16 + 16] for f in range(2)]
            prev = jnp.concatenate(parts, 0)
        prev = mm(place, prev).astype(BF).reshape(2, cols, SLOTS, CH)
        for k, row in enumerate(range(rows + 2)[both]):
            acts_ref[row, 1 : cols + 1] = acts_ref[row, 1 : cols + 1] + prev[k]

    def rows_of(q, _):
        total = None
        for i in range(3):
            for j in range(3):
                left = acts_ref[pl.ds(4 * q + i, 4), j : j + cols].reshape(4 * cols * SLOTS, CH)
                term = mm(left, ws_ref[i * 3 + j])
                total = term if total is None else total + term
        sp_ref[pl.ds(4 * q, 4)] = total.astype(BF).reshape(4, cols, SLOTS, CH)
        return 0

    lax.fori_loop(0, rows // 4, rows_of, 0)


def grad_spatial_kernel(
    blocks, bands, count_ref, at_ref, cot_ref, nxt_ref, wt_ref, wd_ref,
    cott_ref, gy_ref, gs_ref, keep_ref, send_ref, *edge_refs,
):
    count = count_ref[0]
    band = lax.axis_index("grp")
    rows, cols = gy_ref.shape[0], gy_ref.shape[1]
    edge = jnp.zeros((rows, SLOTS, CH), BF)
    gs_ref[:, 0] = edge
    gs_ref[:, cols + 1] = edge

    place_next = to_slots(16, SLOTS, own_and_next(count, blocks))
    halves = []
    for q in range(rows * cols // 64):
        four = slice(q * 4, q * 4 + 4)
        piece = jnp.concatenate(
            [cot_ref[0:OWN, four].reshape(OWN, 16, CH), nxt_ref[:, four].reshape(2, 16, CH)], 0
        ).reshape(SLOTS * 16, CH)
        halves.append(mm(place_next, piece).astype(BF))
    placed = jnp.concatenate(halves, 0)
    cott_ref[...] = placed.reshape(rows // 2, cols // 2, SLOTS, CH)
    for i in range(2):
        for j in range(2):
            g = mm_nt(placed, wd_ref[i * 2 + j]).astype(BF).reshape(rows // 2, cols // 2, SLOTS, CH)
            for r in range(rows // 2):
                for c in range(cols // 2):
                    gy_ref[2 * r + i, 2 * c + j] = g[r, c]
    last = cott_ref[rows // 2 - 1].reshape(cols // 2 * SLOTS, CH)
    first = cott_ref[0].reshape(cols // 2 * SLOTS, CH)
    if bands == 2:
        edge_refs[0][...] = jnp.where(band == 0, last, first)
    else:
        edge_refs[0][...] = last
        edge_refs[1][...] = first

    def grads_of(q, _):
        g = gy_ref[pl.ds(8 * q, 8)].reshape(8 * cols, SLOTS, CH)
        s = grad_of_temporal(g, wt_ref, count)
        gs_ref[pl.ds(8 * q, 8), 1 : cols + 1] = s.reshape(8, cols, SLOTS, CH)
        g = jnp.where(slot_mask(g.shape, count), g.astype(F32), 0.0)
        gy_ref[pl.ds(8 * q, 8)] = g.astype(BF).reshape(8, cols, SLOTS, CH)
        return 0

    lax.fori_loop(0, rows // 8, grads_of, 0)

    wide = rows * cols * SLOTS
    for j in range(3):
        right = gs_ref[:, 2 - j : 2 - j + cols].reshape(wide, CH)
        value = mm(at_ref[:, 256 : 256 + wide], right)
        for i in range(3):
            split_cores(value[i * CH : i * CH + CH], keep_ref, send_ref, i * 3 + j)


def forward_kernel(
    count_ref, xt_ref, sp_ref, cott_ref, gy_ref, wt_ref, wd_ref, *rest
):
    down_ref, keep_ref, send_ref, y_ref, st_ref, yt_ref = rest[-6:]
    count = count_ref[0]
    rows, cols = xt_ref.shape[0], xt_ref.shape[1]
    def rows_of(q, _):
        s = sp_ref[pl.ds(8 * q, 8)].reshape(8 * cols * SLOTS, CH).astype(F32)
        s = s.reshape(8 * cols, SLOTS, CH)
        total = None
        for k in range(3):
            shifted = s if k == 2 else pltpu.roll(s, 2 - k, 1)
            shifted = shifted.astype(BF).reshape(8 * cols * SLOTS, CH)
            at = pl.ds(pl.multiple_of(q * 1024, 1024), 1024)
            st_ref[k * CH : k * CH + CH, at] = shifted.T
            term = mm(shifted, wt_ref[k])
            total = term if total is None else total + term
        x = xt_ref[pl.ds(8 * q, 8)].reshape(8 * cols, SLOTS, CH).astype(F32)
        y = jnp.where(slot_mask(x.shape, count), x + total.reshape(x.shape), 0.0).astype(BF)
        y_ref[pl.ds(8 * q, 8)] = y.reshape(8, cols, SLOTS, CH)
        return 0

    lax.fori_loop(0, rows // 8, rows_of, 0)

    wide = rows * cols * SLOTS
    value = mm(st_ref[...], gy_ref[...].reshape(wide, CH))
    for k in range(3):
        split_cores(value[k * CH : k * CH + CH], keep_ref, send_ref, k)

    small = wide // 4
    total = None
    for i in range(2):
        for j in range(2):
            tiles = [
                y_ref[2 * r + i, 2 * c + j] for r in range(rows // 2) for c in range(cols // 2)
            ]
            piece = jnp.concatenate(tiles, axis=0)
            k = i * 2 + j
            yt_ref[k * CH : k * CH + CH] = piece.T
            term = mm(piece, wd_ref[k])
            total = term if total is None else total + term
    down_ref[...] = total.astype(BF)
    value = mm(yt_ref[...], cott_ref[...].reshape(small, CH))
    for k in range(4):
        split_cores(value[k * CH : k * CH + CH], keep_ref, send_ref, 3 + k)


def grad_x_kernel(
    bands, count_ref, xt_ref, gy_ref, gs_ref, top_ref, bot_ref, wt_ref, wd_ref, ws_ref, slot_ref, *rest
):
    out_ref, down_ref, token_ref, pad_ref, buf, sems = rest[-6:]
    token_ref[...] = jnp.zeros_like(token_ref)
    count = count_ref[0]
    band = lax.axis_index("grp")
    rows, cols = xt_ref.shape[0], xt_ref.shape[1]
    pad_ref[1 : rows + 1] = gs_ref[...]
    edge = jnp.zeros((SLOTS, CH), BF)
    for ref, flag, i, row in ((top_ref, band > 0, 1, 0), (bot_ref, band < bands - 1, 0, rows + 1)):
        pair = [
            mm_nt(ref[...], wd_ref[i * 2 + j]).astype(BF).reshape(cols // 2, SLOTS, CH)
            for j in range(2)
        ]
        g = jnp.stack(pair, axis=1).reshape(cols, SLOTS, CH)
        pad_ref[row, 0] = edge
        pad_ref[row, 1 : cols + 1] = grad_of_temporal(g, wt_ref, jnp.where(flag, count, 0))
        pad_ref[row, cols + 1] = edge
    back = to_frames(16)

    def rows_of(q, _):
        total = None
        for i in range(3):
            for j in range(3):
                left = pad_ref[pl.ds(4 * q + 2 - i, 4), 2 - j : 2 - j + cols].reshape(
                    4 * cols * SLOTS, CH
                )
                term = mm_nt(left, ws_ref[i * 3 + j])
                total = term if total is None else total + term
        at = 4 * q
        v = xt_ref[pl.ds(at, 4)].reshape(4 * cols * SLOTS, CH).astype(F32)
        r = lax.rsqrt(jnp.mean(v * v, axis=-1, keepdims=True) + 1e-06)
        u = v * r
        s = 0.5 + 0.5 * jnp.tanh(0.5 * u)
        gu = total * (s * (1.0 + u * (1.0 - s)))
        dot = jnp.mean(gu * u, axis=-1, keepdims=True)
        gv = r * (gu - u * dot)
        gx = gy_ref[pl.ds(at, 4)].reshape(4 * cols * SLOTS, CH).astype(F32) + gv
        gx = gx.reshape(4 * cols, SLOTS, CH)
        gx = jnp.where(slot_mask(gx.shape, count), gx, 0.0).astype(BF).reshape(4 * cols * SLOTS, CH)
        for k in range(2):
            o = mm(back, gx[k * 256 : k * 256 + 256]).astype(BF)
            buf[:, pl.ds(pl.multiple_of((2 * q + k) * 16, 16), 16), :] = o.reshape(SLOTS, 16, CH)
        return 0

    lax.fori_loop(0, rows // 4, rows_of, 0)
    copy = pltpu.make_async_copy(buf, out_ref, sems.at[0])
    copy.start()
    for q in range(down_ref.shape[1] // 4):
        o = mm(back, slot_ref[q * 256 : q * 256 + 256]).astype(BF)
        down_ref[:, q * 4 : q * 4 + 4] = o.reshape(SLOTS, 4, cols // 2, CH)
    copy.wait()


ORDER = (0, 3, 2, 1)


def plane_send_kernel(keep_ref, got_ref, *rest):
    _, p, _ = place_bits()
    for r, out in zip(ORDER, rest[-4:]):
        at = pl.ds((p ^ r) * 4, 4)
        out[...] = (keep_ref[at].astype(F32) + got_ref[at].astype(F32)).astype(BF)


def line_send_kernel(*refs):
    outs = refs[8:]
    _, _, z = place_bits()
    for out, r in zip(outs, ORDER):
        at = 0
        for chain in (refs[:4], refs[4:8]):
            parts = [ref[z ^ r].astype(F32) for ref in chain]
            n = parts[0].shape[0]
            out[at : at + n] = (parts[0] + parts[1] + parts[2] + parts[3]).astype(BF)
            at += n


def line_sum_kernel(a_ref, b_ref, c_ref, d_ref, *rest):
    out_ref = rest[-1]
    parts = [ref[...].astype(F32) for ref in (a_ref, b_ref, c_ref, d_ref)]
    out_ref[...] = (parts[0] + parts[1] + parts[2] + parts[3]).astype(BF)


def line_gather_kernel(a_ref, b_ref, c_ref, d_ref, out_ref):
    _, _, z = place_bits()
    for r, ref in zip(ORDER, (a_ref, b_ref, c_ref, d_ref)):
        out_ref[z ^ r] = ref[...]


def plane_gather_kernel(a_ref, b_ref, c_ref, d_ref, _, out_ref):
    _, p, _ = place_bits()
    for r, ref in zip(ORDER, (a_ref, b_ref, c_ref, d_ref)):
        out_ref[pl.ds((p ^ r) * 4, 4)] = ref[...]


def add_kernel(a_ref, b_ref, out_ref):
    out_ref[...] = (a_ref[...].astype(F32) + b_ref[...].astype(F32)).astype(BF)


def pass_kernel(*_):
    pass


def finish_kernel(own, half_ref, *rest):
    buf, sems = rest[-2:]
    outs = rest[-5:-2]
    core, _, _ = place_bits()
    at = pl.multiple_of((core if own else 1 - core) * (CH // 2), CH // 2)
    copies = []
    k = 0
    for out in outs:
        for m in range(out.shape[0]):
            buf[k] = half_ref[:, k].reshape(CH, CH // 2).astype(F32)
            copies.append(
                pltpu.make_async_copy(buf.at[k], out.at[m, :, pl.ds(at, CH // 2)], sems.at[k])
            )
            copies[-1].start()
            k += 1
    for copy in copies:
        copy.wait()


VMEM = pl.BlockSpec(memory_space=pltpu.VMEM)
SMEM = pl.BlockSpec(memory_space=pltpu.SMEM)
ANY = pl.BlockSpec(memory_space=pl.ANY)
HBM = pl.BlockSpec(memory_space=pltpu.HBM)
TOKEN = (VMEM, (8, 128), F32)


def call(kernel, name, ins, outs, scratch=(), flops=0, alias=None, grant=10, moved=None):
    shapes = [jax.ShapeDtypeStruct(o[1], o[2] if len(o) > 2 else BF) for o in outs]
    if moved is None:
        moved = sum(a.size * a.dtype.itemsize for s, a in ins if s is not ANY)
        moved += sum(s.size * s.dtype.itemsize for s in shapes)
    return pl.pallas_call(
        kernel,
        out_shape=shapes,
        in_specs=[s for s, _ in ins],
        out_specs=[o[0] for o in outs],
        scratch_shapes=list(scratch),
        compiler_params=pltpu.CompilerParams(vmem_limit_bytes=grant * 2**20),
        cost_estimate=pl.CostEstimate(flops=flops, bytes_accessed=moved, transcendentals=0),
        input_output_aliases=alias or {},
        name=name,
    )(*[a for _, a in ins])


AXES = ("tm", "grp")


def plan(tm, grp):
    low, total = grp.bit_length() - 1, (tm * grp).bit_length() - 1
    plane, line = [low + 1, 0], [low + 2, low + 3]
    return low, plane, line, [b for b in range(total) if b not in [low] + plane + line]


def swap(value, tm, grp, *bits):
    flip = sum(1 << b for b in bits)
    return lax.ppermute(value, AXES, [(d, d ^ flip) for d in range(tm * grp)])


def core_round(value, tm, grp):
    return swap(value, tm, grp, plan(tm, grp)[0])


def four_round(parts, bits, tm, grp):
    return [
        parts[0],
        swap(parts[1], tm, grp, *bits),
        swap(parts[2], tm, grp, bits[1]),
        swap(parts[3], tm, grp, bits[0]),
    ]


def plane_send(keep, got, after):
    ins = [(VMEM, keep), (VMEM, got)] + [(ANY, a) for a in after]
    shape = (4, keep.shape[1], 16, CH // 2)
    return list(call(plane_send_kernel, "plane_send", ins, [(VMEM, shape)] * 4))


def passed(value, after):
    ins = [(ANY, value)] + [(ANY, a) for a in after]
    return call(pass_kernel, "pass", ins, [(ANY, value.shape)], alias={0: 0})[0]


def finish(own, half, before):
    n = half.shape[1]
    return list(
        call(
            functools.partial(finish_kernel, own),
            "finish",
            [(VMEM, half)] + [(HBM, a) for a in before],
            [(HBM, (m, CH, CH), F32) for m in (9, 3, 4)],
            [pltpu.VMEM((n, CH, CH // 2), F32), pltpu.SemaphoreType.DMA((n,))],
            alias={1 + i: i for i in range(len(before))},
        )
    )


def along(value, axis, by):
    count = lax.axis_size(axis)
    pairs = [(i, i + by) for i in range(count) if 0 <= i + by < count]
    return lax.ppermute(value, axis, pairs)


def around(value, axis, by):
    count = lax.axis_size(axis)
    return lax.ppermute(value, axis, [(i, (i + by) % count) for i in range(count)])


def from_bands(parts):
    if len(parts) == 1:
        got = lax.ppermute(parts[0], "grp", [(0, 1), (1, 0)])
        return got, got
    return along(parts[0], "grp", 1), along(parts[1], "grp", -1)


def body(tm, grp, frames_in, span_frames, w_spatial, w_temporal, w_down, cotangent):
    slots, rows, cols, ch = frames_in.shape
    wide = rows * cols
    x = frames_in.reshape(slots, wide, ch)
    ws = w_spatial.reshape(9, ch, ch)
    wd = w_down.reshape(4, ch, ch)
    wt = w_temporal
    count = (SMEM, span_frames)
    tap = 2 * slots * wide * ch * ch
    tile = (rows, cols, slots, ch)
    padded = (rows + 2, cols + 2, slots, ch)
    dma = pltpu.SemaphoreType.DMA

    sides = 1 if grp == 2 else 2
    edge = call(
        functools.partial(edges_kernel, grp),
        "edges",
        [count, (VMEM, x)],
        [(VMEM, (cols * slots, ch))] * sides,
        flops=tap // 8,
    )
    top, bot = from_bands(edge)
    last_shape = (2 * wide + 32, ch)
    at_shape = (3 * ch, (rows + 4) * 128)
    xt, acts, at, last_two = call(
        acts_kernel,
        "acts",
        [count, (VMEM, x), (ANY, edge[0])],
        [(VMEM, tile), (VMEM, padded), (VMEM, at_shape), (VMEM, last_shape)],
        flops=2 * tap,
    )
    (nxt,) = call(
        next_kernel,
        "next",
        [(VMEM, cotangent), (ANY, last_two)],
        [(VMEM, (2,) + cotangent.shape[1:])],
        moved=1024,
    )
    nxt_got = around(nxt, "tm", -1)
    acts, at, last_two = call(
        functools.partial(halo_kernel, grp),
        "halo",
        [count, (VMEM, top), (VMEM, bot), (VMEM, acts), (VMEM, at), (VMEM, last_two), (ANY, nxt),
         (VMEM, cotangent), (VMEM, wt), (VMEM, wd)],
        [(VMEM, padded), (VMEM, at_shape), (VMEM, last_shape)],
        alias={3: 0, 4: 1, 5: 2},
        moved=1024,
    )
    prev = around(last_two, "tm", 1)
    half = (16, 9, 16, ch // 2)
    cott, gy, gs, keep_a, send_a, *edge = call(
        functools.partial(grad_spatial_kernel, tm, grp),
        "grad_spatial",
        [count, (VMEM, at), (VMEM, cotangent), (VMEM, nxt_got), (VMEM, wt), (VMEM, wd)],
        [(VMEM, (rows // 2, cols // 2, slots, ch)), (VMEM, tile),
         (VMEM, (rows, cols + 2, slots, ch)), (VMEM, half), (VMEM, half)]
        + [(VMEM, (cols // 2 * slots, ch))] * sides,
        flops=14 * tap,
    )
    send_a = passed(send_a, [prev])
    got_a = core_round(send_a, tm, grp)
    cot_top, cot_bot = from_bands(edge)
    acts, sp = call(
        spatial_kernel,
        "spatial",
        [count, (VMEM, acts), (VMEM, prev), (VMEM, ws), (ANY, send_a)],
        [(VMEM, padded), (VMEM, tile)],
        flops=9 * tap,
        alias={1: 0},
    )
    _, plane, line, others = plan(tm, grp)
    parts_a = plane_send(keep_a, got_a, [sp])
    half = (16, 7, 16, ch // 2)
    down, keep_b, send_b = call(
        forward_kernel,
        "forward",
        [count, (VMEM, xt), (VMEM, sp), (VMEM, cott), (VMEM, gy), (VMEM, wt), (VMEM, wd),
         *((ANY, a) for a in parts_a)],
        [(VMEM, (slots * wide // 4, ch)), (VMEM, half), (VMEM, half)],
        [pltpu.VMEM(v, BF) for v in (tile, (3 * ch, slots * wide), (4 * ch, slots * wide // 4))],
        flops=10 * tap,
        grant=14,
    )
    parts_a = four_round(parts_a, plane, tm, grp)
    send_b = passed(send_b, parts_a[1:2])
    parts_b = plane_send(keep_b, core_round(send_b, tm, grp), [])
    parts_b = four_round(parts_b, plane, tm, grp)
    parts = call(
        line_send_kernel,
        "line_send",
        [(VMEM, a) for a in parts_a + parts_b],
        [(VMEM, (16, 16, ch // 2))] * 4,
    )
    parts = four_round(list(parts), line, tm, grp)
    ins = [(VMEM, a) for a in parts]
    (mine,) = call(line_sum_kernel, "line_sum", ins, [(VMEM, parts[0].shape)])
    for bit in others:
        got = swap(mine, tm, grp, bit)
        (mine,) = call(add_kernel, "add", [(VMEM, mine), (VMEM, got)], [(VMEM, mine.shape)])
    parts = four_round([mine] * 4, line, tm, grp)
    (mine,) = call(
        line_gather_kernel, "line_gather", [(VMEM, a) for a in parts], [(VMEM, (4,) + mine.shape)]
    )
    parts = four_round([mine] * 4, plane, tm, grp)
    grad_x, down, token = call(
        functools.partial(grad_x_kernel, grp),
        "grad_x",
        [count, (VMEM, xt), (VMEM, gy), (VMEM, gs), (VMEM, cot_top), (VMEM, cot_bot), (VMEM, wt),
         (VMEM, wd), (VMEM, ws), (VMEM, down), (ANY, mine)],
        [(HBM, (slots, wide, ch)), (VMEM, cotangent.shape), TOKEN],
        [pltpu.VMEM(padded, BF), pltpu.VMEM((slots, wide, ch), BF), dma((1,))],
        flops=10 * tap,
    )
    ins = [(VMEM, a) for a in parts] + [(ANY, token)]
    (mine,) = call(plane_gather_kernel, "plane_gather", ins, [(VMEM, (16,) + mine.shape[1:])])
    got = core_round(mine, tm, grp)
    outs = finish(True, mine, [])
    sum_s, sum_t, sum_d = finish(False, got, outs)
    return (
        down,
        grad_x.reshape(frames_in.shape),
        sum_s.reshape(w_spatial.shape),
        sum_t,
        sum_d.reshape(w_down.shape),
    )


def solution(mesh):
    return jax.shard_map(
        functools.partial(body, mesh.shape["tm"], mesh.shape["grp"]),
        mesh=mesh,
        in_specs=(P("tm", "grp", None, None), P("tm"), P(), P(), P(), P("tm", "grp", None, None)),
        out_specs=(P("tm", "grp", None, None), P("tm", "grp", None, None), P(), P(), P()),
        check_vma=False,
    )
```

```python
import functools

import jax
import jax.numpy as jnp
from jax import lax
from jax.experimental import pallas as pl
from jax.experimental.pallas import tpu as pltpu
from jax.sharding import PartitionSpec as P

SLOTS = 16
OWN = 14
CH = 256
BF = jnp.bfloat16
F32 = jnp.float32


def mm(a, b):
    return lax.dot_general(a, b, (((1,), (0,)), ((), ())), preferred_element_type=F32)


def mm_nt(a, b):
    return lax.dot_general(a, b, (((1,), (1,)), ((), ())), preferred_element_type=F32)


def iotas(rows, cols):
    return (
        lax.broadcasted_iota(jnp.int32, (rows, cols), 0),
        lax.broadcasted_iota(jnp.int32, (rows, cols), 1),
    )


def to_slots(rows, frames, keep):
    a, b = iotas(rows * SLOTS, frames * rows)
    bits = rows.bit_length() - 1
    hit = ((a >> 4) == (b & (rows - 1))) & keep(b >> bits, a & 15)
    return jnp.where(hit, 1.0, 0.0).astype(BF)


def to_frames(rows):
    a, b = iotas(SLOTS * rows, rows * SLOTS)
    bits = rows.bit_length() - 1
    hit = ((a & (rows - 1)) == (b >> 4)) & ((a >> bits) == (b & 15))
    return jnp.where(hit, 1.0, 0.0).astype(BF)


def own_frames(count):
    return lambda frame, slot: (frame == slot) & (slot < count)


def own_and_next(count, blocks):
    after = jnp.where(lax.axis_index("tm") < blocks - 1, count, 64)
    return lambda frame, slot: ((frame < OWN) & (frame == slot) & (slot < count)) | (
        (frame >= OWN) & (slot == after + frame - OWN)
    )


def silu_norm(v):
    scaled = v * lax.rsqrt(jnp.mean(v * v, axis=-1, keepdims=True) + 1e-06)
    return scaled * (0.5 + 0.5 * jnp.tanh(0.5 * scaled))


def slot_mask(shape, count):
    return lax.broadcasted_iota(jnp.int32, shape, len(shape) - 2) < count


def grad_of_temporal(gy, wt_ref, count):
    n = gy.shape[0]
    flat = gy.reshape(n * SLOTS, CH)
    total = mm_nt(flat, wt_ref[2]).reshape(n, SLOTS, CH)
    for k in (1, 0):
        term = mm_nt(flat, wt_ref[k]).reshape(n, SLOTS, CH)
        total = total + pltpu.roll(term, SLOTS - (2 - k), 1)
    return jnp.where(slot_mask(total.shape, count), total, 0.0).astype(BF)


def place_bits():
    t, g = lax.axis_index("tm"), lax.axis_index("grp")
    return t & 1, ((t >> 1) & 1) + 2 * (g & 1), (t >> 2) & 3


def split_cores(value, keep_ref, send_ref, k):
    core, _, _ = place_bits()
    low, high = value[:, : CH // 2].astype(BF), value[:, CH // 2 :].astype(BF)
    keep_ref[:, k] = jnp.where(core == 0, low, high).reshape(16, 16, CH // 2)
    send_ref[:, k] = jnp.where(core == 0, high, low).reshape(16, 16, CH // 2)


def edges_kernel(bands, count_ref, x_ref, *outs):
    count = count_ref[0]
    band = lax.axis_index("grp")
    wide = x_ref.shape[1]
    if bands == 2:
        starts, lower = [jnp.where(band == 0, wide - 16, 0)], [band == 0]
    else:
        starts, lower = [wide - 16, 0], [True, False]
    place = to_slots(16, SLOTS, own_frames(count))
    for k, at in enumerate(starts):
        piece = x_ref[:, pl.ds(pl.multiple_of(at, 16), 16), :].reshape(SLOTS * 16, CH)
        v = mm(place, piece)
        v = jnp.where(lower[k], v[128:], v[:128])
        outs[k][...] = silu_norm(v).astype(BF)


def acts_kernel(count_ref, x_ref, _, xt_ref, acts_ref, at_ref, last_ref):
    count = count_ref[0]
    rows, cols = xt_ref.shape[0], xt_ref.shape[1]
    edge = jnp.zeros((rows + 2, SLOTS, CH), BF)
    acts_ref[:, 0] = edge
    acts_ref[:, cols + 1] = edge
    place = to_slots(16, SLOTS, own_frames(count))
    last = silu_norm(x_ref[pl.ds(count - 2, 2)].reshape(2 * rows * cols, CH).astype(F32))
    last_ref[0 : 2 * rows * cols] = last.astype(BF)

    def rows_of(q, _):
        at = pl.multiple_of(q * 16, 16)
        piece = x_ref[:, pl.ds(at, 16), :].reshape(SLOTS * 16, CH)
        v = mm(place, piece)
        xt_ref[pl.ds(2 * q, 2)] = v.astype(BF).reshape(2, cols, SLOTS, CH)
        a = silu_norm(v).astype(BF)
        acts_ref[pl.ds(2 * q + 1, 2), 1 : cols + 1] = a.reshape(2, cols, SLOTS, CH)
        flipped = a.T
        for i in range(3):
            at = pl.multiple_of((2 * q + 3 - i) * 128, 128)
            at_ref[i * CH : i * CH + CH, pl.ds(at, 256)] = flipped
        return 0

    lax.fori_loop(0, rows // 2, rows_of, 0, unroll=4)


def next_kernel(cot_ref, _, nxt_ref):
    nxt_ref[...] = cot_ref[0:2]


def halo_kernel(bands, count_ref, top_ref, bot_ref, *rest):
    acts_ref, at_ref, last_ref = rest[-3:]
    count = count_ref[0]
    band = lax.axis_index("grp")
    rows, cols = acts_ref.shape[0] - 2, acts_ref.shape[1] - 2
    halo = []
    for ref, flag, i, row in ((top_ref, band > 0, 0, 0), (bot_ref, band < bands - 1, 2, rows + 1)):
        a = jnp.where(flag, ref[...].astype(F32), 0.0).astype(BF)
        acts_ref[row, 1 : cols + 1] = a.reshape(cols, SLOTS, CH)
        at = (row - i + 2) * 128
        at_ref[i * CH : i * CH + CH, at : at + 128] = a.T
        halo.append(a)
    a, b = iotas(32, 256)
    pick = ((a & 15) == (b >> 4)) & ((b & 15) == count - 2 + (a >> 4))
    pick = jnp.where(pick, 1.0, 0.0).astype(BF)
    last_ref[2 * rows * cols :] = mm(pick, jnp.concatenate(halo, 0)).astype(BF)


def conv_rows(acts_ref, ws_ref, sp_ref, start):
    rows, cols = sp_ref.shape[0], sp_ref.shape[1]

    def rows_of(q, _):
        total = None
        for i in range(3):
            for j in range(3):
                left = acts_ref[pl.ds(start + 4 * q + i, 4), j : j + cols].reshape(
                    4 * cols * SLOTS, CH
                )
                term = mm(left, ws_ref[i * 3 + j])
                total = term if total is None else total + term
        sp_ref[pl.ds(4 * q, 4)] = total.astype(BF).reshape(4, cols, SLOTS, CH)
        return 0

    lax.fori_loop(0, rows // 4, rows_of, 0)


def upper_kernel(acts_in, prev_ref, ws_ref, _, acts_ref, sp_ref):
    rows, cols = acts_ref.shape[0] - 2, acts_ref.shape[1] - 2
    a, b = iotas(256, 32)
    place = ((a >> 4) == (b & 15)) & ((a & 15) == OWN + (b >> 4)) & (lax.axis_index("tm") > 0)
    place = jnp.where(place, 1.0, 0.0).astype(BF)
    size = rows * cols
    for q in range(rows // 2 + 1):
        if q == rows // 2:
            both, prev = slice(0, rows + 2, rows + 1), prev_ref[2 * size :]
        else:
            both = slice(2 * q + 1, 2 * q + 3)
            parts = [prev_ref[f * size + q * 16 : f * size + q * 16 + 16] for f in range(2)]
            prev = jnp.concatenate(parts, 0)
        prev = mm(place, prev).astype(BF).reshape(2, cols, SLOTS, CH)
        for k, row in enumerate(range(rows + 2)[both]):
            acts_ref[row, 1 : cols + 1] = acts_ref[row, 1 : cols + 1] + prev[k]

    conv_rows(acts_ref, ws_ref, sp_ref, 0)


def lower_kernel(acts_ref, ws_ref, *rest):
    sp_ref = rest[-1]
    conv_rows(acts_ref, ws_ref, sp_ref, sp_ref.shape[0])


def grad_spatial_kernel(
    blocks, bands, count_ref, at_ref, cot_ref, nxt_ref, wt_ref, wd_ref,
    cott_ref, gy_ref, gs_ref, keep_ref, send_ref, *edge_refs,
):
    count = count_ref[0]
    band = lax.axis_index("grp")
    rows, cols = gy_ref.shape[0], gy_ref.shape[1]
    edge = jnp.zeros((rows, SLOTS, CH), BF)
    gs_ref[:, 0] = edge
    gs_ref[:, cols + 1] = edge

    place_next = to_slots(16, SLOTS, own_and_next(count, blocks))
    halves = []
    for q in range(rows * cols // 64):
        four = slice(q * 4, q * 4 + 4)
        piece = jnp.concatenate(
            [cot_ref[0:OWN, four].reshape(OWN, 16, CH), nxt_ref[:, four].reshape(2, 16, CH)], 0
        ).reshape(SLOTS * 16, CH)
        halves.append(mm(place_next, piece).astype(BF))
    placed = jnp.concatenate(halves, 0)
    cott_ref[...] = placed.reshape(rows // 2, cols // 2, SLOTS, CH)
    for i in range(2):
        for j in range(2):
            g = mm_nt(placed, wd_ref[i * 2 + j]).astype(BF).reshape(rows // 2, cols // 2, SLOTS, CH)
            for r in range(rows // 2):
                for c in range(cols // 2):
                    gy_ref[2 * r + i, 2 * c + j] = g[r, c]
    last = cott_ref[rows // 2 - 1].reshape(cols // 2 * SLOTS, CH)
    first = cott_ref[0].reshape(cols // 2 * SLOTS, CH)
    if bands == 2:
        edge_refs[0][...] = jnp.where(band == 0, last, first)
    else:
        edge_refs[0][...] = last
        edge_refs[1][...] = first

    def grads_of(q, _):
        g = gy_ref[pl.ds(8 * q, 8)].reshape(8 * cols, SLOTS, CH)
        s = grad_of_temporal(g, wt_ref, count)
        gs_ref[pl.ds(8 * q, 8), 1 : cols + 1] = s.reshape(8, cols, SLOTS, CH)
        g = jnp.where(slot_mask(g.shape, count), g.astype(F32), 0.0)
        gy_ref[pl.ds(8 * q, 8)] = g.astype(BF).reshape(8, cols, SLOTS, CH)
        return 0

    lax.fori_loop(0, rows // 8, grads_of, 0)

    wide = rows * cols * SLOTS
    for j in range(3):
        right = gs_ref[:, 2 - j : 2 - j + cols].reshape(wide, CH)
        value = mm(at_ref[:, 256 : 256 + wide], right)
        for i in range(3):
            split_cores(value[i * CH : i * CH + CH], keep_ref, send_ref, i * 3 + j)


def forward_kernel(
    count_ref, xt_ref, upper_ref, lower_ref, cott_ref, gy_ref, wt_ref, wd_ref, *rest
):
    down_ref, keep_ref, send_ref, y_ref, st_ref, yt_ref = rest[-6:]
    count = count_ref[0]
    rows, cols = xt_ref.shape[0], xt_ref.shape[1]
    for q, sp_ref in enumerate((upper_ref, lower_ref)):
        s = sp_ref[...].reshape(8 * cols * SLOTS, CH).astype(F32)
        s = s.reshape(8 * cols, SLOTS, CH)
        total = None
        for k in range(3):
            shifted = s if k == 2 else pltpu.roll(s, 2 - k, 1)
            shifted = shifted.astype(BF).reshape(8 * cols * SLOTS, CH)
            at = slice(q * 1024, q * 1024 + 1024)
            st_ref[k * CH : k * CH + CH, at] = shifted.T
            term = mm(shifted, wt_ref[k])
            total = term if total is None else total + term
        x = xt_ref[8 * q : 8 * q + 8].reshape(8 * cols, SLOTS, CH).astype(F32)
        y = jnp.where(slot_mask(x.shape, count), x + total.reshape(x.shape), 0.0).astype(BF)
        y_ref[8 * q : 8 * q + 8] = y.reshape(8, cols, SLOTS, CH)

    wide = rows * cols * SLOTS
    value = mm(st_ref[...], gy_ref[...].reshape(wide, CH))
    for k in range(3):
        split_cores(value[k * CH : k * CH + CH], keep_ref, send_ref, k)

    small = wide // 4
    total = None
    for i in range(2):
        for j in range(2):
            tiles = [
                y_ref[2 * r + i, 2 * c + j] for r in range(rows // 2) for c in range(cols // 2)
            ]
            piece = jnp.concatenate(tiles, axis=0)
            k = i * 2 + j
            yt_ref[k * CH : k * CH + CH] = piece.T
            term = mm(piece, wd_ref[k])
            total = term if total is None else total + term
    down_ref[...] = total.astype(BF)
    value = mm(yt_ref[...], cott_ref[...].reshape(small, CH))
    for k in range(4):
        split_cores(value[k * CH : k * CH + CH], keep_ref, send_ref, 3 + k)


def grad_x_kernel(
    bands, count_ref, xt_ref, gy_ref, gs_ref, top_ref, bot_ref, wt_ref, wd_ref, ws_ref, slot_ref, *rest
):
    out_ref, down_ref, token_ref, pad_ref, buf, sems = rest[-6:]
    token_ref[...] = jnp.zeros_like(token_ref)
    count = count_ref[0]
    band = lax.axis_index("grp")
    rows, cols = xt_ref.shape[0], xt_ref.shape[1]
    pad_ref[1 : rows + 1] = gs_ref[...]
    edge = jnp.zeros((SLOTS, CH), BF)
    for ref, flag, i, row in ((top_ref, band > 0, 1, 0), (bot_ref, band < bands - 1, 0, rows + 1)):
        pair = [
            mm_nt(ref[...], wd_ref[i * 2 + j]).astype(BF).reshape(cols // 2, SLOTS, CH)
            for j in range(2)
        ]
        g = jnp.stack(pair, axis=1).reshape(cols, SLOTS, CH)
        pad_ref[row, 0] = edge
        pad_ref[row, 1 : cols + 1] = grad_of_temporal(g, wt_ref, jnp.where(flag, count, 0))
        pad_ref[row, cols + 1] = edge
    back = to_frames(16)

    def rows_of(q, _):
        total = None
        for i in range(3):
            for j in range(3):
                left = pad_ref[pl.ds(4 * q + 2 - i, 4), 2 - j : 2 - j + cols].reshape(
                    4 * cols * SLOTS, CH
                )
                term = mm_nt(left, ws_ref[i * 3 + j])
                total = term if total is None else total + term
        at = 4 * q
        v = xt_ref[pl.ds(at, 4)].reshape(4 * cols * SLOTS, CH).astype(F32)
        r = lax.rsqrt(jnp.mean(v * v, axis=-1, keepdims=True) + 1e-06)
        u = v * r
        s = 0.5 + 0.5 * jnp.tanh(0.5 * u)
        gu = total * (s * (1.0 + u * (1.0 - s)))
        dot = jnp.mean(gu * u, axis=-1, keepdims=True)
        gv = r * (gu - u * dot)
        gx = gy_ref[pl.ds(at, 4)].reshape(4 * cols * SLOTS, CH).astype(F32) + gv
        gx = gx.reshape(4 * cols, SLOTS, CH)
        gx = jnp.where(slot_mask(gx.shape, count), gx, 0.0).astype(BF).reshape(4 * cols * SLOTS, CH)
        for k in range(2):
            o = mm(back, gx[k * 256 : k * 256 + 256]).astype(BF)
            buf[:, pl.ds(pl.multiple_of((2 * q + k) * 16, 16), 16), :] = o.reshape(SLOTS, 16, CH)
        return 0

    lax.fori_loop(0, rows // 4, rows_of, 0)
    copy = pltpu.make_async_copy(buf, out_ref, sems.at[0])
    copy.start()
    for q in range(down_ref.shape[1] // 4):
        o = mm(back, slot_ref[q * 256 : q * 256 + 256]).astype(BF)
        down_ref[:, q * 4 : q * 4 + 4] = o.reshape(SLOTS, 4, cols // 2, CH)
    copy.wait()


ORDER = (0, 3, 2, 1)


def plane_send_kernel(keep_ref, got_ref, *rest):
    _, p, _ = place_bits()
    for r, out in zip(ORDER, rest[-4:]):
        at = pl.ds((p ^ r) * 4, 4)
        out[...] = (keep_ref[at].astype(F32) + got_ref[at].astype(F32)).astype(BF)


def line_send_kernel(*refs):
    outs = refs[8:]
    _, _, z = place_bits()
    for out, r in zip(outs, ORDER):
        at = 0
        for chain in (refs[:4], refs[4:8]):
            parts = [ref[z ^ r].astype(F32) for ref in chain]
            n = parts[0].shape[0]
            out[at : at + n] = (parts[0] + parts[1] + parts[2] + parts[3]).astype(BF)
            at += n


def line_sum_kernel(a_ref, b_ref, c_ref, d_ref, *rest):
    out_ref = rest[-1]
    parts = [ref[...].astype(F32) for ref in (a_ref, b_ref, c_ref, d_ref)]
    out_ref[...] = (parts[0] + parts[1] + parts[2] + parts[3]).astype(BF)


def line_gather_kernel(a_ref, b_ref, c_ref, d_ref, out_ref):
    _, _, z = place_bits()
    for r, ref in zip(ORDER, (a_ref, b_ref, c_ref, d_ref)):
        out_ref[z ^ r] = ref[...]


def plane_gather_kernel(a_ref, b_ref, c_ref, d_ref, _, out_ref):
    _, p, _ = place_bits()
    for r, ref in zip(ORDER, (a_ref, b_ref, c_ref, d_ref)):
        out_ref[pl.ds((p ^ r) * 4, 4)] = ref[...]


def add_kernel(a_ref, b_ref, out_ref):
    out_ref[...] = (a_ref[...].astype(F32) + b_ref[...].astype(F32)).astype(BF)


def pass_kernel(*_):
    pass


def finish_kernel(own, half_ref, *rest):
    buf, sems = rest[-2:]
    outs = rest[-5:-2]
    core, _, _ = place_bits()
    at = pl.multiple_of((core if own else 1 - core) * (CH // 2), CH // 2)
    copies = []
    k = 0
    for out in outs:
        for m in range(out.shape[0]):
            buf[k] = half_ref[:, k].reshape(CH, CH // 2).astype(F32)
            copies.append(
                pltpu.make_async_copy(buf.at[k], out.at[m, :, pl.ds(at, CH // 2)], sems.at[k])
            )
            copies[-1].start()
            k += 1
    for copy in copies:
        copy.wait()


VMEM = pl.BlockSpec(memory_space=pltpu.VMEM)
SMEM = pl.BlockSpec(memory_space=pltpu.SMEM)
ANY = pl.BlockSpec(memory_space=pl.ANY)
HBM = pl.BlockSpec(memory_space=pltpu.HBM)
TOKEN = (VMEM, (8, 128), F32)


def call(kernel, name, ins, outs, scratch=(), flops=0, alias=None, grant=10, moved=None):
    shapes = [jax.ShapeDtypeStruct(o[1], o[2] if len(o) > 2 else BF) for o in outs]
    if moved is None:
        moved = sum(a.size * a.dtype.itemsize for s, a in ins if s is not ANY)
        moved += sum(s.size * s.dtype.itemsize for s in shapes)
    return pl.pallas_call(
        kernel,
        out_shape=shapes,
        in_specs=[s for s, _ in ins],
        out_specs=[o[0] for o in outs],
        scratch_shapes=list(scratch),
        compiler_params=pltpu.CompilerParams(vmem_limit_bytes=grant * 2**20),
        cost_estimate=pl.CostEstimate(flops=flops, bytes_accessed=moved, transcendentals=0),
        input_output_aliases=alias or {},
        name=name,
    )(*[a for _, a in ins])


AXES = ("tm", "grp")


def plan(tm, grp):
    low, total = grp.bit_length() - 1, (tm * grp).bit_length() - 1
    plane, line = [low + 1, 0], [low + 2, low + 3]
    return low, plane, line, [b for b in range(total) if b not in [low] + plane + line]


def swap(value, tm, grp, *bits):
    flip = sum(1 << b for b in bits)
    return lax.ppermute(value, AXES, [(d, d ^ flip) for d in range(tm * grp)])


def core_round(value, tm, grp):
    return swap(value, tm, grp, plan(tm, grp)[0])


def four_round(parts, bits, tm, grp):
    return [
        parts[0],
        swap(parts[1], tm, grp, *bits),
        swap(parts[2], tm, grp, bits[1]),
        swap(parts[3], tm, grp, bits[0]),
    ]


def plane_send(keep, got, after):
    ins = [(VMEM, keep), (VMEM, got)] + [(ANY, a) for a in after]
    shape = (4, keep.shape[1], 16, CH // 2)
    return list(call(plane_send_kernel, "plane_send", ins, [(VMEM, shape)] * 4))


def passed(value, after):
    ins = [(ANY, value)] + [(ANY, a) for a in after]
    return call(pass_kernel, "pass", ins, [(ANY, value.shape)], alias={0: 0})[0]


def finish(own, half, before):
    n = half.shape[1]
    return list(
        call(
            functools.partial(finish_kernel, own),
            "finish",
            [(VMEM, half)] + [(HBM, a) for a in before],
            [(HBM, (m, CH, CH), F32) for m in (9, 3, 4)],
            [pltpu.VMEM((n, CH, CH // 2), F32), pltpu.SemaphoreType.DMA((n,))],
            alias={1 + i: i for i in range(len(before))},
        )
    )


def along(value, axis, by):
    count = lax.axis_size(axis)
    pairs = [(i, i + by) for i in range(count) if 0 <= i + by < count]
    return lax.ppermute(value, axis, pairs)


def around(value, axis, by):
    count = lax.axis_size(axis)
    return lax.ppermute(value, axis, [(i, (i + by) % count) for i in range(count)])


def from_bands(parts):
    if len(parts) == 1:
        got = lax.ppermute(parts[0], "grp", [(0, 1), (1, 0)])
        return got, got
    return along(parts[0], "grp", 1), along(parts[1], "grp", -1)


def body(tm, grp, frames_in, span_frames, w_spatial, w_temporal, w_down, cotangent):
    slots, rows, cols, ch = frames_in.shape
    wide = rows * cols
    x = frames_in.reshape(slots, wide, ch)
    ws = w_spatial.reshape(9, ch, ch)
    wd = w_down.reshape(4, ch, ch)
    wt = w_temporal
    count = (SMEM, span_frames)
    tap = 2 * slots * wide * ch * ch
    tile = (rows, cols, slots, ch)
    padded = (rows + 2, cols + 2, slots, ch)
    dma = pltpu.SemaphoreType.DMA

    sides = 1 if grp == 2 else 2
    edge = call(
        functools.partial(edges_kernel, grp),
        "edges",
        [count, (VMEM, x)],
        [(VMEM, (cols * slots, ch))] * sides,
        flops=tap // 8,
    )
    top, bot = from_bands(edge)
    last_shape = (2 * wide + 32, ch)
    at_shape = (3 * ch, (rows + 4) * 128)
    xt, acts, at, last_two = call(
        acts_kernel,
        "acts",
        [count, (VMEM, x), (ANY, edge[0])],
        [(VMEM, tile), (VMEM, padded), (VMEM, at_shape), (VMEM, last_shape)],
        flops=2 * tap,
    )
    (nxt,) = call(
        next_kernel,
        "next",
        [(VMEM, cotangent), (ANY, last_two)],
        [(VMEM, (2,) + cotangent.shape[1:])],
        moved=1024,
    )
    nxt_got = around(nxt, "tm", -1)
    acts, at, last_two = call(
        functools.partial(halo_kernel, grp),
        "halo",
        [count, (VMEM, top), (VMEM, bot), (VMEM, acts), (VMEM, at), (VMEM, last_two), (ANY, nxt),
         (VMEM, cotangent), (VMEM, wt), (VMEM, wd)],
        [(VMEM, padded), (VMEM, at_shape), (VMEM, last_shape)],
        alias={3: 0, 4: 1, 5: 2},
        moved=1024,
    )
    prev = around(last_two, "tm", 1)
    half = (16, 9, 16, ch // 2)
    cott, gy, gs, keep_a, send_a, *edge = call(
        functools.partial(grad_spatial_kernel, tm, grp),
        "grad_spatial",
        [count, (VMEM, at), (VMEM, cotangent), (VMEM, nxt_got), (VMEM, wt), (VMEM, wd)],
        [(VMEM, (rows // 2, cols // 2, slots, ch)), (VMEM, tile),
         (VMEM, (rows, cols + 2, slots, ch)), (VMEM, half), (VMEM, half)]
        + [(VMEM, (cols // 2 * slots, ch))] * sides,
        flops=14 * tap,
    )
    send_a = passed(send_a, [prev])
    got_a = core_round(send_a, tm, grp)
    cot_top, cot_bot = from_bands(edge)
    half_tile = (rows // 2, cols, slots, ch)
    acts, upper = call(
        upper_kernel,
        "spatial_upper",
        [(VMEM, acts), (VMEM, prev), (VMEM, ws), (ANY, send_a)],
        [(VMEM, padded), (VMEM, half_tile)],
        flops=5 * tap,
        alias={0: 0},
    )
    _, plane, line, others = plan(tm, grp)
    parts_a = plane_send(keep_a, got_a, [upper])
    (lower,) = call(
        lower_kernel,
        "spatial_lower",
        [(VMEM, acts), (VMEM, ws)] + [(ANY, a) for a in parts_a],
        [(VMEM, half_tile)],
        flops=4 * tap,
    )
    half = (16, 7, 16, ch // 2)
    down, keep_b, send_b = call(
        forward_kernel,
        "forward",
        [count, (VMEM, xt), (VMEM, upper), (VMEM, lower), (VMEM, cott), (VMEM, gy), (VMEM, wt), (VMEM, wd),
         *((ANY, a) for a in parts_a)],
        [(VMEM, (slots * wide // 4, ch)), (VMEM, half), (VMEM, half)],
        [pltpu.VMEM(v, BF) for v in (tile, (3 * ch, slots * wide), (4 * ch, slots * wide // 4))],
        moved=1024,
        grant=14,
    )
    parts_a = four_round(parts_a, plane, tm, grp)
    send_b = passed(send_b, parts_a[1:3])
    parts_b = plane_send(keep_b, core_round(send_b, tm, grp), [])
    parts_b = four_round(parts_b, plane, tm, grp)
    parts = call(
        line_send_kernel,
        "line_send",
        [(VMEM, a) for a in parts_a + parts_b],
        [(VMEM, (16, 16, ch // 2))] * 4,
    )
    parts = four_round(list(parts), line, tm, grp)
    ins = [(VMEM, a) for a in parts]
    (mine,) = call(line_sum_kernel, "line_sum", ins, [(VMEM, parts[0].shape)])
    for bit in others:
        got = swap(mine, tm, grp, bit)
        (mine,) = call(add_kernel, "add", [(VMEM, mine), (VMEM, got)], [(VMEM, mine.shape)])
    parts = four_round([mine] * 4, line, tm, grp)
    (mine,) = call(
        line_gather_kernel, "line_gather", [(VMEM, a) for a in parts], [(VMEM, (4,) + mine.shape)]
    )
    parts = four_round([mine] * 4, plane, tm, grp)
    grad_x, down, token = call(
        functools.partial(grad_x_kernel, grp),
        "grad_x",
        [count, (VMEM, xt), (VMEM, gy), (VMEM, gs), (VMEM, cot_top), (VMEM, cot_bot), (VMEM, wt),
         (VMEM, wd), (VMEM, ws), (VMEM, down), (ANY, mine)],
        [(HBM, (slots, wide, ch)), (VMEM, cotangent.shape), TOKEN],
        [pltpu.VMEM(padded, BF), pltpu.VMEM((slots, wide, ch), BF), dma((1,))],
        flops=10 * tap,
    )
    ins = [(VMEM, a) for a in parts] + [(ANY, token)]
    (mine,) = call(plane_gather_kernel, "plane_gather", ins, [(VMEM, (16,) + mine.shape[1:])])
    got = core_round(mine, tm, grp)
    outs = finish(True, mine, [])
    sum_s, sum_t, sum_d = finish(False, got, outs)
    return (
        down,
        grad_x.reshape(frames_in.shape),
        sum_s.reshape(w_spatial.shape),
        sum_t,
        sum_d.reshape(w_down.shape),
    )


def solution(mesh):
    return jax.shard_map(
        functools.partial(body, mesh.shape["tm"], mesh.shape["grp"]),
        mesh=mesh,
        in_specs=(P("tm", "grp", None, None), P("tm"), P(), P(), P(), P("tm", "grp", None, None)),
        out_specs=(P("tm", "grp", None, None), P("tm", "grp", None, None), P(), P(), P()),
        check_vma=False,
    )
```

```python
import functools

import jax
import jax.numpy as jnp
from jax import lax
from jax.experimental import pallas as pl
from jax.experimental.pallas import tpu as pltpu
from jax.sharding import PartitionSpec as P

SLOTS = 16
OWN = 14
CH = 256
BF = jnp.bfloat16
F32 = jnp.float32


def mm(a, b):
    return lax.dot_general(a, b, (((1,), (0,)), ((), ())), preferred_element_type=F32)


def mm_nt(a, b):
    return lax.dot_general(a, b, (((1,), (1,)), ((), ())), preferred_element_type=F32)


def iotas(rows, cols):
    return (
        lax.broadcasted_iota(jnp.int32, (rows, cols), 0),
        lax.broadcasted_iota(jnp.int32, (rows, cols), 1),
    )


def to_slots(rows, frames, keep):
    a, b = iotas(rows * SLOTS, frames * rows)
    bits = rows.bit_length() - 1
    hit = ((a >> 4) == (b & (rows - 1))) & keep(b >> bits, a & 15)
    return jnp.where(hit, 1.0, 0.0).astype(BF)


def to_frames(rows):
    a, b = iotas(SLOTS * rows, rows * SLOTS)
    bits = rows.bit_length() - 1
    hit = ((a & (rows - 1)) == (b >> 4)) & ((a >> bits) == (b & 15))
    return jnp.where(hit, 1.0, 0.0).astype(BF)


def own_frames(count):
    return lambda frame, slot: (frame == slot) & (slot < count)


def own_and_next(count, blocks):
    after = jnp.where(lax.axis_index("tm") < blocks - 1, count, 64)
    return lambda frame, slot: ((frame < OWN) & (frame == slot) & (slot < count)) | (
        (frame >= OWN) & (slot == after + frame - OWN)
    )


def silu_norm(v):
    scaled = v * lax.rsqrt(jnp.mean(v * v, axis=-1, keepdims=True) + 1e-06)
    return scaled * (0.5 + 0.5 * jnp.tanh(0.5 * scaled))


def slot_mask(shape, count):
    return lax.broadcasted_iota(jnp.int32, shape, len(shape) - 2) < count


def grad_of_temporal(gy, wt_ref, count):
    n = gy.shape[0]
    flat = gy.reshape(n * SLOTS, CH)
    total = mm_nt(flat, wt_ref[2]).reshape(n, SLOTS, CH)
    for k in (1, 0):
        term = mm_nt(flat, wt_ref[k]).reshape(n, SLOTS, CH)
        total = total + pltpu.roll(term, SLOTS - (2 - k), 1)
    return jnp.where(slot_mask(total.shape, count), total, 0.0).astype(BF)


def place_bits():
    t, g = lax.axis_index("tm"), lax.axis_index("grp")
    return t & 1, ((t >> 1) & 1) + 2 * (g & 1), (t >> 2) & 3


def split_cores(value, keep_ref, send_ref, k):
    core, _, _ = place_bits()
    low, high = value[:, : CH // 2].astype(BF), value[:, CH // 2 :].astype(BF)
    keep_ref[:, k] = jnp.where(core == 0, low, high).reshape(16, 16, CH // 2)
    send_ref[:, k] = jnp.where(core == 0, high, low).reshape(16, 16, CH // 2)


def edges_kernel(bands, count_ref, x_ref, *outs):
    count = count_ref[0]
    band = lax.axis_index("grp")
    wide = x_ref.shape[1]
    if bands == 2:
        starts, lower = [jnp.where(band == 0, wide - 16, 0)], [band == 0]
    else:
        starts, lower = [wide - 16, 0], [True, False]
    place = to_slots(16, SLOTS, own_frames(count))
    for k, at in enumerate(starts):
        piece = x_ref[:, pl.ds(pl.multiple_of(at, 16), 16), :].reshape(SLOTS * 16, CH)
        v = mm(place, piece)
        v = jnp.where(lower[k], v[128:], v[:128])
        outs[k][...] = silu_norm(v).astype(BF)


def acts_kernel(count_ref, x_ref, _, xt_ref, acts_ref, at_ref, last_ref):
    count = count_ref[0]
    rows, cols = xt_ref.shape[0], xt_ref.shape[1]
    edge = jnp.zeros((rows + 2, SLOTS, CH), BF)
    acts_ref[:, 0] = edge
    acts_ref[:, cols + 1] = edge
    place = to_slots(16, SLOTS, own_frames(count))
    last = silu_norm(x_ref[pl.ds(count - 2, 2)].reshape(2 * rows * cols, CH).astype(F32))
    last_ref[0 : 2 * rows * cols] = last.astype(BF)

    def rows_of(q, _):
        at = pl.multiple_of(q * 16, 16)
        piece = x_ref[:, pl.ds(at, 16), :].reshape(SLOTS * 16, CH)
        v = mm(place, piece)
        xt_ref[pl.ds(2 * q, 2)] = v.astype(BF).reshape(2, cols, SLOTS, CH)
        a = silu_norm(v).astype(BF)
        acts_ref[pl.ds(2 * q + 1, 2), 1 : cols + 1] = a.reshape(2, cols, SLOTS, CH)
        flipped = a.T
        for i in range(3):
            at = pl.multiple_of((2 * q + 3 - i) * 128, 128)
            at_ref[i * CH : i * CH + CH, pl.ds(at, 256)] = flipped
        return 0

    lax.fori_loop(0, rows // 2, rows_of, 0, unroll=4)


def next_kernel(cot_ref, _, nxt_ref):
    nxt_ref[...] = cot_ref[0:2]


def halo_kernel(bands, count_ref, top_ref, bot_ref, *rest):
    acts_ref, at_ref, last_ref = rest[-3:]
    count = count_ref[0]
    band = lax.axis_index("grp")
    rows, cols = acts_ref.shape[0] - 2, acts_ref.shape[1] - 2
    halo = []
    for ref, flag, i, row in ((top_ref, band > 0, 0, 0), (bot_ref, band < bands - 1, 2, rows + 1)):
        a = jnp.where(flag, ref[...].astype(F32), 0.0).astype(BF)
        acts_ref[row, 1 : cols + 1] = a.reshape(cols, SLOTS, CH)
        at = (row - i + 2) * 128
        at_ref[i * CH : i * CH + CH, at : at + 128] = a.T
        halo.append(a)
    a, b = iotas(32, 256)
    pick = ((a & 15) == (b >> 4)) & ((b & 15) == count - 2 + (a >> 4))
    pick = jnp.where(pick, 1.0, 0.0).astype(BF)
    last_ref[2 * rows * cols :] = mm(pick, jnp.concatenate(halo, 0)).astype(BF)


def conv_rows(acts_ref, ws_ref, sp_ref, start):
    rows, cols = sp_ref.shape[0], sp_ref.shape[1]

    def rows_of(q, _):
        total = None
        for i in range(3):
            for j in range(3):
                left = acts_ref[pl.ds(start + 4 * q + i, 4), j : j + cols].reshape(
                    4 * cols * SLOTS, CH
                )
                term = mm(left, ws_ref[i * 3 + j])
                total = term if total is None else total + term
        sp_ref[pl.ds(4 * q, 4)] = total.astype(BF).reshape(4, cols, SLOTS, CH)
        return 0

    lax.fori_loop(0, rows // 4, rows_of, 0)


def upper_kernel(acts_in, prev_ref, ws_ref, _, acts_ref, sp_ref):
    rows, cols = acts_ref.shape[0] - 2, acts_ref.shape[1] - 2
    a, b = iotas(256, 32)
    place = ((a >> 4) == (b & 15)) & ((a & 15) == OWN + (b >> 4)) & (lax.axis_index("tm") > 0)
    place = jnp.where(place, 1.0, 0.0).astype(BF)
    size = rows * cols
    for q in range(rows // 2 + 1):
        if q == rows // 2:
            both, prev = slice(0, rows + 2, rows + 1), prev_ref[2 * size :]
        else:
            both = slice(2 * q + 1, 2 * q + 3)
            parts = [prev_ref[f * size + q * 16 : f * size + q * 16 + 16] for f in range(2)]
            prev = jnp.concatenate(parts, 0)
        prev = mm(place, prev).astype(BF).reshape(2, cols, SLOTS, CH)
        for k, row in enumerate(range(rows + 2)[both]):
            acts_ref[row, 1 : cols + 1] = acts_ref[row, 1 : cols + 1] + prev[k]

    conv_rows(acts_ref, ws_ref, sp_ref, 0)


def lower_kernel(acts_ref, ws_ref, *rest):
    sp_ref = rest[-1]
    conv_rows(acts_ref, ws_ref, sp_ref, sp_ref.shape[0])


def grad_spatial_kernel(
    blocks, bands, count_ref, at_ref, cot_ref, nxt_ref, wt_ref, wd_ref,
    cott_ref, gy_ref, gs_ref, keep_ref, send_ref, *edge_refs,
):
    count = count_ref[0]
    band = lax.axis_index("grp")
    rows, cols = gy_ref.shape[0], gy_ref.shape[1]
    edge = jnp.zeros((rows, SLOTS, CH), BF)
    gs_ref[:, 0] = edge
    gs_ref[:, cols + 1] = edge

    place_next = to_slots(16, SLOTS, own_and_next(count, blocks))
    halves = []
    for q in range(rows * cols // 64):
        four = slice(q * 4, q * 4 + 4)
        piece = jnp.concatenate(
            [cot_ref[0:OWN, four].reshape(OWN, 16, CH), nxt_ref[:, four].reshape(2, 16, CH)], 0
        ).reshape(SLOTS * 16, CH)
        halves.append(mm(place_next, piece).astype(BF))
    placed = jnp.concatenate(halves, 0)
    cott_ref[...] = placed.reshape(rows // 2, cols // 2, SLOTS, CH)
    for i in range(2):
        for j in range(2):
            g = mm_nt(placed, wd_ref[i * 2 + j]).astype(BF).reshape(rows // 2, cols // 2, SLOTS, CH)
            for r in range(rows // 2):
                for c in range(cols // 2):
                    gy_ref[2 * r + i, 2 * c + j] = g[r, c]
    last = cott_ref[rows // 2 - 1].reshape(cols // 2 * SLOTS, CH)
    first = cott_ref[0].reshape(cols // 2 * SLOTS, CH)
    if bands == 2:
        edge_refs[0][...] = jnp.where(band == 0, last, first)
    else:
        edge_refs[0][...] = last
        edge_refs[1][...] = first

    def grads_of(q, _):
        g = gy_ref[pl.ds(8 * q, 8)].reshape(8 * cols, SLOTS, CH)
        s = grad_of_temporal(g, wt_ref, count)
        gs_ref[pl.ds(8 * q, 8), 1 : cols + 1] = s.reshape(8, cols, SLOTS, CH)
        g = jnp.where(slot_mask(g.shape, count), g.astype(F32), 0.0)
        gy_ref[pl.ds(8 * q, 8)] = g.astype(BF).reshape(8, cols, SLOTS, CH)
        return 0

    lax.fori_loop(0, rows // 8, grads_of, 0)

    wide = rows * cols * SLOTS
    for j in range(3):
        right = gs_ref[:, 2 - j : 2 - j + cols].reshape(wide, CH)
        value = mm(at_ref[:, 256 : 256 + wide], right)
        for i in range(3):
            split_cores(value[i * CH : i * CH + CH], keep_ref, send_ref, i * 3 + j)


def forward_kernel(
    count_ref, xt_ref, upper_ref, lower_ref, cott_ref, gy_ref, wt_ref, wd_ref, *rest
):
    down_ref, keep_ref, send_ref, y_ref, st_ref, yt_ref = rest[-6:]
    count = count_ref[0]
    rows, cols = xt_ref.shape[0], xt_ref.shape[1]
    for q, sp_ref in enumerate((upper_ref, lower_ref)):
        s = sp_ref[...].reshape(8 * cols * SLOTS, CH).astype(F32)
        s = s.reshape(8 * cols, SLOTS, CH)
        total = None
        for k in range(3):
            shifted = s if k == 2 else pltpu.roll(s, 2 - k, 1)
            shifted = shifted.astype(BF).reshape(8 * cols * SLOTS, CH)
            at = slice(q * 1024, q * 1024 + 1024)
            st_ref[k * CH : k * CH + CH, at] = shifted.T
            term = mm(shifted, wt_ref[k])
            total = term if total is None else total + term
        x = xt_ref[8 * q : 8 * q + 8].reshape(8 * cols, SLOTS, CH).astype(F32)
        y = jnp.where(slot_mask(x.shape, count), x + total.reshape(x.shape), 0.0).astype(BF)
        y_ref[8 * q : 8 * q + 8] = y.reshape(8, cols, SLOTS, CH)

    wide = rows * cols * SLOTS
    value = mm(st_ref[...], gy_ref[...].reshape(wide, CH))
    for k in range(3):
        split_cores(value[k * CH : k * CH + CH], keep_ref, send_ref, k)

    small = wide // 4
    total = None
    for i in range(2):
        for j in range(2):
            tiles = [
                y_ref[2 * r + i, 2 * c + j] for r in range(rows // 2) for c in range(cols // 2)
            ]
            piece = jnp.concatenate(tiles, axis=0)
            k = i * 2 + j
            yt_ref[k * CH : k * CH + CH] = piece.T
            term = mm(piece, wd_ref[k])
            total = term if total is None else total + term
    down_ref[...] = total.astype(BF)
    value = mm(yt_ref[...], cott_ref[...].reshape(small, CH))
    for k in range(4):
        split_cores(value[k * CH : k * CH + CH], keep_ref, send_ref, 3 + k)


def grad_x_kernel(
    bands, count_ref, xt_ref, gy_ref, gs_ref, top_ref, bot_ref, wt_ref, wd_ref, ws_ref, slot_ref, *rest
):
    out_ref, down_ref, token_ref, pad_ref, buf, sems = rest[-6:]
    token_ref[...] = jnp.zeros_like(token_ref)
    count = count_ref[0]
    band = lax.axis_index("grp")
    rows, cols = xt_ref.shape[0], xt_ref.shape[1]
    pad_ref[1 : rows + 1] = gs_ref[...]
    edge = jnp.zeros((SLOTS, CH), BF)
    for ref, flag, i, row in ((top_ref, band > 0, 1, 0), (bot_ref, band < bands - 1, 0, rows + 1)):
        pair = [
            mm_nt(ref[...], wd_ref[i * 2 + j]).astype(BF).reshape(cols // 2, SLOTS, CH)
            for j in range(2)
        ]
        g = jnp.stack(pair, axis=1).reshape(cols, SLOTS, CH)
        pad_ref[row, 0] = edge
        pad_ref[row, 1 : cols + 1] = grad_of_temporal(g, wt_ref, jnp.where(flag, count, 0))
        pad_ref[row, cols + 1] = edge
    back = to_frames(16)

    def rows_of(q, _):
        total = None
        for i in range(3):
            for j in range(3):
                left = pad_ref[pl.ds(4 * q + 2 - i, 4), 2 - j : 2 - j + cols].reshape(
                    4 * cols * SLOTS, CH
                )
                term = mm_nt(left, ws_ref[i * 3 + j])
                total = term if total is None else total + term
        at = 4 * q
        v = xt_ref[pl.ds(at, 4)].reshape(4 * cols * SLOTS, CH).astype(F32)
        r = lax.rsqrt(jnp.mean(v * v, axis=-1, keepdims=True) + 1e-06)
        u = v * r
        s = 0.5 + 0.5 * jnp.tanh(0.5 * u)
        gu = total * (s * (1.0 + u * (1.0 - s)))
        dot = jnp.mean(gu * u, axis=-1, keepdims=True)
        gv = r * (gu - u * dot)
        gx = gy_ref[pl.ds(at, 4)].reshape(4 * cols * SLOTS, CH).astype(F32) + gv
        gx = gx.reshape(4 * cols, SLOTS, CH)
        gx = jnp.where(slot_mask(gx.shape, count), gx, 0.0).astype(BF).reshape(4 * cols * SLOTS, CH)
        for k in range(2):
            o = mm(back, gx[k * 256 : k * 256 + 256]).astype(BF)
            buf[:, pl.ds(pl.multiple_of((2 * q + k) * 16, 16), 16), :] = o.reshape(SLOTS, 16, CH)
        return 0

    lax.fori_loop(0, rows // 4, rows_of, 0)
    copy = pltpu.make_async_copy(buf, out_ref, sems.at[0])
    copy.start()
    for q in range(down_ref.shape[1] // 4):
        o = mm(back, slot_ref[q * 256 : q * 256 + 256]).astype(BF)
        down_ref[:, q * 4 : q * 4 + 4] = o.reshape(SLOTS, 4, cols // 2, CH)
    copy.wait()


ORDER = (0, 3, 2, 1)


def plane_send_kernel(keep_ref, got_ref, *rest):
    _, p, _ = place_bits()
    for r, out in zip(ORDER, rest[-4:]):
        at = pl.ds((p ^ r) * 4, 4)
        out[...] = (keep_ref[at].astype(F32) + got_ref[at].astype(F32)).astype(BF)


def line_send_kernel(*refs):
    outs = refs[8:]
    _, _, z = place_bits()
    for out, r in zip(outs, ORDER):
        at = 0
        for chain in (refs[:4], refs[4:8]):
            parts = [ref[z ^ r].astype(F32) for ref in chain]
            n = parts[0].shape[0]
            out[at : at + n] = (parts[0] + parts[1] + parts[2] + parts[3]).astype(BF)
            at += n


def line_sum_kernel(a_ref, b_ref, c_ref, d_ref, *rest):
    out_ref = rest[-1]
    parts = [ref[...].astype(F32) for ref in (a_ref, b_ref, c_ref, d_ref)]
    out_ref[...] = (parts[0] + parts[1] + parts[2] + parts[3]).astype(BF)


def line_gather_kernel(a_ref, b_ref, c_ref, d_ref, out_ref):
    _, _, z = place_bits()
    for r, ref in zip(ORDER, (a_ref, b_ref, c_ref, d_ref)):
        out_ref[z ^ r] = ref[...]


def plane_gather_kernel(a_ref, b_ref, c_ref, d_ref, _, out_ref):
    _, p, _ = place_bits()
    for r, ref in zip(ORDER, (a_ref, b_ref, c_ref, d_ref)):
        out_ref[pl.ds((p ^ r) * 4, 4)] = ref[...]


def add_kernel(a_ref, b_ref, out_ref):
    out_ref[...] = (a_ref[...].astype(F32) + b_ref[...].astype(F32)).astype(BF)


def pass_kernel(*_):
    pass


def finish_kernel(own, half_ref, *rest):
    buf, sems = rest[-2:]
    outs = rest[-5:-2]
    core, _, _ = place_bits()
    at = pl.multiple_of((core if own else 1 - core) * (CH // 2), CH // 2)
    copies = []
    k = 0
    for out in outs:
        for m in range(out.shape[0]):
            buf[k] = half_ref[:, k].reshape(CH, CH // 2).astype(F32)
            copies.append(
                pltpu.make_async_copy(buf.at[k], out.at[m, :, pl.ds(at, CH // 2)], sems.at[k])
            )
            copies[-1].start()
            k += 1
    for copy in copies:
        copy.wait()


VMEM = pl.BlockSpec(memory_space=pltpu.VMEM)
SMEM = pl.BlockSpec(memory_space=pltpu.SMEM)
ANY = pl.BlockSpec(memory_space=pl.ANY)
HBM = pl.BlockSpec(memory_space=pltpu.HBM)
TOKEN = (VMEM, (8, 128), F32)


def call(kernel, name, ins, outs, scratch=(), flops=0, alias=None, grant=10, moved=None):
    shapes = [jax.ShapeDtypeStruct(o[1], o[2] if len(o) > 2 else BF) for o in outs]
    if moved is None:
        moved = sum(a.size * a.dtype.itemsize for s, a in ins if s is not ANY)
        moved += sum(s.size * s.dtype.itemsize for s in shapes)
    return pl.pallas_call(
        kernel,
        out_shape=shapes,
        in_specs=[s for s, _ in ins],
        out_specs=[o[0] for o in outs],
        scratch_shapes=list(scratch),
        compiler_params=pltpu.CompilerParams(vmem_limit_bytes=grant * 2**20),
        cost_estimate=pl.CostEstimate(flops=flops, bytes_accessed=moved, transcendentals=0),
        input_output_aliases=alias or {},
        name=name,
    )(*[a for _, a in ins])


AXES = ("tm", "grp")


def plan(tm, grp):
    low, total = grp.bit_length() - 1, (tm * grp).bit_length() - 1
    plane, line = [low + 1, 0], [low + 2, low + 3]
    return low, plane, line, [b for b in range(total) if b not in [low] + plane + line]


def swap(value, tm, grp, *bits):
    flip = sum(1 << b for b in bits)
    return lax.ppermute(value, AXES, [(d, d ^ flip) for d in range(tm * grp)])


def core_round(value, tm, grp):
    return swap(value, tm, grp, plan(tm, grp)[0])


def four_round(parts, bits, tm, grp):
    return [
        parts[0],
        swap(parts[1], tm, grp, *bits),
        swap(parts[2], tm, grp, bits[1]),
        swap(parts[3], tm, grp, bits[0]),
    ]


def plane_send(keep, got, after):
    ins = [(VMEM, keep), (VMEM, got)] + [(ANY, a) for a in after]
    shape = (4, keep.shape[1], 16, CH // 2)
    return list(call(plane_send_kernel, "plane_send", ins, [(VMEM, shape)] * 4))


def passed(value, after):
    ins = [(ANY, value)] + [(ANY, a) for a in after]
    return call(pass_kernel, "pass", ins, [(ANY, value.shape)], alias={0: 0})[0]


def finish(own, half, before):
    n = half.shape[1]
    return list(
        call(
            functools.partial(finish_kernel, own),
            "finish",
            [(VMEM, half)] + [(HBM, a) for a in before],
            [(HBM, (m, CH, CH), F32) for m in (9, 3, 4)],
            [pltpu.VMEM((n, CH, CH // 2), F32), pltpu.SemaphoreType.DMA((n,))],
            alias={1 + i: i for i in range(len(before))},
        )
    )


def along(value, axis, by):
    count = lax.axis_size(axis)
    pairs = [(i, i + by) for i in range(count) if 0 <= i + by < count]
    return lax.ppermute(value, axis, pairs)


def around(value, axis, by):
    count = lax.axis_size(axis)
    return lax.ppermute(value, axis, [(i, (i + by) % count) for i in range(count)])


def from_bands(parts):
    if len(parts) == 1:
        got = lax.ppermute(parts[0], "grp", [(0, 1), (1, 0)])
        return got, got
    return along(parts[0], "grp", 1), along(parts[1], "grp", -1)


def body(tm, grp, frames_in, span_frames, w_spatial, w_temporal, w_down, cotangent):
    slots, rows, cols, ch = frames_in.shape
    wide = rows * cols
    x = frames_in.reshape(slots, wide, ch)
    ws = w_spatial.reshape(9, ch, ch)
    wd = w_down.reshape(4, ch, ch)
    wt = w_temporal
    count = (SMEM, span_frames)
    tap = 2 * slots * wide * ch * ch
    tile = (rows, cols, slots, ch)
    padded = (rows + 2, cols + 2, slots, ch)
    dma = pltpu.SemaphoreType.DMA

    sides = 1 if grp == 2 else 2
    edge = call(
        functools.partial(edges_kernel, grp),
        "edges",
        [count, (VMEM, x)],
        [(VMEM, (cols * slots, ch))] * sides,
        flops=tap // 8,
    )
    top, bot = from_bands(edge)
    last_shape = (2 * wide + 32, ch)
    at_shape = (3 * ch, (rows + 4) * 128)
    xt, acts, at, last_two = call(
        acts_kernel,
        "acts",
        [count, (VMEM, x), (ANY, edge[0])],
        [(VMEM, tile), (VMEM, padded), (VMEM, at_shape), (VMEM, last_shape)],
        flops=2 * tap,
    )
    (nxt,) = call(
        next_kernel,
        "next",
        [(VMEM, cotangent), (ANY, last_two)],
        [(VMEM, (2,) + cotangent.shape[1:])],
        moved=1024,
    )
    nxt_got = around(nxt, "tm", -1)
    acts, at, last_two = call(
        functools.partial(halo_kernel, grp),
        "halo",
        [count, (VMEM, top), (VMEM, bot), (VMEM, acts), (VMEM, at), (VMEM, last_two), (ANY, nxt),
         (VMEM, cotangent), (VMEM, wt), (VMEM, wd)],
        [(VMEM, padded), (VMEM, at_shape), (VMEM, last_shape)],
        alias={3: 0, 4: 1, 5: 2},
        moved=1024,
    )
    prev = around(last_two, "tm", 1)
    half = (16, 9, 16, ch // 2)
    cott, gy, gs, keep_a, send_a, *edge = call(
        functools.partial(grad_spatial_kernel, tm, grp),
        "grad_spatial",
        [count, (VMEM, at), (VMEM, cotangent), (VMEM, nxt_got), (VMEM, wt), (VMEM, wd)],
        [(VMEM, (rows // 2, cols // 2, slots, ch)), (VMEM, tile),
         (VMEM, (rows, cols + 2, slots, ch)), (VMEM, half), (VMEM, half)]
        + [(VMEM, (cols // 2 * slots, ch))] * sides,
        flops=14 * tap,
    )
    send_a = passed(send_a, [prev])
    got_a = core_round(send_a, tm, grp)
    cot_top, cot_bot = from_bands(edge)
    half_tile = (rows // 2, cols, slots, ch)
    acts, upper = call(
        upper_kernel,
        "spatial_upper",
        [(VMEM, acts), (VMEM, prev), (VMEM, ws), (ANY, send_a)],
        [(VMEM, padded), (VMEM, half_tile)],
        flops=5 * tap,
        alias={0: 0},
    )
    _, plane, line, others = plan(tm, grp)
    parts_a = plane_send(keep_a, got_a, [upper])
    (lower,) = call(
        lower_kernel,
        "spatial_lower",
        [(VMEM, acts), (VMEM, ws)] + [(ANY, a) for a in parts_a],
        [(VMEM, half_tile)],
        flops=4 * tap,
    )
    half = (16, 7, 16, ch // 2)
    down, keep_b, send_b = call(
        forward_kernel,
        "forward",
        [count, (VMEM, xt), (VMEM, upper), (VMEM, lower), (VMEM, cott), (VMEM, gy), (VMEM, wt), (VMEM, wd),
         *((ANY, a) for a in parts_a)],
        [(VMEM, (slots * wide // 4, ch)), (VMEM, half), (VMEM, half)],
        [pltpu.VMEM(v, BF) for v in (tile, (3 * ch, slots * wide), (4 * ch, slots * wide // 4))],
        moved=1024,
        grant=14,
    )
    parts_a = four_round(parts_a, plane, tm, grp)
    send_b = passed(send_b, parts_a[1:2])
    parts_b = plane_send(keep_b, core_round(send_b, tm, grp), [])
    parts_b = four_round(parts_b, plane, tm, grp)
    parts = call(
        line_send_kernel,
        "line_send",
        [(VMEM, a) for a in parts_a + parts_b],
        [(VMEM, (16, 16, ch // 2))] * 4,
    )
    parts = four_round(list(parts), line, tm, grp)
    ins = [(VMEM, a) for a in parts]
    (mine,) = call(line_sum_kernel, "line_sum", ins, [(VMEM, parts[0].shape)])
    for bit in others:
        got = swap(mine, tm, grp, bit)
        (mine,) = call(add_kernel, "add", [(VMEM, mine), (VMEM, got)], [(VMEM, mine.shape)])
    parts = four_round([mine] * 4, line, tm, grp)
    (mine,) = call(
        line_gather_kernel, "line_gather", [(VMEM, a) for a in parts], [(VMEM, (4,) + mine.shape)]
    )
    parts = four_round([mine] * 4, plane, tm, grp)
    grad_x, down, token = call(
        functools.partial(grad_x_kernel, grp),
        "grad_x",
        [count, (VMEM, xt), (VMEM, gy), (VMEM, gs), (VMEM, cot_top), (VMEM, cot_bot), (VMEM, wt),
         (VMEM, wd), (VMEM, ws), (VMEM, down), (ANY, mine)],
        [(HBM, (slots, wide, ch)), (VMEM, cotangent.shape), TOKEN],
        [pltpu.VMEM(padded, BF), pltpu.VMEM((slots, wide, ch), BF), dma((1,))],
        flops=10 * tap,
    )
    ins = [(VMEM, a) for a in parts] + [(ANY, token)]
    (mine,) = call(plane_gather_kernel, "plane_gather", ins, [(VMEM, (16,) + mine.shape[1:])])
    got = core_round(mine, tm, grp)
    outs = finish(True, mine, [])
    sum_s, sum_t, sum_d = finish(False, got, outs)
    return (
        down,
        grad_x.reshape(frames_in.shape),
        sum_s.reshape(w_spatial.shape),
        sum_t,
        sum_d.reshape(w_down.shape),
    )


def solution(mesh):
    return jax.shard_map(
        functools.partial(body, mesh.shape["tm"], mesh.shape["grp"]),
        mesh=mesh,
        in_specs=(P("tm", "grp", None, None), P("tm"), P(), P(), P(), P("tm", "grp", None, None)),
        out_specs=(P("tm", "grp", None, None), P("tm", "grp", None, None), P(), P(), P()),
        check_vma=False,
    )
```

```python
import functools

import jax
import jax.numpy as jnp
from jax import lax
from jax.experimental import pallas as pl
from jax.experimental.pallas import tpu as pltpu
from jax.sharding import PartitionSpec as P

SLOTS = 16
OWN = 14
CH = 256
BF = jnp.bfloat16
F32 = jnp.float32


def mm(a, b):
    return lax.dot_general(a, b, (((1,), (0,)), ((), ())), preferred_element_type=F32)


def mm_nt(a, b):
    return lax.dot_general(a, b, (((1,), (1,)), ((), ())), preferred_element_type=F32)


def iotas(rows, cols):
    return (
        lax.broadcasted_iota(jnp.int32, (rows, cols), 0),
        lax.broadcasted_iota(jnp.int32, (rows, cols), 1),
    )


def to_slots(rows, frames, keep):
    a, b = iotas(rows * SLOTS, frames * rows)
    bits = rows.bit_length() - 1
    hit = ((a >> 4) == (b & (rows - 1))) & keep(b >> bits, a & 15)
    return jnp.where(hit, 1.0, 0.0).astype(BF)


def to_frames(rows):
    a, b = iotas(SLOTS * rows, rows * SLOTS)
    bits = rows.bit_length() - 1
    hit = ((a & (rows - 1)) == (b >> 4)) & ((a >> bits) == (b & 15))
    return jnp.where(hit, 1.0, 0.0).astype(BF)


def own_frames(count):
    return lambda frame, slot: (frame == slot) & (slot < count)


def own_and_next(count, blocks):
    after = jnp.where(lax.axis_index("tm") < blocks - 1, count, 64)
    return lambda frame, slot: ((frame < OWN) & (frame == slot) & (slot < count)) | (
        (frame >= OWN) & (slot == after + frame - OWN)
    )


def silu_norm(v):
    scaled = v * lax.rsqrt(jnp.mean(v * v, axis=-1, keepdims=True) + 1e-06)
    return scaled * (0.5 + 0.5 * jnp.tanh(0.5 * scaled))


def pick_of(flag, a, b):
    return jnp.where(flag, a.astype(F32), b.astype(F32)).astype(BF)


def slot_mask(shape, count):
    return lax.broadcasted_iota(jnp.int32, shape, len(shape) - 2) < count


def grad_of_temporal(gy, wt_ref, count):
    n = gy.shape[0]
    flat = gy.reshape(n * SLOTS, CH)
    total = mm_nt(flat, wt_ref[2]).reshape(n, SLOTS, CH)
    for k in (1, 0):
        term = mm_nt(flat, wt_ref[k]).reshape(n, SLOTS, CH)
        total = total + pltpu.roll(term, SLOTS - (2 - k), 1)
    return jnp.where(slot_mask(total.shape, count), total, 0.0).astype(BF)


def place_bits():
    t, g = lax.axis_index("tm"), lax.axis_index("grp")
    return t & 1, ((t >> 1) & 1) + 2 * (g & 1), (t >> 2) & 3


def split_cores(value, keep_ref, send_ref, k):
    core, _, _ = place_bits()
    low, high = value[:, : CH // 2].astype(BF), value[:, CH // 2 :].astype(BF)
    keep_ref[:, k] = jnp.where(core == 0, low, high).reshape(16, 16, CH // 2)
    send_ref[:, k] = jnp.where(core == 0, high, low).reshape(16, 16, CH // 2)


def edges_kernel(bands, count_ref, x_ref, *outs):
    count = count_ref[0]
    band = lax.axis_index("grp")
    wide = x_ref.shape[1]
    if bands == 2:
        starts, lower = [jnp.where(band == 0, wide - 16, 0)], [band == 0]
    else:
        starts, lower = [wide - 16, 0], [True, False]
    place = to_slots(16, SLOTS, own_frames(count))
    for k, at in enumerate(starts):
        piece = x_ref[:, pl.ds(pl.multiple_of(at, 16), 16), :].reshape(SLOTS * 16, CH)
        v = mm(place, piece)
        v = jnp.where(lower[k], v[128:], v[:128])
        outs[k][...] = silu_norm(v).astype(BF)


def acts_kernel(count_ref, x_ref, _, xt_ref, acts_ref, at_ref, last_ref):
    count = count_ref[0]
    rows, cols = xt_ref.shape[0], xt_ref.shape[1]
    edge = jnp.zeros((rows + 2, SLOTS, CH), BF)
    acts_ref[:, 0] = edge
    acts_ref[:, cols + 1] = edge
    place = to_slots(16, SLOTS, own_frames(count))
    last = silu_norm(x_ref[pl.ds(count - 2, 2)].reshape(2 * rows * cols, CH).astype(F32))
    last_ref[0 : 2 * rows * cols] = last.astype(BF)

    def rows_of(q, _):
        at = pl.multiple_of(q * 16, 16)
        piece = x_ref[:, pl.ds(at, 16), :].reshape(SLOTS * 16, CH)
        v = mm(place, piece)
        xt_ref[pl.ds(2 * q, 2)] = v.astype(BF).reshape(2, cols, SLOTS, CH)
        a = silu_norm(v).astype(BF)
        acts_ref[pl.ds(2 * q + 1, 2), 1 : cols + 1] = a.reshape(2, cols, SLOTS, CH)
        flipped = a.T
        for i in range(3):
            at = pl.multiple_of((2 * q + 3 - i) * 128, 128)
            at_ref[i * CH : i * CH + CH, pl.ds(at, 256)] = flipped
        return 0

    lax.fori_loop(0, rows // 2, rows_of, 0, unroll=4)


def next_kernel(cot_ref, _, nxt_ref):
    nxt_ref[...] = cot_ref[0:2]


def halo_kernel(bands, count_ref, top_ref, bot_ref, *rest):
    acts_ref, at_ref, last_ref = rest[-3:]
    count = count_ref[0]
    band = lax.axis_index("grp")
    rows, cols = acts_ref.shape[0] - 2, acts_ref.shape[1] - 2
    halo = []
    for ref, flag, i, row in ((top_ref, band > 0, 0, 0), (bot_ref, band < bands - 1, 2, rows + 1)):
        a = jnp.where(flag, ref[...].astype(F32), 0.0).astype(BF)
        acts_ref[row, 1 : cols + 1] = a.reshape(cols, SLOTS, CH)
        at = (row - i + 2) * 128
        at_ref[i * CH : i * CH + CH, at : at + 128] = a.T
        halo.append(a)
    a, b = iotas(32, 256)
    pick = ((a & 15) == (b >> 4)) & ((b & 15) == count - 2 + (a >> 4))
    pick = jnp.where(pick, 1.0, 0.0).astype(BF)
    last_ref[2 * rows * cols :] = mm(pick, jnp.concatenate(halo, 0)).astype(BF)


def conv_rows(acts_ref, ws_ref, sp_ref, start):
    rows, cols = sp_ref.shape[0], sp_ref.shape[1]

    def rows_of(q, _):
        total = None
        for i in range(3):
            for j in range(3):
                left = acts_ref[pl.ds(start + 4 * q + i, 4), j : j + cols].reshape(
                    4 * cols * SLOTS, CH
                )
                term = mm(left, ws_ref[i * 3 + j])
                total = term if total is None else total + term
        sp_ref[pl.ds(4 * q, 4)] = total.astype(BF).reshape(4, cols, SLOTS, CH)
        return 0

    lax.fori_loop(0, rows // 4, rows_of, 0)


def upper_kernel(acts_in, inner_ref, outer_ref, ws_ref, _, acts_ref, sp_ref):
    rows, cols = acts_ref.shape[0] - 2, acts_ref.shape[1] - 2
    a, b = iotas(256, 32)
    place = ((a >> 4) == (b & 15)) & ((a & 15) == OWN + (b >> 4)) & (lax.axis_index("tm") > 0)
    place = jnp.where(place, 1.0, 0.0).astype(BF)
    size = rows * cols
    core, _, _ = place_bits()

    def prev_of(at, n):
        return pick_of(core == 1, inner_ref[at : at + n], outer_ref[at : at + n])

    for q in range(rows // 2 + 1):
        if q == rows // 2:
            both, prev = slice(0, rows + 2, rows + 1), prev_of(2 * size, 32)
        else:
            both = slice(2 * q + 1, 2 * q + 3)
            parts = [prev_of(f * size + q * 16, 16) for f in range(2)]
            prev = jnp.concatenate(parts, 0)
        prev = mm(place, prev).astype(BF).reshape(2, cols, SLOTS, CH)
        for k, row in enumerate(range(rows + 2)[both]):
            acts_ref[row, 1 : cols + 1] = acts_ref[row, 1 : cols + 1] + prev[k]

    conv_rows(acts_ref, ws_ref, sp_ref, 0)


def lower_kernel(acts_ref, ws_ref, *rest):
    sp_ref = rest[-1]
    conv_rows(acts_ref, ws_ref, sp_ref, sp_ref.shape[0])


def grad_spatial_kernel(
    blocks, bands, count_ref, at_ref, cot_ref, inner_ref, outer_ref, wt_ref, wd_ref,
    cott_ref, gy_ref, gs_ref, keep_ref, send_ref, *edge_refs,
):
    count = count_ref[0]
    band = lax.axis_index("grp")
    rows, cols = gy_ref.shape[0], gy_ref.shape[1]
    edge = jnp.zeros((rows, SLOTS, CH), BF)
    gs_ref[:, 0] = edge
    gs_ref[:, cols + 1] = edge

    place_next = to_slots(16, SLOTS, own_and_next(count, blocks))
    halves = []
    core, _, _ = place_bits()
    for q in range(rows * cols // 64):
        four = slice(q * 4, q * 4 + 4)
        piece = jnp.concatenate(
            [cot_ref[0:OWN, four].reshape(OWN, 16, CH), pick_of(core == 0, inner_ref[:, four], outer_ref[:, four]).reshape(2, 16, CH)], 0
        ).reshape(SLOTS * 16, CH)
        halves.append(mm(place_next, piece).astype(BF))
    placed = jnp.concatenate(halves, 0)
    cott_ref[...] = placed.reshape(rows // 2, cols // 2, SLOTS, CH)
    for i in range(2):
        for j in range(2):
            g = mm_nt(placed, wd_ref[i * 2 + j]).astype(BF).reshape(rows // 2, cols // 2, SLOTS, CH)
            for r in range(rows // 2):
                for c in range(cols // 2):
                    gy_ref[2 * r + i, 2 * c + j] = g[r, c]
    last = cott_ref[rows // 2 - 1].reshape(cols // 2 * SLOTS, CH)
    first = cott_ref[0].reshape(cols // 2 * SLOTS, CH)
    if bands == 2:
        edge_refs[0][...] = jnp.where(band == 0, last, first)
    else:
        edge_refs[0][...] = last
        edge_refs[1][...] = first

    def grads_of(q, _):
        g = gy_ref[pl.ds(8 * q, 8)].reshape(8 * cols, SLOTS, CH)
        s = grad_of_temporal(g, wt_ref, count)
        gs_ref[pl.ds(8 * q, 8), 1 : cols + 1] = s.reshape(8, cols, SLOTS, CH)
        g = jnp.where(slot_mask(g.shape, count), g.astype(F32), 0.0)
        gy_ref[pl.ds(8 * q, 8)] = g.astype(BF).reshape(8, cols, SLOTS, CH)
        return 0

    lax.fori_loop(0, rows // 8, grads_of, 0)

    wide = rows * cols * SLOTS
    for j in range(3):
        right = gs_ref[:, 2 - j : 2 - j + cols].reshape(wide, CH)
        value = mm(at_ref[:, 256 : 256 + wide], right)
        for i in range(3):
            split_cores(value[i * CH : i * CH + CH], keep_ref, send_ref, i * 3 + j)


def forward_kernel(
    count_ref, xt_ref, upper_ref, lower_ref, cott_ref, gy_ref, wt_ref, wd_ref, *rest
):
    down_ref, keep_ref, send_ref, y_ref, st_ref, yt_ref = rest[-6:]
    count = count_ref[0]
    rows, cols = xt_ref.shape[0], xt_ref.shape[1]
    for q, sp_ref in enumerate((upper_ref, lower_ref)):
        s = sp_ref[...].reshape(8 * cols * SLOTS, CH).astype(F32)
        s = s.reshape(8 * cols, SLOTS, CH)
        total = None
        for k in range(3):
            shifted = s if k == 2 else pltpu.roll(s, 2 - k, 1)
            shifted = shifted.astype(BF).reshape(8 * cols * SLOTS, CH)
            at = slice(q * 1024, q * 1024 + 1024)
            st_ref[k * CH : k * CH + CH, at] = shifted.T
            term = mm(shifted, wt_ref[k])
            total = term if total is None else total + term
        x = xt_ref[8 * q : 8 * q + 8].reshape(8 * cols, SLOTS, CH).astype(F32)
        y = jnp.where(slot_mask(x.shape, count), x + total.reshape(x.shape), 0.0).astype(BF)
        y_ref[8 * q : 8 * q + 8] = y.reshape(8, cols, SLOTS, CH)

    wide = rows * cols * SLOTS
    value = mm(st_ref[...], gy_ref[...].reshape(wide, CH))
    for k in range(3):
        split_cores(value[k * CH : k * CH + CH], keep_ref, send_ref, k)

    small = wide // 4
    total = None
    for i in range(2):
        for j in range(2):
            tiles = [
                y_ref[2 * r + i, 2 * c + j] for r in range(rows // 2) for c in range(cols // 2)
            ]
            piece = jnp.concatenate(tiles, axis=0)
            k = i * 2 + j
            yt_ref[k * CH : k * CH + CH] = piece.T
            term = mm(piece, wd_ref[k])
            total = term if total is None else total + term
    down_ref[...] = total.astype(BF)
    value = mm(yt_ref[...], cott_ref[...].reshape(small, CH))
    for k in range(4):
        split_cores(value[k * CH : k * CH + CH], keep_ref, send_ref, 3 + k)


def grad_x_kernel(
    bands, count_ref, xt_ref, gy_ref, gs_ref, top_ref, bot_ref, wt_ref, wd_ref, ws_ref, slot_ref, *rest
):
    out_ref, down_ref, token_ref, pad_ref, buf, sems = rest[-6:]
    token_ref[...] = jnp.zeros_like(token_ref)
    count = count_ref[0]
    band = lax.axis_index("grp")
    rows, cols = xt_ref.shape[0], xt_ref.shape[1]
    pad_ref[1 : rows + 1] = gs_ref[...]
    edge = jnp.zeros((SLOTS, CH), BF)
    for ref, flag, i, row in ((top_ref, band > 0, 1, 0), (bot_ref, band < bands - 1, 0, rows + 1)):
        pair = [
            mm_nt(ref[...], wd_ref[i * 2 + j]).astype(BF).reshape(cols // 2, SLOTS, CH)
            for j in range(2)
        ]
        g = jnp.stack(pair, axis=1).reshape(cols, SLOTS, CH)
        pad_ref[row, 0] = edge
        pad_ref[row, 1 : cols + 1] = grad_of_temporal(g, wt_ref, jnp.where(flag, count, 0))
        pad_ref[row, cols + 1] = edge
    back = to_frames(16)

    def rows_of(q, _):
        total = None
        for i in range(3):
            for j in range(3):
                left = pad_ref[pl.ds(4 * q + 2 - i, 4), 2 - j : 2 - j + cols].reshape(
                    4 * cols * SLOTS, CH
                )
                term = mm_nt(left, ws_ref[i * 3 + j])
                total = term if total is None else total + term
        at = 4 * q
        v = xt_ref[pl.ds(at, 4)].reshape(4 * cols * SLOTS, CH).astype(F32)
        r = lax.rsqrt(jnp.mean(v * v, axis=-1, keepdims=True) + 1e-06)
        u = v * r
        s = 0.5 + 0.5 * jnp.tanh(0.5 * u)
        gu = total * (s * (1.0 + u * (1.0 - s)))
        dot = jnp.mean(gu * u, axis=-1, keepdims=True)
        gv = r * (gu - u * dot)
        gx = gy_ref[pl.ds(at, 4)].reshape(4 * cols * SLOTS, CH).astype(F32) + gv
        gx = gx.reshape(4 * cols, SLOTS, CH)
        gx = jnp.where(slot_mask(gx.shape, count), gx, 0.0).astype(BF).reshape(4 * cols * SLOTS, CH)
        for k in range(2):
            o = mm(back, gx[k * 256 : k * 256 + 256]).astype(BF)
            buf[:, pl.ds(pl.multiple_of((2 * q + k) * 16, 16), 16), :] = o.reshape(SLOTS, 16, CH)
        return 0

    lax.fori_loop(0, rows // 4, rows_of, 0)
    copy = pltpu.make_async_copy(buf, out_ref, sems.at[0])
    copy.start()
    for q in range(down_ref.shape[1] // 4):
        o = mm(back, slot_ref[q * 256 : q * 256 + 256]).astype(BF)
        down_ref[:, q * 4 : q * 4 + 4] = o.reshape(SLOTS, 4, cols // 2, CH)
    copy.wait()


ORDER = (0, 3, 2, 1)


def plane_send_kernel(keep_ref, got_ref, *rest):
    _, p, _ = place_bits()
    for r, out in zip(ORDER, rest[-4:]):
        at = pl.ds((p ^ r) * 4, 4)
        out[...] = (keep_ref[at].astype(F32) + got_ref[at].astype(F32)).astype(BF)


def line_send_kernel(*refs):
    outs = refs[8:]
    _, _, z = place_bits()
    for out, r in zip(outs, ORDER):
        at = 0
        for chain in (refs[:4], refs[4:8]):
            parts = [ref[z ^ r].astype(F32) for ref in chain]
            n = parts[0].shape[0]
            out[at : at + n] = (parts[0] + parts[1] + parts[2] + parts[3]).astype(BF)
            at += n


def line_sum_kernel(a_ref, b_ref, c_ref, d_ref, *rest):
    out_ref = rest[-1]
    parts = [ref[...].astype(F32) for ref in (a_ref, b_ref, c_ref, d_ref)]
    out_ref[...] = (parts[0] + parts[1] + parts[2] + parts[3]).astype(BF)


def line_gather_kernel(a_ref, b_ref, c_ref, d_ref, out_ref):
    _, _, z = place_bits()
    for r, ref in zip(ORDER, (a_ref, b_ref, c_ref, d_ref)):
        out_ref[z ^ r] = ref[...]


def plane_gather_kernel(a_ref, b_ref, c_ref, d_ref, _, out_ref):
    _, p, _ = place_bits()
    for r, ref in zip(ORDER, (a_ref, b_ref, c_ref, d_ref)):
        out_ref[pl.ds((p ^ r) * 4, 4)] = ref[...]


def add_kernel(a_ref, b_ref, out_ref):
    out_ref[...] = (a_ref[...].astype(F32) + b_ref[...].astype(F32)).astype(BF)


def pass_kernel(*_):
    pass


def finish_kernel(own, half_ref, *rest):
    buf, sems = rest[-2:]
    outs = rest[-5:-2]
    core, _, _ = place_bits()
    at = pl.multiple_of((core if own else 1 - core) * (CH // 2), CH // 2)
    copies = []
    k = 0
    for out in outs:
        for m in range(out.shape[0]):
            buf[k] = half_ref[:, k].reshape(CH, CH // 2).astype(F32)
            copies.append(
                pltpu.make_async_copy(buf.at[k], out.at[m, :, pl.ds(at, CH // 2)], sems.at[k])
            )
            copies[-1].start()
            k += 1
    for copy in copies:
        copy.wait()


VMEM = pl.BlockSpec(memory_space=pltpu.VMEM)
SMEM = pl.BlockSpec(memory_space=pltpu.SMEM)
ANY = pl.BlockSpec(memory_space=pl.ANY)
HBM = pl.BlockSpec(memory_space=pltpu.HBM)
TOKEN = (VMEM, (8, 128), F32)


def call(kernel, name, ins, outs, scratch=(), flops=0, alias=None, grant=10, moved=None):
    shapes = [jax.ShapeDtypeStruct(o[1], o[2] if len(o) > 2 else BF) for o in outs]
    if moved is None:
        moved = sum(a.size * a.dtype.itemsize for s, a in ins if s is not ANY)
        moved += sum(s.size * s.dtype.itemsize for s in shapes)
    return pl.pallas_call(
        kernel,
        out_shape=shapes,
        in_specs=[s for s, _ in ins],
        out_specs=[o[0] for o in outs],
        scratch_shapes=list(scratch),
        compiler_params=pltpu.CompilerParams(vmem_limit_bytes=grant * 2**20),
        cost_estimate=pl.CostEstimate(flops=flops, bytes_accessed=moved, transcendentals=0),
        input_output_aliases=alias or {},
        name=name,
    )(*[a for _, a in ins])


AXES = ("tm", "grp")


def plan(tm, grp):
    low, total = grp.bit_length() - 1, (tm * grp).bit_length() - 1
    plane, line = [low + 1, 0], [low + 2, low + 3]
    return low, plane, line, [b for b in range(total) if b not in [low] + plane + line]


def swap(value, tm, grp, *bits):
    flip = sum(1 << b for b in bits)
    return lax.ppermute(value, AXES, [(d, d ^ flip) for d in range(tm * grp)])


def core_round(value, tm, grp):
    return swap(value, tm, grp, plan(tm, grp)[0])


def four_round(parts, bits, tm, grp):
    return [
        parts[0],
        swap(parts[1], tm, grp, *bits),
        swap(parts[2], tm, grp, bits[1]),
        swap(parts[3], tm, grp, bits[0]),
    ]


def plane_send(keep, got, after):
    ins = [(VMEM, keep), (VMEM, got)] + [(ANY, a) for a in after]
    shape = (4, keep.shape[1], 16, CH // 2)
    return list(call(plane_send_kernel, "plane_send", ins, [(VMEM, shape)] * 4))


def passed(value, after):
    ins = [(ANY, value)] + [(ANY, a) for a in after]
    return call(pass_kernel, "pass", ins, [(ANY, value.shape)], alias={0: 0})[0]


def finish(own, half, before):
    n = half.shape[1]
    return list(
        call(
            functools.partial(finish_kernel, own),
            "finish",
            [(VMEM, half)] + [(HBM, a) for a in before],
            [(HBM, (m, CH, CH), F32) for m in (9, 3, 4)],
            [pltpu.VMEM((n, CH, CH // 2), F32), pltpu.SemaphoreType.DMA((n,))],
            alias={1 + i: i for i in range(len(before))},
        )
    )


def along(value, axis, by):
    count = lax.axis_size(axis)
    pairs = [(i, i + by) for i in range(count) if 0 <= i + by < count]
    return lax.ppermute(value, axis, pairs)


def both_neighbours(value):
    count = lax.axis_size("tm")
    inner = [(i, i ^ 1) for i in range(count)]
    outer = [(i, min(max(((i + 1) ^ 1) - 1, 0), count - 1)) for i in range(count)]
    return lax.ppermute(value, "tm", inner), lax.ppermute(value, "tm", outer)


def from_bands(parts):
    if len(parts) == 1:
        got = lax.ppermute(parts[0], "grp", [(0, 1), (1, 0)])
        return got, got
    return along(parts[0], "grp", 1), along(parts[1], "grp", -1)


def body(tm, grp, frames_in, span_frames, w_spatial, w_temporal, w_down, cotangent):
    slots, rows, cols, ch = frames_in.shape
    wide = rows * cols
    x = frames_in.reshape(slots, wide, ch)
    ws = w_spatial.reshape(9, ch, ch)
    wd = w_down.reshape(4, ch, ch)
    wt = w_temporal
    count = (SMEM, span_frames)
    tap = 2 * slots * wide * ch * ch
    tile = (rows, cols, slots, ch)
    padded = (rows + 2, cols + 2, slots, ch)
    dma = pltpu.SemaphoreType.DMA

    sides = 1 if grp == 2 else 2
    edge = call(
        functools.partial(edges_kernel, grp),
        "edges",
        [count, (VMEM, x)],
        [(VMEM, (cols * slots, ch))] * sides,
        flops=tap // 8,
    )
    top, bot = from_bands(edge)
    last_shape = (2 * wide + 32, ch)
    at_shape = (3 * ch, (rows + 4) * 128)
    xt, acts, at, last_two = call(
        acts_kernel,
        "acts",
        [count, (VMEM, x), (ANY, edge[0])],
        [(VMEM, tile), (VMEM, padded), (VMEM, at_shape), (VMEM, last_shape)],
        flops=2 * tap,
    )
    (nxt,) = call(
        next_kernel,
        "next",
        [(VMEM, cotangent), (ANY, last_two)],
        [(VMEM, (2,) + cotangent.shape[1:])],
        moved=1024,
    )
    nxt_got = both_neighbours(nxt)
    acts, at, last_two = call(
        functools.partial(halo_kernel, grp),
        "halo",
        [count, (VMEM, top), (VMEM, bot), (VMEM, acts), (VMEM, at), (VMEM, last_two), (ANY, nxt),
         (VMEM, cotangent), (VMEM, wt), (VMEM, wd)],
        [(VMEM, padded), (VMEM, at_shape), (VMEM, last_shape)],
        alias={3: 0, 4: 1, 5: 2},
        moved=1024,
    )
    prev = both_neighbours(last_two)
    half = (16, 9, 16, ch // 2)
    cott, gy, gs, keep_a, send_a, *edge = call(
        functools.partial(grad_spatial_kernel, tm, grp),
        "grad_spatial",
        [count, (VMEM, at), (VMEM, cotangent), (VMEM, nxt_got[0]), (VMEM, nxt_got[1]), (VMEM, wt), (VMEM, wd)],
        [(VMEM, (rows // 2, cols // 2, slots, ch)), (VMEM, tile),
         (VMEM, (rows, cols + 2, slots, ch)), (VMEM, half), (VMEM, half)]
        + [(VMEM, (cols // 2 * slots, ch))] * sides,
        flops=14 * tap,
    )
    send_a = passed(send_a, list(prev))
    got_a = core_round(send_a, tm, grp)
    cot_top, cot_bot = from_bands(edge)
    half_tile = (rows // 2, cols, slots, ch)
    acts, upper = call(
        upper_kernel,
        "spatial_upper",
        [(VMEM, acts), (VMEM, prev[0]), (VMEM, prev[1]), (VMEM, ws), (ANY, send_a)],
        [(VMEM, padded), (VMEM, half_tile)],
        flops=5 * tap,
        alias={0: 0},
    )
    _, plane, line, others = plan(tm, grp)
    parts_a = plane_send(keep_a, got_a, [upper])
    (lower,) = call(
        lower_kernel,
        "spatial_lower",
        [(VMEM, acts), (VMEM, ws)] + [(ANY, a) for a in parts_a],
        [(VMEM, half_tile)],
        flops=4 * tap,
    )
    half = (16, 7, 16, ch // 2)
    down, keep_b, send_b = call(
        forward_kernel,
        "forward",
        [count, (VMEM, xt), (VMEM, upper), (VMEM, lower), (VMEM, cott), (VMEM, gy), (VMEM, wt), (VMEM, wd),
         *((ANY, a) for a in parts_a)],
        [(VMEM, (slots * wide // 4, ch)), (VMEM, half), (VMEM, half)],
        [pltpu.VMEM(v, BF) for v in (tile, (3 * ch, slots * wide), (4 * ch, slots * wide // 4))],
        moved=1024,
        grant=14,
    )
    parts_a = four_round(parts_a, plane, tm, grp)
    send_b = passed(send_b, parts_a[1:2])
    parts_b = plane_send(keep_b, core_round(send_b, tm, grp), [])
    parts_b = four_round(parts_b, plane, tm, grp)
    parts = call(
        line_send_kernel,
        "line_send",
        [(VMEM, a) for a in parts_a + parts_b],
        [(VMEM, (16, 16, ch // 2))] * 4,
    )
    parts = four_round(list(parts), line, tm, grp)
    ins = [(VMEM, a) for a in parts]
    (mine,) = call(line_sum_kernel, "line_sum", ins, [(VMEM, parts[0].shape)])
    for bit in others:
        got = swap(mine, tm, grp, bit)
        (mine,) = call(add_kernel, "add", [(VMEM, mine), (VMEM, got)], [(VMEM, mine.shape)])
    parts = four_round([mine] * 4, line, tm, grp)
    (mine,) = call(
        line_gather_kernel, "line_gather", [(VMEM, a) for a in parts], [(VMEM, (4,) + mine.shape)]
    )
    parts = four_round([mine] * 4, plane, tm, grp)
    grad_x, down, token = call(
        functools.partial(grad_x_kernel, grp),
        "grad_x",
        [count, (VMEM, xt), (VMEM, gy), (VMEM, gs), (VMEM, cot_top), (VMEM, cot_bot), (VMEM, wt),
         (VMEM, wd), (VMEM, ws), (VMEM, down), (ANY, mine)],
        [(HBM, (slots, wide, ch)), (VMEM, cotangent.shape), TOKEN],
        [pltpu.VMEM(padded, BF), pltpu.VMEM((slots, wide, ch), BF), dma((1,))],
        flops=10 * tap,
    )
    ins = [(VMEM, a) for a in parts] + [(ANY, token)]
    (mine,) = call(plane_gather_kernel, "plane_gather", ins, [(VMEM, (16,) + mine.shape[1:])])
    got = core_round(mine, tm, grp)
    outs = finish(True, mine, [])
    sum_s, sum_t, sum_d = finish(False, got, outs)
    return (
        down,
        grad_x.reshape(frames_in.shape),
        sum_s.reshape(w_spatial.shape),
        sum_t,
        sum_d.reshape(w_down.shape),
    )


def solution(mesh):
    return jax.shard_map(
        functools.partial(body, mesh.shape["tm"], mesh.shape["grp"]),
        mesh=mesh,
        in_specs=(P("tm", "grp", None, None), P("tm"), P(), P(), P(), P("tm", "grp", None, None)),
        out_specs=(P("tm", "grp", None, None), P("tm", "grp", None, None), P(), P(), P()),
        check_vma=False,
    )
```

```python
import functools

import jax
import jax.numpy as jnp
from jax import lax
from jax.experimental import pallas as pl
from jax.experimental.pallas import tpu as pltpu
from jax.sharding import PartitionSpec as P

SLOTS = 16
OWN = 14
CH = 256
BF = jnp.bfloat16
F32 = jnp.float32


def mm(a, b):
    return lax.dot_general(a, b, (((1,), (0,)), ((), ())), preferred_element_type=F32)


def mm_nt(a, b):
    return lax.dot_general(a, b, (((1,), (1,)), ((), ())), preferred_element_type=F32)


def iotas(rows, cols):
    return (
        lax.broadcasted_iota(jnp.int32, (rows, cols), 0),
        lax.broadcasted_iota(jnp.int32, (rows, cols), 1),
    )


def to_slots(rows, frames, keep):
    a, b = iotas(rows * SLOTS, frames * rows)
    bits = rows.bit_length() - 1
    hit = ((a >> 4) == (b & (rows - 1))) & keep(b >> bits, a & 15)
    return jnp.where(hit, 1.0, 0.0).astype(BF)


def to_frames(rows):
    a, b = iotas(SLOTS * rows, rows * SLOTS)
    bits = rows.bit_length() - 1
    hit = ((a & (rows - 1)) == (b >> 4)) & ((a >> bits) == (b & 15))
    return jnp.where(hit, 1.0, 0.0).astype(BF)


def own_frames(count):
    return lambda frame, slot: (frame == slot) & (slot < count)


def own_and_next(count, blocks):
    after = jnp.where(lax.axis_index("tm") < blocks - 1, count, 64)
    return lambda frame, slot: ((frame < OWN) & (frame == slot) & (slot < count)) | (
        (frame >= OWN) & (slot == after + frame - OWN)
    )


def silu_norm(v):
    scaled = v * lax.rsqrt(jnp.mean(v * v, axis=-1, keepdims=True) + 1e-06)
    return scaled * (0.5 + 0.5 * jnp.tanh(0.5 * scaled))


def slot_mask(shape, count):
    return lax.broadcasted_iota(jnp.int32, shape, len(shape) - 2) < count


def grad_of_temporal(gy, wt_ref, count):
    n = gy.shape[0]
    flat = gy.reshape(n * SLOTS, CH)
    total = mm_nt(flat, wt_ref[2]).reshape(n, SLOTS, CH)
    for k in (1, 0):
        term = mm_nt(flat, wt_ref[k]).reshape(n, SLOTS, CH)
        total = total + pltpu.roll(term, SLOTS - (2 - k), 1)
    return jnp.where(slot_mask(total.shape, count), total, 0.0).astype(BF)


def place_bits():
    t, g = lax.axis_index("tm"), lax.axis_index("grp")
    return t & 1, ((t >> 1) & 1) + 2 * (g & 1), (t >> 2) & 3


def split_cores(value, keep_ref, send_ref, k):
    core, _, _ = place_bits()
    low, high = value[:, : CH // 2].astype(BF), value[:, CH // 2 :].astype(BF)
    keep_ref[:, k] = jnp.where(core == 0, low, high).reshape(16, 16, CH // 2)
    send_ref[:, k] = jnp.where(core == 0, high, low).reshape(16, 16, CH // 2)


def edges_kernel(bands, count_ref, x_ref, *outs):
    count = count_ref[0]
    band = lax.axis_index("grp")
    wide = x_ref.shape[1]
    if bands == 2:
        starts, lower = [jnp.where(band == 0, wide - 16, 0)], [band == 0]
    else:
        starts, lower = [wide - 16, 0], [True, False]
    place = to_slots(16, SLOTS, own_frames(count))
    for k, at in enumerate(starts):
        piece = x_ref[:, pl.ds(pl.multiple_of(at, 16), 16), :].reshape(SLOTS * 16, CH)
        v = mm(place, piece)
        v = jnp.where(lower[k], v[128:], v[:128])
        outs[k][...] = silu_norm(v).astype(BF)


def acts_kernel(count_ref, x_ref, _, xt_ref, acts_ref, at_ref, last_ref):
    count = count_ref[0]
    rows, cols = xt_ref.shape[0], xt_ref.shape[1]
    edge = jnp.zeros((rows + 2, SLOTS, CH), BF)
    acts_ref[:, 0] = edge
    acts_ref[:, cols + 1] = edge
    place = to_slots(16, SLOTS, own_frames(count))
    last = silu_norm(x_ref[pl.ds(count - 2, 2)].reshape(2 * rows * cols, CH).astype(F32))
    last_ref[0 : 2 * rows * cols] = last.astype(BF)

    def rows_of(q, _):
        at = pl.multiple_of(q * 16, 16)
        piece = x_ref[:, pl.ds(at, 16), :].reshape(SLOTS * 16, CH)
        v = mm(place, piece)
        xt_ref[pl.ds(2 * q, 2)] = v.astype(BF).reshape(2, cols, SLOTS, CH)
        a = silu_norm(v).astype(BF)
        acts_ref[pl.ds(2 * q + 1, 2), 1 : cols + 1] = a.reshape(2, cols, SLOTS, CH)
        flipped = a.T
        for i in range(3):
            at = pl.multiple_of((2 * q + 3 - i) * 128, 128)
            at_ref[i * CH : i * CH + CH, pl.ds(at, 256)] = flipped
        return 0

    lax.fori_loop(0, rows // 2, rows_of, 0, unroll=4)


def next_kernel(cot_ref, _, nxt_ref):
    nxt_ref[...] = cot_ref[0:2]


def halo_kernel(bands, count_ref, top_ref, bot_ref, *rest):
    acts_ref, at_ref, last_ref = rest[-3:]
    count = count_ref[0]
    band = lax.axis_index("grp")
    rows, cols = acts_ref.shape[0] - 2, acts_ref.shape[1] - 2
    halo = []
    for ref, flag, i, row in ((top_ref, band > 0, 0, 0), (bot_ref, band < bands - 1, 2, rows + 1)):
        a = jnp.where(flag, ref[...].astype(F32), 0.0).astype(BF)
        acts_ref[row, 1 : cols + 1] = a.reshape(cols, SLOTS, CH)
        at = (row - i + 2) * 128
        at_ref[i * CH : i * CH + CH, at : at + 128] = a.T
        halo.append(a)
    a, b = iotas(32, 256)
    pick = ((a & 15) == (b >> 4)) & ((b & 15) == count - 2 + (a >> 4))
    pick = jnp.where(pick, 1.0, 0.0).astype(BF)
    last_ref[2 * rows * cols :] = mm(pick, jnp.concatenate(halo, 0)).astype(BF)


def conv_rows(acts_ref, ws_ref, sp_ref, start):
    rows, cols = sp_ref.shape[0], sp_ref.shape[1]

    def rows_of(q, _):
        total = None
        for i in range(3):
            for j in range(3):
                left = acts_ref[pl.ds(start + 4 * q + i, 4), j : j + cols].reshape(
                    4 * cols * SLOTS, CH
                )
                term = mm(left, ws_ref[i * 3 + j])
                total = term if total is None else total + term
        sp_ref[pl.ds(4 * q, 4)] = total.astype(BF).reshape(4, cols, SLOTS, CH)
        return 0

    lax.fori_loop(0, rows // 4, rows_of, 0)


def upper_kernel(acts_in, prev_ref, ws_ref, _, acts_ref, sp_ref):
    rows, cols = acts_ref.shape[0] - 2, acts_ref.shape[1] - 2
    a, b = iotas(256, 32)
    place = ((a >> 4) == (b & 15)) & ((a & 15) == OWN + (b >> 4)) & (lax.axis_index("tm") > 0)
    place = jnp.where(place, 1.0, 0.0).astype(BF)
    size = rows * cols
    for q in range(rows // 2 + 1):
        if q == rows // 2:
            both, prev = slice(0, rows + 2, rows + 1), prev_ref[2 * size :]
        else:
            both = slice(2 * q + 1, 2 * q + 3)
            parts = [prev_ref[f * size + q * 16 : f * size + q * 16 + 16] for f in range(2)]
            prev = jnp.concatenate(parts, 0)
        prev = mm(place, prev).astype(BF).reshape(2, cols, SLOTS, CH)
        for k, row in enumerate(range(rows + 2)[both]):
            acts_ref[row, 1 : cols + 1] = acts_ref[row, 1 : cols + 1] + prev[k]

    conv_rows(acts_ref, ws_ref, sp_ref, 0)


def lower_kernel(acts_ref, ws_ref, *rest):
    sp_ref = rest[-1]
    conv_rows(acts_ref, ws_ref, sp_ref, sp_ref.shape[0])


def grad_spatial_kernel(
    blocks, bands, count_ref, at_ref, cot_ref, nxt_ref, wt_ref, wd_ref,
    cott_ref, gy_ref, gs_ref, keep_ref, send_ref, *edge_refs,
):
    count = count_ref[0]
    band = lax.axis_index("grp")
    rows, cols = gy_ref.shape[0], gy_ref.shape[1]
    edge = jnp.zeros((rows, SLOTS, CH), BF)
    gs_ref[:, 0] = edge
    gs_ref[:, cols + 1] = edge

    place_next = to_slots(16, SLOTS, own_and_next(count, blocks))
    halves = []
    for q in range(rows * cols // 64):
        four = slice(q * 4, q * 4 + 4)
        piece = jnp.concatenate(
            [cot_ref[0:OWN, four].reshape(OWN, 16, CH), nxt_ref[:, four].reshape(2, 16, CH)], 0
        ).reshape(SLOTS * 16, CH)
        halves.append(mm(place_next, piece).astype(BF))
    placed = jnp.concatenate(halves, 0)
    cott_ref[...] = placed.reshape(rows // 2, cols // 2, SLOTS, CH)
    for i in range(2):
        for j in range(2):
            g = mm_nt(placed, wd_ref[i * 2 + j]).astype(BF).reshape(rows // 2, cols // 2, SLOTS, CH)
            for r in range(rows // 2):
                for c in range(cols // 2):
                    gy_ref[2 * r + i, 2 * c + j] = g[r, c]
    last = cott_ref[rows // 2 - 1].reshape(cols // 2 * SLOTS, CH)
    first = cott_ref[0].reshape(cols // 2 * SLOTS, CH)
    if bands == 2:
        edge_refs[0][...] = jnp.where(band == 0, last, first)
    else:
        edge_refs[0][...] = last
        edge_refs[1][...] = first

    def grads_of(q, _):
        g = gy_ref[pl.ds(8 * q, 8)].reshape(8 * cols, SLOTS, CH)
        s = grad_of_temporal(g, wt_ref, count)
        gs_ref[pl.ds(8 * q, 8), 1 : cols + 1] = s.reshape(8, cols, SLOTS, CH)
        g = jnp.where(slot_mask(g.shape, count), g.astype(F32), 0.0)
        gy_ref[pl.ds(8 * q, 8)] = g.astype(BF).reshape(8, cols, SLOTS, CH)
        return 0

    lax.fori_loop(0, rows // 8, grads_of, 0)

    wide = rows * cols * SLOTS
    for j in range(3):
        right = gs_ref[:, 2 - j : 2 - j + cols].reshape(wide, CH)
        value = mm(at_ref[:, 256 : 256 + wide], right)
        for i in range(3):
            split_cores(value[i * CH : i * CH + CH], keep_ref, send_ref, i * 3 + j)


def forward_kernel(
    count_ref, xt_ref, upper_ref, lower_ref, cott_ref, gy_ref, wt_ref, wd_ref, *rest
):
    down_ref, keep_ref, send_ref, y_ref, st_ref, yt_ref = rest[-6:]
    count = count_ref[0]
    rows, cols = xt_ref.shape[0], xt_ref.shape[1]
    for q, sp_ref in enumerate((upper_ref, lower_ref)):
        s = sp_ref[...].reshape(8 * cols * SLOTS, CH).astype(F32)
        s = s.reshape(8 * cols, SLOTS, CH)
        total = None
        for k in range(3):
            shifted = s if k == 2 else pltpu.roll(s, 2 - k, 1)
            shifted = shifted.astype(BF).reshape(8 * cols * SLOTS, CH)
            at = slice(q * 1024, q * 1024 + 1024)
            st_ref[k * CH : k * CH + CH, at] = shifted.T
            term = mm(shifted, wt_ref[k])
            total = term if total is None else total + term
        x = xt_ref[8 * q : 8 * q + 8].reshape(8 * cols, SLOTS, CH).astype(F32)
        y = jnp.where(slot_mask(x.shape, count), x + total.reshape(x.shape), 0.0).astype(BF)
        y_ref[8 * q : 8 * q + 8] = y.reshape(8, cols, SLOTS, CH)

    wide = rows * cols * SLOTS
    value = mm(st_ref[...], gy_ref[...].reshape(wide, CH))
    for k in range(3):
        split_cores(value[k * CH : k * CH + CH], keep_ref, send_ref, k)

    small = wide // 4
    total = None
    for i in range(2):
        for j in range(2):
            tiles = [
                y_ref[2 * r + i, 2 * c + j] for r in range(rows // 2) for c in range(cols // 2)
            ]
            piece = jnp.concatenate(tiles, axis=0)
            k = i * 2 + j
            yt_ref[k * CH : k * CH + CH] = piece.T
            term = mm(piece, wd_ref[k])
            total = term if total is None else total + term
    down_ref[...] = total.astype(BF)
    value = mm(yt_ref[...], cott_ref[...].reshape(small, CH))
    for k in range(4):
        split_cores(value[k * CH : k * CH + CH], keep_ref, send_ref, 3 + k)


def grad_x_kernel(
    bands, count_ref, xt_ref, gy_ref, gs_ref, top_ref, bot_ref, wt_ref, wd_ref, ws_ref, slot_ref, *rest
):
    out_ref, down_ref, token_ref, pad_ref, buf, sems = rest[-6:]
    token_ref[...] = jnp.zeros_like(token_ref)
    count = count_ref[0]
    band = lax.axis_index("grp")
    rows, cols = xt_ref.shape[0], xt_ref.shape[1]
    pad_ref[1 : rows + 1] = gs_ref[...]
    edge = jnp.zeros((SLOTS, CH), BF)
    for ref, flag, i, row in ((top_ref, band > 0, 1, 0), (bot_ref, band < bands - 1, 0, rows + 1)):
        pair = [
            mm_nt(ref[...], wd_ref[i * 2 + j]).astype(BF).reshape(cols // 2, SLOTS, CH)
            for j in range(2)
        ]
        g = jnp.stack(pair, axis=1).reshape(cols, SLOTS, CH)
        pad_ref[row, 0] = edge
        pad_ref[row, 1 : cols + 1] = grad_of_temporal(g, wt_ref, jnp.where(flag, count, 0))
        pad_ref[row, cols + 1] = edge
    back = to_frames(16)

    def rows_of(q, _):
        total = None
        for i in range(3):
            for j in range(3):
                left = pad_ref[pl.ds(4 * q + 2 - i, 4), 2 - j : 2 - j + cols].reshape(
                    4 * cols * SLOTS, CH
                )
                term = mm_nt(left, ws_ref[i * 3 + j])
                total = term if total is None else total + term
        at = 4 * q
        v = xt_ref[pl.ds(at, 4)].reshape(4 * cols * SLOTS, CH).astype(F32)
        r = lax.rsqrt(jnp.mean(v * v, axis=-1, keepdims=True) + 1e-06)
        u = v * r
        s = 0.5 + 0.5 * jnp.tanh(0.5 * u)
        gu = total * (s * (1.0 + u * (1.0 - s)))
        dot = jnp.mean(gu * u, axis=-1, keepdims=True)
        gv = r * (gu - u * dot)
        gx = gy_ref[pl.ds(at, 4)].reshape(4 * cols * SLOTS, CH).astype(F32) + gv
        gx = gx.reshape(4 * cols, SLOTS, CH)
        gx = jnp.where(slot_mask(gx.shape, count), gx, 0.0).astype(BF).reshape(4 * cols * SLOTS, CH)
        for k in range(2):
            o = mm(back, gx[k * 256 : k * 256 + 256]).astype(BF)
            buf[:, pl.ds(pl.multiple_of((2 * q + k) * 16, 16), 16), :] = o.reshape(SLOTS, 16, CH)
        return 0

    lax.fori_loop(0, rows // 4, rows_of, 0)
    copy = pltpu.make_async_copy(buf, out_ref, sems.at[0])
    copy.start()
    for q in range(down_ref.shape[1] // 4):
        o = mm(back, slot_ref[q * 256 : q * 256 + 256]).astype(BF)
        down_ref[:, q * 4 : q * 4 + 4] = o.reshape(SLOTS, 4, cols // 2, CH)
    copy.wait()


ORDER = (0, 3, 2, 1)


def plane_send_kernel(keep_ref, got_ref, *rest):
    _, p, _ = place_bits()
    for r, out in zip(ORDER, rest[-4:]):
        at = pl.ds((p ^ r) * 4, 4)
        out[...] = (keep_ref[at].astype(F32) + got_ref[at].astype(F32)).astype(BF)


def line_send_kernel(*refs):
    outs = refs[8:]
    _, _, z = place_bits()
    for out, r in zip(outs, ORDER):
        at = 0
        for chain in (refs[:4], refs[4:8]):
            parts = [ref[z ^ r].astype(F32) for ref in chain]
            n = parts[0].shape[0]
            out[at : at + n] = (parts[0] + parts[1] + parts[2] + parts[3]).astype(BF)
            at += n


def line_sum_kernel(a_ref, b_ref, c_ref, d_ref, *rest):
    out_ref = rest[-1]
    parts = [ref[...].astype(F32) for ref in (a_ref, b_ref, c_ref, d_ref)]
    out_ref[...] = (parts[0] + parts[1] + parts[2] + parts[3]).astype(BF)


def line_gather_kernel(a_ref, b_ref, c_ref, d_ref, out_ref):
    _, _, z = place_bits()
    for r, ref in zip(ORDER, (a_ref, b_ref, c_ref, d_ref)):
        out_ref[z ^ r] = ref[...]


def plane_gather_kernel(a_ref, b_ref, c_ref, d_ref, _, out_ref):
    _, p, _ = place_bits()
    for r, ref in zip(ORDER, (a_ref, b_ref, c_ref, d_ref)):
        out_ref[pl.ds((p ^ r) * 4, 4)] = ref[...]


def add_kernel(a_ref, b_ref, out_ref):
    out_ref[...] = (a_ref[...].astype(F32) + b_ref[...].astype(F32)).astype(BF)


def pass_kernel(*_):
    pass


def finish_kernel(own, half_ref, *rest):
    buf, sems = rest[-2:]
    outs = rest[-5:-2]
    core, _, _ = place_bits()
    at = pl.multiple_of((core if own else 1 - core) * (CH // 2), CH // 2)
    copies = []
    k = 0
    for out in outs:
        for m in range(out.shape[0]):
            buf[k] = half_ref[:, k].reshape(CH, CH // 2).astype(F32)
            copies.append(
                pltpu.make_async_copy(buf.at[k], out.at[m, :, pl.ds(at, CH // 2)], sems.at[k])
            )
            copies[-1].start()
            k += 1
    for copy in copies:
        copy.wait()


VMEM = pl.BlockSpec(memory_space=pltpu.VMEM)
SMEM = pl.BlockSpec(memory_space=pltpu.SMEM)
ANY = pl.BlockSpec(memory_space=pl.ANY)
HBM = pl.BlockSpec(memory_space=pltpu.HBM)
TOKEN = (VMEM, (8, 128), F32)


def call(kernel, name, ins, outs, scratch=(), flops=0, alias=None, grant=10, moved=None):
    shapes = [jax.ShapeDtypeStruct(o[1], o[2] if len(o) > 2 else BF) for o in outs]
    if moved is None:
        moved = sum(a.size * a.dtype.itemsize for s, a in ins if s is not ANY)
        moved += sum(s.size * s.dtype.itemsize for s in shapes)
    return pl.pallas_call(
        kernel,
        out_shape=shapes,
        in_specs=[s for s, _ in ins],
        out_specs=[o[0] for o in outs],
        scratch_shapes=list(scratch),
        compiler_params=pltpu.CompilerParams(vmem_limit_bytes=grant * 2**20),
        cost_estimate=pl.CostEstimate(flops=flops, bytes_accessed=moved, transcendentals=0),
        input_output_aliases=alias or {},
        name=name,
    )(*[a for _, a in ins])


AXES = ("tm", "grp")


def plan(tm, grp):
    low, total = grp.bit_length() - 1, (tm * grp).bit_length() - 1
    plane, line = [low + 1, 0], [low + 2, low + 3]
    return low, plane, line, [b for b in range(total) if b not in [low] + plane + line]


def swap(value, tm, grp, *bits):
    flip = sum(1 << b for b in bits)
    return lax.ppermute(value, AXES, [(d, d ^ flip) for d in range(tm * grp)])


def core_round(value, tm, grp):
    return swap(value, tm, grp, plan(tm, grp)[0])


def four_round(parts, bits, tm, grp):
    return [
        parts[0],
        swap(parts[1], tm, grp, *bits),
        swap(parts[2], tm, grp, bits[1]),
        swap(parts[3], tm, grp, bits[0]),
    ]


def plane_send(keep, got, after):
    ins = [(VMEM, keep), (VMEM, got)] + [(ANY, a) for a in after]
    shape = (4, keep.shape[1], 16, CH // 2)
    return list(call(plane_send_kernel, "plane_send", ins, [(VMEM, shape)] * 4))


def passed(value, after):
    ins = [(ANY, value)] + [(ANY, a) for a in after]
    return call(pass_kernel, "pass", ins, [(ANY, value.shape)], alias={0: 0})[0]


def finish(own, half, before):
    n = half.shape[1]
    return list(
        call(
            functools.partial(finish_kernel, own),
            "finish",
            [(VMEM, half)] + [(HBM, a) for a in before],
            [(HBM, (m, CH, CH), F32) for m in (9, 3, 4)],
            [pltpu.VMEM((n, CH, CH // 2), F32), pltpu.SemaphoreType.DMA((n,))],
            alias={1 + i: i for i in range(len(before))},
        )
    )


def along(value, axis, by):
    count = lax.axis_size(axis)
    pairs = [(i, i + by) for i in range(count) if 0 <= i + by < count]
    return lax.ppermute(value, axis, pairs)


def around(value, axis, by):
    count = lax.axis_size(axis)
    return lax.ppermute(value, axis, [(i, (i + by) % count) for i in range(count)])


def from_bands(parts):
    if len(parts) == 1:
        got = lax.ppermute(parts[0], "grp", [(0, 1), (1, 0)])
        return got, got
    return along(parts[0], "grp", 1), along(parts[1], "grp", -1)


def body(tm, grp, frames_in, span_frames, w_spatial, w_temporal, w_down, cotangent):
    slots, rows, cols, ch = frames_in.shape
    wide = rows * cols
    x = frames_in.reshape(slots, wide, ch)
    ws = w_spatial.reshape(9, ch, ch)
    wd = w_down.reshape(4, ch, ch)
    wt = w_temporal
    count = (SMEM, span_frames)
    tap = 2 * slots * wide * ch * ch
    tile = (rows, cols, slots, ch)
    padded = (rows + 2, cols + 2, slots, ch)
    dma = pltpu.SemaphoreType.DMA

    sides = 1 if grp == 2 else 2
    edge = call(
        functools.partial(edges_kernel, grp),
        "edges",
        [count, (VMEM, x)],
        [(VMEM, (cols * slots, ch))] * sides,
        flops=tap // 8,
    )
    top, bot = from_bands(edge)
    last_shape = (2 * wide + 32, ch)
    at_shape = (3 * ch, (rows + 4) * 128)
    xt, acts, at, last_two = call(
        acts_kernel,
        "acts",
        [count, (VMEM, x), (ANY, edge[0])],
        [(VMEM, tile), (VMEM, padded), (VMEM, at_shape), (VMEM, last_shape)],
        flops=2 * tap,
    )
    (nxt,) = call(
        next_kernel,
        "next",
        [(VMEM, cotangent), (ANY, last_two)],
        [(VMEM, (2,) + cotangent.shape[1:])],
        moved=1024,
    )
    nxt_got = along(nxt, "tm", -1)
    acts, at, last_two = call(
        functools.partial(halo_kernel, grp),
        "halo",
        [count, (VMEM, top), (VMEM, bot), (VMEM, acts), (VMEM, at), (VMEM, last_two), (ANY, nxt),
         (VMEM, cotangent), (VMEM, wt), (VMEM, wd)],
        [(VMEM, padded), (VMEM, at_shape), (VMEM, last_shape)],
        alias={3: 0, 4: 1, 5: 2},
        moved=1024,
    )
    prev = around(last_two, "tm", 1)
    half = (16, 9, 16, ch // 2)
    cott, gy, gs, keep_a, send_a, *edge = call(
        functools.partial(grad_spatial_kernel, tm, grp),
        "grad_spatial",
        [count, (VMEM, at), (VMEM, cotangent), (VMEM, nxt_got), (VMEM, wt), (VMEM, wd)],
        [(VMEM, (rows // 2, cols // 2, slots, ch)), (VMEM, tile),
         (VMEM, (rows, cols + 2, slots, ch)), (VMEM, half), (VMEM, half)]
        + [(VMEM, (cols // 2 * slots, ch))] * sides,
        flops=14 * tap,
    )
    send_a = passed(send_a, [prev])
    got_a = core_round(send_a, tm, grp)
    cot_top, cot_bot = from_bands(edge)
    half_tile = (rows // 2, cols, slots, ch)
    acts, upper = call(
        upper_kernel,
        "spatial_upper",
        [(VMEM, acts), (VMEM, prev), (VMEM, ws), (ANY, send_a)],
        [(VMEM, padded), (VMEM, half_tile)],
        flops=5 * tap,
        alias={0: 0},
    )
    _, plane, line, others = plan(tm, grp)
    parts_a = plane_send(keep_a, got_a, [upper])
    (lower,) = call(
        lower_kernel,
        "spatial_lower",
        [(VMEM, acts), (VMEM, ws)] + [(ANY, a) for a in parts_a],
        [(VMEM, half_tile)],
        flops=4 * tap,
    )
    half = (16, 7, 16, ch // 2)
    down, keep_b, send_b = call(
        forward_kernel,
        "forward",
        [count, (VMEM, xt), (VMEM, upper), (VMEM, lower), (VMEM, cott), (VMEM, gy), (VMEM, wt), (VMEM, wd),
         *((ANY, a) for a in parts_a)],
        [(VMEM, (slots * wide // 4, ch)), (VMEM, half), (VMEM, half)],
        [pltpu.VMEM(v, BF) for v in (tile, (3 * ch, slots * wide), (4 * ch, slots * wide // 4))],
        moved=1024,
        grant=14,
    )
    parts_a = four_round(parts_a, plane, tm, grp)
    send_b = passed(send_b, parts_a[1:2])
    parts_b = plane_send(keep_b, core_round(send_b, tm, grp), [])
    parts_b = four_round(parts_b, plane, tm, grp)
    parts = call(
        line_send_kernel,
        "line_send",
        [(VMEM, a) for a in parts_a + parts_b],
        [(VMEM, (16, 16, ch // 2))] * 4,
    )
    parts = four_round(list(parts), line, tm, grp)
    ins = [(VMEM, a) for a in parts]
    (mine,) = call(line_sum_kernel, "line_sum", ins, [(VMEM, parts[0].shape)])
    for bit in others:
        got = swap(mine, tm, grp, bit)
        (mine,) = call(add_kernel, "add", [(VMEM, mine), (VMEM, got)], [(VMEM, mine.shape)])
    parts = four_round([mine] * 4, line, tm, grp)
    (mine,) = call(
        line_gather_kernel, "line_gather", [(VMEM, a) for a in parts], [(VMEM, (4,) + mine.shape)]
    )
    parts = four_round([mine] * 4, plane, tm, grp)
    grad_x, down, token = call(
        functools.partial(grad_x_kernel, grp),
        "grad_x",
        [count, (VMEM, xt), (VMEM, gy), (VMEM, gs), (VMEM, cot_top), (VMEM, cot_bot), (VMEM, wt),
         (VMEM, wd), (VMEM, ws), (VMEM, down), (ANY, mine)],
        [(HBM, (slots, wide, ch)), (VMEM, cotangent.shape), TOKEN],
        [pltpu.VMEM(padded, BF), pltpu.VMEM((slots, wide, ch), BF), dma((1,))],
        flops=10 * tap,
    )
    ins = [(VMEM, a) for a in parts] + [(ANY, token)]
    (mine,) = call(plane_gather_kernel, "plane_gather", ins, [(VMEM, (16,) + mine.shape[1:])])
    got = core_round(mine, tm, grp)
    outs = finish(True, mine, [])
    sum_s, sum_t, sum_d = finish(False, got, outs)
    return (
        down,
        grad_x.reshape(frames_in.shape),
        sum_s.reshape(w_spatial.shape),
        sum_t,
        sum_d.reshape(w_down.shape),
    )


def solution(mesh):
    return jax.shard_map(
        functools.partial(body, mesh.shape["tm"], mesh.shape["grp"]),
        mesh=mesh,
        in_specs=(P("tm", "grp", None, None), P("tm"), P(), P(), P(), P("tm", "grp", None, None)),
        out_specs=(P("tm", "grp", None, None), P("tm", "grp", None, None), P(), P(), P()),
        check_vma=False,
    )
```

```python
import functools

import jax
import jax.numpy as jnp
from jax import lax
from jax.experimental import pallas as pl
from jax.experimental.pallas import tpu as pltpu
from jax.sharding import PartitionSpec as P

SLOTS = 16
OWN = 14
CH = 256
BF = jnp.bfloat16
F32 = jnp.float32


def mm(a, b):
    return lax.dot_general(a, b, (((1,), (0,)), ((), ())), preferred_element_type=F32)


def mm_nt(a, b):
    return lax.dot_general(a, b, (((1,), (1,)), ((), ())), preferred_element_type=F32)


def iotas(rows, cols):
    return (
        lax.broadcasted_iota(jnp.int32, (rows, cols), 0),
        lax.broadcasted_iota(jnp.int32, (rows, cols), 1),
    )


def to_slots(rows, frames, keep):
    a, b = iotas(rows * SLOTS, frames * rows)
    bits = rows.bit_length() - 1
    hit = ((a >> 4) == (b & (rows - 1))) & keep(b >> bits, a & 15)
    return jnp.where(hit, 1.0, 0.0).astype(BF)


def to_frames(rows):
    a, b = iotas(SLOTS * rows, rows * SLOTS)
    bits = rows.bit_length() - 1
    hit = ((a & (rows - 1)) == (b >> 4)) & ((a >> bits) == (b & 15))
    return jnp.where(hit, 1.0, 0.0).astype(BF)


def own_frames(count):
    return lambda frame, slot: (frame == slot) & (slot < count)


def own_and_next(count, blocks):
    after = jnp.where(lax.axis_index("tm") < blocks - 1, count, 64)
    return lambda frame, slot: ((frame < OWN) & (frame == slot) & (slot < count)) | (
        (frame >= OWN) & (slot == after + frame - OWN)
    )


def silu_norm(v):
    scaled = v * lax.rsqrt(jnp.mean(v * v, axis=-1, keepdims=True) + 1e-06)
    return scaled * (0.5 + 0.5 * jnp.tanh(0.5 * scaled))


def slot_mask(shape, count):
    return lax.broadcasted_iota(jnp.int32, shape, len(shape) - 2) < count


def grad_of_temporal(gy, wt_ref, count):
    n = gy.shape[0]
    flat = gy.reshape(n * SLOTS, CH)
    total = mm_nt(flat, wt_ref[2]).reshape(n, SLOTS, CH)
    for k in (1, 0):
        term = mm_nt(flat, wt_ref[k]).reshape(n, SLOTS, CH)
        total = total + pltpu.roll(term, SLOTS - (2 - k), 1)
    return jnp.where(slot_mask(total.shape, count), total, 0.0).astype(BF)


def place_bits():
    t, g = lax.axis_index("tm"), lax.axis_index("grp")
    return t & 1, ((t >> 1) & 1) + 2 * (g & 1), (t >> 2) & 3


def split_cores(value, keep_ref, send_ref, k):
    core, _, _ = place_bits()
    low, high = value[:, : CH // 2].astype(BF), value[:, CH // 2 :].astype(BF)
    keep_ref[:, k] = jnp.where(core == 0, low, high).reshape(16, 16, CH // 2)
    send_ref[:, k] = jnp.where(core == 0, high, low).reshape(16, 16, CH // 2)


def edges_kernel(bands, count_ref, x_ref, *outs):
    count = count_ref[0]
    band = lax.axis_index("grp")
    wide = x_ref.shape[1]
    if bands == 2:
        starts, lower = [jnp.where(band == 0, wide - 16, 0)], [band == 0]
    else:
        starts, lower = [wide - 16, 0], [True, False]
    place = to_slots(16, SLOTS, own_frames(count))
    for k, at in enumerate(starts):
        piece = x_ref[:, pl.ds(pl.multiple_of(at, 16), 16), :].reshape(SLOTS * 16, CH)
        v = mm(place, piece)
        v = jnp.where(lower[k], v[128:], v[:128])
        outs[k][...] = silu_norm(v).astype(BF)


def acts_kernel(count_ref, x_ref, _, xt_ref, acts_ref, at_ref, last_ref):
    count = count_ref[0]
    rows, cols = xt_ref.shape[0], xt_ref.shape[1]
    edge = jnp.zeros((rows + 2, SLOTS, CH), BF)
    acts_ref[:, 0] = edge
    acts_ref[:, cols + 1] = edge
    place = to_slots(16, SLOTS, own_frames(count))
    last = silu_norm(x_ref[pl.ds(count - 2, 2)].reshape(2 * rows * cols, CH).astype(F32))
    last_ref[0 : 2 * rows * cols] = last.astype(BF)

    def rows_of(q, _):
        at = pl.multiple_of(q * 16, 16)
        piece = x_ref[:, pl.ds(at, 16), :].reshape(SLOTS * 16, CH)
        v = mm(place, piece)
        xt_ref[pl.ds(2 * q, 2)] = v.astype(BF).reshape(2, cols, SLOTS, CH)
        a = silu_norm(v).astype(BF)
        acts_ref[pl.ds(2 * q + 1, 2), 1 : cols + 1] = a.reshape(2, cols, SLOTS, CH)
        flipped = a.T
        for i in range(3):
            at = pl.multiple_of((2 * q + 3 - i) * 128, 128)
            at_ref[i * CH : i * CH + CH, pl.ds(at, 256)] = flipped
        return 0

    lax.fori_loop(0, rows // 2, rows_of, 0, unroll=True)


def next_kernel(cot_ref, _, nxt_ref):
    nxt_ref[...] = cot_ref[0:2]


def halo_kernel(bands, count_ref, top_ref, bot_ref, *rest):
    acts_ref, at_ref, last_ref = rest[-3:]
    count = count_ref[0]
    band = lax.axis_index("grp")
    rows, cols = acts_ref.shape[0] - 2, acts_ref.shape[1] - 2
    halo = []
    for ref, flag, i, row in ((top_ref, band > 0, 0, 0), (bot_ref, band < bands - 1, 2, rows + 1)):
        a = jnp.where(flag, ref[...].astype(F32), 0.0).astype(BF)
        acts_ref[row, 1 : cols + 1] = a.reshape(cols, SLOTS, CH)
        at = (row - i + 2) * 128
        at_ref[i * CH : i * CH + CH, at : at + 128] = a.T
        halo.append(a)
    a, b = iotas(32, 256)
    pick = ((a & 15) == (b >> 4)) & ((b & 15) == count - 2 + (a >> 4))
    pick = jnp.where(pick, 1.0, 0.0).astype(BF)
    last_ref[2 * rows * cols :] = mm(pick, jnp.concatenate(halo, 0)).astype(BF)


def conv_rows(acts_ref, ws_ref, sp_ref, start):
    rows, cols = sp_ref.shape[0], sp_ref.shape[1]

    def rows_of(q, _):
        total = None
        for i in range(3):
            for j in range(3):
                left = acts_ref[pl.ds(start + 4 * q + i, 4), j : j + cols].reshape(
                    4 * cols * SLOTS, CH
                )
                term = mm(left, ws_ref[i * 3 + j])
                total = term if total is None else total + term
        sp_ref[pl.ds(4 * q, 4)] = total.astype(BF).reshape(4, cols, SLOTS, CH)
        return 0

    lax.fori_loop(0, rows // 4, rows_of, 0, unroll=True)


def upper_kernel(acts_in, prev_ref, ws_ref, _, acts_ref, sp_ref):
    rows, cols = acts_ref.shape[0] - 2, acts_ref.shape[1] - 2
    a, b = iotas(256, 32)
    place = ((a >> 4) == (b & 15)) & ((a & 15) == OWN + (b >> 4)) & (lax.axis_index("tm") > 0)
    place = jnp.where(place, 1.0, 0.0).astype(BF)
    size = rows * cols
    for q in range(rows // 2 + 1):
        if q == rows // 2:
            both, prev = slice(0, rows + 2, rows + 1), prev_ref[2 * size :]
        else:
            both = slice(2 * q + 1, 2 * q + 3)
            parts = [prev_ref[f * size + q * 16 : f * size + q * 16 + 16] for f in range(2)]
            prev = jnp.concatenate(parts, 0)
        prev = mm(place, prev).astype(BF).reshape(2, cols, SLOTS, CH)
        for k, row in enumerate(range(rows + 2)[both]):
            acts_ref[row, 1 : cols + 1] = acts_ref[row, 1 : cols + 1] + prev[k]

    conv_rows(acts_ref, ws_ref, sp_ref, 0)


def lower_kernel(acts_ref, ws_ref, *rest):
    sp_ref = rest[-1]
    conv_rows(acts_ref, ws_ref, sp_ref, sp_ref.shape[0])


def grad_spatial_kernel(
    blocks, bands, count_ref, at_ref, cot_ref, nxt_ref, wt_ref, wd_ref,
    cott_ref, gy_ref, gs_ref, keep_ref, send_ref, *edge_refs,
):
    count = count_ref[0]
    band = lax.axis_index("grp")
    rows, cols = gy_ref.shape[0], gy_ref.shape[1]
    edge = jnp.zeros((rows, SLOTS, CH), BF)
    gs_ref[:, 0] = edge
    gs_ref[:, cols + 1] = edge

    place_next = to_slots(16, SLOTS, own_and_next(count, blocks))
    halves = []
    for q in range(rows * cols // 64):
        four = slice(q * 4, q * 4 + 4)
        piece = jnp.concatenate(
            [cot_ref[0:OWN, four].reshape(OWN, 16, CH), nxt_ref[:, four].reshape(2, 16, CH)], 0
        ).reshape(SLOTS * 16, CH)
        halves.append(mm(place_next, piece).astype(BF))
    placed = jnp.concatenate(halves, 0)
    cott_ref[...] = placed.reshape(rows // 2, cols // 2, SLOTS, CH)
    for i in range(2):
        for j in range(2):
            g = mm_nt(placed, wd_ref[i * 2 + j]).astype(BF).reshape(rows // 2, cols // 2, SLOTS, CH)
            for r in range(rows // 2):
                for c in range(cols // 2):
                    gy_ref[2 * r + i, 2 * c + j] = g[r, c]
    last = cott_ref[rows // 2 - 1].reshape(cols // 2 * SLOTS, CH)
    first = cott_ref[0].reshape(cols // 2 * SLOTS, CH)
    if bands == 2:
        edge_refs[0][...] = jnp.where(band == 0, last, first)
    else:
        edge_refs[0][...] = last
        edge_refs[1][...] = first

    def grads_of(q, _):
        g = gy_ref[pl.ds(8 * q, 8)].reshape(8 * cols, SLOTS, CH)
        s = grad_of_temporal(g, wt_ref, count)
        gs_ref[pl.ds(8 * q, 8), 1 : cols + 1] = s.reshape(8, cols, SLOTS, CH)
        g = jnp.where(slot_mask(g.shape, count), g.astype(F32), 0.0)
        gy_ref[pl.ds(8 * q, 8)] = g.astype(BF).reshape(8, cols, SLOTS, CH)
        return 0

    lax.fori_loop(0, rows // 8, grads_of, 0)

    wide = rows * cols * SLOTS
    for j in range(3):
        right = gs_ref[:, 2 - j : 2 - j + cols].reshape(wide, CH)
        value = mm(at_ref[:, 256 : 256 + wide], right)
        for i in range(3):
            split_cores(value[i * CH : i * CH + CH], keep_ref, send_ref, i * 3 + j)


def forward_kernel(
    count_ref, xt_ref, upper_ref, lower_ref, cott_ref, gy_ref, wt_ref, wd_ref, *rest
):
    down_ref, keep_ref, send_ref, y_ref, st_ref, yt_ref = rest[-6:]
    count = count_ref[0]
    rows, cols = xt_ref.shape[0], xt_ref.shape[1]
    for q, sp_ref in enumerate((upper_ref, lower_ref)):
        s = sp_ref[...].reshape(8 * cols * SLOTS, CH).astype(F32)
        s = s.reshape(8 * cols, SLOTS, CH)
        total = None
        for k in range(3):
            shifted = s if k == 2 else pltpu.roll(s, 2 - k, 1)
            shifted = shifted.astype(BF).reshape(8 * cols * SLOTS, CH)
            at = slice(q * 1024, q * 1024 + 1024)
            st_ref[k * CH : k * CH + CH, at] = shifted.T
            term = mm(shifted, wt_ref[k])
            total = term if total is None else total + term
        x = xt_ref[8 * q : 8 * q + 8].reshape(8 * cols, SLOTS, CH).astype(F32)
        y = jnp.where(slot_mask(x.shape, count), x + total.reshape(x.shape), 0.0).astype(BF)
        y_ref[8 * q : 8 * q + 8] = y.reshape(8, cols, SLOTS, CH)

    wide = rows * cols * SLOTS
    value = mm(st_ref[...], gy_ref[...].reshape(wide, CH))
    for k in range(3):
        split_cores(value[k * CH : k * CH + CH], keep_ref, send_ref, k)

    small = wide // 4
    total = None
    for i in range(2):
        for j in range(2):
            tiles = [
                y_ref[2 * r + i, 2 * c + j] for r in range(rows // 2) for c in range(cols // 2)
            ]
            piece = jnp.concatenate(tiles, axis=0)
            k = i * 2 + j
            yt_ref[k * CH : k * CH + CH] = piece.T
            term = mm(piece, wd_ref[k])
            total = term if total is None else total + term
    down_ref[...] = total.astype(BF)
    value = mm(yt_ref[...], cott_ref[...].reshape(small, CH))
    for k in range(4):
        split_cores(value[k * CH : k * CH + CH], keep_ref, send_ref, 3 + k)


def grad_x_kernel(
    bands, count_ref, xt_ref, gy_ref, gs_ref, top_ref, bot_ref, wt_ref, wd_ref, ws_ref, slot_ref, *rest
):
    out_ref, down_ref, token_ref, pad_ref, buf, sems = rest[-6:]
    token_ref[...] = jnp.zeros_like(token_ref)
    count = count_ref[0]
    band = lax.axis_index("grp")
    rows, cols = xt_ref.shape[0], xt_ref.shape[1]
    pad_ref[1 : rows + 1] = gs_ref[...]
    edge = jnp.zeros((SLOTS, CH), BF)
    for ref, flag, i, row in ((top_ref, band > 0, 1, 0), (bot_ref, band < bands - 1, 0, rows + 1)):
        pair = [
            mm_nt(ref[...], wd_ref[i * 2 + j]).astype(BF).reshape(cols // 2, SLOTS, CH)
            for j in range(2)
        ]
        g = jnp.stack(pair, axis=1).reshape(cols, SLOTS, CH)
        pad_ref[row, 0] = edge
        pad_ref[row, 1 : cols + 1] = grad_of_temporal(g, wt_ref, jnp.where(flag, count, 0))
        pad_ref[row, cols + 1] = edge
    back = to_frames(16)

    def rows_of(q, _):
        total = None
        for i in range(3):
            for j in range(3):
                left = pad_ref[pl.ds(4 * q + 2 - i, 4), 2 - j : 2 - j + cols].reshape(
                    4 * cols * SLOTS, CH
                )
                term = mm_nt(left, ws_ref[i * 3 + j])
                total = term if total is None else total + term
        at = 4 * q
        v = xt_ref[pl.ds(at, 4)].reshape(4 * cols * SLOTS, CH).astype(F32)
        r = lax.rsqrt(jnp.mean(v * v, axis=-1, keepdims=True) + 1e-06)
        u = v * r
        s = 0.5 + 0.5 * jnp.tanh(0.5 * u)
        gu = total * (s * (1.0 + u * (1.0 - s)))
        dot = jnp.mean(gu * u, axis=-1, keepdims=True)
        gv = r * (gu - u * dot)
        gx = gy_ref[pl.ds(at, 4)].reshape(4 * cols * SLOTS, CH).astype(F32) + gv
        gx = gx.reshape(4 * cols, SLOTS, CH)
        gx = jnp.where(slot_mask(gx.shape, count), gx, 0.0).astype(BF).reshape(4 * cols * SLOTS, CH)
        for k in range(2):
            o = mm(back, gx[k * 256 : k * 256 + 256]).astype(BF)
            buf[:, pl.ds(pl.multiple_of((2 * q + k) * 16, 16), 16), :] = o.reshape(SLOTS, 16, CH)
        return 0

    lax.fori_loop(0, rows // 4, rows_of, 0)
    copy = pltpu.make_async_copy(buf, out_ref, sems.at[0])
    copy.start()
    for q in range(down_ref.shape[1] // 4):
        o = mm(back, slot_ref[q * 256 : q * 256 + 256]).astype(BF)
        down_ref[:, q * 4 : q * 4 + 4] = o.reshape(SLOTS, 4, cols // 2, CH)
    copy.wait()


ORDER = (0, 3, 2, 1)


def plane_send_kernel(keep_ref, got_ref, *rest):
    _, p, _ = place_bits()
    for r, out in zip(ORDER, rest[-4:]):
        at = pl.ds((p ^ r) * 4, 4)
        out[...] = (keep_ref[at].astype(F32) + got_ref[at].astype(F32)).astype(BF)


def line_send_kernel(*refs):
    outs = refs[8:]
    _, _, z = place_bits()
    for out, r in zip(outs, ORDER):
        at = 0
        for chain in (refs[:4], refs[4:8]):
            parts = [ref[z ^ r].astype(F32) for ref in chain]
            n = parts[0].shape[0]
            out[at : at + n] = (parts[0] + parts[1] + parts[2] + parts[3]).astype(BF)
            at += n


def line_sum_kernel(a_ref, b_ref, c_ref, d_ref, *rest):
    out_ref = rest[-1]
    parts = [ref[...].astype(F32) for ref in (a_ref, b_ref, c_ref, d_ref)]
    out_ref[...] = (parts[0] + parts[1] + parts[2] + parts[3]).astype(BF)


def line_gather_kernel(a_ref, b_ref, c_ref, d_ref, out_ref):
    _, _, z = place_bits()
    for r, ref in zip(ORDER, (a_ref, b_ref, c_ref, d_ref)):
        out_ref[z ^ r] = ref[...]


def plane_gather_kernel(a_ref, b_ref, c_ref, d_ref, _, out_ref):
    _, p, _ = place_bits()
    for r, ref in zip(ORDER, (a_ref, b_ref, c_ref, d_ref)):
        out_ref[pl.ds((p ^ r) * 4, 4)] = ref[...]


def add_kernel(a_ref, b_ref, out_ref):
    out_ref[...] = (a_ref[...].astype(F32) + b_ref[...].astype(F32)).astype(BF)


def pass_kernel(*_):
    pass


def finish_kernel(own, half_ref, *rest):
    buf, sems = rest[-2:]
    outs = rest[-5:-2]
    core, _, _ = place_bits()
    at = pl.multiple_of((core if own else 1 - core) * (CH // 2), CH // 2)
    copies = []
    k = 0
    for out in outs:
        for m in range(out.shape[0]):
            buf[k] = half_ref[:, k].reshape(CH, CH // 2).astype(F32)
            copies.append(
                pltpu.make_async_copy(buf.at[k], out.at[m, :, pl.ds(at, CH // 2)], sems.at[k])
            )
            copies[-1].start()
            k += 1
    for copy in copies:
        copy.wait()


VMEM = pl.BlockSpec(memory_space=pltpu.VMEM)
SMEM = pl.BlockSpec(memory_space=pltpu.SMEM)
ANY = pl.BlockSpec(memory_space=pl.ANY)
HBM = pl.BlockSpec(memory_space=pltpu.HBM)
TOKEN = (VMEM, (8, 128), F32)


def call(kernel, name, ins, outs, scratch=(), flops=0, alias=None, grant=10, moved=None):
    shapes = [jax.ShapeDtypeStruct(o[1], o[2] if len(o) > 2 else BF) for o in outs]
    if moved is None:
        moved = sum(a.size * a.dtype.itemsize for s, a in ins if s is not ANY)
        moved += sum(s.size * s.dtype.itemsize for s in shapes)
    return pl.pallas_call(
        kernel,
        out_shape=shapes,
        in_specs=[s for s, _ in ins],
        out_specs=[o[0] for o in outs],
        scratch_shapes=list(scratch),
        compiler_params=pltpu.CompilerParams(vmem_limit_bytes=grant * 2**20),
        cost_estimate=pl.CostEstimate(flops=flops, bytes_accessed=moved, transcendentals=0),
        input_output_aliases=alias or {},
        name=name,
    )(*[a for _, a in ins])


AXES = ("tm", "grp")


def plan(tm, grp):
    low, total = grp.bit_length() - 1, (tm * grp).bit_length() - 1
    plane, line = [low + 1, 0], [low + 2, low + 3]
    return low, plane, line, [b for b in range(total) if b not in [low] + plane + line]


def swap(value, tm, grp, *bits):
    flip = sum(1 << b for b in bits)
    return lax.ppermute(value, AXES, [(d, d ^ flip) for d in range(tm * grp)])


def core_round(value, tm, grp):
    return swap(value, tm, grp, plan(tm, grp)[0])


def four_round(parts, bits, tm, grp):
    return [
        parts[0],
        swap(parts[1], tm, grp, *bits),
        swap(parts[2], tm, grp, bits[1]),
        swap(parts[3], tm, grp, bits[0]),
    ]


def plane_send(keep, got, after):
    ins = [(VMEM, keep), (VMEM, got)] + [(ANY, a) for a in after]
    shape = (4, keep.shape[1], 16, CH // 2)
    return list(call(plane_send_kernel, "plane_send", ins, [(VMEM, shape)] * 4))


def passed(value, after):
    ins = [(ANY, value)] + [(ANY, a) for a in after]
    return call(pass_kernel, "pass", ins, [(ANY, value.shape)], alias={0: 0})[0]


def finish(own, half, before):
    n = half.shape[1]
    return list(
        call(
            functools.partial(finish_kernel, own),
            "finish",
            [(VMEM, half)] + [(HBM, a) for a in before],
            [(HBM, (m, CH, CH), F32) for m in (9, 3, 4)],
            [pltpu.VMEM((n, CH, CH // 2), F32), pltpu.SemaphoreType.DMA((n,))],
            alias={1 + i: i for i in range(len(before))},
        )
    )


def along(value, axis, by):
    count = lax.axis_size(axis)
    pairs = [(i, i + by) for i in range(count) if 0 <= i + by < count]
    return lax.ppermute(value, axis, pairs)


def around(value, axis, by):
    count = lax.axis_size(axis)
    return lax.ppermute(value, axis, [(i, (i + by) % count) for i in range(count)])


def from_bands(parts):
    if len(parts) == 1:
        got = lax.ppermute(parts[0], "grp", [(0, 1), (1, 0)])
        return got, got
    return along(parts[0], "grp", 1), along(parts[1], "grp", -1)


def body(tm, grp, frames_in, span_frames, w_spatial, w_temporal, w_down, cotangent):
    slots, rows, cols, ch = frames_in.shape
    wide = rows * cols
    x = frames_in.reshape(slots, wide, ch)
    ws = w_spatial.reshape(9, ch, ch)
    wd = w_down.reshape(4, ch, ch)
    wt = w_temporal
    count = (SMEM, span_frames)
    tap = 2 * slots * wide * ch * ch
    tile = (rows, cols, slots, ch)
    padded = (rows + 2, cols + 2, slots, ch)
    dma = pltpu.SemaphoreType.DMA

    sides = 1 if grp == 2 else 2
    edge = call(
        functools.partial(edges_kernel, grp),
        "edges",
        [count, (VMEM, x)],
        [(VMEM, (cols * slots, ch))] * sides,
        flops=tap // 8,
    )
    top, bot = from_bands(edge)
    last_shape = (2 * wide + 32, ch)
    at_shape = (3 * ch, (rows + 4) * 128)
    xt, acts, at, last_two = call(
        acts_kernel,
        "acts",
        [count, (VMEM, x), (ANY, edge[0])],
        [(VMEM, tile), (VMEM, padded), (VMEM, at_shape), (VMEM, last_shape)],
        flops=2 * tap,
    )
    (nxt,) = call(
        next_kernel,
        "next",
        [(VMEM, cotangent), (ANY, last_two)],
        [(VMEM, (2,) + cotangent.shape[1:])],
        moved=1024,
    )
    nxt_got = along(nxt, "tm", -1)
    acts, at, last_two = call(
        functools.partial(halo_kernel, grp),
        "halo",
        [count, (VMEM, top), (VMEM, bot), (VMEM, acts), (VMEM, at), (VMEM, last_two), (ANY, nxt),
         (VMEM, cotangent), (VMEM, wt), (VMEM, wd)],
        [(VMEM, padded), (VMEM, at_shape), (VMEM, last_shape)],
        alias={3: 0, 4: 1, 5: 2},
        moved=1024,
    )
    prev = around(last_two, "tm", 1)
    half = (16, 9, 16, ch // 2)
    cott, gy, gs, keep_a, send_a, *edge = call(
        functools.partial(grad_spatial_kernel, tm, grp),
        "grad_spatial",
        [count, (VMEM, at), (VMEM, cotangent), (VMEM, nxt_got), (VMEM, wt), (VMEM, wd)],
        [(VMEM, (rows // 2, cols // 2, slots, ch)), (VMEM, tile),
         (VMEM, (rows, cols + 2, slots, ch)), (VMEM, half), (VMEM, half)]
        + [(VMEM, (cols // 2 * slots, ch))] * sides,
        flops=14 * tap,
    )
    send_a = passed(send_a, [prev])
    got_a = core_round(send_a, tm, grp)
    cot_top, cot_bot = from_bands(edge)
    half_tile = (rows // 2, cols, slots, ch)
    acts, upper = call(
        upper_kernel,
        "spatial_upper",
        [(VMEM, acts), (VMEM, prev), (VMEM, ws), (ANY, send_a)],
        [(VMEM, padded), (VMEM, half_tile)],
        flops=5 * tap,
        alias={0: 0},
    )
    _, plane, line, others = plan(tm, grp)
    parts_a = plane_send(keep_a, got_a, [upper])
    (lower,) = call(
        lower_kernel,
        "spatial_lower",
        [(VMEM, acts), (VMEM, ws)] + [(ANY, a) for a in parts_a],
        [(VMEM, half_tile)],
        flops=4 * tap,
    )
    half = (16, 7, 16, ch // 2)
    down, keep_b, send_b = call(
        forward_kernel,
        "forward",
        [count, (VMEM, xt), (VMEM, upper), (VMEM, lower), (VMEM, cott), (VMEM, gy), (VMEM, wt), (VMEM, wd),
         *((ANY, a) for a in parts_a)],
        [(VMEM, (slots * wide // 4, ch)), (VMEM, half), (VMEM, half)],
        [pltpu.VMEM(v, BF) for v in (tile, (3 * ch, slots * wide), (4 * ch, slots * wide // 4))],
        moved=1024,
        grant=14,
    )
    parts_a = four_round(parts_a, plane, tm, grp)
    send_b = passed(send_b, parts_a[1:2])
    parts_b = plane_send(keep_b, core_round(send_b, tm, grp), [])
    parts_b = four_round(parts_b, plane, tm, grp)
    parts = call(
        line_send_kernel,
        "line_send",
        [(VMEM, a) for a in parts_a + parts_b],
        [(VMEM, (16, 16, ch // 2))] * 4,
    )
    parts = four_round(list(parts), line, tm, grp)
    ins = [(VMEM, a) for a in parts]
    (mine,) = call(line_sum_kernel, "line_sum", ins, [(VMEM, parts[0].shape)])
    for bit in others:
        got = swap(mine, tm, grp, bit)
        (mine,) = call(add_kernel, "add", [(VMEM, mine), (VMEM, got)], [(VMEM, mine.shape)])
    parts = four_round([mine] * 4, line, tm, grp)
    (mine,) = call(
        line_gather_kernel, "line_gather", [(VMEM, a) for a in parts], [(VMEM, (4,) + mine.shape)]
    )
    parts = four_round([mine] * 4, plane, tm, grp)
    grad_x, down, token = call(
        functools.partial(grad_x_kernel, grp),
        "grad_x",
        [count, (VMEM, xt), (VMEM, gy), (VMEM, gs), (VMEM, cot_top), (VMEM, cot_bot), (VMEM, wt),
         (VMEM, wd), (VMEM, ws), (VMEM, down), (ANY, mine)],
        [(HBM, (slots, wide, ch)), (VMEM, cotangent.shape), TOKEN],
        [pltpu.VMEM(padded, BF), pltpu.VMEM((slots, wide, ch), BF), dma((1,))],
        flops=10 * tap,
    )
    ins = [(VMEM, a) for a in parts] + [(ANY, token)]
    (mine,) = call(plane_gather_kernel, "plane_gather", ins, [(VMEM, (16,) + mine.shape[1:])])
    got = core_round(mine, tm, grp)
    outs = finish(True, mine, [])
    sum_s, sum_t, sum_d = finish(False, got, outs)
    return (
        down,
        grad_x.reshape(frames_in.shape),
        sum_s.reshape(w_spatial.shape),
        sum_t,
        sum_d.reshape(w_down.shape),
    )


def solution(mesh):
    return jax.shard_map(
        functools.partial(body, mesh.shape["tm"], mesh.shape["grp"]),
        mesh=mesh,
        in_specs=(P("tm", "grp", None, None), P("tm"), P(), P(), P(), P("tm", "grp", None, None)),
        out_specs=(P("tm", "grp", None, None), P("tm", "grp", None, None), P(), P(), P()),
        check_vma=False,
    )
```

```python
import functools

import jax
import jax.numpy as jnp
from jax import lax
from jax.experimental import pallas as pl
from jax.experimental.pallas import tpu as pltpu
from jax.sharding import PartitionSpec as P

SLOTS = 16
OWN = 14
CH = 256
BF = jnp.bfloat16
F32 = jnp.float32


def mm(a, b):
    return lax.dot_general(a, b, (((1,), (0,)), ((), ())), preferred_element_type=F32)


def mm_nt(a, b):
    return lax.dot_general(a, b, (((1,), (1,)), ((), ())), preferred_element_type=F32)


def iotas(rows, cols):
    return (
        lax.broadcasted_iota(jnp.int32, (rows, cols), 0),
        lax.broadcasted_iota(jnp.int32, (rows, cols), 1),
    )


def to_slots(rows, frames, keep):
    a, b = iotas(rows * SLOTS, frames * rows)
    bits = rows.bit_length() - 1
    hit = ((a >> 4) == (b & (rows - 1))) & keep(b >> bits, a & 15)
    return jnp.where(hit, 1.0, 0.0).astype(BF)


def to_frames(rows):
    a, b = iotas(SLOTS * rows, rows * SLOTS)
    bits = rows.bit_length() - 1
    hit = ((a & (rows - 1)) == (b >> 4)) & ((a >> bits) == (b & 15))
    return jnp.where(hit, 1.0, 0.0).astype(BF)


def own_frames(count):
    return lambda frame, slot: (frame == slot) & (slot < count)


def own_and_next(count, blocks):
    after = jnp.where(lax.axis_index("tm") < blocks - 1, count, 64)
    return lambda frame, slot: ((frame < OWN) & (frame == slot) & (slot < count)) | (
        (frame >= OWN) & (slot == after + frame - OWN)
    )


def silu_norm(v):
    scaled = v * lax.rsqrt(jnp.mean(v * v, axis=-1, keepdims=True) + 1e-06)
    return scaled * (0.5 + 0.5 * jnp.tanh(0.5 * scaled))


def slot_mask(shape, count):
    return lax.broadcasted_iota(jnp.int32, shape, len(shape) - 2) < count


def grad_of_temporal(gy, wt_ref, count):
    n = gy.shape[0]
    flat = gy.reshape(n * SLOTS, CH)
    total = mm_nt(flat, wt_ref[2]).reshape(n, SLOTS, CH)
    for k in (1, 0):
        term = mm_nt(flat, wt_ref[k]).reshape(n, SLOTS, CH)
        total = total + pltpu.roll(term, SLOTS - (2 - k), 1)
    return jnp.where(slot_mask(total.shape, count), total, 0.0).astype(BF)


def place_bits():
    t, g = lax.axis_index("tm"), lax.axis_index("grp")
    return t & 1, ((t >> 1) & 1) + 2 * (g & 1), (t >> 2) & 3


def split_cores(value, keep_ref, send_ref, k):
    core, _, _ = place_bits()
    low, high = value[:, : CH // 2].astype(BF), value[:, CH // 2 :].astype(BF)
    keep_ref[:, k] = jnp.where(core == 0, low, high).reshape(16, 16, CH // 2)
    send_ref[:, k] = jnp.where(core == 0, high, low).reshape(16, 16, CH // 2)


def edges_kernel(bands, count_ref, x_ref, *outs):
    count = count_ref[0]
    band = lax.axis_index("grp")
    wide = x_ref.shape[1]
    if bands == 2:
        starts, lower = [jnp.where(band == 0, wide - 16, 0)], [band == 0]
    else:
        starts, lower = [wide - 16, 0], [True, False]
    place = to_slots(16, SLOTS, own_frames(count))
    for k, at in enumerate(starts):
        piece = x_ref[:, pl.ds(pl.multiple_of(at, 16), 16), :].reshape(SLOTS * 16, CH)
        v = mm(place, piece)
        v = jnp.where(lower[k], v[128:], v[:128])
        outs[k][...] = silu_norm(v).astype(BF)


def acts_kernel(count_ref, x_ref, _, xt_ref, acts_ref, at_ref, last_ref):
    count = count_ref[0]
    rows, cols = xt_ref.shape[0], xt_ref.shape[1]
    edge = jnp.zeros((rows + 2, SLOTS, CH), BF)
    acts_ref[:, 0] = edge
    acts_ref[:, cols + 1] = edge
    place = to_slots(16, SLOTS, own_frames(count))
    last = silu_norm(x_ref[pl.ds(count - 2, 2)].reshape(2 * rows * cols, CH).astype(F32))
    last_ref[0 : 2 * rows * cols] = last.astype(BF)

    def rows_of(q, _):
        at = pl.multiple_of(q * 16, 16)
        piece = x_ref[:, pl.ds(at, 16), :].reshape(SLOTS * 16, CH)
        v = mm(place, piece)
        xt_ref[pl.ds(2 * q, 2)] = v.astype(BF).reshape(2, cols, SLOTS, CH)
        a = silu_norm(v).astype(BF)
        acts_ref[pl.ds(2 * q + 1, 2), 1 : cols + 1] = a.reshape(2, cols, SLOTS, CH)
        flipped = a.T
        for i in range(3):
            at = pl.multiple_of((2 * q + 3 - i) * 128, 128)
            at_ref[i * CH : i * CH + CH, pl.ds(at, 256)] = flipped
        return 0

    lax.fori_loop(0, rows // 2, rows_of, 0, unroll=True)


def next_kernel(cot_ref, _, nxt_ref):
    nxt_ref[...] = cot_ref[0:2]


def halo_kernel(bands, count_ref, top_ref, bot_ref, *rest):
    acts_ref, at_ref, last_ref = rest[-3:]
    count = count_ref[0]
    band = lax.axis_index("grp")
    rows, cols = acts_ref.shape[0] - 2, acts_ref.shape[1] - 2
    halo = []
    for ref, flag, i, row in ((top_ref, band > 0, 0, 0), (bot_ref, band < bands - 1, 2, rows + 1)):
        a = jnp.where(flag, ref[...].astype(F32), 0.0).astype(BF)
        acts_ref[row, 1 : cols + 1] = a.reshape(cols, SLOTS, CH)
        at = (row - i + 2) * 128
        at_ref[i * CH : i * CH + CH, at : at + 128] = a.T
        halo.append(a)
    a, b = iotas(32, 256)
    pick = ((a & 15) == (b >> 4)) & ((b & 15) == count - 2 + (a >> 4))
    pick = jnp.where(pick, 1.0, 0.0).astype(BF)
    last_ref[2 * rows * cols :] = mm(pick, jnp.concatenate(halo, 0)).astype(BF)


def conv_rows(acts_ref, ws_ref, sp_ref, start):
    rows, cols = sp_ref.shape[0], sp_ref.shape[1]

    def rows_of(q, _):
        total = None
        for i in range(3):
            for j in range(3):
                left = acts_ref[pl.ds(start + 4 * q + i, 4), j : j + cols].reshape(
                    4 * cols * SLOTS, CH
                )
                term = mm(left, ws_ref[i * 3 + j])
                total = term if total is None else total + term
        sp_ref[pl.ds(4 * q, 4)] = total.astype(BF).reshape(4, cols, SLOTS, CH)
        return 0

    lax.fori_loop(0, rows // 4, rows_of, 0, unroll=True)


def upper_kernel(acts_in, prev_ref, ws_ref, _, acts_ref, sp_ref):
    rows, cols = acts_ref.shape[0] - 2, acts_ref.shape[1] - 2
    a, b = iotas(256, 32)
    place = ((a >> 4) == (b & 15)) & ((a & 15) == OWN + (b >> 4)) & (lax.axis_index("tm") > 0)
    place = jnp.where(place, 1.0, 0.0).astype(BF)
    size = rows * cols
    for q in range(rows // 2 + 1):
        if q == rows // 2:
            both, prev = slice(0, rows + 2, rows + 1), prev_ref[2 * size :]
        else:
            both = slice(2 * q + 1, 2 * q + 3)
            parts = [prev_ref[f * size + q * 16 : f * size + q * 16 + 16] for f in range(2)]
            prev = jnp.concatenate(parts, 0)
        prev = mm(place, prev).astype(BF).reshape(2, cols, SLOTS, CH)
        for k, row in enumerate(range(rows + 2)[both]):
            acts_ref[row, 1 : cols + 1] = acts_ref[row, 1 : cols + 1] + prev[k]

    conv_rows(acts_ref, ws_ref, sp_ref, 0)


def lower_kernel(acts_ref, ws_ref, *rest):
    sp_ref = rest[-1]
    conv_rows(acts_ref, ws_ref, sp_ref, sp_ref.shape[0])


def grad_spatial_kernel(
    blocks, bands, count_ref, at_ref, cot_ref, nxt_ref, wt_ref, wd_ref,
    cott_ref, gy_ref, gs_ref, keep_ref, send_ref, *edge_refs,
):
    count = count_ref[0]
    band = lax.axis_index("grp")
    rows, cols = gy_ref.shape[0], gy_ref.shape[1]
    edge = jnp.zeros((rows, SLOTS, CH), BF)
    gs_ref[:, 0] = edge
    gs_ref[:, cols + 1] = edge

    place_next = to_slots(16, SLOTS, own_and_next(count, blocks))
    halves = []
    for q in range(rows * cols // 64):
        four = slice(q * 4, q * 4 + 4)
        piece = jnp.concatenate(
            [cot_ref[0:OWN, four].reshape(OWN, 16, CH), nxt_ref[:, four].reshape(2, 16, CH)], 0
        ).reshape(SLOTS * 16, CH)
        halves.append(mm(place_next, piece).astype(BF))
    placed = jnp.concatenate(halves, 0)
    cott_ref[...] = placed.reshape(rows // 2, cols // 2, SLOTS, CH)
    for i in range(2):
        for j in range(2):
            g = mm_nt(placed, wd_ref[i * 2 + j]).astype(BF).reshape(rows // 2, cols // 2, SLOTS, CH)
            for r in range(rows // 2):
                for c in range(cols // 2):
                    gy_ref[2 * r + i, 2 * c + j] = g[r, c]
    last = cott_ref[rows // 2 - 1].reshape(cols // 2 * SLOTS, CH)
    first = cott_ref[0].reshape(cols // 2 * SLOTS, CH)
    if bands == 2:
        edge_refs[0][...] = jnp.where(band == 0, last, first)
    else:
        edge_refs[0][...] = last
        edge_refs[1][...] = first

    def grads_of(q, _):
        g = gy_ref[pl.ds(8 * q, 8)].reshape(8 * cols, SLOTS, CH)
        s = grad_of_temporal(g, wt_ref, count)
        gs_ref[pl.ds(8 * q, 8), 1 : cols + 1] = s.reshape(8, cols, SLOTS, CH)
        g = jnp.where(slot_mask(g.shape, count), g.astype(F32), 0.0)
        gy_ref[pl.ds(8 * q, 8)] = g.astype(BF).reshape(8, cols, SLOTS, CH)
        return 0

    lax.fori_loop(0, rows // 8, grads_of, 0, unroll=True)

    wide = rows * cols * SLOTS
    for j in range(3):
        right = gs_ref[:, 2 - j : 2 - j + cols].reshape(wide, CH)
        value = mm(at_ref[:, 256 : 256 + wide], right)
        for i in range(3):
            split_cores(value[i * CH : i * CH + CH], keep_ref, send_ref, i * 3 + j)


def forward_kernel(
    count_ref, xt_ref, upper_ref, lower_ref, cott_ref, gy_ref, wt_ref, wd_ref, *rest
):
    down_ref, keep_ref, send_ref, y_ref, st_ref, yt_ref = rest[-6:]
    count = count_ref[0]
    rows, cols = xt_ref.shape[0], xt_ref.shape[1]
    for q, sp_ref in enumerate((upper_ref, lower_ref)):
        s = sp_ref[...].reshape(8 * cols * SLOTS, CH).astype(F32)
        s = s.reshape(8 * cols, SLOTS, CH)
        total = None
        for k in range(3):
            shifted = s if k == 2 else pltpu.roll(s, 2 - k, 1)
            shifted = shifted.astype(BF).reshape(8 * cols * SLOTS, CH)
            at = slice(q * 1024, q * 1024 + 1024)
            st_ref[k * CH : k * CH + CH, at] = shifted.T
            term = mm(shifted, wt_ref[k])
            total = term if total is None else total + term
        x = xt_ref[8 * q : 8 * q + 8].reshape(8 * cols, SLOTS, CH).astype(F32)
        y = jnp.where(slot_mask(x.shape, count), x + total.reshape(x.shape), 0.0).astype(BF)
        y_ref[8 * q : 8 * q + 8] = y.reshape(8, cols, SLOTS, CH)

    wide = rows * cols * SLOTS
    value = mm(st_ref[...], gy_ref[...].reshape(wide, CH))
    for k in range(3):
        split_cores(value[k * CH : k * CH + CH], keep_ref, send_ref, k)

    small = wide // 4
    total = None
    for i in range(2):
        for j in range(2):
            tiles = [
                y_ref[2 * r + i, 2 * c + j] for r in range(rows // 2) for c in range(cols // 2)
            ]
            piece = jnp.concatenate(tiles, axis=0)
            k = i * 2 + j
            yt_ref[k * CH : k * CH + CH] = piece.T
            term = mm(piece, wd_ref[k])
            total = term if total is None else total + term
    down_ref[...] = total.astype(BF)
    value = mm(yt_ref[...], cott_ref[...].reshape(small, CH))
    for k in range(4):
        split_cores(value[k * CH : k * CH + CH], keep_ref, send_ref, 3 + k)


def grad_x_kernel(
    bands, count_ref, xt_ref, gy_ref, gs_ref, top_ref, bot_ref, wt_ref, wd_ref, ws_ref, slot_ref, *rest
):
    out_ref, down_ref, token_ref, pad_ref, buf, sems = rest[-6:]
    token_ref[...] = jnp.zeros_like(token_ref)
    count = count_ref[0]
    band = lax.axis_index("grp")
    rows, cols = xt_ref.shape[0], xt_ref.shape[1]
    pad_ref[1 : rows + 1] = gs_ref[...]
    edge = jnp.zeros((SLOTS, CH), BF)
    for ref, flag, i, row in ((top_ref, band > 0, 1, 0), (bot_ref, band < bands - 1, 0, rows + 1)):
        pair = [
            mm_nt(ref[...], wd_ref[i * 2 + j]).astype(BF).reshape(cols // 2, SLOTS, CH)
            for j in range(2)
        ]
        g = jnp.stack(pair, axis=1).reshape(cols, SLOTS, CH)
        pad_ref[row, 0] = edge
        pad_ref[row, 1 : cols + 1] = grad_of_temporal(g, wt_ref, jnp.where(flag, count, 0))
        pad_ref[row, cols + 1] = edge
    back = to_frames(16)

    def rows_of(q, _):
        total = None
        for i in range(3):
            for j in range(3):
                left = pad_ref[pl.ds(4 * q + 2 - i, 4), 2 - j : 2 - j + cols].reshape(
                    4 * cols * SLOTS, CH
                )
                term = mm_nt(left, ws_ref[i * 3 + j])
                total = term if total is None else total + term
        at = 4 * q
        v = xt_ref[pl.ds(at, 4)].reshape(4 * cols * SLOTS, CH).astype(F32)
        r = lax.rsqrt(jnp.mean(v * v, axis=-1, keepdims=True) + 1e-06)
        u = v * r
        s = 0.5 + 0.5 * jnp.tanh(0.5 * u)
        gu = total * (s * (1.0 + u * (1.0 - s)))
        dot = jnp.mean(gu * u, axis=-1, keepdims=True)
        gv = r * (gu - u * dot)
        gx = gy_ref[pl.ds(at, 4)].reshape(4 * cols * SLOTS, CH).astype(F32) + gv
        gx = gx.reshape(4 * cols, SLOTS, CH)
        gx = jnp.where(slot_mask(gx.shape, count), gx, 0.0).astype(BF).reshape(4 * cols * SLOTS, CH)
        for k in range(2):
            o = mm(back, gx[k * 256 : k * 256 + 256]).astype(BF)
            buf[:, pl.ds(pl.multiple_of((2 * q + k) * 16, 16), 16), :] = o.reshape(SLOTS, 16, CH)
        return 0

    lax.fori_loop(0, rows // 4, rows_of, 0)
    copy = pltpu.make_async_copy(buf, out_ref, sems.at[0])
    copy.start()
    for q in range(down_ref.shape[1] // 4):
        o = mm(back, slot_ref[q * 256 : q * 256 + 256]).astype(BF)
        down_ref[:, q * 4 : q * 4 + 4] = o.reshape(SLOTS, 4, cols // 2, CH)
    copy.wait()


ORDER = (0, 3, 2, 1)


def plane_send_kernel(keep_ref, got_ref, *rest):
    _, p, _ = place_bits()
    for r, out in zip(ORDER, rest[-4:]):
        at = pl.ds((p ^ r) * 4, 4)
        out[...] = (keep_ref[at].astype(F32) + got_ref[at].astype(F32)).astype(BF)


def line_send_kernel(*refs):
    outs = refs[8:]
    _, _, z = place_bits()
    for out, r in zip(outs, ORDER):
        at = 0
        for chain in (refs[:4], refs[4:8]):
            parts = [ref[z ^ r].astype(F32) for ref in chain]
            n = parts[0].shape[0]
            out[at : at + n] = (parts[0] + parts[1] + parts[2] + parts[3]).astype(BF)
            at += n


def line_sum_kernel(a_ref, b_ref, c_ref, d_ref, *rest):
    out_ref = rest[-1]
    parts = [ref[...].astype(F32) for ref in (a_ref, b_ref, c_ref, d_ref)]
    out_ref[...] = (parts[0] + parts[1] + parts[2] + parts[3]).astype(BF)


def line_gather_kernel(a_ref, b_ref, c_ref, d_ref, out_ref):
    _, _, z = place_bits()
    for r, ref in zip(ORDER, (a_ref, b_ref, c_ref, d_ref)):
        out_ref[z ^ r] = ref[...]


def plane_gather_kernel(a_ref, b_ref, c_ref, d_ref, _, out_ref):
    _, p, _ = place_bits()
    for r, ref in zip(ORDER, (a_ref, b_ref, c_ref, d_ref)):
        out_ref[pl.ds((p ^ r) * 4, 4)] = ref[...]


def add_kernel(a_ref, b_ref, out_ref):
    out_ref[...] = (a_ref[...].astype(F32) + b_ref[...].astype(F32)).astype(BF)


def pass_kernel(*_):
    pass


def finish_kernel(own, half_ref, *rest):
    buf, sems = rest[-2:]
    outs = rest[-5:-2]
    core, _, _ = place_bits()
    at = pl.multiple_of((core if own else 1 - core) * (CH // 2), CH // 2)
    copies = []
    k = 0
    for out in outs:
        for m in range(out.shape[0]):
            buf[k] = half_ref[:, k].reshape(CH, CH // 2).astype(F32)
            copies.append(
                pltpu.make_async_copy(buf.at[k], out.at[m, :, pl.ds(at, CH // 2)], sems.at[k])
            )
            copies[-1].start()
            k += 1
    for copy in copies:
        copy.wait()


VMEM = pl.BlockSpec(memory_space=pltpu.VMEM)
SMEM = pl.BlockSpec(memory_space=pltpu.SMEM)
ANY = pl.BlockSpec(memory_space=pl.ANY)
HBM = pl.BlockSpec(memory_space=pltpu.HBM)
TOKEN = (VMEM, (8, 128), F32)


def call(kernel, name, ins, outs, scratch=(), flops=0, alias=None, grant=10, moved=None):
    shapes = [jax.ShapeDtypeStruct(o[1], o[2] if len(o) > 2 else BF) for o in outs]
    if moved is None:
        moved = sum(a.size * a.dtype.itemsize for s, a in ins if s is not ANY)
        moved += sum(s.size * s.dtype.itemsize for s in shapes)
    return pl.pallas_call(
        kernel,
        out_shape=shapes,
        in_specs=[s for s, _ in ins],
        out_specs=[o[0] for o in outs],
        scratch_shapes=list(scratch),
        compiler_params=pltpu.CompilerParams(vmem_limit_bytes=grant * 2**20),
        cost_estimate=pl.CostEstimate(flops=flops, bytes_accessed=moved, transcendentals=0),
        input_output_aliases=alias or {},
        name=name,
    )(*[a for _, a in ins])


AXES = ("tm", "grp")


def plan(tm, grp):
    low, total = grp.bit_length() - 1, (tm * grp).bit_length() - 1
    plane, line = [low + 1, 0], [low + 2, low + 3]
    return low, plane, line, [b for b in range(total) if b not in [low] + plane + line]


def swap(value, tm, grp, *bits):
    flip = sum(1 << b for b in bits)
    return lax.ppermute(value, AXES, [(d, d ^ flip) for d in range(tm * grp)])


def core_round(value, tm, grp):
    return swap(value, tm, grp, plan(tm, grp)[0])


def four_round(parts, bits, tm, grp):
    return [
        parts[0],
        swap(parts[1], tm, grp, *bits),
        swap(parts[2], tm, grp, bits[1]),
        swap(parts[3], tm, grp, bits[0]),
    ]


def plane_send(keep, got, after):
    ins = [(VMEM, keep), (VMEM, got)] + [(ANY, a) for a in after]
    shape = (4, keep.shape[1], 16, CH // 2)
    return list(call(plane_send_kernel, "plane_send", ins, [(VMEM, shape)] * 4))


def passed(value, after):
    ins = [(ANY, value)] + [(ANY, a) for a in after]
    return call(pass_kernel, "pass", ins, [(ANY, value.shape)], alias={0: 0})[0]


def finish(own, half, before):
    n = half.shape[1]
    return list(
        call(
            functools.partial(finish_kernel, own),
            "finish",
            [(VMEM, half)] + [(HBM, a) for a in before],
            [(HBM, (m, CH, CH), F32) for m in (9, 3, 4)],
            [pltpu.VMEM((n, CH, CH // 2), F32), pltpu.SemaphoreType.DMA((n,))],
            alias={1 + i: i for i in range(len(before))},
        )
    )


def along(value, axis, by):
    count = lax.axis_size(axis)
    pairs = [(i, i + by) for i in range(count) if 0 <= i + by < count]
    return lax.ppermute(value, axis, pairs)


def around(value, axis, by):
    count = lax.axis_size(axis)
    return lax.ppermute(value, axis, [(i, (i + by) % count) for i in range(count)])


def from_bands(parts):
    if len(parts) == 1:
        got = lax.ppermute(parts[0], "grp", [(0, 1), (1, 0)])
        return got, got
    return along(parts[0], "grp", 1), along(parts[1], "grp", -1)


def body(tm, grp, frames_in, span_frames, w_spatial, w_temporal, w_down, cotangent):
    slots, rows, cols, ch = frames_in.shape
    wide = rows * cols
    x = frames_in.reshape(slots, wide, ch)
    ws = w_spatial.reshape(9, ch, ch)
    wd = w_down.reshape(4, ch, ch)
    wt = w_temporal
    count = (SMEM, span_frames)
    tap = 2 * slots * wide * ch * ch
    tile = (rows, cols, slots, ch)
    padded = (rows + 2, cols + 2, slots, ch)
    dma = pltpu.SemaphoreType.DMA

    sides = 1 if grp == 2 else 2
    edge = call(
        functools.partial(edges_kernel, grp),
        "edges",
        [count, (VMEM, x)],
        [(VMEM, (cols * slots, ch))] * sides,
        flops=tap // 8,
    )
    top, bot = from_bands(edge)
    last_shape = (2 * wide + 32, ch)
    at_shape = (3 * ch, (rows + 4) * 128)
    xt, acts, at, last_two = call(
        acts_kernel,
        "acts",
        [count, (VMEM, x), (ANY, edge[0])],
        [(VMEM, tile), (VMEM, padded), (VMEM, at_shape), (VMEM, last_shape)],
        flops=2 * tap,
    )
    (nxt,) = call(
        next_kernel,
        "next",
        [(VMEM, cotangent), (ANY, last_two)],
        [(VMEM, (2,) + cotangent.shape[1:])],
        moved=1024,
    )
    nxt_got = along(nxt, "tm", -1)
    acts, at, last_two = call(
        functools.partial(halo_kernel, grp),
        "halo",
        [count, (VMEM, top), (VMEM, bot), (VMEM, acts), (VMEM, at), (VMEM, last_two), (ANY, nxt),
         (VMEM, cotangent), (VMEM, wt), (VMEM, wd)],
        [(VMEM, padded), (VMEM, at_shape), (VMEM, last_shape)],
        alias={3: 0, 4: 1, 5: 2},
        moved=1024,
    )
    prev = around(last_two, "tm", 1)
    half = (16, 9, 16, ch // 2)
    cott, gy, gs, keep_a, send_a, *edge = call(
        functools.partial(grad_spatial_kernel, tm, grp),
        "grad_spatial",
        [count, (VMEM, at), (VMEM, cotangent), (VMEM, nxt_got), (VMEM, wt), (VMEM, wd)],
        [(VMEM, (rows // 2, cols // 2, slots, ch)), (VMEM, tile),
         (VMEM, (rows, cols + 2, slots, ch)), (VMEM, half), (VMEM, half)]
        + [(VMEM, (cols // 2 * slots, ch))] * sides,
        flops=14 * tap,
    )
    send_a = passed(send_a, [prev])
    got_a = core_round(send_a, tm, grp)
    cot_top, cot_bot = from_bands(edge)
    half_tile = (rows // 2, cols, slots, ch)
    acts, upper = call(
        upper_kernel,
        "spatial_upper",
        [(VMEM, acts), (VMEM, prev), (VMEM, ws), (ANY, send_a)],
        [(VMEM, padded), (VMEM, half_tile)],
        flops=5 * tap,
        alias={0: 0},
    )
    _, plane, line, others = plan(tm, grp)
    parts_a = plane_send(keep_a, got_a, [upper])
    (lower,) = call(
        lower_kernel,
        "spatial_lower",
        [(VMEM, acts), (VMEM, ws)] + [(ANY, a) for a in parts_a],
        [(VMEM, half_tile)],
        flops=4 * tap,
    )
    half = (16, 7, 16, ch // 2)
    down, keep_b, send_b = call(
        forward_kernel,
        "forward",
        [count, (VMEM, xt), (VMEM, upper), (VMEM, lower), (VMEM, cott), (VMEM, gy), (VMEM, wt), (VMEM, wd),
         *((ANY, a) for a in parts_a)],
        [(VMEM, (slots * wide // 4, ch)), (VMEM, half), (VMEM, half)],
        [pltpu.VMEM(v, BF) for v in (tile, (3 * ch, slots * wide), (4 * ch, slots * wide // 4))],
        moved=1024,
        grant=14,
    )
    parts_a = four_round(parts_a, plane, tm, grp)
    send_b = passed(send_b, parts_a[1:2])
    parts_b = plane_send(keep_b, core_round(send_b, tm, grp), [])
    parts_b = four_round(parts_b, plane, tm, grp)
    parts = call(
        line_send_kernel,
        "line_send",
        [(VMEM, a) for a in parts_a + parts_b],
        [(VMEM, (16, 16, ch // 2))] * 4,
    )
    parts = four_round(list(parts), line, tm, grp)
    ins = [(VMEM, a) for a in parts]
    (mine,) = call(line_sum_kernel, "line_sum", ins, [(VMEM, parts[0].shape)])
    for bit in others:
        got = swap(mine, tm, grp, bit)
        (mine,) = call(add_kernel, "add", [(VMEM, mine), (VMEM, got)], [(VMEM, mine.shape)])
    parts = four_round([mine] * 4, line, tm, grp)
    (mine,) = call(
        line_gather_kernel, "line_gather", [(VMEM, a) for a in parts], [(VMEM, (4,) + mine.shape)]
    )
    parts = four_round([mine] * 4, plane, tm, grp)
    grad_x, down, token = call(
        functools.partial(grad_x_kernel, grp),
        "grad_x",
        [count, (VMEM, xt), (VMEM, gy), (VMEM, gs), (VMEM, cot_top), (VMEM, cot_bot), (VMEM, wt),
         (VMEM, wd), (VMEM, ws), (VMEM, down), (ANY, mine)],
        [(HBM, (slots, wide, ch)), (VMEM, cotangent.shape), TOKEN],
        [pltpu.VMEM(padded, BF), pltpu.VMEM((slots, wide, ch), BF), dma((1,))],
        flops=10 * tap,
    )
    ins = [(VMEM, a) for a in parts] + [(ANY, token)]
    (mine,) = call(plane_gather_kernel, "plane_gather", ins, [(VMEM, (16,) + mine.shape[1:])])
    got = core_round(mine, tm, grp)
    outs = finish(True, mine, [])
    sum_s, sum_t, sum_d = finish(False, got, outs)
    return (
        down,
        grad_x.reshape(frames_in.shape),
        sum_s.reshape(w_spatial.shape),
        sum_t,
        sum_d.reshape(w_down.shape),
    )


def solution(mesh):
    return jax.shard_map(
        functools.partial(body, mesh.shape["tm"], mesh.shape["grp"]),
        mesh=mesh,
        in_specs=(P("tm", "grp", None, None), P("tm"), P(), P(), P(), P("tm", "grp", None, None)),
        out_specs=(P("tm", "grp", None, None), P("tm", "grp", None, None), P(), P(), P()),
        check_vma=False,
    )
```

```python
import functools

import jax
import jax.numpy as jnp
from jax import lax
from jax.experimental import pallas as pl
from jax.experimental.pallas import tpu as pltpu
from jax.sharding import PartitionSpec as P

SLOTS = 16
OWN = 14
CH = 256
BF = jnp.bfloat16
F32 = jnp.float32


def mm(a, b):
    return lax.dot_general(a, b, (((1,), (0,)), ((), ())), preferred_element_type=F32)


def mm_nt(a, b):
    return lax.dot_general(a, b, (((1,), (1,)), ((), ())), preferred_element_type=F32)


def iotas(rows, cols):
    return (
        lax.broadcasted_iota(jnp.int32, (rows, cols), 0),
        lax.broadcasted_iota(jnp.int32, (rows, cols), 1),
    )


def to_slots(rows, frames, keep):
    a, b = iotas(rows * SLOTS, frames * rows)
    bits = rows.bit_length() - 1
    hit = ((a >> 4) == (b & (rows - 1))) & keep(b >> bits, a & 15)
    return jnp.where(hit, 1.0, 0.0).astype(BF)


def to_frames(rows):
    a, b = iotas(SLOTS * rows, rows * SLOTS)
    bits = rows.bit_length() - 1
    hit = ((a & (rows - 1)) == (b >> 4)) & ((a >> bits) == (b & 15))
    return jnp.where(hit, 1.0, 0.0).astype(BF)


def own_frames(count):
    return lambda frame, slot: (frame == slot) & (slot < count)


def own_and_next(count, blocks):
    after = jnp.where(lax.axis_index("tm") < blocks - 1, count, 64)
    return lambda frame, slot: ((frame < OWN) & (frame == slot) & (slot < count)) | (
        (frame >= OWN) & (slot == after + frame - OWN)
    )


def silu_norm(v):
    scaled = v * lax.rsqrt(jnp.mean(v * v, axis=-1, keepdims=True) + 1e-06)
    return scaled * (0.5 + 0.5 * jnp.tanh(0.5 * scaled))


def slot_mask(shape, count):
    return lax.broadcasted_iota(jnp.int32, shape, len(shape) - 2) < count


def grad_of_temporal(gy, wt_ref, count):
    n = gy.shape[0]
    flat = gy.reshape(n * SLOTS, CH)
    total = mm_nt(flat, wt_ref[2]).reshape(n, SLOTS, CH)
    for k in (1, 0):
        term = mm_nt(flat, wt_ref[k]).reshape(n, SLOTS, CH)
        total = total + pltpu.roll(term, SLOTS - (2 - k), 1)
    return jnp.where(slot_mask(total.shape, count), total, 0.0).astype(BF)


def place_bits():
    t, g = lax.axis_index("tm"), lax.axis_index("grp")
    return t & 1, ((t >> 1) & 1) + 2 * (g & 1), (t >> 2) & 3


def split_cores(value, keep_ref, send_ref, k):
    core, _, _ = place_bits()
    low, high = value[:, : CH // 2].astype(BF), value[:, CH // 2 :].astype(BF)
    keep_ref[:, k] = jnp.where(core == 0, low, high).reshape(16, 16, CH // 2)
    send_ref[:, k] = jnp.where(core == 0, high, low).reshape(16, 16, CH // 2)


def edges_kernel(bands, count_ref, x_ref, *outs):
    count = count_ref[0]
    band = lax.axis_index("grp")
    wide = x_ref.shape[1]
    if bands == 2:
        starts, lower = [jnp.where(band == 0, wide - 16, 0)], [band == 0]
    else:
        starts, lower = [wide - 16, 0], [True, False]
    place = to_slots(16, SLOTS, own_frames(count))
    for k, at in enumerate(starts):
        piece = x_ref[:, pl.ds(pl.multiple_of(at, 16), 16), :].reshape(SLOTS * 16, CH)
        v = mm(place, piece)
        v = jnp.where(lower[k], v[128:], v[:128])
        outs[k][...] = silu_norm(v).astype(BF)


def acts_kernel(count_ref, x_ref, _, xt_ref, acts_ref, at_ref, last_ref):
    count = count_ref[0]
    rows, cols = xt_ref.shape[0], xt_ref.shape[1]
    edge = jnp.zeros((rows + 2, SLOTS, CH), BF)
    acts_ref[:, 0] = edge
    acts_ref[:, cols + 1] = edge
    place = to_slots(16, SLOTS, own_frames(count))
    last = silu_norm(x_ref[pl.ds(count - 2, 2)].reshape(2 * rows * cols, CH).astype(F32))
    last_ref[0 : 2 * rows * cols] = last.astype(BF)

    def rows_of(q, _):
        at = pl.multiple_of(q * 16, 16)
        piece = x_ref[:, pl.ds(at, 16), :].reshape(SLOTS * 16, CH)
        v = mm(place, piece)
        xt_ref[pl.ds(2 * q, 2)] = v.astype(BF).reshape(2, cols, SLOTS, CH)
        a = silu_norm(v).astype(BF)
        acts_ref[pl.ds(2 * q + 1, 2), 1 : cols + 1] = a.reshape(2, cols, SLOTS, CH)
        flipped = a.T
        for i in range(3):
            at = pl.multiple_of((2 * q + 3 - i) * 128, 128)
            at_ref[i * CH : i * CH + CH, pl.ds(at, 256)] = flipped
        return 0

    lax.fori_loop(0, rows // 2, rows_of, 0, unroll=True)


def next_kernel(cot_ref, _, nxt_ref):
    nxt_ref[...] = cot_ref[0:2]


def halo_kernel(bands, count_ref, top_ref, bot_ref, *rest):
    acts_ref, at_ref, last_ref = rest[-3:]
    count = count_ref[0]
    band = lax.axis_index("grp")
    rows, cols = acts_ref.shape[0] - 2, acts_ref.shape[1] - 2
    halo = []
    for ref, flag, i, row in ((top_ref, band > 0, 0, 0), (bot_ref, band < bands - 1, 2, rows + 1)):
        a = jnp.where(flag, ref[...].astype(F32), 0.0).astype(BF)
        acts_ref[row, 1 : cols + 1] = a.reshape(cols, SLOTS, CH)
        at = (row - i + 2) * 128
        at_ref[i * CH : i * CH + CH, at : at + 128] = a.T
        halo.append(a)
    a, b = iotas(32, 256)
    pick = ((a & 15) == (b >> 4)) & ((b & 15) == count - 2 + (a >> 4))
    pick = jnp.where(pick, 1.0, 0.0).astype(BF)
    last_ref[2 * rows * cols :] = mm(pick, jnp.concatenate(halo, 0)).astype(BF)


def conv_rows(acts_ref, ws_ref, sp_ref, start):
    rows, cols = sp_ref.shape[0], sp_ref.shape[1]

    def rows_of(q, _):
        total = None
        for i in range(3):
            for j in range(3):
                left = acts_ref[pl.ds(start + 4 * q + i, 4), j : j + cols].reshape(
                    4 * cols * SLOTS, CH
                )
                term = mm(left, ws_ref[i * 3 + j])
                total = term if total is None else total + term
        sp_ref[pl.ds(4 * q, 4)] = total.astype(BF).reshape(4, cols, SLOTS, CH)
        return 0

    lax.fori_loop(0, rows // 4, rows_of, 0, unroll=True)


def upper_kernel(acts_in, prev_ref, ws_ref, _, acts_ref, sp_ref):
    rows, cols = acts_ref.shape[0] - 2, acts_ref.shape[1] - 2
    a, b = iotas(256, 32)
    place = ((a >> 4) == (b & 15)) & ((a & 15) == OWN + (b >> 4)) & (lax.axis_index("tm") > 0)
    place = jnp.where(place, 1.0, 0.0).astype(BF)
    size = rows * cols
    for q in range(rows // 2 + 1):
        if q == rows // 2:
            both, prev = slice(0, rows + 2, rows + 1), prev_ref[2 * size :]
        else:
            both = slice(2 * q + 1, 2 * q + 3)
            parts = [prev_ref[f * size + q * 16 : f * size + q * 16 + 16] for f in range(2)]
            prev = jnp.concatenate(parts, 0)
        prev = mm(place, prev).astype(BF).reshape(2, cols, SLOTS, CH)
        for k, row in enumerate(range(rows + 2)[both]):
            acts_ref[row, 1 : cols + 1] = acts_ref[row, 1 : cols + 1] + prev[k]

    conv_rows(acts_ref, ws_ref, sp_ref, 0)


def lower_kernel(acts_ref, ws_ref, *rest):
    sp_ref = rest[-1]
    conv_rows(acts_ref, ws_ref, sp_ref, sp_ref.shape[0])


def grad_spatial_kernel(
    blocks, bands, count_ref, at_ref, cot_ref, nxt_ref, wt_ref, wd_ref,
    cott_ref, gy_ref, gs_ref, keep_ref, send_ref, *edge_refs,
):
    count = count_ref[0]
    band = lax.axis_index("grp")
    rows, cols = gy_ref.shape[0], gy_ref.shape[1]
    edge = jnp.zeros((rows, SLOTS, CH), BF)
    gs_ref[:, 0] = edge
    gs_ref[:, cols + 1] = edge

    place_next = to_slots(16, SLOTS, own_and_next(count, blocks))
    halves = []
    for q in range(rows * cols // 64):
        four = slice(q * 4, q * 4 + 4)
        piece = jnp.concatenate(
            [cot_ref[0:OWN, four].reshape(OWN, 16, CH), nxt_ref[:, four].reshape(2, 16, CH)], 0
        ).reshape(SLOTS * 16, CH)
        halves.append(mm(place_next, piece).astype(BF))
    placed = jnp.concatenate(halves, 0)
    cott_ref[...] = placed.reshape(rows // 2, cols // 2, SLOTS, CH)
    for i in range(2):
        for j in range(2):
            g = mm_nt(placed, wd_ref[i * 2 + j]).astype(BF).reshape(rows // 2, cols // 2, SLOTS, CH)
            for r in range(rows // 2):
                for c in range(cols // 2):
                    gy_ref[2 * r + i, 2 * c + j] = g[r, c]
    last = cott_ref[rows // 2 - 1].reshape(cols // 2 * SLOTS, CH)
    first = cott_ref[0].reshape(cols // 2 * SLOTS, CH)
    if bands == 2:
        edge_refs[0][...] = jnp.where(band == 0, last, first)
    else:
        edge_refs[0][...] = last
        edge_refs[1][...] = first

    def grads_of(q, _):
        g = gy_ref[pl.ds(8 * q, 8)].reshape(8 * cols, SLOTS, CH)
        s = grad_of_temporal(g, wt_ref, count)
        gs_ref[pl.ds(8 * q, 8), 1 : cols + 1] = s.reshape(8, cols, SLOTS, CH)
        g = jnp.where(slot_mask(g.shape, count), g.astype(F32), 0.0)
        gy_ref[pl.ds(8 * q, 8)] = g.astype(BF).reshape(8, cols, SLOTS, CH)
        return 0

    lax.fori_loop(0, rows // 8, grads_of, 0)

    wide = rows * cols * SLOTS
    for j in range(3):
        right = gs_ref[:, 2 - j : 2 - j + cols].reshape(wide, CH)
        value = mm(at_ref[:, 256 : 256 + wide], right)
        for i in range(3):
            split_cores(value[i * CH : i * CH + CH], keep_ref, send_ref, i * 3 + j)


def forward_kernel(
    count_ref, xt_ref, upper_ref, lower_ref, cott_ref, gy_ref, wt_ref, wd_ref, *rest
):
    down_ref, keep_ref, send_ref, y_ref, st_ref, yt_ref = rest[-6:]
    count = count_ref[0]
    rows, cols = xt_ref.shape[0], xt_ref.shape[1]
    for q, sp_ref in enumerate((upper_ref, lower_ref)):
        s = sp_ref[...].reshape(8 * cols * SLOTS, CH).astype(F32)
        s = s.reshape(8 * cols, SLOTS, CH)
        total = None
        for k in range(3):
            shifted = s if k == 2 else pltpu.roll(s, 2 - k, 1)
            shifted = shifted.astype(BF).reshape(8 * cols * SLOTS, CH)
            at = slice(q * 1024, q * 1024 + 1024)
            st_ref[k * CH : k * CH + CH, at] = shifted.T
            term = mm(shifted, wt_ref[k])
            total = term if total is None else total + term
        x = xt_ref[8 * q : 8 * q + 8].reshape(8 * cols, SLOTS, CH).astype(F32)
        y = jnp.where(slot_mask(x.shape, count), x + total.reshape(x.shape), 0.0).astype(BF)
        y_ref[8 * q : 8 * q + 8] = y.reshape(8, cols, SLOTS, CH)

    wide = rows * cols * SLOTS
    value = mm(st_ref[...], gy_ref[...].reshape(wide, CH))
    for k in range(3):
        split_cores(value[k * CH : k * CH + CH], keep_ref, send_ref, k)

    small = wide // 4
    total = None
    for i in range(2):
        for j in range(2):
            tiles = [
                y_ref[2 * r + i, 2 * c + j] for r in range(rows // 2) for c in range(cols // 2)
            ]
            piece = jnp.concatenate(tiles, axis=0)
            k = i * 2 + j
            yt_ref[k * CH : k * CH + CH] = piece.T
            term = mm(piece, wd_ref[k])
            total = term if total is None else total + term
    down_ref[...] = total.astype(BF)
    value = mm(yt_ref[...], cott_ref[...].reshape(small, CH))
    for k in range(4):
        split_cores(value[k * CH : k * CH + CH], keep_ref, send_ref, 3 + k)


def grad_x_kernel(
    bands, count_ref, xt_ref, gy_ref, gs_ref, top_ref, bot_ref, wt_ref, wd_ref, ws_ref, slot_ref, *rest
):
    out_ref, down_ref, token_ref, pad_ref, buf, sems = rest[-6:]
    token_ref[...] = jnp.zeros_like(token_ref)
    count = count_ref[0]
    band = lax.axis_index("grp")
    rows, cols = xt_ref.shape[0], xt_ref.shape[1]
    pad_ref[1 : rows + 1] = gs_ref[...]
    edge = jnp.zeros((SLOTS, CH), BF)
    for ref, flag, i, row in ((top_ref, band > 0, 1, 0), (bot_ref, band < bands - 1, 0, rows + 1)):
        pair = [
            mm_nt(ref[...], wd_ref[i * 2 + j]).astype(BF).reshape(cols // 2, SLOTS, CH)
            for j in range(2)
        ]
        g = jnp.stack(pair, axis=1).reshape(cols, SLOTS, CH)
        pad_ref[row, 0] = edge
        pad_ref[row, 1 : cols + 1] = grad_of_temporal(g, wt_ref, jnp.where(flag, count, 0))
        pad_ref[row, cols + 1] = edge
    back = to_frames(16)

    def rows_of(q, _):
        total = None
        for i in range(3):
            for j in range(3):
                left = pad_ref[pl.ds(4 * q + 2 - i, 4), 2 - j : 2 - j + cols].reshape(
                    4 * cols * SLOTS, CH
                )
                term = mm_nt(left, ws_ref[i * 3 + j])
                total = term if total is None else total + term
        at = 4 * q
        v = xt_ref[pl.ds(at, 4)].reshape(4 * cols * SLOTS, CH).astype(F32)
        r = lax.rsqrt(jnp.mean(v * v, axis=-1, keepdims=True) + 1e-06)
        u = v * r
        s = 0.5 + 0.5 * jnp.tanh(0.5 * u)
        gu = total * (s * (1.0 + u * (1.0 - s)))
        dot = jnp.mean(gu * u, axis=-1, keepdims=True)
        gv = r * (gu - u * dot)
        gx = gy_ref[pl.ds(at, 4)].reshape(4 * cols * SLOTS, CH).astype(F32) + gv
        gx = gx.reshape(4 * cols, SLOTS, CH)
        gx = jnp.where(slot_mask(gx.shape, count), gx, 0.0).astype(BF).reshape(4 * cols * SLOTS, CH)
        for k in range(2):
            o = mm(back, gx[k * 256 : k * 256 + 256]).astype(BF)
            buf[:, pl.ds(pl.multiple_of((2 * q + k) * 16, 16), 16), :] = o.reshape(SLOTS, 16, CH)
        return 0

    lax.fori_loop(0, rows // 4, rows_of, 0)
    copy = pltpu.make_async_copy(buf, out_ref, sems.at[0])
    copy.start()
    for q in range(down_ref.shape[1] // 4):
        o = mm(back, slot_ref[q * 256 : q * 256 + 256]).astype(BF)
        down_ref[:, q * 4 : q * 4 + 4] = o.reshape(SLOTS, 4, cols // 2, CH)
    copy.wait()


ORDER = (0, 3, 2, 1)


def plane_send_kernel(keep_ref, got_ref, *rest):
    _, p, _ = place_bits()
    for r, out in zip(ORDER, rest[-4:]):
        at = pl.ds((p ^ r) * 4, 4)
        out[...] = (keep_ref[at].astype(F32) + got_ref[at].astype(F32)).astype(BF)


def line_send_kernel(*refs):
    outs = refs[-4:]
    _, _, z = place_bits()
    for out, r in zip(outs, ORDER):
        at = 0
        for chain in (refs[:4], refs[4:8]):
            parts = [ref[z ^ r].astype(F32) for ref in chain]
            n = parts[0].shape[0]
            out[at : at + n] = (parts[0] + parts[1] + parts[2] + parts[3]).astype(BF)
            at += n


def line_sum_kernel(a_ref, b_ref, c_ref, d_ref, *rest):
    out_ref = rest[-1]
    parts = [ref[...].astype(F32) for ref in (a_ref, b_ref, c_ref, d_ref)]
    out_ref[...] = (parts[0] + parts[1] + parts[2] + parts[3]).astype(BF)


def line_gather_kernel(a_ref, b_ref, c_ref, d_ref, out_ref):
    _, _, z = place_bits()
    for r, ref in zip(ORDER, (a_ref, b_ref, c_ref, d_ref)):
        out_ref[z ^ r] = ref[...]


def plane_gather_kernel(a_ref, b_ref, c_ref, d_ref, _, out_ref):
    _, p, _ = place_bits()
    for r, ref in zip(ORDER, (a_ref, b_ref, c_ref, d_ref)):
        out_ref[pl.ds((p ^ r) * 4, 4)] = ref[...]


def add_kernel(a_ref, b_ref, out_ref):
    out_ref[...] = (a_ref[...].astype(F32) + b_ref[...].astype(F32)).astype(BF)


def pass_kernel(*_):
    pass


def finish_kernel(own, half_ref, *rest):
    buf, sems = rest[-2:]
    outs = rest[-5:-2]
    core, _, _ = place_bits()
    at = pl.multiple_of((core if own else 1 - core) * (CH // 2), CH // 2)
    copies = []
    k = 0
    for out in outs:
        for m in range(out.shape[0]):
            buf[k] = half_ref[:, k].reshape(CH, CH // 2).astype(F32)
            copies.append(
                pltpu.make_async_copy(buf.at[k], out.at[m, :, pl.ds(at, CH // 2)], sems.at[k])
            )
            copies[-1].start()
            k += 1
    for copy in copies:
        copy.wait()


VMEM = pl.BlockSpec(memory_space=pltpu.VMEM)
SMEM = pl.BlockSpec(memory_space=pltpu.SMEM)
ANY = pl.BlockSpec(memory_space=pl.ANY)
HBM = pl.BlockSpec(memory_space=pltpu.HBM)
TOKEN = (VMEM, (8, 128), F32)


def call(kernel, name, ins, outs, scratch=(), flops=0, alias=None, grant=10, moved=None):
    shapes = [jax.ShapeDtypeStruct(o[1], o[2] if len(o) > 2 else BF) for o in outs]
    if moved is None:
        moved = sum(a.size * a.dtype.itemsize for s, a in ins if s is not ANY)
        moved += sum(s.size * s.dtype.itemsize for s in shapes)
    return pl.pallas_call(
        kernel,
        out_shape=shapes,
        in_specs=[s for s, _ in ins],
        out_specs=[o[0] for o in outs],
        scratch_shapes=list(scratch),
        compiler_params=pltpu.CompilerParams(vmem_limit_bytes=grant * 2**20),
        cost_estimate=pl.CostEstimate(flops=flops, bytes_accessed=moved, transcendentals=0),
        input_output_aliases=alias or {},
        name=name,
    )(*[a for _, a in ins])


AXES = ("tm", "grp")


def plan(tm, grp):
    low, total = grp.bit_length() - 1, (tm * grp).bit_length() - 1
    plane, line = [low + 1, 0], [low + 2, low + 3]
    return low, plane, line, [b for b in range(total) if b not in [low] + plane + line]


def swap(value, tm, grp, *bits):
    flip = sum(1 << b for b in bits)
    return lax.ppermute(value, AXES, [(d, d ^ flip) for d in range(tm * grp)])


def core_round(value, tm, grp):
    return swap(value, tm, grp, plan(tm, grp)[0])


def four_round(parts, bits, tm, grp):
    return [
        parts[0],
        swap(parts[1], tm, grp, *bits),
        swap(parts[2], tm, grp, bits[1]),
        swap(parts[3], tm, grp, bits[0]),
    ]


def plane_send(keep, got, after):
    ins = [(VMEM, keep), (VMEM, got)] + [(ANY, a) for a in after]
    shape = (4, keep.shape[1], 16, CH // 2)
    return list(call(plane_send_kernel, "plane_send", ins, [(VMEM, shape)] * 4))


def passed(value, after):
    ins = [(ANY, value)] + [(ANY, a) for a in after]
    return call(pass_kernel, "pass", ins, [(ANY, value.shape)], alias={0: 0})[0]


def finish(own, half, before):
    n = half.shape[1]
    return list(
        call(
            functools.partial(finish_kernel, own),
            "finish",
            [(VMEM, half)] + [(HBM, a) for a in before],
            [(HBM, (m, CH, CH), F32) for m in (9, 3, 4)],
            [pltpu.VMEM((n, CH, CH // 2), F32), pltpu.SemaphoreType.DMA((n,))],
            alias={1 + i: i for i in range(len(before))},
        )
    )


def along(value, axis, by):
    count = lax.axis_size(axis)
    pairs = [(i, i + by) for i in range(count) if 0 <= i + by < count]
    return lax.ppermute(value, axis, pairs)


def around(value, axis, by):
    count = lax.axis_size(axis)
    return lax.ppermute(value, axis, [(i, (i + by) % count) for i in range(count)])


def from_bands(parts):
    if len(parts) == 1:
        got = lax.ppermute(parts[0], "grp", [(0, 1), (1, 0)])
        return got, got
    return along(parts[0], "grp", 1), along(parts[1], "grp", -1)


def body(tm, grp, frames_in, span_frames, w_spatial, w_temporal, w_down, cotangent):
    slots, rows, cols, ch = frames_in.shape
    wide = rows * cols
    x = frames_in.reshape(slots, wide, ch)
    ws = w_spatial.reshape(9, ch, ch)
    wd = w_down.reshape(4, ch, ch)
    wt = w_temporal
    count = (SMEM, span_frames)
    tap = 2 * slots * wide * ch * ch
    tile = (rows, cols, slots, ch)
    padded = (rows + 2, cols + 2, slots, ch)
    dma = pltpu.SemaphoreType.DMA

    sides = 1 if grp == 2 else 2
    edge = call(
        functools.partial(edges_kernel, grp),
        "edges",
        [count, (VMEM, x)],
        [(VMEM, (cols * slots, ch))] * sides,
        flops=tap // 8,
    )
    top, bot = from_bands(edge)
    last_shape = (2 * wide + 32, ch)
    at_shape = (3 * ch, (rows + 4) * 128)
    xt, acts, at, last_two = call(
        acts_kernel,
        "acts",
        [count, (VMEM, x), (ANY, edge[0])],
        [(VMEM, tile), (VMEM, padded), (VMEM, at_shape), (VMEM, last_shape)],
        flops=2 * tap,
    )
    (nxt,) = call(
        next_kernel,
        "next",
        [(VMEM, cotangent), (ANY, last_two)],
        [(VMEM, (2,) + cotangent.shape[1:])],
        moved=1024,
    )
    nxt_got = along(nxt, "tm", -1)
    acts, at, last_two = call(
        functools.partial(halo_kernel, grp),
        "halo",
        [count, (VMEM, top), (VMEM, bot), (VMEM, acts), (VMEM, at), (VMEM, last_two), (ANY, nxt),
         (VMEM, cotangent), (VMEM, wt), (VMEM, wd)],
        [(VMEM, padded), (VMEM, at_shape), (VMEM, last_shape)],
        alias={3: 0, 4: 1, 5: 2},
        moved=1024,
    )
    prev = around(last_two, "tm", 1)
    half = (16, 9, 16, ch // 2)
    cott, gy, gs, keep_a, send_a, *edge = call(
        functools.partial(grad_spatial_kernel, tm, grp),
        "grad_spatial",
        [count, (VMEM, at), (VMEM, cotangent), (VMEM, nxt_got), (VMEM, wt), (VMEM, wd)],
        [(VMEM, (rows // 2, cols // 2, slots, ch)), (VMEM, tile),
         (VMEM, (rows, cols + 2, slots, ch)), (VMEM, half), (VMEM, half)]
        + [(VMEM, (cols // 2 * slots, ch))] * sides,
        flops=14 * tap,
    )
    send_a = passed(send_a, [prev])
    got_a = core_round(send_a, tm, grp)
    cot_top, cot_bot = from_bands(edge)
    half_tile = (rows // 2, cols, slots, ch)
    acts, upper = call(
        upper_kernel,
        "spatial_upper",
        [(VMEM, acts), (VMEM, prev), (VMEM, ws), (ANY, send_a)],
        [(VMEM, padded), (VMEM, half_tile)],
        flops=5 * tap,
        alias={0: 0},
    )
    _, plane, line, others = plan(tm, grp)
    parts_a = plane_send(keep_a, got_a, [upper])
    (lower,) = call(
        lower_kernel,
        "spatial_lower",
        [(VMEM, acts), (VMEM, ws)] + [(ANY, a) for a in parts_a],
        [(VMEM, half_tile)],
        flops=4 * tap,
    )
    half = (16, 7, 16, ch // 2)
    down, keep_b, send_b = call(
        forward_kernel,
        "forward",
        [count, (VMEM, xt), (VMEM, upper), (VMEM, lower), (VMEM, cott), (VMEM, gy), (VMEM, wt), (VMEM, wd),
         *((ANY, a) for a in parts_a)],
        [(VMEM, (slots * wide // 4, ch)), (VMEM, half), (VMEM, half)],
        [pltpu.VMEM(v, BF) for v in (tile, (3 * ch, slots * wide), (4 * ch, slots * wide // 4))],
        moved=1024,
        grant=14,
    )
    parts_a = four_round(parts_a, plane, tm, grp)
    send_b = passed(send_b, parts_a[1:2])
    parts_b = plane_send(keep_b, core_round(send_b, tm, grp), [])
    parts_b = four_round(parts_b, plane, tm, grp)
    parts = call(
        line_send_kernel,
        "line_send",
        [(VMEM, a) for a in parts_a + parts_b] + [(ANY, a) for a in [cot_top, cot_bot][:sides]],
        [(VMEM, (16, 16, ch // 2))] * 4,
    )
    parts = four_round(list(parts), line, tm, grp)
    ins = [(VMEM, a) for a in parts]
    (mine,) = call(line_sum_kernel, "line_sum", ins, [(VMEM, parts[0].shape)])
    for bit in others:
        got = swap(mine, tm, grp, bit)
        (mine,) = call(add_kernel, "add", [(VMEM, mine), (VMEM, got)], [(VMEM, mine.shape)])
    parts = four_round([mine] * 4, line, tm, grp)
    (mine,) = call(
        line_gather_kernel, "line_gather", [(VMEM, a) for a in parts], [(VMEM, (4,) + mine.shape)]
    )
    parts = four_round([mine] * 4, plane, tm, grp)
    grad_x, down, token = call(
        functools.partial(grad_x_kernel, grp),
        "grad_x",
        [count, (VMEM, xt), (VMEM, gy), (VMEM, gs), (VMEM, cot_top), (VMEM, cot_bot), (VMEM, wt),
         (VMEM, wd), (VMEM, ws), (VMEM, down), (ANY, mine)],
        [(HBM, (slots, wide, ch)), (VMEM, cotangent.shape), TOKEN],
        [pltpu.VMEM(padded, BF), pltpu.VMEM((slots, wide, ch), BF), dma((1,))],
        flops=10 * tap,
    )
    ins = [(VMEM, a) for a in parts] + [(ANY, token)]
    (mine,) = call(plane_gather_kernel, "plane_gather", ins, [(VMEM, (16,) + mine.shape[1:])])
    got = core_round(mine, tm, grp)
    outs = finish(True, mine, [])
    sum_s, sum_t, sum_d = finish(False, got, outs)
    return (
        down,
        grad_x.reshape(frames_in.shape),
        sum_s.reshape(w_spatial.shape),
        sum_t,
        sum_d.reshape(w_down.shape),
    )


def solution(mesh):
    return jax.shard_map(
        functools.partial(body, mesh.shape["tm"], mesh.shape["grp"]),
        mesh=mesh,
        in_specs=(P("tm", "grp", None, None), P("tm"), P(), P(), P(), P("tm", "grp", None, None)),
        out_specs=(P("tm", "grp", None, None), P("tm", "grp", None, None), P(), P(), P()),
        check_vma=False,
    )
```

```python
import functools

import jax
import jax.numpy as jnp
from jax import lax
from jax.experimental import pallas as pl
from jax.experimental.pallas import tpu as pltpu
from jax.sharding import PartitionSpec as P

SLOTS = 16
OWN = 14
CH = 256
BF = jnp.bfloat16
F32 = jnp.float32


def mm(a, b):
    return lax.dot_general(a, b, (((1,), (0,)), ((), ())), preferred_element_type=F32)


def mm_nt(a, b):
    return lax.dot_general(a, b, (((1,), (1,)), ((), ())), preferred_element_type=F32)


def iotas(rows, cols):
    return (
        lax.broadcasted_iota(jnp.int32, (rows, cols), 0),
        lax.broadcasted_iota(jnp.int32, (rows, cols), 1),
    )


def to_slots(rows, frames, keep):
    a, b = iotas(rows * SLOTS, frames * rows)
    bits = rows.bit_length() - 1
    hit = ((a >> 4) == (b & (rows - 1))) & keep(b >> bits, a & 15)
    return jnp.where(hit, 1.0, 0.0).astype(BF)


def to_frames(rows):
    a, b = iotas(SLOTS * rows, rows * SLOTS)
    bits = rows.bit_length() - 1
    hit = ((a & (rows - 1)) == (b >> 4)) & ((a >> bits) == (b & 15))
    return jnp.where(hit, 1.0, 0.0).astype(BF)


def own_frames(count):
    return lambda frame, slot: (frame == slot) & (slot < count)


def own_and_next(count, blocks):
    after = jnp.where(lax.axis_index("tm") < blocks - 1, count, 64)
    return lambda frame, slot: ((frame < OWN) & (frame == slot) & (slot < count)) | (
        (frame >= OWN) & (slot == after + frame - OWN)
    )


def silu_norm(v):
    scaled = v * lax.rsqrt(jnp.mean(v * v, axis=-1, keepdims=True) + 1e-06)
    return scaled * (0.5 + 0.5 * jnp.tanh(0.5 * scaled))


def slot_mask(shape, count):
    return lax.broadcasted_iota(jnp.int32, shape, len(shape) - 2) < count


def grad_of_temporal(gy, wt_ref, count):
    n = gy.shape[0]
    flat = gy.reshape(n * SLOTS, CH)
    total = mm_nt(flat, wt_ref[2]).reshape(n, SLOTS, CH)
    for k in (1, 0):
        term = mm_nt(flat, wt_ref[k]).reshape(n, SLOTS, CH)
        total = total + pltpu.roll(term, SLOTS - (2 - k), 1)
    return jnp.where(slot_mask(total.shape, count), total, 0.0).astype(BF)


def place_bits():
    t, g = lax.axis_index("tm"), lax.axis_index("grp")
    return t & 1, ((t >> 1) & 1) + 2 * (g & 1), (t >> 2) & 3


def split_cores(value, keep_ref, send_ref, k):
    core, _, _ = place_bits()
    low, high = value[:, : CH // 2].astype(BF), value[:, CH // 2 :].astype(BF)
    keep_ref[:, k] = jnp.where(core == 0, low, high).reshape(16, 16, CH // 2)
    send_ref[:, k] = jnp.where(core == 0, high, low).reshape(16, 16, CH // 2)


def edges_kernel(bands, count_ref, x_ref, *outs):
    count = count_ref[0]
    band = lax.axis_index("grp")
    wide = x_ref.shape[1]
    if bands == 2:
        starts, lower = [jnp.where(band == 0, wide - 16, 0)], [band == 0]
    else:
        starts, lower = [wide - 16, 0], [True, False]
    place = to_slots(16, SLOTS, own_frames(count))
    for k, at in enumerate(starts):
        piece = x_ref[:, pl.ds(pl.multiple_of(at, 16), 16), :].reshape(SLOTS * 16, CH)
        v = mm(place, piece)
        v = jnp.where(lower[k], v[128:], v[:128])
        outs[k][...] = silu_norm(v).astype(BF)


def acts_kernel(count_ref, x_ref, _, xt_ref, acts_ref, at_ref, last_ref):
    count = count_ref[0]
    rows, cols = xt_ref.shape[0], xt_ref.shape[1]
    edge = jnp.zeros((rows + 2, SLOTS, CH), BF)
    acts_ref[:, 0] = edge
    acts_ref[:, cols + 1] = edge
    place = to_slots(16, SLOTS, own_frames(count))
    last = silu_norm(x_ref[pl.ds(count - 2, 2)].reshape(2 * rows * cols, CH).astype(F32))
    last_ref[0 : 2 * rows * cols] = last.astype(BF)

    def rows_of(q, _):
        at = pl.multiple_of(q * 16, 16)
        piece = x_ref[:, pl.ds(at, 16), :].reshape(SLOTS * 16, CH)
        v = mm(place, piece)
        xt_ref[pl.ds(2 * q, 2)] = v.astype(BF).reshape(2, cols, SLOTS, CH)
        a = silu_norm(v).astype(BF)
        acts_ref[pl.ds(2 * q + 1, 2), 1 : cols + 1] = a.reshape(2, cols, SLOTS, CH)
        flipped = a.T
        for i in range(3):
            at = pl.multiple_of((2 * q + 3 - i) * 128, 128)
            at_ref[i * CH : i * CH + CH, pl.ds(at, 256)] = flipped
        return 0

    lax.fori_loop(0, rows // 2, rows_of, 0, unroll=True)


def next_kernel(cot_ref, _, nxt_ref):
    nxt_ref[...] = cot_ref[0:2]


def halo_kernel(bands, count_ref, top_ref, bot_ref, *rest):
    acts_ref, at_ref, last_ref = rest[-3:]
    count = count_ref[0]
    band = lax.axis_index("grp")
    rows, cols = acts_ref.shape[0] - 2, acts_ref.shape[1] - 2
    halo = []
    for ref, flag, i, row in ((top_ref, band > 0, 0, 0), (bot_ref, band < bands - 1, 2, rows + 1)):
        a = jnp.where(flag, ref[...].astype(F32), 0.0).astype(BF)
        acts_ref[row, 1 : cols + 1] = a.reshape(cols, SLOTS, CH)
        at = (row - i + 2) * 128
        at_ref[i * CH : i * CH + CH, at : at + 128] = a.T
        halo.append(a)
    a, b = iotas(32, 256)
    pick = ((a & 15) == (b >> 4)) & ((b & 15) == count - 2 + (a >> 4))
    pick = jnp.where(pick, 1.0, 0.0).astype(BF)
    last_ref[2 * rows * cols :] = mm(pick, jnp.concatenate(halo, 0)).astype(BF)


def conv_rows(acts_ref, ws_ref, sp_ref, start):
    rows, cols = sp_ref.shape[0], sp_ref.shape[1]

    def rows_of(q, _):
        total = None
        for i in range(3):
            for j in range(3):
                left = acts_ref[pl.ds(start + 4 * q + i, 4), j : j + cols].reshape(
                    4 * cols * SLOTS, CH
                )
                term = mm(left, ws_ref[i * 3 + j])
                total = term if total is None else total + term
        sp_ref[pl.ds(4 * q, 4)] = total.astype(BF).reshape(4, cols, SLOTS, CH)
        return 0

    lax.fori_loop(0, rows // 4, rows_of, 0, unroll=True)


def upper_kernel(acts_in, prev_ref, ws_ref, _, acts_ref, sp_ref):
    rows, cols = acts_ref.shape[0] - 2, acts_ref.shape[1] - 2
    a, b = iotas(256, 32)
    place = ((a >> 4) == (b & 15)) & ((a & 15) == OWN + (b >> 4)) & (lax.axis_index("tm") > 0)
    place = jnp.where(place, 1.0, 0.0).astype(BF)
    size = rows * cols
    for q in range(rows // 2 + 1):
        if q == rows // 2:
            both, prev = slice(0, rows + 2, rows + 1), prev_ref[2 * size :]
        else:
            both = slice(2 * q + 1, 2 * q + 3)
            parts = [prev_ref[f * size + q * 16 : f * size + q * 16 + 16] for f in range(2)]
            prev = jnp.concatenate(parts, 0)
        prev = mm(place, prev).astype(BF).reshape(2, cols, SLOTS, CH)
        for k, row in enumerate(range(rows + 2)[both]):
            acts_ref[row, 1 : cols + 1] = acts_ref[row, 1 : cols + 1] + prev[k]

    conv_rows(acts_ref, ws_ref, sp_ref, 0)


def lower_kernel(acts_ref, ws_ref, *rest):
    sp_ref = rest[-1]
    conv_rows(acts_ref, ws_ref, sp_ref, sp_ref.shape[0])


def grad_spatial_kernel(
    blocks, bands, count_ref, at_ref, cot_ref, nxt_ref, wt_ref, wd_ref,
    cott_ref, gy_ref, gs_ref, keep_ref, send_ref, *edge_refs,
):
    count = count_ref[0]
    band = lax.axis_index("grp")
    rows, cols = gy_ref.shape[0], gy_ref.shape[1]
    edge = jnp.zeros((rows, SLOTS, CH), BF)
    gs_ref[:, 0] = edge
    gs_ref[:, cols + 1] = edge

    place_next = to_slots(16, SLOTS, own_and_next(count, blocks))
    halves = []
    for q in range(rows * cols // 64):
        four = slice(q * 4, q * 4 + 4)
        piece = jnp.concatenate(
            [cot_ref[0:OWN, four].reshape(OWN, 16, CH), nxt_ref[:, four].reshape(2, 16, CH)], 0
        ).reshape(SLOTS * 16, CH)
        halves.append(mm(place_next, piece).astype(BF))
    placed = jnp.concatenate(halves, 0)
    cott_ref[...] = placed.reshape(rows // 2, cols // 2, SLOTS, CH)
    for i in range(2):
        for j in range(2):
            g = mm_nt(placed, wd_ref[i * 2 + j]).astype(BF).reshape(rows // 2, cols // 2, SLOTS, CH)
            for r in range(rows // 2):
                for c in range(cols // 2):
                    gy_ref[2 * r + i, 2 * c + j] = g[r, c]
    last = cott_ref[rows // 2 - 1].reshape(cols // 2 * SLOTS, CH)
    first = cott_ref[0].reshape(cols // 2 * SLOTS, CH)
    if bands == 2:
        edge_refs[0][...] = jnp.where(band == 0, last, first)
    else:
        edge_refs[0][...] = last
        edge_refs[1][...] = first

    def grads_of(q, _):
        g = gy_ref[pl.ds(8 * q, 8)].reshape(8 * cols, SLOTS, CH)
        s = grad_of_temporal(g, wt_ref, count)
        gs_ref[pl.ds(8 * q, 8), 1 : cols + 1] = s.reshape(8, cols, SLOTS, CH)
        g = jnp.where(slot_mask(g.shape, count), g.astype(F32), 0.0)
        gy_ref[pl.ds(8 * q, 8)] = g.astype(BF).reshape(8, cols, SLOTS, CH)
        return 0

    lax.fori_loop(0, rows // 8, grads_of, 0)

    wide = rows * cols * SLOTS
    for j in range(3):
        right = gs_ref[:, 2 - j : 2 - j + cols].reshape(wide, CH)
        value = mm(at_ref[:, 256 : 256 + wide], right)
        for i in range(3):
            split_cores(value[i * CH : i * CH + CH], keep_ref, send_ref, i * 3 + j)


def forward_kernel(
    count_ref, xt_ref, upper_ref, lower_ref, cott_ref, gy_ref, wt_ref, wd_ref, *rest
):
    down_ref, keep_ref, send_ref, y_ref, st_ref, yt_ref = rest[-6:]
    count = count_ref[0]
    rows, cols = xt_ref.shape[0], xt_ref.shape[1]
    for q, sp_ref in enumerate((upper_ref, lower_ref)):
        s = sp_ref[...].reshape(8 * cols * SLOTS, CH).astype(F32)
        s = s.reshape(8 * cols, SLOTS, CH)
        total = None
        for k in range(3):
            shifted = s if k == 2 else pltpu.roll(s, 2 - k, 1)
            shifted = shifted.astype(BF).reshape(8 * cols * SLOTS, CH)
            at = slice(q * 1024, q * 1024 + 1024)
            st_ref[k * CH : k * CH + CH, at] = shifted.T
            term = mm(shifted, wt_ref[k])
            total = term if total is None else total + term
        x = xt_ref[8 * q : 8 * q + 8].reshape(8 * cols, SLOTS, CH).astype(F32)
        y = jnp.where(slot_mask(x.shape, count), x + total.reshape(x.shape), 0.0).astype(BF)
        y_ref[8 * q : 8 * q + 8] = y.reshape(8, cols, SLOTS, CH)

    wide = rows * cols * SLOTS
    value = mm(st_ref[...], gy_ref[...].reshape(wide, CH))
    for k in range(3):
        split_cores(value[k * CH : k * CH + CH], keep_ref, send_ref, k)

    small = wide // 4
    total = None
    for i in range(2):
        for j in range(2):
            tiles = [
                y_ref[2 * r + i, 2 * c + j] for r in range(rows // 2) for c in range(cols // 2)
            ]
            piece = jnp.concatenate(tiles, axis=0)
            k = i * 2 + j
            yt_ref[k * CH : k * CH + CH] = piece.T
            term = mm(piece, wd_ref[k])
            total = term if total is None else total + term
    down_ref[...] = total.astype(BF)
    value = mm(yt_ref[...], cott_ref[...].reshape(small, CH))
    for k in range(4):
        split_cores(value[k * CH : k * CH + CH], keep_ref, send_ref, 3 + k)


def grad_x_kernel(
    bands, count_ref, xt_ref, gy_ref, gs_ref, top_ref, bot_ref, wt_ref, wd_ref, ws_ref, slot_ref, *rest
):
    out_ref, down_ref, token_ref, pad_ref, buf, sems = rest[-6:]
    token_ref[...] = jnp.zeros_like(token_ref)
    count = count_ref[0]
    band = lax.axis_index("grp")
    rows, cols = xt_ref.shape[0], xt_ref.shape[1]
    pad_ref[1 : rows + 1] = gs_ref[...]
    edge = jnp.zeros((SLOTS, CH), BF)
    for ref, flag, i, row in ((top_ref, band > 0, 1, 0), (bot_ref, band < bands - 1, 0, rows + 1)):
        pair = [
            mm_nt(ref[...], wd_ref[i * 2 + j]).astype(BF).reshape(cols // 2, SLOTS, CH)
            for j in range(2)
        ]
        g = jnp.stack(pair, axis=1).reshape(cols, SLOTS, CH)
        pad_ref[row, 0] = edge
        pad_ref[row, 1 : cols + 1] = grad_of_temporal(g, wt_ref, jnp.where(flag, count, 0))
        pad_ref[row, cols + 1] = edge
    back = to_frames(16)

    def rows_of(q, _):
        total = None
        for i in range(3):
            for j in range(3):
                left = pad_ref[pl.ds(4 * q + 2 - i, 4), 2 - j : 2 - j + cols].reshape(
                    4 * cols * SLOTS, CH
                )
                term = mm_nt(left, ws_ref[i * 3 + j])
                total = term if total is None else total + term
        at = 4 * q
        v = xt_ref[pl.ds(at, 4)].reshape(4 * cols * SLOTS, CH).astype(F32)
        r = lax.rsqrt(jnp.mean(v * v, axis=-1, keepdims=True) + 1e-06)
        u = v * r
        s = 0.5 + 0.5 * jnp.tanh(0.5 * u)
        gu = total * (s * (1.0 + u * (1.0 - s)))
        dot = jnp.mean(gu * u, axis=-1, keepdims=True)
        gv = r * (gu - u * dot)
        gx = gy_ref[pl.ds(at, 4)].reshape(4 * cols * SLOTS, CH).astype(F32) + gv
        gx = gx.reshape(4 * cols, SLOTS, CH)
        gx = jnp.where(slot_mask(gx.shape, count), gx, 0.0).astype(BF).reshape(4 * cols * SLOTS, CH)
        for k in range(2):
            o = mm(back, gx[k * 256 : k * 256 + 256]).astype(BF)
            buf[:, pl.ds(pl.multiple_of((2 * q + k) * 16, 16), 16), :] = o.reshape(SLOTS, 16, CH)
        return 0

    lax.fori_loop(0, rows // 4, rows_of, 0)
    copy = pltpu.make_async_copy(buf, out_ref, sems.at[0])
    copy.start()
    for q in range(down_ref.shape[1] // 4):
        o = mm(back, slot_ref[q * 256 : q * 256 + 256]).astype(BF)
        down_ref[:, q * 4 : q * 4 + 4] = o.reshape(SLOTS, 4, cols // 2, CH)
    copy.wait()


ORDER = (0, 3, 2, 1)


def plane_send_kernel(keep_ref, got_ref, *rest):
    _, p, _ = place_bits()
    for r, out in zip(ORDER, rest[-4:]):
        at = pl.ds((p ^ r) * 4, 4)
        out[...] = (keep_ref[at].astype(F32) + got_ref[at].astype(F32)).astype(BF)


def line_send_kernel(*refs):
    outs = refs[8:]
    _, _, z = place_bits()
    for out, r in zip(outs, ORDER):
        at = 0
        for chain in (refs[:4], refs[4:8]):
            parts = [ref[z ^ r].astype(F32) for ref in chain]
            n = parts[0].shape[0]
            out[at : at + n] = (parts[0] + parts[1] + parts[2] + parts[3]).astype(BF)
            at += n


def line_sum_kernel(a_ref, b_ref, c_ref, d_ref, *rest):
    out_ref = rest[-1]
    parts = [ref[...].astype(F32) for ref in (a_ref, b_ref, c_ref, d_ref)]
    out_ref[...] = (parts[0] + parts[1] + parts[2] + parts[3]).astype(BF)


def line_gather_kernel(a_ref, b_ref, c_ref, d_ref, out_ref):
    _, _, z = place_bits()
    for r, ref in zip(ORDER, (a_ref, b_ref, c_ref, d_ref)):
        out_ref[z ^ r] = ref[...]


def plane_gather_kernel(a_ref, b_ref, c_ref, d_ref, _, out_ref):
    _, p, _ = place_bits()
    for r, ref in zip(ORDER, (a_ref, b_ref, c_ref, d_ref)):
        out_ref[pl.ds((p ^ r) * 4, 4)] = ref[...]


def add_kernel(a_ref, b_ref, out_ref):
    out_ref[...] = (a_ref[...].astype(F32) + b_ref[...].astype(F32)).astype(BF)


def pass_kernel(*_):
    pass


def finish_kernel(own, half_ref, *rest):
    buf, sems = rest[-2:]
    outs = rest[-5:-2]
    core, _, _ = place_bits()
    at = pl.multiple_of((core if own else 1 - core) * (CH // 2), CH // 2)
    copies = []
    k = 0
    for out in outs:
        for m in range(out.shape[0]):
            buf[k] = half_ref[:, k].reshape(CH, CH // 2).astype(F32)
            copies.append(
                pltpu.make_async_copy(buf.at[k], out.at[m, :, pl.ds(at, CH // 2)], sems.at[k])
            )
            copies[-1].start()
            k += 1
    for copy in copies:
        copy.wait()


VMEM = pl.BlockSpec(memory_space=pltpu.VMEM)
SMEM = pl.BlockSpec(memory_space=pltpu.SMEM)
ANY = pl.BlockSpec(memory_space=pl.ANY)
HBM = pl.BlockSpec(memory_space=pltpu.HBM)
TOKEN = (VMEM, (8, 128), F32)


def call(kernel, name, ins, outs, scratch=(), flops=0, alias=None, grant=10, moved=None):
    shapes = [jax.ShapeDtypeStruct(o[1], o[2] if len(o) > 2 else BF) for o in outs]
    if moved is None:
        moved = sum(a.size * a.dtype.itemsize for s, a in ins if s is not ANY)
        moved += sum(s.size * s.dtype.itemsize for s in shapes)
    return pl.pallas_call(
        kernel,
        out_shape=shapes,
        in_specs=[s for s, _ in ins],
        out_specs=[o[0] for o in outs],
        scratch_shapes=list(scratch),
        compiler_params=pltpu.CompilerParams(vmem_limit_bytes=grant * 2**20),
        cost_estimate=pl.CostEstimate(flops=flops, bytes_accessed=moved, transcendentals=0),
        input_output_aliases=alias or {},
        name=name,
    )(*[a for _, a in ins])


AXES = ("tm", "grp")


def plan(tm, grp):
    low, total = grp.bit_length() - 1, (tm * grp).bit_length() - 1
    plane, line = [low + 1, 0], [low + 2, low + 3]
    return low, plane, line, [b for b in range(total) if b not in [low] + plane + line]


def swap(value, tm, grp, *bits):
    flip = sum(1 << b for b in bits)
    return lax.ppermute(value, AXES, [(d, d ^ flip) for d in range(tm * grp)])


def core_round(value, tm, grp):
    return swap(value, tm, grp, plan(tm, grp)[0])


def four_round(parts, bits, tm, grp):
    return [
        parts[0],
        swap(parts[1], tm, grp, *bits),
        swap(parts[2], tm, grp, bits[1]),
        swap(parts[3], tm, grp, bits[0]),
    ]


def plane_send(keep, got, after):
    ins = [(VMEM, keep), (VMEM, got)] + [(ANY, a) for a in after]
    shape = (4, keep.shape[1], 16, CH // 2)
    return list(call(plane_send_kernel, "plane_send", ins, [(VMEM, shape)] * 4))


def passed(value, after):
    ins = [(ANY, value)] + [(ANY, a) for a in after]
    return call(pass_kernel, "pass", ins, [(ANY, value.shape)], alias={0: 0})[0]


def finish(own, half, before):
    n = half.shape[1]
    return list(
        call(
            functools.partial(finish_kernel, own),
            "finish",
            [(VMEM, half)] + [(HBM, a) for a in before],
            [(HBM, (m, CH, CH), F32) for m in (9, 3, 4)],
            [pltpu.VMEM((n, CH, CH // 2), F32), pltpu.SemaphoreType.DMA((n,))],
            alias={1 + i: i for i in range(len(before))},
        )
    )


def along(value, axis, by):
    count = lax.axis_size(axis)
    pairs = [(i, i + by) for i in range(count) if 0 <= i + by < count]
    return lax.ppermute(value, axis, pairs)


def around(value, axis, by):
    count = lax.axis_size(axis)
    return lax.ppermute(value, axis, [(i, (i + by) % count) for i in range(count)])


def from_bands(parts):
    if len(parts) == 1:
        got = lax.ppermute(parts[0], "grp", [(0, 1), (1, 0)])
        return got, got
    return along(parts[0], "grp", 1), along(parts[1], "grp", -1)


def body(tm, grp, frames_in, span_frames, w_spatial, w_temporal, w_down, cotangent):
    slots, rows, cols, ch = frames_in.shape
    wide = rows * cols
    x = frames_in.reshape(slots, wide, ch)
    ws = w_spatial.reshape(9, ch, ch)
    wd = w_down.reshape(4, ch, ch)
    wt = w_temporal
    count = (SMEM, span_frames)
    tap = 2 * slots * wide * ch * ch
    tile = (rows, cols, slots, ch)
    padded = (rows + 2, cols + 2, slots, ch)
    dma = pltpu.SemaphoreType.DMA

    sides = 1 if grp == 2 else 2
    edge = call(
        functools.partial(edges_kernel, grp),
        "edges",
        [count, (VMEM, x)],
        [(VMEM, (cols * slots, ch))] * sides,
        flops=tap // 8,
    )
    top, bot = from_bands(edge)
    last_shape = (2 * wide + 32, ch)
    at_shape = (3 * ch, (rows + 4) * 128)
    xt, acts, at, last_two = call(
        acts_kernel,
        "acts",
        [count, (VMEM, x), (ANY, edge[0])],
        [(VMEM, tile), (VMEM, padded), (VMEM, at_shape), (VMEM, last_shape)],
        flops=2 * tap,
    )
    (nxt,) = call(
        next_kernel,
        "next",
        [(VMEM, cotangent), (ANY, last_two)],
        [(VMEM, (2,) + cotangent.shape[1:])],
        moved=1024,
    )
    nxt_got = along(nxt, "tm", -1)
    acts, at, last_two = call(
        functools.partial(halo_kernel, grp),
        "halo",
        [count, (VMEM, top), (VMEM, bot), (VMEM, acts), (VMEM, at), (VMEM, last_two), (ANY, nxt),
         (VMEM, cotangent), (VMEM, wt), (VMEM, wd)],
        [(VMEM, padded), (VMEM, at_shape), (VMEM, last_shape)],
        alias={3: 0, 4: 1, 5: 2},
        moved=1024,
    )
    prev = around(last_two, "tm", 1)
    half = (16, 9, 16, ch // 2)
    cott, gy, gs, keep_a, send_a, *edge = call(
        functools.partial(grad_spatial_kernel, tm, grp),
        "grad_spatial",
        [count, (VMEM, at), (VMEM, cotangent), (VMEM, nxt_got), (VMEM, wt), (VMEM, wd)],
        [(VMEM, (rows // 2, cols // 2, slots, ch)), (VMEM, tile),
         (VMEM, (rows, cols + 2, slots, ch)), (VMEM, half), (VMEM, half)]
        + [(VMEM, (cols // 2 * slots, ch))] * sides,
        flops=14 * tap,
    )
    send_a = passed(send_a, [prev])
    got_a = core_round(send_a, tm, grp)
    half_tile = (rows // 2, cols, slots, ch)
    acts, upper = call(
        upper_kernel,
        "spatial_upper",
        [(VMEM, acts), (VMEM, prev), (VMEM, ws), (ANY, send_a)],
        [(VMEM, padded), (VMEM, half_tile)],
        flops=5 * tap,
        alias={0: 0},
    )
    _, plane, line, others = plan(tm, grp)
    parts_a = plane_send(keep_a, got_a, [upper])
    cot_top, cot_bot = from_bands([passed(e, [parts_a[1]]) for e in edge])
    (lower,) = call(
        lower_kernel,
        "spatial_lower",
        [(VMEM, acts), (VMEM, ws)] + [(ANY, a) for a in parts_a],
        [(VMEM, half_tile)],
        flops=4 * tap,
    )
    half = (16, 7, 16, ch // 2)
    down, keep_b, send_b = call(
        forward_kernel,
        "forward",
        [count, (VMEM, xt), (VMEM, upper), (VMEM, lower), (VMEM, cott), (VMEM, gy), (VMEM, wt), (VMEM, wd),
         *((ANY, a) for a in parts_a)],
        [(VMEM, (slots * wide // 4, ch)), (VMEM, half), (VMEM, half)],
        [pltpu.VMEM(v, BF) for v in (tile, (3 * ch, slots * wide), (4 * ch, slots * wide // 4))],
        moved=1024,
        grant=14,
    )
    parts_a = four_round(parts_a, plane, tm, grp)
    send_b = passed(send_b, parts_a[1:2] + [cot_top, cot_bot][:sides])
    parts_b = plane_send(keep_b, core_round(send_b, tm, grp), [])
    parts_b = four_round(parts_b, plane, tm, grp)
    parts = call(
        line_send_kernel,
        "line_send",
        [(VMEM, a) for a in parts_a + parts_b],
        [(VMEM, (16, 16, ch // 2))] * 4,
    )
    parts = four_round(list(parts), line, tm, grp)
    ins = [(VMEM, a) for a in parts]
    (mine,) = call(line_sum_kernel, "line_sum", ins, [(VMEM, parts[0].shape)])
    for bit in others:
        got = swap(mine, tm, grp, bit)
        (mine,) = call(add_kernel, "add", [(VMEM, mine), (VMEM, got)], [(VMEM, mine.shape)])
    parts = four_round([mine] * 4, line, tm, grp)
    (mine,) = call(
        line_gather_kernel, "line_gather", [(VMEM, a) for a in parts], [(VMEM, (4,) + mine.shape)]
    )
    parts = four_round([mine] * 4, plane, tm, grp)
    grad_x, down, token = call(
        functools.partial(grad_x_kernel, grp),
        "grad_x",
        [count, (VMEM, xt), (VMEM, gy), (VMEM, gs), (VMEM, cot_top), (VMEM, cot_bot), (VMEM, wt),
         (VMEM, wd), (VMEM, ws), (VMEM, down), (ANY, mine)],
        [(HBM, (slots, wide, ch)), (VMEM, cotangent.shape), TOKEN],
        [pltpu.VMEM(padded, BF), pltpu.VMEM((slots, wide, ch), BF), dma((1,))],
        flops=10 * tap,
    )
    ins = [(VMEM, a) for a in parts] + [(ANY, token)]
    (mine,) = call(plane_gather_kernel, "plane_gather", ins, [(VMEM, (16,) + mine.shape[1:])])
    got = core_round(mine, tm, grp)
    outs = finish(True, mine, [])
    sum_s, sum_t, sum_d = finish(False, got, outs)
    return (
        down,
        grad_x.reshape(frames_in.shape),
        sum_s.reshape(w_spatial.shape),
        sum_t,
        sum_d.reshape(w_down.shape),
    )


def solution(mesh):
    return jax.shard_map(
        functools.partial(body, mesh.shape["tm"], mesh.shape["grp"]),
        mesh=mesh,
        in_specs=(P("tm", "grp", None, None), P("tm"), P(), P(), P(), P("tm", "grp", None, None)),
        out_specs=(P("tm", "grp", None, None), P("tm", "grp", None, None), P(), P(), P()),
        check_vma=False,
    )
```

```python
import functools

import jax
import jax.numpy as jnp
from jax import lax
from jax.experimental import pallas as pl
from jax.experimental.pallas import tpu as pltpu
from jax.sharding import PartitionSpec as P

SLOTS = 16
OWN = 14
CH = 256
BF = jnp.bfloat16
F32 = jnp.float32


def mm(a, b):
    return lax.dot_general(a, b, (((1,), (0,)), ((), ())), preferred_element_type=F32)


def mm_nt(a, b):
    return lax.dot_general(a, b, (((1,), (1,)), ((), ())), preferred_element_type=F32)


def iotas(rows, cols):
    return (
        lax.broadcasted_iota(jnp.int32, (rows, cols), 0),
        lax.broadcasted_iota(jnp.int32, (rows, cols), 1),
    )


def to_slots(rows, frames, keep):
    a, b = iotas(rows * SLOTS, frames * rows)
    bits = rows.bit_length() - 1
    hit = ((a >> 4) == (b & (rows - 1))) & keep(b >> bits, a & 15)
    return jnp.where(hit, 1.0, 0.0).astype(BF)


def to_frames(rows):
    a, b = iotas(SLOTS * rows, rows * SLOTS)
    bits = rows.bit_length() - 1
    hit = ((a & (rows - 1)) == (b >> 4)) & ((a >> bits) == (b & 15))
    return jnp.where(hit, 1.0, 0.0).astype(BF)


def own_frames(count):
    return lambda frame, slot: (frame == slot) & (slot < count)


def own_and_next(count, blocks):
    after = jnp.where(lax.axis_index("tm") < blocks - 1, count, 64)
    return lambda frame, slot: ((frame < OWN) & (frame == slot) & (slot < count)) | (
        (frame >= OWN) & (slot == after + frame - OWN)
    )


def silu_norm(v):
    scaled = v * lax.rsqrt(jnp.mean(v * v, axis=-1, keepdims=True) + 1e-06)
    return scaled * (0.5 + 0.5 * jnp.tanh(0.5 * scaled))


def slot_mask(shape, count):
    return lax.broadcasted_iota(jnp.int32, shape, len(shape) - 2) < count


def grad_of_temporal(gy, wt_ref, count):
    n = gy.shape[0]
    terms = mm_nt(gy.reshape(n * SLOTS, CH), wt_ref[...].reshape(3 * CH, CH))
    total = terms[:, 2 * CH :].reshape(n, SLOTS, CH)
    for k in (1, 0):
        term = terms[:, k * CH : k * CH + CH].reshape(n, SLOTS, CH)
        total = total + pltpu.roll(term, SLOTS - (2 - k), 1)
    return jnp.where(slot_mask(total.shape, count), total, 0.0).astype(BF)


def place_bits():
    t, g = lax.axis_index("tm"), lax.axis_index("grp")
    return t & 1, ((t >> 1) & 1) + 2 * (g & 1), (t >> 2) & 3


def split_cores(value, keep_ref, send_ref, k):
    core, _, _ = place_bits()
    low, high = value[:, : CH // 2].astype(BF), value[:, CH // 2 :].astype(BF)
    keep_ref[:, k] = jnp.where(core == 0, low, high).reshape(16, 16, CH // 2)
    send_ref[:, k] = jnp.where(core == 0, high, low).reshape(16, 16, CH // 2)


def edges_kernel(bands, count_ref, x_ref, *outs):
    count = count_ref[0]
    band = lax.axis_index("grp")
    wide = x_ref.shape[1]
    if bands == 2:
        starts, lower = [jnp.where(band == 0, wide - 16, 0)], [band == 0]
    else:
        starts, lower = [wide - 16, 0], [True, False]
    place = to_slots(16, SLOTS, own_frames(count))
    for k, at in enumerate(starts):
        piece = x_ref[:, pl.ds(pl.multiple_of(at, 16), 16), :].reshape(SLOTS * 16, CH)
        v = mm(place, piece)
        v = jnp.where(lower[k], v[128:], v[:128])
        outs[k][...] = silu_norm(v).astype(BF)


def acts_kernel(count_ref, x_ref, _, xt_ref, acts_ref, at_ref, last_ref):
    count = count_ref[0]
    rows, cols = xt_ref.shape[0], xt_ref.shape[1]
    edge = jnp.zeros((rows + 2, SLOTS, CH), BF)
    acts_ref[:, 0] = edge
    acts_ref[:, cols + 1] = edge
    place = to_slots(16, SLOTS, own_frames(count))
    last = silu_norm(x_ref[pl.ds(count - 2, 2)].reshape(2 * rows * cols, CH).astype(F32))
    last_ref[0 : 2 * rows * cols] = last.astype(BF)

    def rows_of(q, _):
        at = pl.multiple_of(q * 16, 16)
        piece = x_ref[:, pl.ds(at, 16), :].reshape(SLOTS * 16, CH)
        v = mm(place, piece)
        xt_ref[pl.ds(2 * q, 2)] = v.astype(BF).reshape(2, cols, SLOTS, CH)
        a = silu_norm(v).astype(BF)
        acts_ref[pl.ds(2 * q + 1, 2), 1 : cols + 1] = a.reshape(2, cols, SLOTS, CH)
        flipped = a.T
        for i in range(3):
            at = pl.multiple_of((2 * q + 3 - i) * 128, 128)
            at_ref[i * CH : i * CH + CH, pl.ds(at, 256)] = flipped
        return 0

    lax.fori_loop(0, rows // 2, rows_of, 0, unroll=True)


def next_kernel(cot_ref, _, nxt_ref):
    nxt_ref[...] = cot_ref[0:2]


def halo_kernel(bands, count_ref, top_ref, bot_ref, *rest):
    acts_ref, at_ref, last_ref = rest[-3:]
    count = count_ref[0]
    band = lax.axis_index("grp")
    rows, cols = acts_ref.shape[0] - 2, acts_ref.shape[1] - 2
    halo = []
    for ref, flag, i, row in ((top_ref, band > 0, 0, 0), (bot_ref, band < bands - 1, 2, rows + 1)):
        a = jnp.where(flag, ref[...].astype(F32), 0.0).astype(BF)
        acts_ref[row, 1 : cols + 1] = a.reshape(cols, SLOTS, CH)
        at = (row - i + 2) * 128
        at_ref[i * CH : i * CH + CH, at : at + 128] = a.T
        halo.append(a)
    a, b = iotas(32, 256)
    pick = ((a & 15) == (b >> 4)) & ((b & 15) == count - 2 + (a >> 4))
    pick = jnp.where(pick, 1.0, 0.0).astype(BF)
    last_ref[2 * rows * cols :] = mm(pick, jnp.concatenate(halo, 0)).astype(BF)


def conv_rows(acts_ref, ws_ref, sp_ref, start):
    rows, cols = sp_ref.shape[0], sp_ref.shape[1]

    def rows_of(q, _):
        total = None
        for i in range(3):
            for j in range(3):
                left = acts_ref[pl.ds(start + 4 * q + i, 4), j : j + cols].reshape(
                    4 * cols * SLOTS, CH
                )
                term = mm(left, ws_ref[i * 3 + j])
                total = term if total is None else total + term
        sp_ref[pl.ds(4 * q, 4)] = total.astype(BF).reshape(4, cols, SLOTS, CH)
        return 0

    lax.fori_loop(0, rows // 4, rows_of, 0, unroll=True)


def upper_kernel(acts_in, prev_ref, ws_ref, _, acts_ref, sp_ref):
    rows, cols = acts_ref.shape[0] - 2, acts_ref.shape[1] - 2
    a, b = iotas(256, 32)
    place = ((a >> 4) == (b & 15)) & ((a & 15) == OWN + (b >> 4)) & (lax.axis_index("tm") > 0)
    place = jnp.where(place, 1.0, 0.0).astype(BF)
    size = rows * cols
    for q in range(rows // 2 + 1):
        if q == rows // 2:
            both, prev = slice(0, rows + 2, rows + 1), prev_ref[2 * size :]
        else:
            both = slice(2 * q + 1, 2 * q + 3)
            parts = [prev_ref[f * size + q * 16 : f * size + q * 16 + 16] for f in range(2)]
            prev = jnp.concatenate(parts, 0)
        prev = mm(place, prev).astype(BF).reshape(2, cols, SLOTS, CH)
        for k, row in enumerate(range(rows + 2)[both]):
            acts_ref[row, 1 : cols + 1] = acts_ref[row, 1 : cols + 1] + prev[k]

    conv_rows(acts_ref, ws_ref, sp_ref, 0)


def lower_kernel(acts_ref, ws_ref, *rest):
    sp_ref = rest[-1]
    conv_rows(acts_ref, ws_ref, sp_ref, sp_ref.shape[0])


def grad_spatial_kernel(
    blocks, bands, count_ref, at_ref, cot_ref, nxt_ref, wt_ref, wd_ref,
    cott_ref, gy_ref, gs_ref, keep_ref, send_ref, *edge_refs,
):
    count = count_ref[0]
    band = lax.axis_index("grp")
    rows, cols = gy_ref.shape[0], gy_ref.shape[1]
    edge = jnp.zeros((rows, SLOTS, CH), BF)
    gs_ref[:, 0] = edge
    gs_ref[:, cols + 1] = edge

    place_next = to_slots(16, SLOTS, own_and_next(count, blocks))
    halves = []
    for q in range(rows * cols // 64):
        four = slice(q * 4, q * 4 + 4)
        piece = jnp.concatenate(
            [cot_ref[0:OWN, four].reshape(OWN, 16, CH), nxt_ref[:, four].reshape(2, 16, CH)], 0
        ).reshape(SLOTS * 16, CH)
        halves.append(mm(place_next, piece).astype(BF))
    placed = jnp.concatenate(halves, 0)
    cott_ref[...] = placed.reshape(rows // 2, cols // 2, SLOTS, CH)
    for i in range(2):
        for j in range(2):
            g = mm_nt(placed, wd_ref[i * 2 + j]).astype(BF).reshape(rows // 2, cols // 2, SLOTS, CH)
            for r in range(rows // 2):
                for c in range(cols // 2):
                    gy_ref[2 * r + i, 2 * c + j] = g[r, c]
    last = cott_ref[rows // 2 - 1].reshape(cols // 2 * SLOTS, CH)
    first = cott_ref[0].reshape(cols // 2 * SLOTS, CH)
    if bands == 2:
        edge_refs[0][...] = jnp.where(band == 0, last, first)
    else:
        edge_refs[0][...] = last
        edge_refs[1][...] = first

    def grads_of(q, _):
        g = gy_ref[pl.ds(4 * q, 4)].reshape(4 * cols, SLOTS, CH)
        s = grad_of_temporal(g, wt_ref, count)
        gs_ref[pl.ds(4 * q, 4), 1 : cols + 1] = s.reshape(4, cols, SLOTS, CH)
        g = jnp.where(slot_mask(g.shape, count), g.astype(F32), 0.0)
        gy_ref[pl.ds(4 * q, 4)] = g.astype(BF).reshape(4, cols, SLOTS, CH)
        return 0

    lax.fori_loop(0, rows // 4, grads_of, 0, unroll=True)

    wide = rows * cols * SLOTS
    for j in range(3):
        right = gs_ref[:, 2 - j : 2 - j + cols].reshape(wide, CH)
        value = mm(at_ref[:, 256 : 256 + wide], right)
        for i in range(3):
            split_cores(value[i * CH : i * CH + CH], keep_ref, send_ref, i * 3 + j)


def forward_kernel(
    count_ref, xt_ref, upper_ref, lower_ref, cott_ref, gy_ref, wt_ref, wd_ref, *rest
):
    down_ref, keep_ref, send_ref, y_ref, st_ref, yt_ref = rest[-6:]
    count = count_ref[0]
    rows, cols = xt_ref.shape[0], xt_ref.shape[1]
    for q, sp_ref in enumerate((upper_ref, lower_ref)):
        s = sp_ref[...].reshape(8 * cols * SLOTS, CH).astype(F32)
        s = s.reshape(8 * cols, SLOTS, CH)
        total = None
        for k in range(3):
            shifted = s if k == 2 else pltpu.roll(s, 2 - k, 1)
            shifted = shifted.astype(BF).reshape(8 * cols * SLOTS, CH)
            at = slice(q * 1024, q * 1024 + 1024)
            st_ref[k * CH : k * CH + CH, at] = shifted.T
            term = mm(shifted, wt_ref[k])
            total = term if total is None else total + term
        x = xt_ref[8 * q : 8 * q + 8].reshape(8 * cols, SLOTS, CH).astype(F32)
        y = jnp.where(slot_mask(x.shape, count), x + total.reshape(x.shape), 0.0).astype(BF)
        y_ref[8 * q : 8 * q + 8] = y.reshape(8, cols, SLOTS, CH)

    wide = rows * cols * SLOTS
    value = mm(st_ref[...], gy_ref[...].reshape(wide, CH))
    for k in range(3):
        split_cores(value[k * CH : k * CH + CH], keep_ref, send_ref, k)

    small = wide // 4
    total = None
    for i in range(2):
        for j in range(2):
            tiles = [
                y_ref[2 * r + i, 2 * c + j] for r in range(rows // 2) for c in range(cols // 2)
            ]
            piece = jnp.concatenate(tiles, axis=0)
            k = i * 2 + j
            yt_ref[k * CH : k * CH + CH] = piece.T
            term = mm(piece, wd_ref[k])
            total = term if total is None else total + term
    down_ref[...] = total.astype(BF)
    value = mm(yt_ref[...], cott_ref[...].reshape(small, CH))
    for k in range(4):
        split_cores(value[k * CH : k * CH + CH], keep_ref, send_ref, 3 + k)


def grad_x_kernel(
    bands, count_ref, xt_ref, gy_ref, gs_ref, top_ref, bot_ref, wt_ref, wd_ref, ws_ref, slot_ref, *rest
):
    out_ref, down_ref, token_ref, pad_ref, buf, sems = rest[-6:]
    token_ref[...] = jnp.zeros_like(token_ref)
    count = count_ref[0]
    band = lax.axis_index("grp")
    rows, cols = xt_ref.shape[0], xt_ref.shape[1]
    pad_ref[1 : rows + 1] = gs_ref[...]
    edge = jnp.zeros((SLOTS, CH), BF)
    for ref, flag, i, row in ((top_ref, band > 0, 1, 0), (bot_ref, band < bands - 1, 0, rows + 1)):
        pair = [
            mm_nt(ref[...], wd_ref[i * 2 + j]).astype(BF).reshape(cols // 2, SLOTS, CH)
            for j in range(2)
        ]
        g = jnp.stack(pair, axis=1).reshape(cols, SLOTS, CH)
        pad_ref[row, 0] = edge
        pad_ref[row, 1 : cols + 1] = grad_of_temporal(g, wt_ref, jnp.where(flag, count, 0))
        pad_ref[row, cols + 1] = edge
    back = to_frames(16)

    def rows_of(q, _):
        total = None
        for i in range(3):
            for j in range(3):
                left = pad_ref[pl.ds(4 * q + 2 - i, 4), 2 - j : 2 - j + cols].reshape(
                    4 * cols * SLOTS, CH
                )
                term = mm_nt(left, ws_ref[i * 3 + j])
                total = term if total is None else total + term
        at = 4 * q
        v = xt_ref[pl.ds(at, 4)].reshape(4 * cols * SLOTS, CH).astype(F32)
        r = lax.rsqrt(jnp.mean(v * v, axis=-1, keepdims=True) + 1e-06)
        u = v * r
        s = 0.5 + 0.5 * jnp.tanh(0.5 * u)
        gu = total * (s * (1.0 + u * (1.0 - s)))
        dot = jnp.mean(gu * u, axis=-1, keepdims=True)
        gv = r * (gu - u * dot)
        gx = gy_ref[pl.ds(at, 4)].reshape(4 * cols * SLOTS, CH).astype(F32) + gv
        gx = gx.reshape(4 * cols, SLOTS, CH)
        gx = jnp.where(slot_mask(gx.shape, count), gx, 0.0).astype(BF).reshape(4 * cols * SLOTS, CH)
        for k in range(2):
            o = mm(back, gx[k * 256 : k * 256 + 256]).astype(BF)
            buf[:, pl.ds(pl.multiple_of((2 * q + k) * 16, 16), 16), :] = o.reshape(SLOTS, 16, CH)
        return 0

    lax.fori_loop(0, rows // 4, rows_of, 0)
    copy = pltpu.make_async_copy(buf, out_ref, sems.at[0])
    copy.start()
    for q in range(down_ref.shape[1] // 4):
        o = mm(back, slot_ref[q * 256 : q * 256 + 256]).astype(BF)
        down_ref[:, q * 4 : q * 4 + 4] = o.reshape(SLOTS, 4, cols // 2, CH)
    copy.wait()


ORDER = (0, 3, 2, 1)


def plane_send_kernel(keep_ref, got_ref, *rest):
    _, p, _ = place_bits()
    for r, out in zip(ORDER, rest[-4:]):
        at = pl.ds((p ^ r) * 4, 4)
        out[...] = (keep_ref[at].astype(F32) + got_ref[at].astype(F32)).astype(BF)


def line_send_kernel(*refs):
    outs = refs[8:]
    _, _, z = place_bits()
    for out, r in zip(outs, ORDER):
        at = 0
        for chain in (refs[:4], refs[4:8]):
            parts = [ref[z ^ r].astype(F32) for ref in chain]
            n = parts[0].shape[0]
            out[at : at + n] = (parts[0] + parts[1] + parts[2] + parts[3]).astype(BF)
            at += n


def line_sum_kernel(a_ref, b_ref, c_ref, d_ref, *rest):
    out_ref = rest[-1]
    parts = [ref[...].astype(F32) for ref in (a_ref, b_ref, c_ref, d_ref)]
    out_ref[...] = (parts[0] + parts[1] + parts[2] + parts[3]).astype(BF)


def line_gather_kernel(a_ref, b_ref, c_ref, d_ref, out_ref):
    _, _, z = place_bits()
    for r, ref in zip(ORDER, (a_ref, b_ref, c_ref, d_ref)):
        out_ref[z ^ r] = ref[...]


def plane_gather_kernel(a_ref, b_ref, c_ref, d_ref, _, out_ref):
    _, p, _ = place_bits()
    for r, ref in zip(ORDER, (a_ref, b_ref, c_ref, d_ref)):
        out_ref[pl.ds((p ^ r) * 4, 4)] = ref[...]


def add_kernel(a_ref, b_ref, out_ref):
    out_ref[...] = (a_ref[...].astype(F32) + b_ref[...].astype(F32)).astype(BF)


def pass_kernel(*_):
    pass


def finish_kernel(own, half_ref, *rest):
    buf, sems = rest[-2:]
    outs = rest[-5:-2]
    core, _, _ = place_bits()
    at = pl.multiple_of((core if own else 1 - core) * (CH // 2), CH // 2)
    copies = []
    k = 0
    for out in outs:
        for m in range(out.shape[0]):
            buf[k] = half_ref[:, k].reshape(CH, CH // 2).astype(F32)
            copies.append(
                pltpu.make_async_copy(buf.at[k], out.at[m, :, pl.ds(at, CH // 2)], sems.at[k])
            )
            copies[-1].start()
            k += 1
    for copy in copies:
        copy.wait()


VMEM = pl.BlockSpec(memory_space=pltpu.VMEM)
SMEM = pl.BlockSpec(memory_space=pltpu.SMEM)
ANY = pl.BlockSpec(memory_space=pl.ANY)
HBM = pl.BlockSpec(memory_space=pltpu.HBM)
TOKEN = (VMEM, (8, 128), F32)


def call(kernel, name, ins, outs, scratch=(), flops=0, alias=None, grant=10, moved=None):
    shapes = [jax.ShapeDtypeStruct(o[1], o[2] if len(o) > 2 else BF) for o in outs]
    if moved is None:
        moved = sum(a.size * a.dtype.itemsize for s, a in ins if s is not ANY)
        moved += sum(s.size * s.dtype.itemsize for s in shapes)
    return pl.pallas_call(
        kernel,
        out_shape=shapes,
        in_specs=[s for s, _ in ins],
        out_specs=[o[0] for o in outs],
        scratch_shapes=list(scratch),
        compiler_params=pltpu.CompilerParams(vmem_limit_bytes=grant * 2**20),
        cost_estimate=pl.CostEstimate(flops=flops, bytes_accessed=moved, transcendentals=0),
        input_output_aliases=alias or {},
        name=name,
    )(*[a for _, a in ins])


AXES = ("tm", "grp")


def plan(tm, grp):
    low, total = grp.bit_length() - 1, (tm * grp).bit_length() - 1
    plane, line = [low + 1, 0], [low + 2, low + 3]
    return low, plane, line, [b for b in range(total) if b not in [low] + plane + line]


def swap(value, tm, grp, *bits):
    flip = sum(1 << b for b in bits)
    return lax.ppermute(value, AXES, [(d, d ^ flip) for d in range(tm * grp)])


def core_round(value, tm, grp):
    return swap(value, tm, grp, plan(tm, grp)[0])


def four_round(parts, bits, tm, grp):
    return [
        parts[0],
        swap(parts[1], tm, grp, *bits),
        swap(parts[2], tm, grp, bits[1]),
        swap(parts[3], tm, grp, bits[0]),
    ]


def plane_send(keep, got, after):
    ins = [(VMEM, keep), (VMEM, got)] + [(ANY, a) for a in after]
    shape = (4, keep.shape[1], 16, CH // 2)
    return list(call(plane_send_kernel, "plane_send", ins, [(VMEM, shape)] * 4))


def passed(value, after):
    ins = [(ANY, value)] + [(ANY, a) for a in after]
    return call(pass_kernel, "pass", ins, [(ANY, value.shape)], alias={0: 0})[0]


def finish(own, half, before):
    n = half.shape[1]
    return list(
        call(
            functools.partial(finish_kernel, own),
            "finish",
            [(VMEM, half)] + [(HBM, a) for a in before],
            [(HBM, (m, CH, CH), F32) for m in (9, 3, 4)],
            [pltpu.VMEM((n, CH, CH // 2), F32), pltpu.SemaphoreType.DMA((n,))],
            alias={1 + i: i for i in range(len(before))},
        )
    )


def along(value, axis, by):
    count = lax.axis_size(axis)
    pairs = [(i, i + by) for i in range(count) if 0 <= i + by < count]
    return lax.ppermute(value, axis, pairs)


def around(value, axis, by):
    count = lax.axis_size(axis)
    return lax.ppermute(value, axis, [(i, (i + by) % count) for i in range(count)])


def from_bands(parts):
    if len(parts) == 1:
        got = lax.ppermute(parts[0], "grp", [(0, 1), (1, 0)])
        return got, got
    return along(parts[0], "grp", 1), along(parts[1], "grp", -1)


def body(tm, grp, frames_in, span_frames, w_spatial, w_temporal, w_down, cotangent):
    slots, rows, cols, ch = frames_in.shape
    wide = rows * cols
    x = frames_in.reshape(slots, wide, ch)
    ws = w_spatial.reshape(9, ch, ch)
    wd = w_down.reshape(4, ch, ch)
    wt = w_temporal
    count = (SMEM, span_frames)
    tap = 2 * slots * wide * ch * ch
    tile = (rows, cols, slots, ch)
    padded = (rows + 2, cols + 2, slots, ch)
    dma = pltpu.SemaphoreType.DMA

    sides = 1 if grp == 2 else 2
    edge = call(
        functools.partial(edges_kernel, grp),
        "edges",
        [count, (VMEM, x)],
        [(VMEM, (cols * slots, ch))] * sides,
        flops=tap // 8,
    )
    top, bot = from_bands(edge)
    last_shape = (2 * wide + 32, ch)
    at_shape = (3 * ch, (rows + 4) * 128)
    xt, acts, at, last_two = call(
        acts_kernel,
        "acts",
        [count, (VMEM, x), (ANY, edge[0])],
        [(VMEM, tile), (VMEM, padded), (VMEM, at_shape), (VMEM, last_shape)],
        flops=2 * tap,
    )
    (nxt,) = call(
        next_kernel,
        "next",
        [(VMEM, cotangent), (ANY, last_two)],
        [(VMEM, (2,) + cotangent.shape[1:])],
        moved=1024,
    )
    nxt_got = along(nxt, "tm", -1)
    acts, at, last_two = call(
        functools.partial(halo_kernel, grp),
        "halo",
        [count, (VMEM, top), (VMEM, bot), (VMEM, acts), (VMEM, at), (VMEM, last_two), (ANY, nxt),
         (VMEM, cotangent), (VMEM, wt), (VMEM, wd)],
        [(VMEM, padded), (VMEM, at_shape), (VMEM, last_shape)],
        alias={3: 0, 4: 1, 5: 2},
        moved=1024,
    )
    prev = around(last_two, "tm", 1)
    half = (16, 9, 16, ch // 2)
    cott, gy, gs, keep_a, send_a, *edge = call(
        functools.partial(grad_spatial_kernel, tm, grp),
        "grad_spatial",
        [count, (VMEM, at), (VMEM, cotangent), (VMEM, nxt_got), (VMEM, wt), (VMEM, wd)],
        [(VMEM, (rows // 2, cols // 2, slots, ch)), (VMEM, tile),
         (VMEM, (rows, cols + 2, slots, ch)), (VMEM, half), (VMEM, half)]
        + [(VMEM, (cols // 2 * slots, ch))] * sides,
        flops=14 * tap,
    )
    send_a = passed(send_a, [prev])
    got_a = core_round(send_a, tm, grp)
    cot_top, cot_bot = from_bands(edge)
    half_tile = (rows // 2, cols, slots, ch)
    acts, upper = call(
        upper_kernel,
        "spatial_upper",
        [(VMEM, acts), (VMEM, prev), (VMEM, ws), (ANY, send_a)],
        [(VMEM, padded), (VMEM, half_tile)],
        flops=5 * tap,
        alias={0: 0},
    )
    _, plane, line, others = plan(tm, grp)
    parts_a = plane_send(keep_a, got_a, [upper])
    (lower,) = call(
        lower_kernel,
        "spatial_lower",
        [(VMEM, acts), (VMEM, ws)] + [(ANY, a) for a in parts_a],
        [(VMEM, half_tile)],
        flops=4 * tap,
    )
    half = (16, 7, 16, ch // 2)
    down, keep_b, send_b = call(
        forward_kernel,
        "forward",
        [count, (VMEM, xt), (VMEM, upper), (VMEM, lower), (VMEM, cott), (VMEM, gy), (VMEM, wt), (VMEM, wd),
         *((ANY, a) for a in parts_a)],
        [(VMEM, (slots * wide // 4, ch)), (VMEM, half), (VMEM, half)],
        [pltpu.VMEM(v, BF) for v in (tile, (3 * ch, slots * wide), (4 * ch, slots * wide // 4))],
        moved=1024,
        grant=14,
    )
    parts_a = four_round(parts_a, plane, tm, grp)
    send_b = passed(send_b, parts_a[1:2])
    parts_b = plane_send(keep_b, core_round(send_b, tm, grp), [])
    parts_b = four_round(parts_b, plane, tm, grp)
    parts = call(
        line_send_kernel,
        "line_send",
        [(VMEM, a) for a in parts_a + parts_b],
        [(VMEM, (16, 16, ch // 2))] * 4,
    )
    parts = four_round(list(parts), line, tm, grp)
    ins = [(VMEM, a) for a in parts]
    (mine,) = call(line_sum_kernel, "line_sum", ins, [(VMEM, parts[0].shape)])
    for bit in others:
        got = swap(mine, tm, grp, bit)
        (mine,) = call(add_kernel, "add", [(VMEM, mine), (VMEM, got)], [(VMEM, mine.shape)])
    parts = four_round([mine] * 4, line, tm, grp)
    (mine,) = call(
        line_gather_kernel, "line_gather", [(VMEM, a) for a in parts], [(VMEM, (4,) + mine.shape)]
    )
    parts = four_round([mine] * 4, plane, tm, grp)
    grad_x, down, token = call(
        functools.partial(grad_x_kernel, grp),
        "grad_x",
        [count, (VMEM, xt), (VMEM, gy), (VMEM, gs), (VMEM, cot_top), (VMEM, cot_bot), (VMEM, wt),
         (VMEM, wd), (VMEM, ws), (VMEM, down), (ANY, mine)],
        [(HBM, (slots, wide, ch)), (VMEM, cotangent.shape), TOKEN],
        [pltpu.VMEM(padded, BF), pltpu.VMEM((slots, wide, ch), BF), dma((1,))],
        flops=10 * tap,
    )
    ins = [(VMEM, a) for a in parts] + [(ANY, token)]
    (mine,) = call(plane_gather_kernel, "plane_gather", ins, [(VMEM, (16,) + mine.shape[1:])])
    got = core_round(mine, tm, grp)
    outs = finish(True, mine, [])
    sum_s, sum_t, sum_d = finish(False, got, outs)
    return (
        down,
        grad_x.reshape(frames_in.shape),
        sum_s.reshape(w_spatial.shape),
        sum_t,
        sum_d.reshape(w_down.shape),
    )


def solution(mesh):
    return jax.shard_map(
        functools.partial(body, mesh.shape["tm"], mesh.shape["grp"]),
        mesh=mesh,
        in_specs=(P("tm", "grp", None, None), P("tm"), P(), P(), P(), P("tm", "grp", None, None)),
        out_specs=(P("tm", "grp", None, None), P("tm", "grp", None, None), P(), P(), P()),
        check_vma=False,
    )
```

```python
import functools

import jax
import jax.numpy as jnp
from jax import lax
from jax.experimental import pallas as pl
from jax.experimental.pallas import tpu as pltpu
from jax.sharding import PartitionSpec as P

SLOTS = 16
OWN = 14
CH = 256
BF = jnp.bfloat16
F32 = jnp.float32


def mm(a, b):
    return lax.dot_general(a, b, (((1,), (0,)), ((), ())), preferred_element_type=F32)


def mm_nt(a, b):
    return lax.dot_general(a, b, (((1,), (1,)), ((), ())), preferred_element_type=F32)


def iotas(rows, cols):
    return (
        lax.broadcasted_iota(jnp.int32, (rows, cols), 0),
        lax.broadcasted_iota(jnp.int32, (rows, cols), 1),
    )


def to_slots(rows, frames, keep):
    a, b = iotas(rows * SLOTS, frames * rows)
    bits = rows.bit_length() - 1
    hit = ((a >> 4) == (b & (rows - 1))) & keep(b >> bits, a & 15)
    return jnp.where(hit, 1.0, 0.0).astype(BF)


def to_frames(rows):
    a, b = iotas(SLOTS * rows, rows * SLOTS)
    bits = rows.bit_length() - 1
    hit = ((a & (rows - 1)) == (b >> 4)) & ((a >> bits) == (b & 15))
    return jnp.where(hit, 1.0, 0.0).astype(BF)


def own_frames(count):
    return lambda frame, slot: (frame == slot) & (slot < count)


def own_and_next(count, blocks):
    after = jnp.where(lax.axis_index("tm") < blocks - 1, count, 64)
    return lambda frame, slot: ((frame < OWN) & (frame == slot) & (slot < count)) | (
        (frame >= OWN) & (slot == after + frame - OWN)
    )


def silu_norm(v):
    scaled = v * lax.rsqrt(jnp.mean(v * v, axis=-1, keepdims=True) + 1e-06)
    return scaled * (0.5 + 0.5 * jnp.tanh(0.5 * scaled))


def slot_mask(shape, count):
    return lax.broadcasted_iota(jnp.int32, shape, len(shape) - 2) < count


def grad_of_temporal(gy, wt_ref, count):
    n = gy.shape[0]
    terms = mm_nt(gy.reshape(n * SLOTS, CH), wt_ref[...].reshape(3 * CH, CH))
    total = terms[:, 2 * CH :].reshape(n, SLOTS, CH)
    for k in (1, 0):
        term = terms[:, k * CH : k * CH + CH].reshape(n, SLOTS, CH)
        total = total + pltpu.roll(term, SLOTS - (2 - k), 1)
    return jnp.where(slot_mask(total.shape, count), total, 0.0).astype(BF)


def place_bits():
    t, g = lax.axis_index("tm"), lax.axis_index("grp")
    return t & 1, ((t >> 1) & 1) + 2 * (g & 1), (t >> 2) & 3


def split_cores(value, keep_ref, send_ref, k):
    core, _, _ = place_bits()
    low, high = value[:, : CH // 2].astype(BF), value[:, CH // 2 :].astype(BF)
    keep_ref[:, k] = jnp.where(core == 0, low, high).reshape(16, 16, CH // 2)
    send_ref[:, k] = jnp.where(core == 0, high, low).reshape(16, 16, CH // 2)


def edges_kernel(bands, count_ref, x_ref, *outs):
    count = count_ref[0]
    band = lax.axis_index("grp")
    wide = x_ref.shape[1]
    if bands == 2:
        starts, lower = [jnp.where(band == 0, wide - 16, 0)], [band == 0]
    else:
        starts, lower = [wide - 16, 0], [True, False]
    place = to_slots(16, SLOTS, own_frames(count))
    for k, at in enumerate(starts):
        piece = x_ref[:, pl.ds(pl.multiple_of(at, 16), 16), :].reshape(SLOTS * 16, CH)
        v = mm(place, piece)
        v = jnp.where(lower[k], v[128:], v[:128])
        outs[k][...] = silu_norm(v).astype(BF)


def acts_kernel(count_ref, x_ref, _, xt_ref, acts_ref, at_ref, last_ref):
    count = count_ref[0]
    rows, cols = xt_ref.shape[0], xt_ref.shape[1]
    edge = jnp.zeros((rows + 2, SLOTS, CH), BF)
    acts_ref[:, 0] = edge
    acts_ref[:, cols + 1] = edge
    place = to_slots(16, SLOTS, own_frames(count))
    last = silu_norm(x_ref[pl.ds(count - 2, 2)].reshape(2 * rows * cols, CH).astype(F32))
    last_ref[0 : 2 * rows * cols] = last.astype(BF)

    def rows_of(q, _):
        at = pl.multiple_of(q * 16, 16)
        piece = x_ref[:, pl.ds(at, 16), :].reshape(SLOTS * 16, CH)
        v = mm(place, piece)
        xt_ref[pl.ds(2 * q, 2)] = v.astype(BF).reshape(2, cols, SLOTS, CH)
        a = silu_norm(v).astype(BF)
        acts_ref[pl.ds(2 * q + 1, 2), 1 : cols + 1] = a.reshape(2, cols, SLOTS, CH)
        flipped = a.T
        for i in range(3):
            at = pl.multiple_of((2 * q + 3 - i) * 128, 128)
            at_ref[i * CH : i * CH + CH, pl.ds(at, 256)] = flipped
        return 0

    lax.fori_loop(0, rows // 2, rows_of, 0, unroll=True)


def next_kernel(cot_ref, _, nxt_ref):
    nxt_ref[...] = cot_ref[0:2]


def halo_kernel(bands, count_ref, top_ref, bot_ref, *rest):
    acts_ref, at_ref, last_ref = rest[-3:]
    count = count_ref[0]
    band = lax.axis_index("grp")
    rows, cols = acts_ref.shape[0] - 2, acts_ref.shape[1] - 2
    halo = []
    for ref, flag, i, row in ((top_ref, band > 0, 0, 0), (bot_ref, band < bands - 1, 2, rows + 1)):
        a = jnp.where(flag, ref[...].astype(F32), 0.0).astype(BF)
        acts_ref[row, 1 : cols + 1] = a.reshape(cols, SLOTS, CH)
        at = (row - i + 2) * 128
        at_ref[i * CH : i * CH + CH, at : at + 128] = a.T
        halo.append(a)
    a, b = iotas(32, 256)
    pick = ((a & 15) == (b >> 4)) & ((b & 15) == count - 2 + (a >> 4))
    pick = jnp.where(pick, 1.0, 0.0).astype(BF)
    last_ref[2 * rows * cols :] = mm(pick, jnp.concatenate(halo, 0)).astype(BF)


def conv_rows(acts_ref, ws_ref, sp_ref, start):
    rows, cols = sp_ref.shape[0], sp_ref.shape[1]

    def rows_of(q, _):
        total = None
        for i in range(3):
            for j in range(3):
                left = acts_ref[pl.ds(start + 4 * q + i, 4), j : j + cols].reshape(
                    4 * cols * SLOTS, CH
                )
                term = mm(left, ws_ref[i * 3 + j])
                total = term if total is None else total + term
        sp_ref[pl.ds(4 * q, 4)] = total.astype(BF).reshape(4, cols, SLOTS, CH)
        return 0

    lax.fori_loop(0, rows // 4, rows_of, 0, unroll=True)


def upper_kernel(acts_in, prev_ref, ws_ref, _, acts_ref, sp_ref):
    rows, cols = acts_ref.shape[0] - 2, acts_ref.shape[1] - 2
    a, b = iotas(256, 32)
    place = ((a >> 4) == (b & 15)) & ((a & 15) == OWN + (b >> 4)) & (lax.axis_index("tm") > 0)
    place = jnp.where(place, 1.0, 0.0).astype(BF)
    size = rows * cols
    for q in range(rows // 2 + 1):
        if q == rows // 2:
            both, prev = slice(0, rows + 2, rows + 1), prev_ref[2 * size :]
        else:
            both = slice(2 * q + 1, 2 * q + 3)
            parts = [prev_ref[f * size + q * 16 : f * size + q * 16 + 16] for f in range(2)]
            prev = jnp.concatenate(parts, 0)
        prev = mm(place, prev).astype(BF).reshape(2, cols, SLOTS, CH)
        for k, row in enumerate(range(rows + 2)[both]):
            acts_ref[row, 1 : cols + 1] = acts_ref[row, 1 : cols + 1] + prev[k]

    conv_rows(acts_ref, ws_ref, sp_ref, 0)


def lower_kernel(acts_ref, ws_ref, *rest):
    sp_ref = rest[-1]
    conv_rows(acts_ref, ws_ref, sp_ref, sp_ref.shape[0])


def grad_spatial_kernel(
    blocks, bands, count_ref, at_ref, cot_ref, nxt_ref, wt_ref, wd_ref,
    cott_ref, gy_ref, gs_ref, keep_ref, send_ref, *edge_refs,
):
    count = count_ref[0]
    band = lax.axis_index("grp")
    rows, cols = gy_ref.shape[0], gy_ref.shape[1]
    edge = jnp.zeros((rows, SLOTS, CH), BF)
    gs_ref[:, 0] = edge
    gs_ref[:, cols + 1] = edge

    place_next = to_slots(16, SLOTS, own_and_next(count, blocks))
    halves = []
    for q in range(rows * cols // 64):
        four = slice(q * 4, q * 4 + 4)
        piece = jnp.concatenate(
            [cot_ref[0:OWN, four].reshape(OWN, 16, CH), nxt_ref[:, four].reshape(2, 16, CH)], 0
        ).reshape(SLOTS * 16, CH)
        halves.append(mm(place_next, piece).astype(BF))
    placed = jnp.concatenate(halves, 0)
    cott_ref[...] = placed.reshape(rows // 2, cols // 2, SLOTS, CH)
    for i in range(2):
        for j in range(2):
            g = mm_nt(placed, wd_ref[i * 2 + j]).astype(BF).reshape(rows // 2, cols // 2, SLOTS, CH)
            for r in range(rows // 2):
                for c in range(cols // 2):
                    gy_ref[2 * r + i, 2 * c + j] = g[r, c]
    last = cott_ref[rows // 2 - 1].reshape(cols // 2 * SLOTS, CH)
    first = cott_ref[0].reshape(cols // 2 * SLOTS, CH)
    if bands == 2:
        edge_refs[0][...] = jnp.where(band == 0, last, first)
    else:
        edge_refs[0][...] = last
        edge_refs[1][...] = first

    def grads_of(q, _):
        g = gy_ref[pl.ds(4 * q, 4)].reshape(4 * cols, SLOTS, CH)
        s = grad_of_temporal(g, wt_ref, count)
        gs_ref[pl.ds(4 * q, 4), 1 : cols + 1] = s.reshape(4, cols, SLOTS, CH)
        g = jnp.where(slot_mask(g.shape, count), g.astype(F32), 0.0)
        gy_ref[pl.ds(4 * q, 4)] = g.astype(BF).reshape(4, cols, SLOTS, CH)
        return 0

    lax.fori_loop(0, rows // 4, grads_of, 0, unroll=True)

    wide = rows * cols * SLOTS
    for j in range(3):
        right = gs_ref[:, 2 - j : 2 - j + cols].reshape(wide, CH)
        value = mm(at_ref[:, 256 : 256 + wide], right)
        for i in range(3):
            split_cores(value[i * CH : i * CH + CH], keep_ref, send_ref, i * 3 + j)


def forward_kernel(
    count_ref, xt_ref, upper_ref, lower_ref, cott_ref, gy_ref, wt_ref, wd_ref, *rest
):
    down_ref, keep_ref, send_ref, y_ref, st_ref, yt_ref = rest[-6:]
    count = count_ref[0]
    rows, cols = xt_ref.shape[0], xt_ref.shape[1]
    for q in range(rows // 4):
        sp_ref = upper_ref if q < rows // 8 else lower_ref
        at = 4 * (q % (rows // 8))
        s = sp_ref[at : at + 4].astype(F32).reshape(4 * cols, SLOTS, CH)
        taps = []
        for k in range(3):
            shifted = s if k == 2 else pltpu.roll(s, 2 - k, 1)
            shifted = shifted.astype(BF).reshape(4 * cols * SLOTS, CH)
            st_ref[k * CH : k * CH + CH, q * 512 : q * 512 + 512] = shifted.T
            taps.append(shifted)
        total = mm(jnp.concatenate(taps, axis=1), wt_ref[...].reshape(3 * CH, CH))
        x = xt_ref[4 * q : 4 * q + 4].reshape(4 * cols, SLOTS, CH).astype(F32)
        y = jnp.where(slot_mask(x.shape, count), x + total.reshape(x.shape), 0.0).astype(BF)
        y_ref[4 * q : 4 * q + 4] = y.reshape(4, cols, SLOTS, CH)

    wide = rows * cols * SLOTS
    value = mm(st_ref[...], gy_ref[...].reshape(wide, CH))
    for k in range(3):
        split_cores(value[k * CH : k * CH + CH], keep_ref, send_ref, k)

    small = wide // 4
    total = None
    for i in range(2):
        for j in range(2):
            tiles = [
                y_ref[2 * r + i, 2 * c + j] for r in range(rows // 2) for c in range(cols // 2)
            ]
            piece = jnp.concatenate(tiles, axis=0)
            k = i * 2 + j
            yt_ref[k * CH : k * CH + CH] = piece.T
            term = mm(piece, wd_ref[k])
            total = term if total is None else total + term
    down_ref[...] = total.astype(BF)
    value = mm(yt_ref[...], cott_ref[...].reshape(small, CH))
    for k in range(4):
        split_cores(value[k * CH : k * CH + CH], keep_ref, send_ref, 3 + k)


def grad_x_kernel(
    bands, count_ref, xt_ref, gy_ref, gs_ref, top_ref, bot_ref, wt_ref, wd_ref, ws_ref, slot_ref, *rest
):
    out_ref, down_ref, token_ref, pad_ref, buf, sems = rest[-6:]
    token_ref[...] = jnp.zeros_like(token_ref)
    count = count_ref[0]
    band = lax.axis_index("grp")
    rows, cols = xt_ref.shape[0], xt_ref.shape[1]
    pad_ref[1 : rows + 1] = gs_ref[...]
    edge = jnp.zeros((SLOTS, CH), BF)
    for ref, flag, i, row in ((top_ref, band > 0, 1, 0), (bot_ref, band < bands - 1, 0, rows + 1)):
        pair = [
            mm_nt(ref[...], wd_ref[i * 2 + j]).astype(BF).reshape(cols // 2, SLOTS, CH)
            for j in range(2)
        ]
        g = jnp.stack(pair, axis=1).reshape(cols, SLOTS, CH)
        pad_ref[row, 0] = edge
        pad_ref[row, 1 : cols + 1] = grad_of_temporal(g, wt_ref, jnp.where(flag, count, 0))
        pad_ref[row, cols + 1] = edge
    back = to_frames(16)

    def rows_of(q, _):
        total = None
        for i in range(3):
            for j in range(3):
                left = pad_ref[pl.ds(4 * q + 2 - i, 4), 2 - j : 2 - j + cols].reshape(
                    4 * cols * SLOTS, CH
                )
                term = mm_nt(left, ws_ref[i * 3 + j])
                total = term if total is None else total + term
        at = 4 * q
        v = xt_ref[pl.ds(at, 4)].reshape(4 * cols * SLOTS, CH).astype(F32)
        r = lax.rsqrt(jnp.mean(v * v, axis=-1, keepdims=True) + 1e-06)
        u = v * r
        s = 0.5 + 0.5 * jnp.tanh(0.5 * u)
        gu = total * (s * (1.0 + u * (1.0 - s)))
        dot = jnp.mean(gu * u, axis=-1, keepdims=True)
        gv = r * (gu - u * dot)
        gx = gy_ref[pl.ds(at, 4)].reshape(4 * cols * SLOTS, CH).astype(F32) + gv
        gx = gx.reshape(4 * cols, SLOTS, CH)
        gx = jnp.where(slot_mask(gx.shape, count), gx, 0.0).astype(BF).reshape(4 * cols * SLOTS, CH)
        for k in range(2):
            o = mm(back, gx[k * 256 : k * 256 + 256]).astype(BF)
            buf[:, pl.ds(pl.multiple_of((2 * q + k) * 16, 16), 16), :] = o.reshape(SLOTS, 16, CH)
        return 0

    lax.fori_loop(0, rows // 4, rows_of, 0)
    copy = pltpu.make_async_copy(buf, out_ref, sems.at[0])
    copy.start()
    for q in range(down_ref.shape[1] // 4):
        o = mm(back, slot_ref[q * 256 : q * 256 + 256]).astype(BF)
        down_ref[:, q * 4 : q * 4 + 4] = o.reshape(SLOTS, 4, cols // 2, CH)
    copy.wait()


ORDER = (0, 3, 2, 1)


def plane_send_kernel(keep_ref, got_ref, *rest):
    _, p, _ = place_bits()
    for r, out in zip(ORDER, rest[-4:]):
        at = pl.ds((p ^ r) * 4, 4)
        out[...] = (keep_ref[at].astype(F32) + got_ref[at].astype(F32)).astype(BF)


def line_send_kernel(*refs):
    outs = refs[8:]
    _, _, z = place_bits()
    for out, r in zip(outs, ORDER):
        at = 0
        for chain in (refs[:4], refs[4:8]):
            parts = [ref[z ^ r].astype(F32) for ref in chain]
            n = parts[0].shape[0]
            out[at : at + n] = (parts[0] + parts[1] + parts[2] + parts[3]).astype(BF)
            at += n


def line_sum_kernel(a_ref, b_ref, c_ref, d_ref, *rest):
    out_ref = rest[-1]
    parts = [ref[...].astype(F32) for ref in (a_ref, b_ref, c_ref, d_ref)]
    out_ref[...] = (parts[0] + parts[1] + parts[2] + parts[3]).astype(BF)


def line_gather_kernel(a_ref, b_ref, c_ref, d_ref, out_ref):
    _, _, z = place_bits()
    for r, ref in zip(ORDER, (a_ref, b_ref, c_ref, d_ref)):
        out_ref[z ^ r] = ref[...]


def plane_gather_kernel(a_ref, b_ref, c_ref, d_ref, _, out_ref):
    _, p, _ = place_bits()
    for r, ref in zip(ORDER, (a_ref, b_ref, c_ref, d_ref)):
        out_ref[pl.ds((p ^ r) * 4, 4)] = ref[...]


def add_kernel(a_ref, b_ref, out_ref):
    out_ref[...] = (a_ref[...].astype(F32) + b_ref[...].astype(F32)).astype(BF)


def pass_kernel(*_):
    pass


def finish_kernel(own, half_ref, *rest):
    buf, sems = rest[-2:]
    outs = rest[-5:-2]
    core, _, _ = place_bits()
    at = pl.multiple_of((core if own else 1 - core) * (CH // 2), CH // 2)
    copies = []
    k = 0
    for out in outs:
        for m in range(out.shape[0]):
            buf[k] = half_ref[:, k].reshape(CH, CH // 2).astype(F32)
            copies.append(
                pltpu.make_async_copy(buf.at[k], out.at[m, :, pl.ds(at, CH // 2)], sems.at[k])
            )
            copies[-1].start()
            k += 1
    for copy in copies:
        copy.wait()


VMEM = pl.BlockSpec(memory_space=pltpu.VMEM)
SMEM = pl.BlockSpec(memory_space=pltpu.SMEM)
ANY = pl.BlockSpec(memory_space=pl.ANY)
HBM = pl.BlockSpec(memory_space=pltpu.HBM)
TOKEN = (VMEM, (8, 128), F32)


def call(kernel, name, ins, outs, scratch=(), flops=0, alias=None, grant=10, moved=None):
    shapes = [jax.ShapeDtypeStruct(o[1], o[2] if len(o) > 2 else BF) for o in outs]
    if moved is None:
        moved = sum(a.size * a.dtype.itemsize for s, a in ins if s is not ANY)
        moved += sum(s.size * s.dtype.itemsize for s in shapes)
    return pl.pallas_call(
        kernel,
        out_shape=shapes,
        in_specs=[s for s, _ in ins],
        out_specs=[o[0] for o in outs],
        scratch_shapes=list(scratch),
        compiler_params=pltpu.CompilerParams(vmem_limit_bytes=grant * 2**20),
        cost_estimate=pl.CostEstimate(flops=flops, bytes_accessed=moved, transcendentals=0),
        input_output_aliases=alias or {},
        name=name,
    )(*[a for _, a in ins])


AXES = ("tm", "grp")


def plan(tm, grp):
    low, total = grp.bit_length() - 1, (tm * grp).bit_length() - 1
    plane, line = [low + 1, 0], [low + 2, low + 3]
    return low, plane, line, [b for b in range(total) if b not in [low] + plane + line]


def swap(value, tm, grp, *bits):
    flip = sum(1 << b for b in bits)
    return lax.ppermute(value, AXES, [(d, d ^ flip) for d in range(tm * grp)])


def core_round(value, tm, grp):
    return swap(value, tm, grp, plan(tm, grp)[0])


def four_round(parts, bits, tm, grp):
    return [
        parts[0],
        swap(parts[1], tm, grp, *bits),
        swap(parts[2], tm, grp, bits[1]),
        swap(parts[3], tm, grp, bits[0]),
    ]


def plane_send(keep, got, after):
    ins = [(VMEM, keep), (VMEM, got)] + [(ANY, a) for a in after]
    shape = (4, keep.shape[1], 16, CH // 2)
    return list(call(plane_send_kernel, "plane_send", ins, [(VMEM, shape)] * 4))


def passed(value, after):
    ins = [(ANY, value)] + [(ANY, a) for a in after]
    return call(pass_kernel, "pass", ins, [(ANY, value.shape)], alias={0: 0})[0]


def finish(own, half, before):
    n = half.shape[1]
    return list(
        call(
            functools.partial(finish_kernel, own),
            "finish",
            [(VMEM, half)] + [(HBM, a) for a in before],
            [(HBM, (m, CH, CH), F32) for m in (9, 3, 4)],
            [pltpu.VMEM((n, CH, CH // 2), F32), pltpu.SemaphoreType.DMA((n,))],
            alias={1 + i: i for i in range(len(before))},
        )
    )


def along(value, axis, by):
    count = lax.axis_size(axis)
    pairs = [(i, i + by) for i in range(count) if 0 <= i + by < count]
    return lax.ppermute(value, axis, pairs)


def around(value, axis, by):
    count = lax.axis_size(axis)
    return lax.ppermute(value, axis, [(i, (i + by) % count) for i in range(count)])


def from_bands(parts):
    if len(parts) == 1:
        got = lax.ppermute(parts[0], "grp", [(0, 1), (1, 0)])
        return got, got
    return along(parts[0], "grp", 1), along(parts[1], "grp", -1)


def body(tm, grp, frames_in, span_frames, w_spatial, w_temporal, w_down, cotangent):
    slots, rows, cols, ch = frames_in.shape
    wide = rows * cols
    x = frames_in.reshape(slots, wide, ch)
    ws = w_spatial.reshape(9, ch, ch)
    wd = w_down.reshape(4, ch, ch)
    wt = w_temporal
    count = (SMEM, span_frames)
    tap = 2 * slots * wide * ch * ch
    tile = (rows, cols, slots, ch)
    padded = (rows + 2, cols + 2, slots, ch)
    dma = pltpu.SemaphoreType.DMA

    sides = 1 if grp == 2 else 2
    edge = call(
        functools.partial(edges_kernel, grp),
        "edges",
        [count, (VMEM, x)],
        [(VMEM, (cols * slots, ch))] * sides,
        flops=tap // 8,
    )
    top, bot = from_bands(edge)
    last_shape = (2 * wide + 32, ch)
    at_shape = (3 * ch, (rows + 4) * 128)
    xt, acts, at, last_two = call(
        acts_kernel,
        "acts",
        [count, (VMEM, x), (ANY, edge[0])],
        [(VMEM, tile), (VMEM, padded), (VMEM, at_shape), (VMEM, last_shape)],
        flops=2 * tap,
    )
    (nxt,) = call(
        next_kernel,
        "next",
        [(VMEM, cotangent), (ANY, last_two)],
        [(VMEM, (2,) + cotangent.shape[1:])],
        moved=1024,
    )
    nxt_got = along(nxt, "tm", -1)
    acts, at, last_two = call(
        functools.partial(halo_kernel, grp),
        "halo",
        [count, (VMEM, top), (VMEM, bot), (VMEM, acts), (VMEM, at), (VMEM, last_two), (ANY, nxt),
         (VMEM, cotangent), (VMEM, wt), (VMEM, wd)],
        [(VMEM, padded), (VMEM, at_shape), (VMEM, last_shape)],
        alias={3: 0, 4: 1, 5: 2},
        moved=1024,
    )
    prev = around(last_two, "tm", 1)
    half = (16, 9, 16, ch // 2)
    cott, gy, gs, keep_a, send_a, *edge = call(
        functools.partial(grad_spatial_kernel, tm, grp),
        "grad_spatial",
        [count, (VMEM, at), (VMEM, cotangent), (VMEM, nxt_got), (VMEM, wt), (VMEM, wd)],
        [(VMEM, (rows // 2, cols // 2, slots, ch)), (VMEM, tile),
         (VMEM, (rows, cols + 2, slots, ch)), (VMEM, half), (VMEM, half)]
        + [(VMEM, (cols // 2 * slots, ch))] * sides,
        flops=14 * tap,
    )
    send_a = passed(send_a, [prev])
    got_a = core_round(send_a, tm, grp)
    cot_top, cot_bot = from_bands(edge)
    half_tile = (rows // 2, cols, slots, ch)
    acts, upper = call(
        upper_kernel,
        "spatial_upper",
        [(VMEM, acts), (VMEM, prev), (VMEM, ws), (ANY, send_a)],
        [(VMEM, padded), (VMEM, half_tile)],
        flops=5 * tap,
        alias={0: 0},
    )
    _, plane, line, others = plan(tm, grp)
    parts_a = plane_send(keep_a, got_a, [upper])
    (lower,) = call(
        lower_kernel,
        "spatial_lower",
        [(VMEM, acts), (VMEM, ws)] + [(ANY, a) for a in parts_a],
        [(VMEM, half_tile)],
        flops=4 * tap,
    )
    half = (16, 7, 16, ch // 2)
    down, keep_b, send_b = call(
        forward_kernel,
        "forward",
        [count, (VMEM, xt), (VMEM, upper), (VMEM, lower), (VMEM, cott), (VMEM, gy), (VMEM, wt), (VMEM, wd),
         *((ANY, a) for a in parts_a)],
        [(VMEM, (slots * wide // 4, ch)), (VMEM, half), (VMEM, half)],
        [pltpu.VMEM(v, BF) for v in (tile, (3 * ch, slots * wide), (4 * ch, slots * wide // 4))],
        moved=1024,
        grant=14,
    )
    parts_a = four_round(parts_a, plane, tm, grp)
    send_b = passed(send_b, parts_a[1:2])
    parts_b = plane_send(keep_b, core_round(send_b, tm, grp), [])
    parts_b = four_round(parts_b, plane, tm, grp)
    parts = call(
        line_send_kernel,
        "line_send",
        [(VMEM, a) for a in parts_a + parts_b],
        [(VMEM, (16, 16, ch // 2))] * 4,
    )
    parts = four_round(list(parts), line, tm, grp)
    ins = [(VMEM, a) for a in parts]
    (mine,) = call(line_sum_kernel, "line_sum", ins, [(VMEM, parts[0].shape)])
    for bit in others:
        got = swap(mine, tm, grp, bit)
        (mine,) = call(add_kernel, "add", [(VMEM, mine), (VMEM, got)], [(VMEM, mine.shape)])
    parts = four_round([mine] * 4, line, tm, grp)
    (mine,) = call(
        line_gather_kernel, "line_gather", [(VMEM, a) for a in parts], [(VMEM, (4,) + mine.shape)]
    )
    parts = four_round([mine] * 4, plane, tm, grp)
    grad_x, down, token = call(
        functools.partial(grad_x_kernel, grp),
        "grad_x",
        [count, (VMEM, xt), (VMEM, gy), (VMEM, gs), (VMEM, cot_top), (VMEM, cot_bot), (VMEM, wt),
         (VMEM, wd), (VMEM, ws), (VMEM, down), (ANY, mine)],
        [(HBM, (slots, wide, ch)), (VMEM, cotangent.shape), TOKEN],
        [pltpu.VMEM(padded, BF), pltpu.VMEM((slots, wide, ch), BF), dma((1,))],
        flops=10 * tap,
    )
    ins = [(VMEM, a) for a in parts] + [(ANY, token)]
    (mine,) = call(plane_gather_kernel, "plane_gather", ins, [(VMEM, (16,) + mine.shape[1:])])
    got = core_round(mine, tm, grp)
    outs = finish(True, mine, [])
    sum_s, sum_t, sum_d = finish(False, got, outs)
    return (
        down,
        grad_x.reshape(frames_in.shape),
        sum_s.reshape(w_spatial.shape),
        sum_t,
        sum_d.reshape(w_down.shape),
    )


def solution(mesh):
    return jax.shard_map(
        functools.partial(body, mesh.shape["tm"], mesh.shape["grp"]),
        mesh=mesh,
        in_specs=(P("tm", "grp", None, None), P("tm"), P(), P(), P(), P("tm", "grp", None, None)),
        out_specs=(P("tm", "grp", None, None), P("tm", "grp", None, None), P(), P(), P()),
        check_vma=False,
    )
```

```python
import functools

import jax
import jax.numpy as jnp
from jax import lax
from jax.experimental import pallas as pl
from jax.experimental.pallas import tpu as pltpu
from jax.sharding import PartitionSpec as P

SLOTS = 16
OWN = 14
CH = 256
BF = jnp.bfloat16
F32 = jnp.float32


def mm(a, b):
    return lax.dot_general(a, b, (((1,), (0,)), ((), ())), preferred_element_type=F32)


def mm_nt(a, b):
    return lax.dot_general(a, b, (((1,), (1,)), ((), ())), preferred_element_type=F32)


def iotas(rows, cols):
    return (
        lax.broadcasted_iota(jnp.int32, (rows, cols), 0),
        lax.broadcasted_iota(jnp.int32, (rows, cols), 1),
    )


def to_slots(rows, frames, keep):
    a, b = iotas(rows * SLOTS, frames * rows)
    bits = rows.bit_length() - 1
    hit = ((a >> 4) == (b & (rows - 1))) & keep(b >> bits, a & 15)
    return jnp.where(hit, 1.0, 0.0).astype(BF)


def to_frames(rows):
    a, b = iotas(SLOTS * rows, rows * SLOTS)
    bits = rows.bit_length() - 1
    hit = ((a & (rows - 1)) == (b >> 4)) & ((a >> bits) == (b & 15))
    return jnp.where(hit, 1.0, 0.0).astype(BF)


def own_frames(count):
    return lambda frame, slot: (frame == slot) & (slot < count)


def own_and_next(count, blocks):
    after = jnp.where(lax.axis_index("tm") < blocks - 1, count, 64)
    return lambda frame, slot: ((frame < OWN) & (frame == slot) & (slot < count)) | (
        (frame >= OWN) & (slot == after + frame - OWN)
    )


def silu_norm(v):
    scaled = v * lax.rsqrt(jnp.mean(v * v, axis=-1, keepdims=True) + 1e-06)
    return scaled * (0.5 + 0.5 * jnp.tanh(0.5 * scaled))


def slot_mask(shape, count):
    return lax.broadcasted_iota(jnp.int32, shape, len(shape) - 2) < count


def grad_of_temporal(gy, wt_ref, count):
    n = gy.shape[0]
    terms = mm_nt(gy.reshape(n * SLOTS, CH), wt_ref[...].reshape(3 * CH, CH))
    total = terms[:, 2 * CH :].reshape(n, SLOTS, CH)
    for k in (1, 0):
        term = terms[:, k * CH : k * CH + CH].reshape(n, SLOTS, CH)
        total = total + pltpu.roll(term, SLOTS - (2 - k), 1)
    return jnp.where(slot_mask(total.shape, count), total, 0.0).astype(BF)


def place_bits():
    t, g = lax.axis_index("tm"), lax.axis_index("grp")
    return t & 1, ((t >> 1) & 1) + 2 * (g & 1), (t >> 2) & 3


def split_cores(value, keep_ref, send_ref, k):
    core, _, _ = place_bits()
    low, high = value[:, : CH // 2].astype(BF), value[:, CH // 2 :].astype(BF)
    keep_ref[:, k] = jnp.where(core == 0, low, high).reshape(16, 16, CH // 2)
    send_ref[:, k] = jnp.where(core == 0, high, low).reshape(16, 16, CH // 2)


def edges_kernel(bands, count_ref, x_ref, *outs):
    count = count_ref[0]
    band = lax.axis_index("grp")
    wide = x_ref.shape[1]
    if bands == 2:
        starts, lower = [jnp.where(band == 0, wide - 16, 0)], [band == 0]
    else:
        starts, lower = [wide - 16, 0], [True, False]
    place = to_slots(16, SLOTS, own_frames(count))
    for k, at in enumerate(starts):
        piece = x_ref[:, pl.ds(pl.multiple_of(at, 16), 16), :].reshape(SLOTS * 16, CH)
        v = mm(place, piece)
        v = jnp.where(lower[k], v[128:], v[:128])
        outs[k][...] = silu_norm(v).astype(BF)


def acts_kernel(count_ref, x_ref, _, xt_ref, acts_ref, at_ref, last_ref):
    count = count_ref[0]
    rows, cols = xt_ref.shape[0], xt_ref.shape[1]
    edge = jnp.zeros((rows + 2, SLOTS, CH), BF)
    acts_ref[:, 0] = edge
    acts_ref[:, cols + 1] = edge
    place = to_slots(16, SLOTS, own_frames(count))
    last = silu_norm(x_ref[pl.ds(count - 2, 2)].reshape(2 * rows * cols, CH).astype(F32))
    last_ref[0 : 2 * rows * cols] = last.astype(BF)

    def rows_of(q, _):
        at = pl.multiple_of(q * 16, 16)
        piece = x_ref[:, pl.ds(at, 16), :].reshape(SLOTS * 16, CH)
        v = mm(place, piece)
        xt_ref[pl.ds(2 * q, 2)] = v.astype(BF).reshape(2, cols, SLOTS, CH)
        a = silu_norm(v).astype(BF)
        acts_ref[pl.ds(2 * q + 1, 2), 1 : cols + 1] = a.reshape(2, cols, SLOTS, CH)
        flipped = a.T
        for i in range(3):
            at = pl.multiple_of((2 * q + 3 - i) * 128, 128)
            at_ref[i * CH : i * CH + CH, pl.ds(at, 256)] = flipped
        return 0

    lax.fori_loop(0, rows // 2, rows_of, 0, unroll=True)


def next_kernel(cot_ref, _, nxt_ref):
    nxt_ref[...] = cot_ref[0:2]


def halo_kernel(bands, count_ref, top_ref, bot_ref, *rest):
    acts_ref, at_ref, last_ref = rest[-3:]
    count = count_ref[0]
    band = lax.axis_index("grp")
    rows, cols = acts_ref.shape[0] - 2, acts_ref.shape[1] - 2
    halo = []
    for ref, flag, i, row in ((top_ref, band > 0, 0, 0), (bot_ref, band < bands - 1, 2, rows + 1)):
        a = jnp.where(flag, ref[...].astype(F32), 0.0).astype(BF)
        acts_ref[row, 1 : cols + 1] = a.reshape(cols, SLOTS, CH)
        at = (row - i + 2) * 128
        at_ref[i * CH : i * CH + CH, at : at + 128] = a.T
        halo.append(a)
    a, b = iotas(32, 256)
    pick = ((a & 15) == (b >> 4)) & ((b & 15) == count - 2 + (a >> 4))
    pick = jnp.where(pick, 1.0, 0.0).astype(BF)
    last_ref[2 * rows * cols :] = mm(pick, jnp.concatenate(halo, 0)).astype(BF)


def conv_rows(acts_ref, ws_ref, sp_ref, start):
    rows, cols = sp_ref.shape[0], sp_ref.shape[1]

    def rows_of(q, _):
        total = None
        for i in range(3):
            for j in range(3):
                left = acts_ref[pl.ds(start + 4 * q + i, 4), j : j + cols].reshape(
                    4 * cols * SLOTS, CH
                )
                term = mm(left, ws_ref[i * 3 + j])
                total = term if total is None else total + term
        sp_ref[pl.ds(4 * q, 4)] = total.astype(BF).reshape(4, cols, SLOTS, CH)
        return 0

    lax.fori_loop(0, rows // 4, rows_of, 0, unroll=True)


def upper_kernel(acts_in, prev_ref, ws_ref, _, acts_ref, sp_ref):
    rows, cols = acts_ref.shape[0] - 2, acts_ref.shape[1] - 2
    a, b = iotas(256, 32)
    place = ((a >> 4) == (b & 15)) & ((a & 15) == OWN + (b >> 4)) & (lax.axis_index("tm") > 0)
    place = jnp.where(place, 1.0, 0.0).astype(BF)
    size = rows * cols
    for q in range(rows // 2 + 1):
        if q == rows // 2:
            both, prev = slice(0, rows + 2, rows + 1), prev_ref[2 * size :]
        else:
            both = slice(2 * q + 1, 2 * q + 3)
            parts = [prev_ref[f * size + q * 16 : f * size + q * 16 + 16] for f in range(2)]
            prev = jnp.concatenate(parts, 0)
        prev = mm(place, prev).astype(BF).reshape(2, cols, SLOTS, CH)
        for k, row in enumerate(range(rows + 2)[both]):
            acts_ref[row, 1 : cols + 1] = acts_ref[row, 1 : cols + 1] + prev[k]

    conv_rows(acts_ref, ws_ref, sp_ref, 0)


def lower_kernel(acts_ref, ws_ref, *rest):
    sp_ref = rest[-1]
    conv_rows(acts_ref, ws_ref, sp_ref, sp_ref.shape[0])


def grad_spatial_kernel(
    blocks, bands, count_ref, at_ref, cot_ref, nxt_ref, wt_ref, wd_ref,
    cott_ref, gy_ref, gs_ref, keep_ref, send_ref, *edge_refs,
):
    count = count_ref[0]
    band = lax.axis_index("grp")
    rows, cols = gy_ref.shape[0], gy_ref.shape[1]
    edge = jnp.zeros((rows, SLOTS, CH), BF)
    gs_ref[:, 0] = edge
    gs_ref[:, cols + 1] = edge

    place_next = to_slots(16, SLOTS, own_and_next(count, blocks))
    halves = []
    for q in range(rows * cols // 64):
        four = slice(q * 4, q * 4 + 4)
        piece = jnp.concatenate(
            [cot_ref[0:OWN, four].reshape(OWN, 16, CH), nxt_ref[:, four].reshape(2, 16, CH)], 0
        ).reshape(SLOTS * 16, CH)
        halves.append(mm(place_next, piece).astype(BF))
    placed = jnp.concatenate(halves, 0)
    cott_ref[...] = placed.reshape(rows // 2, cols // 2, SLOTS, CH)
    all_four = mm_nt(placed, wd_ref[...].reshape(4 * CH, CH)).astype(BF)
    for i in range(2):
        for j in range(2):
            at = (i * 2 + j) * CH
            g = all_four[:, at : at + CH].reshape(rows // 2, cols // 2, SLOTS, CH)
            for r in range(rows // 2):
                for c in range(cols // 2):
                    gy_ref[2 * r + i, 2 * c + j] = g[r, c]
    last = cott_ref[rows // 2 - 1].reshape(cols // 2 * SLOTS, CH)
    first = cott_ref[0].reshape(cols // 2 * SLOTS, CH)
    if bands == 2:
        edge_refs[0][...] = jnp.where(band == 0, last, first)
    else:
        edge_refs[0][...] = last
        edge_refs[1][...] = first

    def grads_of(q, _):
        g = gy_ref[pl.ds(4 * q, 4)].reshape(4 * cols, SLOTS, CH)
        s = grad_of_temporal(g, wt_ref, count)
        gs_ref[pl.ds(4 * q, 4), 1 : cols + 1] = s.reshape(4, cols, SLOTS, CH)
        g = jnp.where(slot_mask(g.shape, count), g.astype(F32), 0.0)
        gy_ref[pl.ds(4 * q, 4)] = g.astype(BF).reshape(4, cols, SLOTS, CH)
        return 0

    lax.fori_loop(0, rows // 4, grads_of, 0, unroll=True)

    wide = rows * cols * SLOTS
    for j in range(3):
        right = gs_ref[:, 2 - j : 2 - j + cols].reshape(wide, CH)
        value = mm(at_ref[:, 256 : 256 + wide], right)
        for i in range(3):
            split_cores(value[i * CH : i * CH + CH], keep_ref, send_ref, i * 3 + j)


def forward_kernel(
    count_ref, xt_ref, upper_ref, lower_ref, cott_ref, gy_ref, wt_ref, wd_ref, *rest
):
    down_ref, keep_ref, send_ref, y_ref, st_ref, yt_ref = rest[-6:]
    count = count_ref[0]
    rows, cols = xt_ref.shape[0], xt_ref.shape[1]
    for q, sp_ref in enumerate((upper_ref, lower_ref)):
        s = sp_ref[...].reshape(8 * cols * SLOTS, CH).astype(F32)
        s = s.reshape(8 * cols, SLOTS, CH)
        total = None
        for k in range(3):
            shifted = s if k == 2 else pltpu.roll(s, 2 - k, 1)
            shifted = shifted.astype(BF).reshape(8 * cols * SLOTS, CH)
            at = slice(q * 1024, q * 1024 + 1024)
            st_ref[k * CH : k * CH + CH, at] = shifted.T
            term = mm(shifted, wt_ref[k])
            total = term if total is None else total + term
        x = xt_ref[8 * q : 8 * q + 8].reshape(8 * cols, SLOTS, CH).astype(F32)
        y = jnp.where(slot_mask(x.shape, count), x + total.reshape(x.shape), 0.0).astype(BF)
        y_ref[8 * q : 8 * q + 8] = y.reshape(8, cols, SLOTS, CH)

    wide = rows * cols * SLOTS
    value = mm(st_ref[...], gy_ref[...].reshape(wide, CH))
    for k in range(3):
        split_cores(value[k * CH : k * CH + CH], keep_ref, send_ref, k)

    small = wide // 4
    total = None
    for i in range(2):
        for j in range(2):
            tiles = [
                y_ref[2 * r + i, 2 * c + j] for r in range(rows // 2) for c in range(cols // 2)
            ]
            piece = jnp.concatenate(tiles, axis=0)
            k = i * 2 + j
            yt_ref[k * CH : k * CH + CH] = piece.T
            term = mm(piece, wd_ref[k])
            total = term if total is None else total + term
    down_ref[...] = total.astype(BF)
    value = mm(yt_ref[...], cott_ref[...].reshape(small, CH))
    for k in range(4):
        split_cores(value[k * CH : k * CH + CH], keep_ref, send_ref, 3 + k)


def grad_x_kernel(
    bands, count_ref, xt_ref, gy_ref, gs_ref, top_ref, bot_ref, wt_ref, wd_ref, ws_ref, slot_ref, *rest
):
    out_ref, down_ref, token_ref, pad_ref, buf, sems = rest[-6:]
    token_ref[...] = jnp.zeros_like(token_ref)
    count = count_ref[0]
    band = lax.axis_index("grp")
    rows, cols = xt_ref.shape[0], xt_ref.shape[1]
    pad_ref[1 : rows + 1] = gs_ref[...]
    edge = jnp.zeros((SLOTS, CH), BF)
    for ref, flag, i, row in ((top_ref, band > 0, 1, 0), (bot_ref, band < bands - 1, 0, rows + 1)):
        pair = [
            mm_nt(ref[...], wd_ref[i * 2 + j]).astype(BF).reshape(cols // 2, SLOTS, CH)
            for j in range(2)
        ]
        g = jnp.stack(pair, axis=1).reshape(cols, SLOTS, CH)
        pad_ref[row, 0] = edge
        pad_ref[row, 1 : cols + 1] = grad_of_temporal(g, wt_ref, jnp.where(flag, count, 0))
        pad_ref[row, cols + 1] = edge
    back = to_frames(16)

    def rows_of(q, _):
        total = None
        for i in range(3):
            for j in range(3):
                left = pad_ref[pl.ds(4 * q + 2 - i, 4), 2 - j : 2 - j + cols].reshape(
                    4 * cols * SLOTS, CH
                )
                term = mm_nt(left, ws_ref[i * 3 + j])
                total = term if total is None else total + term
        at = 4 * q
        v = xt_ref[pl.ds(at, 4)].reshape(4 * cols * SLOTS, CH).astype(F32)
        r = lax.rsqrt(jnp.mean(v * v, axis=-1, keepdims=True) + 1e-06)
        u = v * r
        s = 0.5 + 0.5 * jnp.tanh(0.5 * u)
        gu = total * (s * (1.0 + u * (1.0 - s)))
        dot = jnp.mean(gu * u, axis=-1, keepdims=True)
        gv = r * (gu - u * dot)
        gx = gy_ref[pl.ds(at, 4)].reshape(4 * cols * SLOTS, CH).astype(F32) + gv
        gx = gx.reshape(4 * cols, SLOTS, CH)
        gx = jnp.where(slot_mask(gx.shape, count), gx, 0.0).astype(BF).reshape(4 * cols * SLOTS, CH)
        for k in range(2):
            o = mm(back, gx[k * 256 : k * 256 + 256]).astype(BF)
            buf[:, pl.ds(pl.multiple_of((2 * q + k) * 16, 16), 16), :] = o.reshape(SLOTS, 16, CH)
        return 0

    lax.fori_loop(0, rows // 4, rows_of, 0)
    copy = pltpu.make_async_copy(buf, out_ref, sems.at[0])
    copy.start()
    for q in range(down_ref.shape[1] // 4):
        o = mm(back, slot_ref[q * 256 : q * 256 + 256]).astype(BF)
        down_ref[:, q * 4 : q * 4 + 4] = o.reshape(SLOTS, 4, cols // 2, CH)
    copy.wait()


ORDER = (0, 3, 2, 1)


def plane_send_kernel(keep_ref, got_ref, *rest):
    _, p, _ = place_bits()
    for r, out in zip(ORDER, rest[-4:]):
        at = pl.ds((p ^ r) * 4, 4)
        out[...] = (keep_ref[at].astype(F32) + got_ref[at].astype(F32)).astype(BF)


def line_send_kernel(*refs):
    outs = refs[8:]
    _, _, z = place_bits()
    for out, r in zip(outs, ORDER):
        at = 0
        for chain in (refs[:4], refs[4:8]):
            parts = [ref[z ^ r].astype(F32) for ref in chain]
            n = parts[0].shape[0]
            out[at : at + n] = (parts[0] + parts[1] + parts[2] + parts[3]).astype(BF)
            at += n


def line_sum_kernel(a_ref, b_ref, c_ref, d_ref, *rest):
    out_ref = rest[-1]
    parts = [ref[...].astype(F32) for ref in (a_ref, b_ref, c_ref, d_ref)]
    out_ref[...] = (parts[0] + parts[1] + parts[2] + parts[3]).astype(BF)


def line_gather_kernel(a_ref, b_ref, c_ref, d_ref, out_ref):
    _, _, z = place_bits()
    for r, ref in zip(ORDER, (a_ref, b_ref, c_ref, d_ref)):
        out_ref[z ^ r] = ref[...]


def plane_gather_kernel(a_ref, b_ref, c_ref, d_ref, _, out_ref):
    _, p, _ = place_bits()
    for r, ref in zip(ORDER, (a_ref, b_ref, c_ref, d_ref)):
        out_ref[pl.ds((p ^ r) * 4, 4)] = ref[...]


def add_kernel(a_ref, b_ref, out_ref):
    out_ref[...] = (a_ref[...].astype(F32) + b_ref[...].astype(F32)).astype(BF)


def pass_kernel(*_):
    pass


def finish_kernel(own, half_ref, *rest):
    buf, sems = rest[-2:]
    outs = rest[-5:-2]
    core, _, _ = place_bits()
    at = pl.multiple_of((core if own else 1 - core) * (CH // 2), CH // 2)
    copies = []
    k = 0
    for out in outs:
        for m in range(out.shape[0]):
            buf[k] = half_ref[:, k].reshape(CH, CH // 2).astype(F32)
            copies.append(
                pltpu.make_async_copy(buf.at[k], out.at[m, :, pl.ds(at, CH // 2)], sems.at[k])
            )
            copies[-1].start()
            k += 1
    for copy in copies:
        copy.wait()


VMEM = pl.BlockSpec(memory_space=pltpu.VMEM)
SMEM = pl.BlockSpec(memory_space=pltpu.SMEM)
ANY = pl.BlockSpec(memory_space=pl.ANY)
HBM = pl.BlockSpec(memory_space=pltpu.HBM)
TOKEN = (VMEM, (8, 128), F32)


def call(kernel, name, ins, outs, scratch=(), flops=0, alias=None, grant=10, moved=None):
    shapes = [jax.ShapeDtypeStruct(o[1], o[2] if len(o) > 2 else BF) for o in outs]
    if moved is None:
        moved = sum(a.size * a.dtype.itemsize for s, a in ins if s is not ANY)
        moved += sum(s.size * s.dtype.itemsize for s in shapes)
    return pl.pallas_call(
        kernel,
        out_shape=shapes,
        in_specs=[s for s, _ in ins],
        out_specs=[o[0] for o in outs],
        scratch_shapes=list(scratch),
        compiler_params=pltpu.CompilerParams(vmem_limit_bytes=grant * 2**20),
        cost_estimate=pl.CostEstimate(flops=flops, bytes_accessed=moved, transcendentals=0),
        input_output_aliases=alias or {},
        name=name,
    )(*[a for _, a in ins])


AXES = ("tm", "grp")


def plan(tm, grp):
    low, total = grp.bit_length() - 1, (tm * grp).bit_length() - 1
    plane, line = [low + 1, 0], [low + 2, low + 3]
    return low, plane, line, [b for b in range(total) if b not in [low] + plane + line]


def swap(value, tm, grp, *bits):
    flip = sum(1 << b for b in bits)
    return lax.ppermute(value, AXES, [(d, d ^ flip) for d in range(tm * grp)])


def core_round(value, tm, grp):
    return swap(value, tm, grp, plan(tm, grp)[0])


def four_round(parts, bits, tm, grp):
    return [
        parts[0],
        swap(parts[1], tm, grp, *bits),
        swap(parts[2], tm, grp, bits[1]),
        swap(parts[3], tm, grp, bits[0]),
    ]


def plane_send(keep, got, after):
    ins = [(VMEM, keep), (VMEM, got)] + [(ANY, a) for a in after]
    shape = (4, keep.shape[1], 16, CH // 2)
    return list(call(plane_send_kernel, "plane_send", ins, [(VMEM, shape)] * 4))


def passed(value, after):
    ins = [(ANY, value)] + [(ANY, a) for a in after]
    return call(pass_kernel, "pass", ins, [(ANY, value.shape)], alias={0: 0})[0]


def finish(own, half, before):
    n = half.shape[1]
    return list(
        call(
            functools.partial(finish_kernel, own),
            "finish",
            [(VMEM, half)] + [(HBM, a) for a in before],
            [(HBM, (m, CH, CH), F32) for m in (9, 3, 4)],
            [pltpu.VMEM((n, CH, CH // 2), F32), pltpu.SemaphoreType.DMA((n,))],
            alias={1 + i: i for i in range(len(before))},
        )
    )


def along(value, axis, by):
    count = lax.axis_size(axis)
    pairs = [(i, i + by) for i in range(count) if 0 <= i + by < count]
    return lax.ppermute(value, axis, pairs)


def around(value, axis, by):
    count = lax.axis_size(axis)
    return lax.ppermute(value, axis, [(i, (i + by) % count) for i in range(count)])


def from_bands(parts):
    if len(parts) == 1:
        got = lax.ppermute(parts[0], "grp", [(0, 1), (1, 0)])
        return got, got
    return along(parts[0], "grp", 1), along(parts[1], "grp", -1)


def body(tm, grp, frames_in, span_frames, w_spatial, w_temporal, w_down, cotangent):
    slots, rows, cols, ch = frames_in.shape
    wide = rows * cols
    x = frames_in.reshape(slots, wide, ch)
    ws = w_spatial.reshape(9, ch, ch)
    wd = w_down.reshape(4, ch, ch)
    wt = w_temporal
    count = (SMEM, span_frames)
    tap = 2 * slots * wide * ch * ch
    tile = (rows, cols, slots, ch)
    padded = (rows + 2, cols + 2, slots, ch)
    dma = pltpu.SemaphoreType.DMA

    sides = 1 if grp == 2 else 2
    edge = call(
        functools.partial(edges_kernel, grp),
        "edges",
        [count, (VMEM, x)],
        [(VMEM, (cols * slots, ch))] * sides,
        flops=tap // 8,
    )
    top, bot = from_bands(edge)
    last_shape = (2 * wide + 32, ch)
    at_shape = (3 * ch, (rows + 4) * 128)
    xt, acts, at, last_two = call(
        acts_kernel,
        "acts",
        [count, (VMEM, x), (ANY, edge[0])],
        [(VMEM, tile), (VMEM, padded), (VMEM, at_shape), (VMEM, last_shape)],
        flops=2 * tap,
    )
    (nxt,) = call(
        next_kernel,
        "next",
        [(VMEM, cotangent), (ANY, last_two)],
        [(VMEM, (2,) + cotangent.shape[1:])],
        moved=1024,
    )
    nxt_got = along(nxt, "tm", -1)
    acts, at, last_two = call(
        functools.partial(halo_kernel, grp),
        "halo",
        [count, (VMEM, top), (VMEM, bot), (VMEM, acts), (VMEM, at), (VMEM, last_two), (ANY, nxt),
         (VMEM, cotangent), (VMEM, wt), (VMEM, wd)],
        [(VMEM, padded), (VMEM, at_shape), (VMEM, last_shape)],
        alias={3: 0, 4: 1, 5: 2},
        moved=1024,
    )
    prev = around(last_two, "tm", 1)
    half = (16, 9, 16, ch // 2)
    cott, gy, gs, keep_a, send_a, *edge = call(
        functools.partial(grad_spatial_kernel, tm, grp),
        "grad_spatial",
        [count, (VMEM, at), (VMEM, cotangent), (VMEM, nxt_got), (VMEM, wt), (VMEM, wd)],
        [(VMEM, (rows // 2, cols // 2, slots, ch)), (VMEM, tile),
         (VMEM, (rows, cols + 2, slots, ch)), (VMEM, half), (VMEM, half)]
        + [(VMEM, (cols // 2 * slots, ch))] * sides,
        flops=14 * tap,
    )
    send_a = passed(send_a, [prev])
    got_a = core_round(send_a, tm, grp)
    cot_top, cot_bot = from_bands(edge)
    half_tile = (rows // 2, cols, slots, ch)
    acts, upper = call(
        upper_kernel,
        "spatial_upper",
        [(VMEM, acts), (VMEM, prev), (VMEM, ws), (ANY, send_a)],
        [(VMEM, padded), (VMEM, half_tile)],
        flops=5 * tap,
        alias={0: 0},
    )
    _, plane, line, others = plan(tm, grp)
    parts_a = plane_send(keep_a, got_a, [upper])
    (lower,) = call(
        lower_kernel,
        "spatial_lower",
        [(VMEM, acts), (VMEM, ws)] + [(ANY, a) for a in parts_a],
        [(VMEM, half_tile)],
        flops=4 * tap,
    )
    half = (16, 7, 16, ch // 2)
    down, keep_b, send_b = call(
        forward_kernel,
        "forward",
        [count, (VMEM, xt), (VMEM, upper), (VMEM, lower), (VMEM, cott), (VMEM, gy), (VMEM, wt), (VMEM, wd),
         *((ANY, a) for a in parts_a)],
        [(VMEM, (slots * wide // 4, ch)), (VMEM, half), (VMEM, half)],
        [pltpu.VMEM(v, BF) for v in (tile, (3 * ch, slots * wide), (4 * ch, slots * wide // 4))],
        moved=1024,
        grant=14,
    )
    parts_a = four_round(parts_a, plane, tm, grp)
    send_b = passed(send_b, parts_a[1:2])
    parts_b = plane_send(keep_b, core_round(send_b, tm, grp), [])
    parts_b = four_round(parts_b, plane, tm, grp)
    parts = call(
        line_send_kernel,
        "line_send",
        [(VMEM, a) for a in parts_a + parts_b],
        [(VMEM, (16, 16, ch // 2))] * 4,
    )
    parts = four_round(list(parts), line, tm, grp)
    ins = [(VMEM, a) for a in parts]
    (mine,) = call(line_sum_kernel, "line_sum", ins, [(VMEM, parts[0].shape)])
    for bit in others:
        got = swap(mine, tm, grp, bit)
        (mine,) = call(add_kernel, "add", [(VMEM, mine), (VMEM, got)], [(VMEM, mine.shape)])
    parts = four_round([mine] * 4, line, tm, grp)
    (mine,) = call(
        line_gather_kernel, "line_gather", [(VMEM, a) for a in parts], [(VMEM, (4,) + mine.shape)]
    )
    parts = four_round([mine] * 4, plane, tm, grp)
    grad_x, down, token = call(
        functools.partial(grad_x_kernel, grp),
        "grad_x",
        [count, (VMEM, xt), (VMEM, gy), (VMEM, gs), (VMEM, cot_top), (VMEM, cot_bot), (VMEM, wt),
         (VMEM, wd), (VMEM, ws), (VMEM, down), (ANY, mine)],
        [(HBM, (slots, wide, ch)), (VMEM, cotangent.shape), TOKEN],
        [pltpu.VMEM(padded, BF), pltpu.VMEM((slots, wide, ch), BF), dma((1,))],
        flops=10 * tap,
    )
    ins = [(VMEM, a) for a in parts] + [(ANY, token)]
    (mine,) = call(plane_gather_kernel, "plane_gather", ins, [(VMEM, (16,) + mine.shape[1:])])
    got = core_round(mine, tm, grp)
    outs = finish(True, mine, [])
    sum_s, sum_t, sum_d = finish(False, got, outs)
    return (
        down,
        grad_x.reshape(frames_in.shape),
        sum_s.reshape(w_spatial.shape),
        sum_t,
        sum_d.reshape(w_down.shape),
    )


def solution(mesh):
    return jax.shard_map(
        functools.partial(body, mesh.shape["tm"], mesh.shape["grp"]),
        mesh=mesh,
        in_specs=(P("tm", "grp", None, None), P("tm"), P(), P(), P(), P("tm", "grp", None, None)),
        out_specs=(P("tm", "grp", None, None), P("tm", "grp", None, None), P(), P(), P()),
        check_vma=False,
    )
```
